32 devices in a mesh: dp: 8 (over y, x, core), mp: 4 (over z).
Axes of the slice: x: 2, y: 2, z: 4, core: 2. Of those that a mesh axis runs over, the one named last changes fastest.
Arguments:
- tokens: bfloat16 [8192, 2048], P('dp'), may hold values from -6 to 6
- cotangent: bfloat16 [8192, 2048], P('dp'), may hold values from -6 to 6
- doc_lengths: int32 [8, 5], P('dp'), may hold values from 1 to 1020, as said below
- w_z: float32 [2048, 4096], P('dp', 'mp'), may hold values from -0.125 to 0.125
- w_x: float32 [2048, 4096], P('dp', 'mp'), may hold values from -0.125 to 0.125
- w_bc: float32 [2048, 256], P('dp', 'mp'), may hold values from -0.125 to 0.125
- w_dt: float32 [2048, 64], P('dp', 'mp'), may hold values from -0.125 to 0.125
- w_out: float32 [4096, 2048], P('mp', 'dp'), may hold values from -0.09375 to 0.09375
- conv_x: float32 [4, 4096], P(None, 'mp'), may hold values from -3 to 3
- conv_x_bias: float32 [4096], P('mp'), may hold values from -3 to 3
- conv_bc: float32 [4, 256], P(None, 'mp'), may hold values from -3 to 3
- conv_bc_bias: float32 [256], P('mp'), may hold values from -3 to 3
- dt_bias: float32 [64], P('mp'), may hold values from -1 to 1
- a_rate: float32 [64], P('mp'), may hold values from 0.0001 to 0.04
- d_skip: float32 [64], P('mp'), may hold values from 0.5 to 1.5
- input_norm_gain: float32 [2048], replicated, may hold values from 0.25 to 1.75
- out_gain: float32 [4096], P('mp'), may hold values from 0.25 to 1.75
Outputs:
- output: bfloat16 [8192, 2048], P('dp', 'mp')
- input_grad: bfloat16 [8192, 2048], P('dp', 'mp')
- w_z_grad: float32 [2048, 4096], P('dp', 'mp')
- w_x_grad: float32 [2048, 4096], P('dp', 'mp')
- w_bc_grad: float32 [2048, 256], P('dp', 'mp')
- w_dt_grad: float32 [2048, 64], P('dp', 'mp')
- w_out_grad: float32 [4096, 2048], P('mp', 'dp')
- conv_x_grad: float32 [4, 4096], P(None, 'mp')
- conv_x_bias_grad: float32 [4096], P('mp')
- conv_bc_grad: float32 [4, 256], P(None, 'mp')
- conv_bc_bias_grad: float32 [256], P('mp')
- dt_bias_grad: float32 [64], P('mp')
- a_rate_grad: float32 [64], P('mp')
- d_skip_grad: float32 [64], P('mp')
- in_gain_grad: float32 [2048], P('mp')
- out_gain_grad: float32 [4096], P('mp')
The draws below stay inside these ranges and needn't reach their ends.
Inputs may be any that keep to these rules, and one draw needn't show every extreme that they name: `doc_lengths`: row s lists the 5 documents of sequence s in order; they sum to 1024. The first two together and the last two together are each shorter than 256 tokens, so the third document starts within the first 256 tokens and ends within the last 256. Some row has a document of 1 token and a third document of 1020 tokens.
All inputs are finite; a program needn't handle non-finite values.
Results may differ from the reference program's by a relative error of at most 0.02.
The reference program's roundings to bfloat16 on the way count: a program that leaves them out, or rounds other values in their place, can miss the bound.
Values may be sent and summed in bfloat16 or wider, within the bound.
A program may use at most 320 MiB of HBM per device.

```python
import math
import jax
import jax.numpy as jnp
from jax import lax

D = 2048
INNER = 4096
HEADS = 64
HEADDIM = 64
STATE = 128
CONV = 4
BLOCK = 256
SHARD = 256
LENGTH = 1024
SEQS = 8
TOKENS = 8192


def draw_doc_lengths(key, part):
    key = jax.random.fold_in(key, 7)
    keys = jax.random.split(key, 5)
    lead_total = jax.random.randint(keys[0], (SEQS,), 2, SHARD)
    tail_total = jax.random.randint(keys[1], (SEQS,), 2, SHARD)
    chosen = jax.random.randint(keys[2], (), 0, SEQS)
    row_ids = jnp.arange(SEQS)
    lead_total = jnp.where(row_ids == chosen, 2, lead_total)
    tail_total = jnp.where(row_ids == chosen, 2, tail_total)
    first_doc = jax.random.randint(keys[3], (SEQS,), 1, lead_total)
    fourth_doc = jax.random.randint(keys[4], (SEQS,), 1, tail_total)
    middle_doc = LENGTH - lead_total - tail_total
    stacked = jnp.stack([first_doc, lead_total - first_doc, middle_doc, fourth_doc, tail_total - fourth_doc], axis=1)
    return stacked.astype(jnp.int32)


def raised(result, stream_key, source, target, parts, factor):
    owner, partner = [(jnp.arange(result.shape[axis_at]) // (result.shape[axis_at] // parts)).reshape([-1 if axis == axis_at else 1 for axis in range(result.ndim)]) for axis_at in (source, target)]
    chosen = jax.random.permutation(stream_key, parts)[partner]
    strong = (owner == chosen) | (owner == (partner + parts // 2) % parts)
    return jnp.where(strong, factor * result, result)


def shard_levels(key, shape, cuts, least, largest):
    def one(dim, parts):
        heights = jax.random.uniform(jax.random.fold_in(jax.random.fold_in(key, 6), dim), (parts,), jnp.float32, least / len(cuts), largest / len(cuts))
        return jnp.repeat(jnp.exp(heights), shape[dim] // parts).reshape((-1,) + (1,) * (len(shape) - dim - 1))

    gain = one(*cuts[0])
    for cut in cuts[1:]:
        gain = gain * one(*cut)
    return gain


def normal_values(own_key, shape, deviation, bound, cuts=(), kind=jnp.bfloat16):
    level = shard_levels(own_key, shape, cuts, -0.22, 0.18) if cuts else 1.0
    drawn = jax.random.normal(own_key, shape, jnp.float32) * deviation * level
    return jnp.minimum(jnp.maximum(drawn, -bound), bound).astype(kind)


def heavy_noise(rng, shape, scale, reach, cuts, heavy, kind=jnp.bfloat16):
    entries = scale * jax.random.normal(rng, shape, jnp.float32)
    if cuts:
        entries = entries * shard_levels(rng, shape, cuts, -0.22, 0.18)
    return jnp.clip(raised(entries, jax.random.fold_in(rng, 3), *heavy), -reach, reach).astype(kind)


def setup_inputs(seed: int = 0) -> dict:
    splits = jax.random.split(jax.random.key(seed), 18)
    tokens = heavy_noise(splits[0], (TOKENS, D), 1.0, 6.0, ((0, 8),), (0, 1, 8, 2.0))
    cotangent = heavy_noise(splits[1], (TOKENS, D), 1.0, 6.0, ((0, 8),), (0, 1, 8, 2.0))
    doc_lengths = draw_doc_lengths(jax.random.fold_in(splits[17], 71), 0)
    w_z = normal_values(splits[3], (D, INNER), D ** -0.5, 0.125, ((0, 8), (1, 4)), jnp.float32)
    w_x = normal_values(splits[4], (D, INNER), D ** -0.5, 0.125, ((0, 8), (1, 4)), jnp.float32)
    w_bc = normal_values(splits[5], (D, 2 * STATE), D ** -0.5, 0.125, ((0, 8), (1, 4)), jnp.float32)
    w_dt = normal_values(splits[6], (D, HEADS), D ** -0.5, 0.125, ((0, 8), (1, 4)), jnp.float32)
    w_out = normal_values(splits[7], (INNER, D), INNER ** -0.5, 0.09375, ((0, 4), (1, 8)), jnp.float32)
    conv_x = normal_values(splits[8], (CONV, INNER), CONV ** -0.5, 3.0, ((1, 4),), jnp.float32)
    conv_x_bias = normal_values(splits[9], (INNER,), 0.5, 3.0, ((0, 4),), jnp.float32)
    conv_bc = normal_values(splits[10], (CONV, 2 * STATE), CONV ** -0.5, 3.0, ((1, 4),), jnp.float32)
    conv_bc_bias = normal_values(splits[11], (2 * STATE,), 0.5, 3.0, ((0, 4),), jnp.float32)
    dt_bias = jnp.clip(jax.random.uniform(splits[12], (HEADS,), jnp.float32, -1.0, 1.0) * shard_levels(splits[12], (HEADS,), ((0, 4),), -0.4, 0.0), -1.0, 1.0)
    a_rate = jnp.clip(jnp.exp(math.log(0.04) - 5.9914646 * jax.random.uniform(splits[13], (HEADS,), jnp.float32) ** shard_levels(splits[13], (HEADS,), ((0, 4),), -0.2, 0.2)), 0.0001, 0.04)
    d_skip = jnp.clip(0.5 + 1.0 * jax.random.uniform(splits[14], (HEADS,), jnp.float32) ** shard_levels(splits[14], (HEADS,), ((0, 4),), -0.2, 0.2), 0.5, 1.5)
    input_norm_gain = jnp.clip(1.0 + 0.15 * jax.random.normal(splits[15], (D,), jnp.float32), 0.25, 1.75)
    out_gain = jnp.clip(1.0 + 0.15 * jax.random.normal(splits[16], (INNER,), jnp.float32), 0.25, 1.75)
    return dict(tokens=tokens, cotangent=cotangent, doc_lengths=doc_lengths, w_z=w_z, w_x=w_x, w_bc=w_bc, w_dt=w_dt, w_out=w_out, conv_x=conv_x, conv_x_bias=conv_x_bias, conv_bc=conv_bc, conv_bc_bias=conv_bc_bias, dt_bias=dt_bias, a_rate=a_rate, d_skip=d_skip, input_norm_gain=input_norm_gain, out_gain=out_gain)


@jax.custom_vjp
def low(v):
    return lax.optimization_barrier(v.astype(jnp.bfloat16)).astype(jnp.float32)

@jax.custom_vjp
def low_back(v):
    return v

def low_keep(v):
    return (low(v), None)

def low_pass(kept, grad):
    return (grad,)

def back_keep(v):
    return (v, None)

def back_low(kept, grad):
    return (low(grad),)
low.defvjp(low_keep, low_pass)
low_back.defvjp(back_keep, back_low)
eps_norm = 1e-05
exact = lax.Precision.HIGHEST

def product(left, right):
    return jnp.dot(left, right, precision=exact, preferred_element_type=jnp.float32)

def document_marks(lengths, positions):
    starts = jnp.cumsum(lengths) - lengths
    doc_ids = lax.optimization_barrier(jnp.sum((positions[:, None] >= starts[None, :]).astype(jnp.int32), axis=1)) - 1
    resets = lax.optimization_barrier(jnp.sum((positions[:, None] == starts[None, :]).astype(jnp.float32), axis=1))
    return (doc_ids, resets)

def causal_conv(values, conv_taps, conv_shift, doc_ids):
    row_count = values.shape[0]
    summed = conv_shift[None, :] + conv_taps[CONV - 1][None, :] * values
    for lag_steps in range(1, CONV):
        shifted_in = jnp.pad(values, ((lag_steps, 0), (0, 0)))[:row_count]
        earlier_doc = jnp.pad(doc_ids, (lag_steps, 0), constant_values=-1)[:row_count]
        summed = summed + conv_taps[CONV - 1 - lag_steps][None, :] * jnp.where((earlier_doc == doc_ids)[:, None], shifted_in, 0.0)
    return jax.nn.silu(summed)

def block_step(carried, pieces):
    x_heads, b_rows, c_rows, dt_rows, decay_rows, reset_rows = pieces
    block_rows = reset_rows.shape[0]
    segment = jnp.cumsum(reset_rows)
    order_ids = jnp.arange(block_rows)
    linked = (segment[:, None] == segment[None, :]) & (order_ids[:, None] >= order_ids[None, :])
    decay_sum = jnp.cumsum(decay_rows, axis=0).T
    log_spans = decay_sum[:, :, None] - decay_sum[:, None, :]
    kernel = jnp.where(linked[None], jnp.exp(jnp.where(linked[None], log_spans, 0.0)), 0.0)
    scores = jnp.dot(c_rows, b_rows.T, precision=exact, preferred_element_type=jnp.float32)
    mixing = kernel * scores[None] * dt_rows.T[:, None, :]
    y_rows = jnp.einsum('hij,jhp->ihp', mixing, x_heads, precision=exact)
    inflow = jnp.where((segment == 0)[None, :], jnp.exp(decay_sum), 0.0)
    y_rows = y_rows + inflow.T[:, :, None] * jnp.einsum('in,hpn->ihp', c_rows, carried, precision=exact)
    ending = segment[block_rows - 1]
    leaving = jnp.where((segment == ending)[None, :], jnp.exp(decay_sum[:, block_rows - 1:] - decay_sum), 0.0) * dt_rows.T
    fresh_part = jnp.einsum('hj,jhp,jn->hpn', leaving, x_heads, b_rows, precision=exact)
    kept_part = jnp.where(ending == 0, jnp.exp(decay_sum[:, block_rows - 1]), 0.0)
    return (kept_part[:, None, None] * carried + fresh_part, y_rows)

def local_scan(seq_x, seq_bc, seq_dt, seq_decay, resets):
    token_count, inner_width = seq_x.shape
    head_count = seq_dt.shape[1]
    blocks = token_count // BLOCK
    pieces = (seq_x.reshape(blocks, BLOCK, head_count, inner_width // head_count), seq_bc[:, :STATE].reshape(blocks, BLOCK, STATE), seq_bc[:, STATE:].reshape(blocks, BLOCK, STATE), seq_dt.reshape(blocks, BLOCK, head_count), seq_decay.reshape(blocks, BLOCK, head_count), resets.reshape(blocks, BLOCK))
    zero_state = jnp.zeros((head_count, inner_width // head_count, STATE), jnp.float32)
    ending, outputs = lax.scan(jax.checkpoint(block_step), zero_state, pieces)
    factor = jnp.exp(lax.optimization_barrier(jnp.sum(seq_decay, axis=0))) * (jnp.sum(resets) == 0).astype(jnp.float32)
    return (outputs.reshape(token_count, inner_width), ending, factor)

def sequence_block(token_rows, lengths, params):
    w_z, w_x, w_bc, w_dt, w_out, conv_x, conv_x_bias, conv_bc, conv_bc_bias, dt_bias, a_rate, d_skip, input_norm_gain, out_gain = params
    doc_ids, resets = document_marks(lengths, jnp.arange(LENGTH, dtype=jnp.int32))
    inverse_root = lax.rsqrt(lax.optimization_barrier(jnp.mean(token_rows * token_rows, axis=1, keepdims=True)) + eps_norm)
    normed = low(token_rows * inverse_root * input_norm_gain)
    gate_in = low_back(product(normed, w_z))
    x_in = low_back(product(normed, w_x))
    bc_in = low_back(product(normed, w_bc))
    dt_in = low_back(product(normed, w_dt))
    x_conv = causal_conv(x_in, conv_x, conv_x_bias, doc_ids)
    bc_conv = causal_conv(bc_in, conv_bc, conv_bc_bias, doc_ids)
    step_size = jax.nn.softplus(dt_in + dt_bias)
    decay_log = -a_rate * step_size
    x_low = low(x_conv)
    ssd_out, ending, factor = local_scan(low_back(x_low), low_back(low(bc_conv)), low_back(low(step_size)), low_back(low(decay_log)), resets)
    mixed_rows = low_back(low(ssd_out)) + jnp.repeat(d_skip, HEADDIM)[None, :] * x_low
    gated = mixed_rows * jax.nn.silu(gate_in)
    inverse_out = lax.rsqrt(lax.optimization_barrier(jnp.mean(gated * gated, axis=1, keepdims=True)) + eps_norm)
    gated_norm = low(gated * inverse_out * out_gain)
    return token_rows + product(gated_norm, w_out)

def reference(tokens, cotangent, doc_lengths, w_z, w_x, w_bc, w_dt, w_out, conv_x, conv_x_bias, conv_bc, conv_bc_bias, dt_bias, a_rate, d_skip, input_norm_gain, out_gain):
    params = (w_z, w_x, w_bc, w_dt, w_out, conv_x, conv_x_bias, conv_bc, conv_bc_bias, dt_bias, a_rate, d_skip, input_norm_gain, out_gain)

    def forward(token_rows, weights):
        rounded = tuple((low(matrix) for matrix in weights[:5])) + tuple(weights[5:])

        def one_sequence(carried, pieces):
            return (carried, jax.checkpoint(sequence_block)(pieces[0], pieces[1], rounded))
        _, outputs = lax.scan(one_sequence, jnp.zeros((), jnp.float32), (token_rows.reshape(SEQS, LENGTH, D), doc_lengths))
        return outputs.reshape(TOKENS, D)
    output, pullback = jax.vjp(forward, tokens.astype(jnp.float32), params)
    input_grad, weight_grads = pullback(cotangent.astype(jnp.float32))
    w_z_grad, w_x_grad, w_bc_grad, w_dt_grad, w_out_grad, conv_x_grad, conv_x_bias_grad, conv_bc_grad, conv_bc_bias_grad, dt_bias_grad, a_rate_grad, d_skip_grad, in_gain_grad, out_gain_grad = weight_grads
    return (output.astype(jnp.bfloat16), input_grad.astype(jnp.bfloat16), w_z_grad, w_x_grad, w_bc_grad, w_dt_grad, w_out_grad, conv_x_grad, conv_x_bias_grad, conv_bc_grad, conv_bc_bias_grad, dt_bias_grad, a_rate_grad, d_skip_grad, in_gain_grad, out_gain_grad)
```

```python
import functools

import jax
import jax.numpy as jnp
from jax import lax
from jax.experimental import pallas as pl
from jax.experimental.pallas import tpu as pltpu
from jax.sharding import PartitionSpec as P

HEADDIM = 64
STATE = 128
CONV = 4
BLOCK = 256
DOCS = 5
LANES = 128
EPS = 1e-05
f32 = jnp.float32
bf16 = jnp.bfloat16
VMEM_LIMIT = 62 * 2**20


def mm(a, b):
    return jnp.dot(a, b, preferred_element_type=f32)


def mm_nt(a, b):
    return lax.dot_general(a, b, (((1,), (1,)), ((), ())), preferred_element_type=f32)


def mm_tn(a, b):
    return lax.dot_general(a, b, (((0,), (0,)), ((), ())), preferred_element_type=f32)


def halves(v):
    high = v.astype(bf16)
    return high, (v - high.astype(f32)).astype(bf16)


def expand(v, spread):
    high, rest = halves(v)
    return mm(high, spread) + mm(rest, spread)


def gather_heads(v, spread):
    high, rest = halves(v)
    return mm_nt(high, spread) + mm_nt(rest, spread)


def logistic(v):
    return 1.0 / (1.0 + jnp.exp(-v))


def tiles(total, size):
    return [(at, min(size, total - at)) for at in range(0, total, size)]


def fold(v):
    return jnp.sum(v.reshape(v.shape[0] // 8, 8, v.shape[1]), axis=0)


def doc_of(starts, place):
    count = (place >= starts[0]).astype(jnp.int32)
    for k in range(1, DOCS):
        count = count + (place >= starts[k]).astype(jnp.int32)
    return count


def fill_spread(spread):
    rows, columns = spread.shape
    head = lax.broadcasted_iota(jnp.int32, (rows, columns), 0)
    channel = lax.broadcasted_iota(jnp.int32, (rows, columns), 1)
    low = head * HEADDIM
    spread[...] = jnp.where((channel >= low) & (channel < low + HEADDIM), 1.0, 0.0).astype(bf16)


def fill_positions(starts, pos, rpos):
    length = pos.shape[0]

    def body(i, carry):
        at = pl.multiple_of(i * BLOCK, BLOCK)
        place = lax.broadcasted_iota(jnp.int32, (BLOCK, LANES), 0) + at
        begin = jnp.zeros_like(place)
        end = jnp.full_like(place, length)
        for k in range(DOCS):
            begin = jnp.maximum(begin, jnp.where(place >= starts[k], starts[k], 0))
            end = jnp.minimum(end, jnp.where(place < starts[k], starts[k], length))
        pos[pl.ds(at, BLOCK), :] = place - begin
        if rpos is not None:
            rpos[pl.ds(at, BLOCK), :] = end - 1 - place
        return carry

    lax.fori_loop(0, length // BLOCK, body, 0)


def normalize(tok, gain, normed, stat):
    step = 64

    def body(i, carry):
        rows = pl.ds(pl.multiple_of(i * step, step), step)
        v = tok[rows, :].astype(f32)
        inverse = lax.rsqrt(jnp.mean(v * v, axis=1, keepdims=True) + EPS)
        normed[rows, :] = (v * inverse * gain[...]).astype(bf16)
        stat[rows, :] = jnp.broadcast_to(inverse, (step, LANES))
        return carry

    lax.fori_loop(0, tok.shape[0] // step, body, 0)


def project_x(normed, wxd, xin, dtin):
    length, width = normed.shape[0], xin.shape[1]
    xin[pl.ds(0, 8), :] = jnp.zeros((8, width), f32)
    rows = 512

    def body(i, carry):
        at = pl.multiple_of(i * rows, rows)
        left = normed[pl.ds(at, rows), :]
        for c, w in tiles(width, 512):
            xin[pl.ds(at + 8, rows), c : c + w] = mm(left, wxd[:, c : c + w])
        dtin[pl.ds(at, rows), :] = mm(left, wxd[:, width : width + LANES])
        return carry

    lax.fori_loop(0, length // rows, body, 0)


def convolve(xin, taps, pos, slope, x_low, bc_low):
    width, inner = xin.shape[1], x_low.shape[1]

    def tile(b, c, out, at):
        rows = pl.ds(pl.multiple_of(b * BLOCK, BLOCK), BLOCK)
        x = xin[pl.ds(pl.multiple_of(b * BLOCK, BLOCK), BLOCK + 8), pl.ds(c, LANES)]
        place = pos[rows, :]
        tap = taps[:, pl.ds(c, LANES)]
        pre = tap[CONV : CONV + 1] + tap[CONV - 1 : CONV] * x[8:]
        for lag in range(1, CONV):
            earlier = pltpu.roll(x, lag, 0)[8:]
            pre = pre + tap[CONV - 1 - lag : CONV - lag] * jnp.where(place >= lag, earlier, 0.0)
        sg = logistic(pre)
        slope[rows, pl.ds(c, LANES)] = sg * (1.0 + pre * (1.0 - sg))
        out[rows, pl.ds(at, LANES)] = (pre * sg).astype(bf16)

    blocks = x_low.shape[0] // BLOCK
    xcols, bcols = inner // LANES, (width - inner) // LANES

    def x_body(i, carry):
        c = pl.multiple_of((i % xcols) * LANES, LANES)
        tile(i // xcols, c, x_low, c)
        return carry

    def bc_body(i, carry):
        c = pl.multiple_of((i % bcols) * LANES, LANES)
        tile(i // bcols, inner + c, bc_low, c)
        return carry

    lax.fori_loop(0, blocks * xcols, x_body, 0)
    lax.fori_loop(0, blocks * bcols, bc_body, 0)


def steps(dtin, dpar, step, sgdt, step_low, decay_low):
    def body(i, carry):
        rows = pl.ds(pl.multiple_of(i * BLOCK, BLOCK), BLOCK)
        v = dtin[rows, :] + dpar[0:1, :]
        soft = jnp.maximum(v, 0.0) + jnp.log1p(jnp.exp(-jnp.abs(v)))
        step[rows, :] = soft
        sgdt[rows, :] = logistic(v)
        step_low[rows, :] = soft.astype(bf16)
        decay_low[rows, :] = (-dpar[1:2, :] * soft).astype(bf16)
        return carry

    lax.fori_loop(0, dtin.shape[0] // BLOCK, body, 0)


def block_marks(starts, b):
    at = b * BLOCK
    column = doc_of(starts, lax.broadcasted_iota(jnp.int32, (BLOCK, 1), 0) + at)
    row = doc_of(starts, lax.broadcasted_iota(jnp.int32, (1, BLOCK), 1) + at)
    before = doc_of(starts, at - 1)
    last = doc_of(starts, at + BLOCK - 1)
    return column, row, before, last


def block_decays(b, starts, decay_low, step_low, spread):
    rows = pl.ds(pl.multiple_of(b * BLOCK, BLOCK), BLOCK)
    column, row, before, last = block_marks(starts, b)
    i0 = lax.broadcasted_iota(jnp.int32, (BLOCK, BLOCK), 0)
    i1 = lax.broadcasted_iota(jnp.int32, (BLOCK, BLOCK), 1)
    lower = jnp.where(i0 >= i1, 1.0, 0.0).astype(bf16)
    cum = mm(lower, decay_low[rows, :])
    step_e = mm(step_low[rows, :], spread[...])
    cum_e = expand(jnp.exp(cum), spread[...])
    kept_e = jnp.where(before == last, cum_e[BLOCK - 1 : BLOCK], 0.0)
    in_e = jnp.where(column == before, cum_e, 0.0)
    out_e = expand(jnp.exp(cum[BLOCK - 1 : BLOCK] - cum), spread[...])
    out_e = jnp.where(column == last, out_e, 0.0)
    return cum, step_e, kept_e, in_e, out_e, column, row


def scan_forward(starts, x_low, bc_low, step_low, decay_low, ssd, states, spread, state, xs, yin, cbm):
    length, inner = x_low.shape
    state[...] = jnp.zeros_like(state)

    def body(b, carry):
        rows = pl.ds(pl.multiple_of(b * BLOCK, BLOCK), BLOCK)
        cum, step_e, kept_e, in_e, out_e, column, row = block_decays(
            b, starts, decay_low, step_low, spread
        )
        bm, cm = bc_low[rows, :STATE], bc_low[rows, STATE:]
        i0 = lax.broadcasted_iota(jnp.int32, (BLOCK, BLOCK), 0)
        i1 = lax.broadcasted_iota(jnp.int32, (BLOCK, BLOCK), 1)
        cbm[...] = jnp.where((column == row) & (i0 >= i1), mm_nt(cm, bm), 0.0)
        stepped = x_low[rows, :].astype(f32) * step_e
        xs[...] = stepped.astype(bf16)
        entering = state[...].astype(bf16)
        states[b] = entering
        yin[...] = in_e * mm(cm, entering)
        state[...] = kept_e * state[...] + mm_tn(bm, (stepped * out_e).astype(bf16))
        cum_t = cum.T
        first = lax.broadcasted_iota(jnp.int32, (BLOCK, LANES), 1) < HEADDIM
        for j in range(inner // LANES):
            cols = slice(j * LANES, (j + 1) * LANES)
            pair = xs[:, cols]
            part = []
            for h in (2 * j, 2 * j + 1):
                span = jnp.minimum(cum[:, h : h + 1] - cum_t[h : h + 1, :], 0.0)
                part.append(mm((jnp.exp(span) * cbm[...]).astype(bf16), pair))
            y = jnp.where(first, part[0], part[1]) + yin[:, cols]
            ssd[rows, cols] = y.astype(bf16)
        return carry

    lax.fori_loop(0, length // BLOCK, body, 0)


def project_rows(left, right, out, rows=512, columns=512):
    def body(i, carry):
        at = pl.ds(pl.multiple_of(i * rows, rows), rows)
        part = left[at, :]
        for c, w in tiles(out.shape[1], columns):
            out[at, c : c + w] = mm(part, right[:, c : c + w]).astype(out.dtype)
        return carry

    lax.fori_loop(0, out.shape[0] // rows, body, 0)


def back_rows(left, right, out, rows=512, columns=512):
    def body(i, carry):
        at = pl.ds(pl.multiple_of(i * rows, rows), rows)
        part = left[at, :]
        for c, w in tiles(out.shape[1], columns):
            out[at, c : c + w] = mm_nt(part, right[c : c + w, :]).astype(out.dtype)
        return carry

    lax.fori_loop(0, out.shape[0] // rows, body, 0)


def weight_rows(left, right, out, rows=256, columns=512):
    def body(i, carry):
        at = pl.ds(pl.multiple_of(i * rows, rows), rows)
        part = left[:, at]
        for c, w in tiles(out.shape[1], columns):
            out[at, c : c + w] = mm_tn(part, right[:, c : c + w]).astype(out.dtype)
        return carry

    lax.fori_loop(0, out.shape[0] // rows, body, 0)


def gate_sums(gate, ssd, x_low, gnorm, crow, stat):
    step, inner = 64, gate.shape[1]

    def body(i, carry):
        rows = pl.ds(pl.multiple_of(i * step, step), step)
        squares = jnp.zeros((step, 256), f32)
        crosses = jnp.zeros((step, 256), f32)
        for c in range(0, inner, 256):
            cols = slice(c, c + 256)
            g = gate[rows, cols]
            mixed = ssd[rows, cols].astype(f32) + crow[1:2, cols] * x_low[rows, cols].astype(f32)
            gated = mixed * (g * logistic(g))
            squares = squares + gated * gated
            crosses = crosses + gnorm[rows, cols] * crow[0:1, cols] * gated
        lane = lax.broadcasted_iota(jnp.int32, (step, LANES), 1)
        s1 = jnp.sum(squares, axis=1, keepdims=True)
        s2 = jnp.sum(crosses, axis=1, keepdims=True)
        stat[rows, :] = jnp.where(lane == 0, s1, jnp.where(lane == 1, s2, 0.0))
        return carry

    lax.fori_loop(0, gate.shape[0] // step, body, 0)


def forward_kernel(
    starts, tok, gain, wxd, wz, taps, dpar,
    normed, inverse, xin, slope, gate, x_low, bc_low, step, sgdt, step_low, decay_low, ssd, states,
    pos, spread, dtin, state, xs, yin, cbm,
):
    fill_spread(spread)
    fill_positions(starts, pos, None)
    normalize(tok, gain, normed, inverse)
    project_x(normed, wxd, xin, dtin)
    convolve(xin, taps, pos, slope, x_low, bc_low)
    steps(dtin, dpar, step, sgdt, step_low, decay_low)
    scan_forward(starts, x_low, bc_low, step_low, decay_low, ssd, states, spread, state, xs, yin, cbm)
    project_rows(normed, wz, gate)


def gate_kernel(cot, wout, gate, ssd, x_low, crow, gnorm, stat):
    back_rows(cot, wout, gnorm)
    gate_sums(gate, ssd, x_low, gnorm, crow, stat)


def gate_backward(gate, ssd, x_low, gnorm, crow, stat, width, gn, low_gate, gs, sums):
    step, inner = 64, gate.shape[1]
    sums[...] = jnp.zeros_like(sums)

    def body(i, carry):
        rows = pl.ds(pl.multiple_of(i * step, step), step)
        inverse = lax.rsqrt(stat[rows, 0:1] / width + EPS)
        mean = inverse * stat[rows, 1:2] / width
        for c in range(0, inner, 256):
            cols = slice(c, c + 256)
            g = gate[rows, cols]
            x = x_low[rows, cols].astype(f32)
            mixed = ssd[rows, cols].astype(f32) + crow[1:2, cols] * x
            sg = logistic(g)
            act = g * sg
            hat = mixed * act * inverse
            gn[rows, cols] = (hat * crow[0:1, cols]).astype(bf16)
            gnorm_here = gnorm[rows, cols]
            grad = inverse * (gnorm_here * crow[0:1, cols] - hat * mean)
            grad_mixed = grad * act
            low_gate[rows, cols] = (grad * mixed * (sg * (1.0 + g * (1.0 - sg)))).astype(bf16)
            gs[rows, cols] = grad_mixed.astype(bf16)
            sums[0:8, cols] += fold(gnorm_here * hat)
            sums[8:16, cols] += fold(grad_mixed * x)
        return carry

    lax.fori_loop(0, gate.shape[0] // step, body, 0)


def middle_kernel(
    cot, wout, normed, gate, x_low, ssd, gnorm, crow, stat,
    branch, dwout, dwz, low_gate, gs, sums,
    gn, *, width,
):
    gate_backward(gate, ssd, x_low, gnorm, crow, stat, width, gn, low_gate, gs, sums)
    project_rows(gn, wout, branch)
    weight_rows(gn, cot, dwout)
    weight_rows(normed, low_gate, dwz)


def scan_backward(
    starts, x_low, bc_low, step_low, decay_low, ssd, states, gs, slope, crow, step, sgdt, dpar,
    gpre, low_xd, dsums, spread, dstate, xs, gx, cbm, acc,
):
    length, inner = x_low.shape
    width = gpre.shape[1]
    blocks = length // BLOCK
    dstate[...] = jnp.zeros_like(dstate)
    dsums[...] = jnp.zeros_like(dsums)
    gpre[pl.ds(length, 8), :] = jnp.zeros((8, width), f32)

    def body(i, carry):
        b = blocks - 1 - i
        rows = pl.ds(pl.multiple_of(b * BLOCK, BLOCK), BLOCK)
        cum, step_e, kept_e, in_e, out_e, column, row = block_decays(
            b, starts, decay_low, step_low, spread
        )
        bm, cm = bc_low[rows, :STATE], bc_low[rows, STATE:]
        i0 = lax.broadcasted_iota(jnp.int32, (BLOCK, BLOCK), 0)
        i1 = lax.broadcasted_iota(jnp.int32, (BLOCK, BLOCK), 1)
        linked = (column == row) & (i0 <= i1)
        cbm[...] = jnp.where(linked, mm_nt(bm, cm), 0.0)
        x = x_low[rows, :].astype(f32)
        stepped = x * step_e
        xs[...] = stepped.astype(bf16)
        cum_t = cum.T
        first = lax.broadcasted_iota(jnp.int32, (BLOCK, LANES), 1) < HEADDIM
        acc[...] = jnp.zeros_like(acc)
        for j in range(inner // LANES):
            cols = slice(j * LANES, (j + 1) * LANES)
            xpair, gpair = xs[:, cols], gs[rows, cols]
            none = jnp.zeros_like(xpair)
            part, total = [], None
            for k in range(2):
                h = 2 * j + k
                kernel = jnp.exp(jnp.minimum(cum_t[h : h + 1, :] - cum[:, h : h + 1], 0.0))
                part.append(mm((kernel * cbm[...]).astype(bf16), gpair))
                own = jnp.where(first, xpair, none) if k == 0 else jnp.where(first, none, xpair)
                here = kernel * mm_nt(own, gpair)
                total = here if total is None else total + here
            acc[...] += total
            gx[:, cols] = jnp.where(first, part[0], part[1])
        dstate_low = dstate[...].astype(bf16)
        entering = states[b]
        leaving = states[jnp.minimum(b + 1, blocks - 1)]
        end = jnp.sum(dstate[...] * leaving.astype(f32), axis=0, keepdims=True)
        g = gs[rows, :].astype(f32)
        g_in = (in_e * g).astype(bf16)
        raw = gx[...] + out_e * mm(bm, dstate_low)
        grad_x = (step_e * raw).astype(bf16).astype(f32)
        gpre[rows, :inner] = (grad_x + crow[1:2, :] * g) * slope[rows, :inner]
        pairs = jnp.where(linked, acc[...], 0.0).astype(bf16)
        db = mm(pairs, cm) + mm_nt((stepped * out_e).astype(bf16), dstate_low)
        dc = mm_tn(pairs, bm) + mm_nt(g_in, entering)
        gpre[rows, inner : inner + STATE] = db * slope[rows, inner : inner + STATE]
        gpre[rows, inner + STATE :] = dc * slope[rows, inner + STATE :]
        raw_x = x * raw
        grad_step = gather_heads(raw_x, spread[...]).astype(bf16).astype(f32)
        dcum = gather_heads(g * ssd[rows, :].astype(f32) - step_e * raw_x, spread[...])
        tail = gather_heads(jnp.broadcast_to(end, (8, inner)), spread[...])[0:1]
        upper = jnp.where(i0 <= i1, 1.0, 0.0).astype(bf16)
        high, rest = halves(dcum)
        later = mm(upper, high) + mm(upper, rest) + tail
        grad_decay = later.astype(bf16).astype(f32)
        total_step = grad_step - dpar[1:2, :] * grad_decay
        grad_dt = total_step * sgdt[rows, :]
        low_xd[rows, width:] = grad_dt.astype(bf16)
        dsums[0:8, :] += fold(grad_dt)
        dsums[8:16, :] -= fold(grad_decay * step[rows, :])
        dstate[...] = kept_e * dstate[...] + mm_tn(cm, g_in)
        return carry

    lax.fori_loop(0, blocks, body, 0)


def convolve_back(xin, gpre, taps, pos, rpos, low_xd, csums):
    width = gpre.shape[1]
    columns = width // LANES
    csums[...] = jnp.zeros_like(csums)

    def body(i, carry):
        at = pl.multiple_of((i // columns) * BLOCK, BLOCK)
        cols = pl.ds(pl.multiple_of((i % columns) * LANES, LANES), LANES)
        rows = pl.ds(at, BLOCK)
        x = xin[pl.ds(at, BLOCK + 8), cols]
        g = gpre[pl.ds(at, BLOCK + 8), cols]
        here = g[:BLOCK]
        place, ahead = pos[rows, :], rpos[rows, :]
        tap = taps[:, cols]
        grad = tap[CONV - 1 : CONV] * here
        csums[pl.ds(8 * CONV, 8), cols] += fold(here)
        csums[pl.ds(8 * (CONV - 1), 8), cols] += fold(here * x[8:])
        for lag in range(1, CONV):
            k = CONV - 1 - lag
            later = pltpu.roll(g, BLOCK + 8 - lag, 0)[:BLOCK]
            earlier = pltpu.roll(x, lag, 0)[8:]
            grad = grad + tap[k : k + 1] * jnp.where(ahead >= lag, later, 0.0)
            csums[pl.ds(8 * k, 8), cols] += fold(here * jnp.where(place >= lag, earlier, 0.0))
        low_xd[rows, cols] = grad.astype(bf16)
        return carry

    lax.fori_loop(0, (xin.shape[0] - 8) // BLOCK * columns, body, 0)


def backward_kernel(
    starts, xin, slope, x_low, bc_low, step, sgdt, step_low, decay_low, ssd, states, gs, taps, crow, dpar,
    low_xd, csums, dsums,
    pos, rpos, spread, gpre, dstate, xs, gx, cbm, acc,
):
    fill_spread(spread)
    fill_positions(starts, pos, rpos)
    scan_backward(
        starts, x_low, bc_low, step_low, decay_low, ssd, states, gs, slope, crow, step, sgdt, dpar,
        gpre, low_xd, dsums, spread, dstate, xs, gx, cbm, acc,
    )
    convolve_back(xin, gpre, taps, pos, rpos, low_xd, csums)


def last_kernel(tok, inverse, gain, normed, low_gate, low_xd, wz, wxd, dwxd, gfull, rowdot):
    weight_rows(normed, low_xd, dwxd)
    rows = 256

    def body(i, carry):
        at = pl.ds(pl.multiple_of(i * rows, rows), rows)
        total = jnp.zeros((rows, 1), f32)
        for c, w in tiles(gfull.shape[1], 512):
            cols = slice(c, c + w)
            part = mm_nt(low_gate[at, :], wz[cols, :]) + mm_nt(low_xd[at, :], wxd[cols, :])
            gfull[at, cols] = part.astype(bf16)
            total = total + jnp.sum(part * gain[:, cols] * tok[at, cols].astype(f32), axis=1, keepdims=True)
        rowdot[at, :] = total * inverse[at, :]
        return carry

    lax.fori_loop(0, gfull.shape[0] // rows, body, 0)


def call(kernel, outs, scratch, smem, *operands):
    whole = pl.BlockSpec(memory_space=pltpu.VMEM)
    scalar = pl.BlockSpec(memory_space=pltpu.SMEM)
    return pl.pallas_call(
        kernel,
        out_shape=[jax.ShapeDtypeStruct(shape, kind) for shape, kind in outs],
        in_specs=[scalar if i < smem else whole for i in range(len(operands))],
        out_specs=[whole] * len(outs),
        scratch_shapes=[pltpu.VMEM(shape, kind) for shape, kind in scratch],
        compiler_params=pltpu.CompilerParams(vmem_limit_bytes=VMEM_LIMIT),
    )(*operands)


def per_device(
    tokens, cotangent, doc_lengths, w_z, w_x, w_bc, w_dt, w_out, conv_x, conv_x_bias, conv_bc,
    conv_bc_bias, dt_bias, a_rate, d_skip, input_norm_gain, out_gain,
):
    group = lax.axis_size("mp")
    rank = lax.axis_index("mp")
    T, D = tokens.shape
    inner, heads = w_x.shape[1], w_dt.shape[1]
    pair = 2 * STATE
    width = inner + pair
    wide = width + LANES
    own = D // group

    lengths = doc_lengths[0]
    starts = jnp.cumsum(lengths) - lengths
    packed = jnp.concatenate([w_bc, conv_bc, conv_bc_bias[None, :]], axis=0)
    packed = lax.all_gather(packed, "mp", axis=1, tiled=True)
    shard = w_bc.shape[0]
    w_bc_all, taps_bc = packed[:shard], packed[shard:]
    wxd = jnp.concatenate(
        [w_x.astype(bf16), w_bc_all.astype(bf16), w_dt.astype(bf16), jnp.zeros((shard, LANES - heads), bf16)],
        axis=1,
    )
    wxd = lax.all_gather(wxd, "dp", axis=0, tiled=True)
    wz = lax.all_gather(w_z.astype(bf16), "dp", axis=0, tiled=True)
    wout = lax.all_gather(w_out.astype(bf16), "dp", axis=1, tiled=True)
    taps = jnp.concatenate([jnp.concatenate([conv_x, conv_x_bias[None, :]], axis=0), taps_bc], axis=1)
    taps = jnp.pad(taps, ((0, 8 - CONV - 1), (0, 0)))
    crow = jnp.pad(jnp.stack([out_gain, jnp.repeat(d_skip, HEADDIM)]), ((0, 6), (0, 0)))
    dpar = jnp.pad(jnp.stack([dt_bias, a_rate]), ((0, 6), (0, LANES - heads)))
    gain = input_norm_gain[None, :]

    blocks = T // BLOCK
    (
        normed, inverse, xin, slope, gate, x_low, bc_low, step, sgdt, step_low, decay_low, ssd, states,
    ) = call(
        forward_kernel,
        [
            ((T, D), bf16), ((T, LANES), f32), ((T + 8, width), f32), ((T, width), f32), ((T, inner), f32),
            ((T, inner), bf16), ((T, pair), bf16), ((T, LANES), f32), ((T, LANES), f32),
            ((T, LANES), bf16), ((T, LANES), bf16), ((T, inner), bf16), ((blocks, STATE, inner), bf16),
        ],
        [
            ((T, LANES), jnp.int32), ((LANES, inner), bf16), ((T, LANES), f32), ((STATE, inner), f32),
            ((BLOCK, inner), bf16), ((BLOCK, inner), f32), ((BLOCK, BLOCK), f32),
        ],
        1, starts, tokens, gain, wxd, wz, taps, dpar,
    )
    gnorm, stat = call(
        gate_kernel,
        [((T, inner), f32), ((T, LANES), f32)],
        [],
        0, cotangent, wout, gate, ssd, x_low, crow,
    )
    stat = jnp.pad(lax.psum(stat[:, :8], "mp"), ((0, 0), (0, LANES - 8)))
    branch, dwout, dwz, low_gate, gs, sums = call(
        functools.partial(middle_kernel, width=inner * group),
        [
            ((T, D), bf16), ((inner, D), bf16), ((D, inner), bf16), ((T, inner), bf16), ((T, inner), bf16),
            ((16, inner), f32),
        ],
        [((T, inner), bf16)],
        0, cotangent, wout, normed, gate, x_low, ssd, gnorm, crow, stat,
    )
    low_xd, csums, dsums = call(
        backward_kernel,
        [((T, wide), bf16), ((8 * CONV + 8, width), f32), ((16, LANES), f32)],
        [
            ((T, LANES), jnp.int32), ((T, LANES), jnp.int32), ((LANES, inner), bf16), ((T + 8, width), f32),
            ((STATE, inner), f32), ((BLOCK, inner), bf16), ((BLOCK, inner), f32), ((BLOCK, BLOCK), f32),
            ((BLOCK, BLOCK), f32),
        ],
        1, starts, xin, slope, x_low, bc_low, step, sgdt, step_low, decay_low, ssd, states, gs, taps, crow,
        dpar,
    )
    dwxd, gfull, rowdot = call(
        last_kernel,
        [((D, wide), bf16), ((T, D), bf16), ((T, LANES), f32)],
        [],
        0, tokens, inverse, gain, normed, low_gate, low_xd, wz, wxd,
    )

    def scatter(v, axis, dim):
        return lax.psum_scatter(v, axis, scatter_dimension=dim, tiled=True)

    token_own = lax.dynamic_slice_in_dim(tokens, rank * own, own, 1).astype(f32)
    output = (token_own + scatter(branch, "mp", 1).astype(f32)).astype(bf16)
    w_out_grad = scatter(dwout, "dp", 1).astype(f32)
    w_z_grad = scatter(dwz, "dp", 0).astype(f32)
    dwxd_own = scatter(dwxd, "dp", 0)
    w_x_grad = dwxd_own[:, :inner].astype(f32)
    w_dt_grad = dwxd_own[:, width : width + heads].astype(f32)
    w_bc_grad = scatter(dwxd_own[:, inner:width], "mp", 1).astype(f32)

    g_own = scatter(gfull, "mp", 1).astype(f32)
    gain_own = lax.dynamic_slice_in_dim(input_norm_gain, rank * own, own, 0)
    row_mean = (lax.psum(rowdot[:, 0], "mp") / D)[:, None]
    inv = inverse[:, :1]
    hat = token_own * inv
    cot_own = lax.dynamic_slice_in_dim(cotangent, rank * own, own, 1).astype(f32)
    input_grad = (cot_own + inv * (g_own * gain_own - hat * row_mean)).astype(bf16)
    in_gain = jnp.sum(g_own * hat, axis=0)

    csums = jnp.sum(csums.reshape(CONV + 1, 8, width), axis=1)
    sums = jnp.sum(sums.reshape(2, 8, inner), axis=1)
    dsums = jnp.sum(dsums.reshape(2, 8, LANES), axis=1)[:, :heads]
    csums_bc = scatter(csums[:, inner:], "mp", 1)
    conv_grad, conv_bc_grad, sums, dsums, in_gain = lax.psum(
        (csums[:, :inner], csums_bc, sums, dsums, in_gain), "dp"
    )
    d_skip_grad = jnp.sum(sums[1].reshape(heads, HEADDIM), axis=1)
    return (
        output, input_grad, w_z_grad, w_x_grad, w_bc_grad, w_dt_grad, w_out_grad,
        conv_grad[:CONV], conv_grad[CONV], conv_bc_grad[:CONV], conv_bc_grad[CONV],
        dsums[0], dsums[1], d_skip_grad, in_gain, sums[0],
    )


def solution(mesh):
    row, block, column = P("dp", None), P("dp", "mp"), P("mp")
    return jax.shard_map(
        per_device,
        mesh=mesh,
        in_specs=(
            row, row, row, block, block, block, block, P("mp", "dp"), P(None, "mp"), column,
            P(None, "mp"), column, column, column, column, P(), column,
        ),
        out_specs=(
            block, block, block, block, block, block, P("mp", "dp"), P(None, "mp"), column,
            P(None, "mp"), column, column, column, column, column, column,
        ),
        check_vma=False,
    )
```

```python
import functools

import jax
import jax.numpy as jnp
from jax import lax
from jax.experimental import pallas as pl
from jax.experimental.pallas import tpu as pltpu
from jax.sharding import PartitionSpec as P

HEADDIM = 64
STATE = 128
CONV = 4
BLOCK = 256
DOCS = 5
LANES = 128
EPS = 1e-05
f32 = jnp.float32
bf16 = jnp.bfloat16
VMEM_LIMIT = 62 * 2**20


def mm(a, b):
    return jnp.dot(a, b, preferred_element_type=f32)


def mm_nt(a, b):
    return lax.dot_general(a, b, (((1,), (1,)), ((), ())), preferred_element_type=f32)


def mm_tn(a, b):
    return lax.dot_general(a, b, (((0,), (0,)), ((), ())), preferred_element_type=f32)


def halves(v):
    high = v.astype(bf16)
    return high, (v - high.astype(f32)).astype(bf16)


def expand(v, spread):
    high, rest = halves(v)
    return mm(high, spread) + mm(rest, spread)


def gather_heads(v, spread):
    high, rest = halves(v)
    return mm_nt(high, spread) + mm_nt(rest, spread)


def logistic(v):
    return 1.0 / (1.0 + jnp.exp(-v))


def tiles(total, size):
    return [(at, min(size, total - at)) for at in range(0, total, size)]


def fold(v):
    return jnp.sum(v.reshape(v.shape[0] // 8, 8, v.shape[1]), axis=0)


def doc_of(starts, place):
    count = (place >= starts[0]).astype(jnp.int32)
    for k in range(1, DOCS):
        count = count + (place >= starts[k]).astype(jnp.int32)
    return count


def fill_spread(spread):
    rows, columns = spread.shape
    head = lax.broadcasted_iota(jnp.int32, (rows, columns), 0)
    channel = lax.broadcasted_iota(jnp.int32, (rows, columns), 1)
    low = head * HEADDIM
    spread[...] = jnp.where((channel >= low) & (channel < low + HEADDIM), 1.0, 0.0).astype(bf16)


def fill_positions(starts, pos, rpos):
    length = pos.shape[0]

    def body(i, carry):
        at = pl.multiple_of(i * BLOCK, BLOCK)
        place = lax.broadcasted_iota(jnp.int32, (BLOCK, LANES), 0) + at
        begin = jnp.zeros_like(place)
        end = jnp.full_like(place, length)
        for k in range(DOCS):
            begin = jnp.maximum(begin, jnp.where(place >= starts[k], starts[k], 0))
            end = jnp.minimum(end, jnp.where(place < starts[k], starts[k], length))
        pos[pl.ds(at, BLOCK), :] = place - begin
        if rpos is not None:
            rpos[pl.ds(at, BLOCK), :] = end - 1 - place
        return carry

    lax.fori_loop(0, length // BLOCK, body, 0)


def normalize(tok, gain, normed, stat):
    step = 64

    def body(i, carry):
        rows = pl.ds(pl.multiple_of(i * step, step), step)
        v = tok[rows, :].astype(f32)
        inverse = lax.rsqrt(jnp.mean(v * v, axis=1, keepdims=True) + EPS)
        normed[rows, :] = (v * inverse * gain[...]).astype(bf16)
        stat[rows, :] = jnp.broadcast_to(inverse, (step, LANES))
        return carry

    lax.fori_loop(0, tok.shape[0] // step, body, 0)


def project_x(normed, wxd, xin, dtin):
    length, width = normed.shape[0], xin.shape[1]
    xin[pl.ds(0, 8), :] = jnp.zeros((8, width), f32)
    rows = 512

    def body(i, carry):
        at = pl.multiple_of(i * rows, rows)
        left = normed[pl.ds(at, rows), :]
        for c, w in tiles(width, 512):
            xin[pl.ds(at + 8, rows), c : c + w] = mm(left, wxd[:, c : c + w])
        dtin[pl.ds(at, rows), :] = mm(left, wxd[:, width : width + LANES])
        return carry

    lax.fori_loop(0, length // rows, body, 0)


def convolve(xin, taps, pos, slope, x_low, bc_low):
    width, inner = xin.shape[1], x_low.shape[1]

    def tile(b, c, out, at):
        rows = pl.ds(pl.multiple_of(b * BLOCK, BLOCK), BLOCK)
        x = xin[pl.ds(pl.multiple_of(b * BLOCK, BLOCK), BLOCK + 8), pl.ds(c, LANES)]
        place = pos[rows, :]
        tap = taps[:, pl.ds(c, LANES)]
        pre = tap[CONV : CONV + 1] + tap[CONV - 1 : CONV] * x[8:]
        for lag in range(1, CONV):
            earlier = pltpu.roll(x, lag, 0)[8:]
            pre = pre + tap[CONV - 1 - lag : CONV - lag] * jnp.where(place >= lag, earlier, 0.0)
        sg = logistic(pre)
        slope[rows, pl.ds(c, LANES)] = (sg * (1.0 + pre * (1.0 - sg))).astype(bf16)
        out[rows, pl.ds(at, LANES)] = (pre * sg).astype(bf16)

    blocks = x_low.shape[0] // BLOCK
    xcols, bcols = inner // LANES, (width - inner) // LANES

    def x_body(i, carry):
        c = pl.multiple_of((i % xcols) * LANES, LANES)
        tile(i // xcols, c, x_low, c)
        return carry

    def bc_body(i, carry):
        c = pl.multiple_of((i % bcols) * LANES, LANES)
        tile(i // bcols, inner + c, bc_low, c)
        return carry

    lax.fori_loop(0, blocks * xcols, x_body, 0)
    lax.fori_loop(0, blocks * bcols, bc_body, 0)


def steps(dtin, dpar, step, sgdt, step_low, decay_low):
    def body(i, carry):
        rows = pl.ds(pl.multiple_of(i * BLOCK, BLOCK), BLOCK)
        v = dtin[rows, :] + dpar[0:1, :]
        soft = jnp.maximum(v, 0.0) + jnp.log1p(jnp.exp(-jnp.abs(v)))
        step[rows, :] = soft
        sgdt[rows, :] = logistic(v)
        step_low[rows, :] = soft.astype(bf16)
        decay_low[rows, :] = (-dpar[1:2, :] * soft).astype(bf16)
        return carry

    lax.fori_loop(0, dtin.shape[0] // BLOCK, body, 0)


def block_marks(starts, b):
    at = b * BLOCK
    column = doc_of(starts, lax.broadcasted_iota(jnp.int32, (BLOCK, 1), 0) + at)
    row = doc_of(starts, lax.broadcasted_iota(jnp.int32, (1, BLOCK), 1) + at)
    before = doc_of(starts, at - 1)
    last = doc_of(starts, at + BLOCK - 1)
    return column, row, before, last


def block_decays(b, starts, decay_low, step_low, spread):
    rows = pl.ds(pl.multiple_of(b * BLOCK, BLOCK), BLOCK)
    column, row, before, last = block_marks(starts, b)
    i0 = lax.broadcasted_iota(jnp.int32, (BLOCK, BLOCK), 0)
    i1 = lax.broadcasted_iota(jnp.int32, (BLOCK, BLOCK), 1)
    lower = jnp.where(i0 >= i1, 1.0, 0.0).astype(bf16)
    cum = mm(lower, decay_low[rows, :])
    step_e = mm(step_low[rows, :], spread[...])
    cum_e = expand(jnp.exp(cum), spread[...])
    kept_e = jnp.where(before == last, cum_e[BLOCK - 1 : BLOCK], 0.0)
    in_e = jnp.where(column == before, cum_e, 0.0)
    out_e = expand(jnp.exp(cum[BLOCK - 1 : BLOCK] - cum), spread[...])
    out_e = jnp.where(column == last, out_e, 0.0)
    return cum, step_e, kept_e, in_e, out_e, column, row


def scan_forward(starts, x_low, bc_low, step_low, decay_low, ssd, states, spread, state, xs, yin, cbm):
    length, inner = x_low.shape
    state[...] = jnp.zeros_like(state)

    def body(b, carry):
        rows = pl.ds(pl.multiple_of(b * BLOCK, BLOCK), BLOCK)
        cum, step_e, kept_e, in_e, out_e, column, row = block_decays(
            b, starts, decay_low, step_low, spread
        )
        bm, cm = bc_low[rows, :STATE], bc_low[rows, STATE:]
        i0 = lax.broadcasted_iota(jnp.int32, (BLOCK, BLOCK), 0)
        i1 = lax.broadcasted_iota(jnp.int32, (BLOCK, BLOCK), 1)
        cbm[...] = jnp.where((column == row) & (i0 >= i1), mm_nt(cm, bm), 0.0)
        stepped = x_low[rows, :].astype(f32) * step_e
        xs[...] = stepped.astype(bf16)
        entering = state[...].astype(bf16)
        states[b] = entering
        yin[...] = in_e * mm(cm, entering)
        state[...] = kept_e * state[...] + mm_tn(bm, (stepped * out_e).astype(bf16))
        cum_t = cum.T
        first = lax.broadcasted_iota(jnp.int32, (BLOCK, LANES), 1) < HEADDIM
        for j in range(inner // LANES):
            cols = slice(j * LANES, (j + 1) * LANES)
            pair = xs[:, cols]
            part = []
            for h in (2 * j, 2 * j + 1):
                span = jnp.minimum(cum[:, h : h + 1] - cum_t[h : h + 1, :], 0.0)
                part.append(mm((jnp.exp(span) * cbm[...]).astype(bf16), pair))
            y = jnp.where(first, part[0], part[1]) + yin[:, cols]
            ssd[rows, cols] = y.astype(bf16)
        return carry

    lax.fori_loop(0, length // BLOCK, body, 0)


def project_rows(left, right, out, rows=512, columns=512):
    def body(i, carry):
        at = pl.ds(pl.multiple_of(i * rows, rows), rows)
        part = left[at, :]
        for c, w in tiles(out.shape[1], columns):
            out[at, c : c + w] = mm(part, right[:, c : c + w]).astype(out.dtype)
        return carry

    lax.fori_loop(0, out.shape[0] // rows, body, 0)


def back_rows(left, right, out, rows=512, columns=512):
    def body(i, carry):
        at = pl.ds(pl.multiple_of(i * rows, rows), rows)
        part = left[at, :]
        for c, w in tiles(out.shape[1], columns):
            out[at, c : c + w] = mm_nt(part, right[c : c + w, :]).astype(out.dtype)
        return carry

    lax.fori_loop(0, out.shape[0] // rows, body, 0)


def weight_rows(left, right, out, rows=256, columns=512):
    def body(i, carry):
        at = pl.ds(pl.multiple_of(i * rows, rows), rows)
        part = left[:, at]
        for c, w in tiles(out.shape[1], columns):
            out[at, c : c + w] = mm_tn(part, right[:, c : c + w]).astype(out.dtype)
        return carry

    lax.fori_loop(0, out.shape[0] // rows, body, 0)


def gate_sums(gate, ssd, x_low, gnorm, crow, stat):
    step, inner = 64, gate.shape[1]

    def body(i, carry):
        rows = pl.ds(pl.multiple_of(i * step, step), step)
        squares = jnp.zeros((step, 256), f32)
        crosses = jnp.zeros((step, 256), f32)
        for c in range(0, inner, 256):
            cols = slice(c, c + 256)
            g = gate[rows, cols]
            mixed = ssd[rows, cols].astype(f32) + crow[1:2, cols] * x_low[rows, cols].astype(f32)
            gated = mixed * (g * logistic(g))
            squares = squares + gated * gated
            crosses = crosses + gnorm[rows, cols] * crow[0:1, cols] * gated
        lane = lax.broadcasted_iota(jnp.int32, (step, LANES), 1)
        s1 = jnp.sum(squares, axis=1, keepdims=True)
        s2 = jnp.sum(crosses, axis=1, keepdims=True)
        stat[rows, :] = jnp.where(lane == 0, s1, jnp.where(lane == 1, s2, 0.0))
        return carry

    lax.fori_loop(0, gate.shape[0] // step, body, 0)


def forward_kernel(
    starts, tok, gain, wxd, wz, taps, dpar,
    normed, inverse, xin, slope, gate, x_low, bc_low, step, sgdt, step_low, decay_low, ssd, states,
    pos, spread, dtin, state, xs, yin, cbm,
):
    fill_spread(spread)
    fill_positions(starts, pos, None)
    normalize(tok, gain, normed, inverse)
    project_x(normed, wxd, xin, dtin)
    convolve(xin, taps, pos, slope, x_low, bc_low)
    steps(dtin, dpar, step, sgdt, step_low, decay_low)
    scan_forward(starts, x_low, bc_low, step_low, decay_low, ssd, states, spread, state, xs, yin, cbm)
    project_rows(normed, wz, gate)


def gate_kernel(cot, wout, gate, ssd, x_low, crow, gnorm, stat):
    back_rows(cot, wout, gnorm)
    gate_sums(gate, ssd, x_low, gnorm, crow, stat)


def gate_backward(gate, ssd, x_low, gnorm, crow, stat, width, gn, low_gate, gs, sums):
    step, inner = 64, gate.shape[1]
    sums[...] = jnp.zeros_like(sums)

    def body(i, carry):
        rows = pl.ds(pl.multiple_of(i * step, step), step)
        inverse = lax.rsqrt(stat[rows, 0:1] / width + EPS)
        mean = inverse * stat[rows, 1:2] / width
        for c in range(0, inner, 256):
            cols = slice(c, c + 256)
            g = gate[rows, cols]
            x = x_low[rows, cols].astype(f32)
            mixed = ssd[rows, cols].astype(f32) + crow[1:2, cols] * x
            sg = logistic(g)
            act = g * sg
            hat = mixed * act * inverse
            gn[rows, cols] = (hat * crow[0:1, cols]).astype(bf16)
            gnorm_here = gnorm[rows, cols]
            grad = inverse * (gnorm_here * crow[0:1, cols] - hat * mean)
            grad_mixed = grad * act
            low_gate[rows, cols] = (grad * mixed * (sg * (1.0 + g * (1.0 - sg)))).astype(bf16)
            gs[rows, cols] = grad_mixed.astype(bf16)
            sums[0:8, cols] += fold(gnorm_here * hat)
            sums[8:16, cols] += fold(grad_mixed * x)
        return carry

    lax.fori_loop(0, gate.shape[0] // step, body, 0)


def middle_kernel(
    cot, wout, normed, gate, x_low, ssd, gnorm, crow, stat,
    branch, dwout, dwz, low_gate, gs, sums,
    gn, *, width,
):
    gate_backward(gate, ssd, x_low, gnorm, crow, stat, width, gn, low_gate, gs, sums)
    project_rows(gn, wout, branch)
    weight_rows(gn, cot, dwout)
    weight_rows(normed, low_gate, dwz)


def scan_backward(
    starts, x_low, bc_low, step_low, decay_low, ssd, states, gs, slope, crow, step, sgdt, dpar,
    gpre, low_xd, dsums, spread, dstate, xs, gx, cbm, acc, tick=None,
):
    length, inner = x_low.shape
    width = gpre.shape[1]
    blocks = length // BLOCK
    dstate[...] = jnp.zeros_like(dstate)
    dsums[...] = jnp.zeros_like(dsums)
    gpre[pl.ds(length, 8), :] = jnp.zeros((8, width), f32)

    def body(i, carry):
        b = blocks - 1 - i
        rows = pl.ds(pl.multiple_of(b * BLOCK, BLOCK), BLOCK)
        cum, step_e, kept_e, in_e, out_e, column, row = block_decays(
            b, starts, decay_low, step_low, spread
        )
        bm, cm = bc_low[rows, :STATE], bc_low[rows, STATE:]
        i0 = lax.broadcasted_iota(jnp.int32, (BLOCK, BLOCK), 0)
        i1 = lax.broadcasted_iota(jnp.int32, (BLOCK, BLOCK), 1)
        linked = (column == row) & (i0 <= i1)
        cbm[...] = jnp.where(linked, mm_nt(bm, cm), 0.0)
        x = x_low[rows, :].astype(f32)
        stepped = x * step_e
        xs[...] = stepped.astype(bf16)
        cum_t = cum.T
        first = lax.broadcasted_iota(jnp.int32, (BLOCK, LANES), 1) < HEADDIM
        acc[...] = jnp.zeros_like(acc)
        for j in range(inner // LANES):
            cols = slice(j * LANES, (j + 1) * LANES)
            xpair, gpair = xs[:, cols], gs[rows, cols]
            none = jnp.zeros_like(xpair)
            part, total = [], None
            for k in range(2):
                h = 2 * j + k
                kernel = jnp.exp(jnp.minimum(cum_t[h : h + 1, :] - cum[:, h : h + 1], 0.0))
                part.append(mm((kernel * cbm[...]).astype(bf16), gpair))
                own = jnp.where(first, xpair, none) if k == 0 else jnp.where(first, none, xpair)
                here = kernel * mm_nt(own, gpair)
                total = here if total is None else total + here
            acc[...] += total
            gx[:, cols] = jnp.where(first, part[0], part[1])
        dstate_low = dstate[...].astype(bf16)
        entering = states[b]
        leaving = states[jnp.minimum(b + 1, blocks - 1)]
        end = jnp.sum(dstate[...] * leaving.astype(f32), axis=0, keepdims=True)
        g = gs[rows, :].astype(f32)
        g_in = (in_e * g).astype(bf16)
        raw = gx[...] + out_e * mm(bm, dstate_low)
        grad_x = (step_e * raw).astype(bf16).astype(f32)
        gpre[rows, :inner] = (grad_x + crow[1:2, :] * g) * slope[rows, :inner]
        pairs = jnp.where(linked, acc[...], 0.0).astype(bf16)
        db = mm(pairs, cm) + mm_nt((stepped * out_e).astype(bf16), dstate_low)
        dc = mm_tn(pairs, bm) + mm_nt(g_in, entering)
        gpre[rows, inner : inner + STATE] = db * slope[rows, inner : inner + STATE]
        gpre[rows, inner + STATE :] = dc * slope[rows, inner + STATE :]
        raw_x = x * raw
        grad_step = gather_heads(raw_x, spread[...]).astype(bf16).astype(f32)
        dcum = gather_heads(g * ssd[rows, :].astype(f32) - step_e * raw_x, spread[...])
        tail = gather_heads(jnp.broadcast_to(end, (8, inner)), spread[...])[0:1]
        upper = jnp.where(i0 <= i1, 1.0, 0.0).astype(bf16)
        high, rest = halves(dcum)
        later = mm(upper, high) + mm(upper, rest) + tail
        grad_decay = later.astype(bf16).astype(f32)
        total_step = grad_step - dpar[1:2, :] * grad_decay
        grad_dt = total_step * sgdt[rows, :]
        low_xd[rows, width:] = grad_dt.astype(bf16)
        dsums[0:8, :] += fold(grad_dt)
        dsums[8:16, :] -= fold(grad_decay * step[rows, :])
        dstate[...] = kept_e * dstate[...] + mm_tn(cm, g_in)
        if tick is not None:
            tick(i)
        return carry

    lax.fori_loop(0, blocks, body, 0)


def convolve_back(xin, gpre, taps, pos, rpos, low_xd, csums):
    width = gpre.shape[1]
    columns = width // LANES
    csums[...] = jnp.zeros_like(csums)

    def body(i, carry):
        at = pl.multiple_of((i // columns) * BLOCK, BLOCK)
        cols = pl.ds(pl.multiple_of((i % columns) * LANES, LANES), LANES)
        rows = pl.ds(at, BLOCK)
        x = xin[pl.ds(at, BLOCK + 8), cols]
        g = gpre[pl.ds(at, BLOCK + 8), cols]
        here = g[:BLOCK]
        place, ahead = pos[rows, :], rpos[rows, :]
        tap = taps[:, cols]
        grad = tap[CONV - 1 : CONV] * here
        csums[pl.ds(8 * CONV, 8), cols] += fold(here)
        csums[pl.ds(8 * (CONV - 1), 8), cols] += fold(here * x[8:])
        for lag in range(1, CONV):
            k = CONV - 1 - lag
            later = pltpu.roll(g, BLOCK + 8 - lag, 0)[:BLOCK]
            earlier = pltpu.roll(x, lag, 0)[8:]
            grad = grad + tap[k : k + 1] * jnp.where(ahead >= lag, later, 0.0)
            csums[pl.ds(8 * k, 8), cols] += fold(here * jnp.where(place >= lag, earlier, 0.0))
        low_xd[rows, cols] = grad.astype(bf16)
        return carry

    lax.fori_loop(0, (xin.shape[0] - 8) // BLOCK * columns, body, 0)


def backward_kernel(
    starts, xin, slope, x_low, bc_low, step, sgdt, step_low, decay_low, ssd, states, gs, taps, crow, dpar,
    low_xd, csums, dsums,
    pos, rpos, spread, gpre, dstate, xs, gx, cbm, acc,
):
    fill_spread(spread)
    fill_positions(starts, pos, rpos)
    scan_backward(
        starts, x_low, bc_low, step_low, decay_low, ssd, states, gs, slope, crow, step, sgdt, dpar,
        gpre, low_xd, dsums, spread, dstate, xs, gx, cbm, acc,
    )
    convolve_back(xin, gpre, taps, pos, rpos, low_xd, csums)


def last_kernel(tok, inverse, gain, normed, low_gate, low_xd, wz, wxd, dwxd, gfull, rowdot):
    weight_rows(normed, low_xd, dwxd)
    rows = 256

    def body(i, carry):
        at = pl.ds(pl.multiple_of(i * rows, rows), rows)
        total = jnp.zeros((rows, 1), f32)
        for c, w in tiles(gfull.shape[1], 512):
            cols = slice(c, c + w)
            part = mm_nt(low_gate[at, :], wz[cols, :]) + mm_nt(low_xd[at, :], wxd[cols, :])
            gfull[at, cols] = part.astype(bf16)
            total = total + jnp.sum(part * gain[:, cols] * tok[at, cols].astype(f32), axis=1, keepdims=True)
        rowdot[at, :] = total * inverse[at, :]
        return carry

    lax.fori_loop(0, gfull.shape[0] // rows, body, 0)


MESH = pl.DeviceIdType.MESH


def remote(source, target, send, receive, **where):
    return pltpu.make_async_remote_copy(
        src_ref=source, dst_ref=target, send_sem=send, recv_sem=receive, device_id=where, device_id_type=MESH
    )


def add_into(target, source, rows=64):
    def body(i, carry):
        at = pl.ds(pl.multiple_of(i * rows, rows), rows)
        target[at, :] = (target[at, :].astype(f32) + source[at, :].astype(f32)).astype(target.dtype)
        return carry

    lax.fori_loop(0, target.shape[0] // rows, body, 0)


class Ring:
    def __init__(self):
        self.me = lax.axis_index("dp")
        self.core = self.me % 2
        chip = self.me // 2
        y = chip // 2
        self.pos = 2 * y + (chip + y) % 2
        self.partner = self.me + 1 - 2 * self.core
        self.right = self.at(self.pos + 1)
        self.left = self.at(self.pos + 3)
        self.across = self.at(self.pos + 2)

    def at(self, pos):
        pos = pos % 4
        y = pos // 2
        return (2 * y + (pos + y) % 2) * 2 + self.core


def greet(ring, everyone):
    barrier = pltpu.get_barrier_semaphore()
    n, z = lax.axis_size("mp"), lax.axis_index("mp")
    if everyone:
        size = lax.axis_size("dp")
        close = [(ring.me + i) % size for i in range(1, size)]
    else:
        close = [ring.partner, ring.right, ring.left]
    for other in close:
        pl.semaphore_signal(barrier, inc=1, device_id={"dp": other}, device_id_type=MESH)
    for i in range(1, n):
        pl.semaphore_signal(barrier, inc=1, device_id={"mp": (z + i) % n}, device_id_type=MESH)
    pl.semaphore_wait(barrier, len(close) + n - 1)


class Scatter:
    def __init__(self, ring, shard, cores, parts, wholes, sems):
        self.ring, self.shard = ring, shard
        self.cores, self.parts, self.wholes = cores, parts, wholes
        self.core_send, self.core_recv, self.ring_send, self.ring_recv = sems
        self.half = cores.shape[1] // 2

    def upper(self, r):
        return self.shard(r).at[pl.ds(0, self.half), :]

    def lower(self, r):
        return self.shard(r).at[pl.ds(self.half, self.half), :]

    def core_copy(self, chip):
        ring = self.ring
        return remote(
            self.shard(2 * chip + 1 - ring.core), self.cores.at[chip],
            self.core_send.at[chip], self.core_recv.at[chip], dp=ring.partner,
        )

    def ring_copy(self, k):
        ring = self.ring
        source = (self.upper(ring.across), self.lower(ring.across), self.shard(ring.right), self.shard(ring.left))[k]
        target = (self.parts.at[0], self.parts.at[1], self.wholes.at[0], self.wholes.at[1])[k]
        return remote(
            source, target, self.ring_send.at[k], self.ring_recv.at[k], dp=(ring.right, ring.left)[k % 2]
        )

    def start(self, chip):
        self.core_copy(chip).start()

    def first(self):
        def body(chip, carry):
            self.core_copy(chip).wait_recv()
            add_into(self.shard(2 * chip + self.ring.core), self.cores.at[chip])
            return carry

        lax.fori_loop(0, 4, body, 0)
        self.ring_copy(0).start()
        self.ring_copy(1).start()

    def second(self):
        self.ring_copy(0).wait_recv()
        add_into(self.upper(self.ring.right), self.parts.at[0])
        self.ring_copy(2).start()
        self.ring_copy(1).wait_recv()
        add_into(self.lower(self.ring.left), self.parts.at[1])
        self.ring_copy(3).start()

    def finish(self, out, rows=64):
        self.ring_copy(2).wait_recv()
        self.ring_copy(3).wait_recv()
        own = self.shard(self.ring.me)

        def body(i, carry):
            at = pl.ds(pl.multiple_of(i * rows, rows), rows)
            out[at, :] = own[at, :].astype(f32) + self.wholes[0, at, :].astype(f32) + self.wholes[1, at, :].astype(f32)
            return carry

        lax.fori_loop(0, out.shape[0] // rows, body, 0)

        def done(chip, carry):
            self.core_copy(chip).wait_send()
            return carry

        lax.fori_loop(0, 4, done, 0)
        for k in range(4):
            self.ring_copy(k).wait_send()


class Line:
    def __init__(self, part, slots, sems, total):
        self.part, self.slots, self.total = part, slots, total
        self.send, self.recv = sems
        self.n, self.z = lax.axis_size("mp"), lax.axis_index("mp")
        self.blocks = part.shape[0] // BLOCK
        self.own = part.shape[1] // self.n
        self.place = (self.z, self.n - 1 - self.z)
        self.count = self.blocks * (self.n - 1)

    def rows(self, t):
        return pl.ds(pl.multiple_of(t * BLOCK, BLOCK), BLOCK)

    def columns(self, q):
        return pl.ds(pl.multiple_of(q * self.own, self.own), self.own)

    def copy(self, side, k):
        d = k // self.blocks
        q = self.n - 1 - d if side == 0 else d
        source = self.part.at[self.rows(k - d * self.blocks), self.columns(q)]
        return remote(
            source, self.slots.at[side, k], self.send.at[side, k], self.recv.at[side, k],
            mp=self.z + 1 if side == 0 else self.z - 1,
        ), source

    def inject(self, k):
        for side in range(2):
            @pl.when(self.place[side] == 0)
            def _():
                self.copy(side, k)[0].start()

    def forward(self, k, hop):
        for side in range(2):
            @pl.when(self.place[side] == hop)
            def _():
                copy, source = self.copy(side, k)
                copy.wait_recv()
                add_into(source, self.slots.at[side, k])
                copy.start()

    def finish(self, t):
        self.total[...] = self.part[self.rows(t), self.columns(self.z)].astype(f32)
        for side in range(2):
            @pl.when(self.place[side] >= 1)
            def _():
                k = (self.n - 1 - self.place[side]) * self.blocks + t
                self.copy(side, k)[0].wait_recv()
                self.total[...] += self.slots[side, k].astype(f32)

    def drain(self):
        def body(k, carry):
            for side in range(2):
                @pl.when(self.place[side] + k // self.blocks <= self.n - 2)
                def _():
                    self.copy(side, k)[0].wait_send()
            return carry

        lax.fori_loop(0, self.count, body, 0)

    def order(self, i):
        z = self.z
        far = jnp.where(z < 2, 3 - i, i)
        near = z + 1 - 2 * (z % 2)
        return jnp.where(i < 2, far, jnp.where(i == 2, near, z))


class Loads:
    def __init__(self, sems):
        self.sems, self.pairs = sems, []

    def start(self, source, target):
        i = len(self.pairs)
        copy = pltpu.make_async_copy(source, target, self.sems.at[i])
        copy.start()
        self.pairs.append(copy)
        return copy


def output_kernel(
    starts, tok, gn, wout, cot, x_low, ssd, states, gs, slope, xin, bc_low, step, sgdt, step_low, decay_low,
    taps, crow, dpar,
    out, dwout, low_xd, csums, dsums,
    v_gn, v_wout, v_cot, v_x, v_ssd, v_states, v_gs, v_slope, v_xin,
    part, slots, cores, parts, wholes,
    pos, rpos, spread, gpre, dstate, xs, gx, cbm, acc,
    load_sems, cot_sems, line_send, line_recv, core_send, core_recv, ring_send, ring_recv,
):
    ring = Ring()
    loads = Loads(load_sems)
    n = lax.axis_size("mp")
    z = lax.axis_index("mp")
    own = part.shape[1] // n
    load_gn = loads.start(gn, v_gn)
    load_wout = loads.start(wout, v_wout)
    later = [
        loads.start(source, target)
        for source, target in (
            (x_low, v_x), (ssd, v_ssd), (states, v_states), (gs, v_gs), (slope, v_slope), (xin, v_xin),
        )
    ]
    greet(ring, False)
    total = gx.at[:, pl.ds(0, own)]
    line = Line(part, slots, (line_send, line_recv), total)
    chunk = v_cot.shape[2]
    shard = dwout.shape[1]

    def cot_copy(j):
        return pltpu.make_async_copy(
            cot.at[:, pl.ds(pl.multiple_of(j * chunk, chunk), chunk)], v_cot.at[j % 2], cot_sems.at[j % 2]
        )

    cot_copy(0).start()
    fill_spread(spread)
    fill_positions(starts, pos, rpos)
    load_gn.wait()
    load_wout.wait()

    def quarter(i, carry):
        q = line.order(i)
        columns = line.columns(q)
        for r in range(0, part.shape[0], 512):
            part[r : r + 512, columns] = mm(v_gn[r : r + 512, :], v_wout[:, columns]).astype(bf16)

        @pl.when(i == 0)
        def _():
            line.inject(0)
            line.inject(1)

        line.inject(i + 2)
        return carry

    lax.fori_loop(0, n, quarter, 0)

    grads = v_wout
    scatter = Scatter(
        ring, lambda r: grads.at[:, pl.ds(pl.multiple_of(r * shard, shard), shard)], cores, parts, wholes,
        (core_send, core_recv, ring_send, ring_recv),
    )

    def weight(j, carry):
        @pl.when(j < 3)
        def _():
            cot_copy(j + 1).start()

        cot_copy(j).wait()
        columns = pl.ds(pl.multiple_of(j * chunk, chunk), chunk)
        for r in range(0, grads.shape[0], 256):
            grads[r : r + 256, columns] = mm_tn(v_gn[:, r : r + 256], v_cot[j % 2]).astype(bf16)
        scatter.start(j)

        @pl.when(j == 2)
        def _():
            line.forward(0, 1)
            line.inject(6)

        return carry

    lax.fori_loop(0, 4, weight, 0)
    v_tok = v_cot.at[0]
    load_tok = loads.start(tok.at[:, pl.ds(pl.multiple_of(z * own, own), own)], v_tok)
    for copy in later[:5]:
        copy.wait()

    def scan_tick(i):
        @pl.when(i == 0)
        def _():
            scatter.first()

        @pl.when(i == 1)
        def _():
            scatter.second()

        line.forward(i + 1, 1)
        line.forward(i, 2)
        line.inject(i + 7)

    scan_backward(
        starts, v_x, bc_low, step_low, decay_low, v_ssd, v_states, v_gs, v_slope, crow, step, sgdt, dpar,
        gpre, low_xd, dsums, spread, dstate, xs, gx, cbm, acc, scan_tick,
    )
    line.inject(11)
    line.forward(5, 1)
    scatter.finish(dwout)
    later[5].wait()
    convolve_back(v_xin, gpre, taps, pos, rpos, low_xd, csums)
    line.forward(6, 1)
    line.forward(7, 1)
    load_tok.wait()

    def last(t, carry):
        line.finish(t)
        out[line.rows(t), :] = (v_tok[line.rows(t), :].astype(f32) + total[...]).astype(bf16)
        return carry

    lax.fori_loop(0, line.blocks, last, 0)
    line.drain()


def input_kernel(
    tok, inverse, gain, normed, low_gate, low_xd, wz, wxd, cot, csums, sums, dsums,
    grad, dwz, dwxd, smalls,
    v_tok, v_normed, v_gate, v_xd, v_wz, v_wxd, v_cot,
    part, slots, total, z_grads, z_cores, z_parts, z_wholes, x_grads, x_cores, x_parts, x_wholes,
    rowacc, rows_own, rows_in, colacc, dp_in, bc_in, gain_in,
    load_sems, line_send, line_recv, z_core_send, z_core_recv, z_ring_send, z_ring_recv,
    x_core_send, x_core_recv, x_ring_send, x_ring_recv,
    rows_send, rows_recv, dp_send, dp_recv, mp_send, mp_recv,
):
    ring = Ring()
    loads = Loads(load_sems)
    n = lax.axis_size("mp")
    z = lax.axis_index("mp")
    size = lax.axis_size("dp")
    length, features = part.shape
    inner = v_gate.shape[1]
    width = smalls.shape[1]
    first = [
        loads.start(source, target)
        for source, target in ((low_gate, v_gate), (wz, v_wz), (low_xd, v_xd), (wxd, v_wxd), (tok, v_tok))
    ]
    own = features // n
    own_columns = pl.ds(pl.multiple_of(z * own, own), own)
    later = [
        loads.start(source, target)
        for source, target in ((normed, v_normed), (cot.at[:, own_columns], v_cot))
    ]
    greet(ring, True)
    line = Line(part, slots, (line_send, line_recv), total)
    rowacc[...] = jnp.zeros_like(rowacc)
    for copy in first:
        copy.wait()

    def quarter(i, carry):
        columns = line.columns(line.order(i))
        for r in range(0, length, 256):
            rows = slice(r, r + 256)
            here = mm_nt(v_gate[rows, :], v_wz[columns, :]) + mm_nt(v_xd[rows, :], v_wxd[columns, :])
            part[rows, columns] = here.astype(bf16)
            along = here * (v_tok[rows, columns].astype(f32) * inverse[rows, :1])
            folded = fold(along)
            if r == 0:
                colacc[:, columns] = folded
            else:
                colacc[:, columns] += folded
            along = along * gain[:, columns]
            sum_lanes = along[:, :LANES]
            for c in range(LANES, own, LANES):
                sum_lanes = sum_lanes + along[:, c : c + LANES]
            rowacc[rows, :] += sum_lanes

        @pl.when(i == 0)
        def _():
            line.inject(0)
            line.inject(1)

        line.inject(i + 2)
        return carry

    lax.fori_loop(0, n, quarter, 0)
    line.forward(0, 1)

    for b in range(length // BLOCK):
        columns = slice(b * BLOCK, (b + 1) * BLOCK)
        line_sum = jnp.sum(rowacc[columns, :].T, axis=0, keepdims=True)
        rows_own[:, columns] = jnp.broadcast_to(line_sum, (8, BLOCK))

    def rows_copy(i):
        return remote(
            rows_own, rows_in.at[i - 1], rows_send.at[i - 1], rows_recv.at[i - 1], mp=(z + i) % n
        )

    def dp_copy(i):
        return remote(
            smalls, dp_in.at[i - 1], dp_send.at[i - 1], dp_recv.at[i - 1], dp=(ring.me + i) % size
        )

    def bc_copy(i):
        return remote(
            smalls.at[pl.ds(0, 8), pl.ds(inner, width - inner)], bc_in.at[i - 1],
            mp_send.at[i - 1], mp_recv.at[i - 1], mp=(z + i) % n,
        )

    def gain_copy(i):
        return remote(
            smalls.at[pl.ds(8, 8), pl.ds(0, inner)], gain_in.at[i - 1],
            mp_send.at[n + i - 2], mp_recv.at[n + i - 2], mp=(z + i) % n,
        )

    smalls[...] = jnp.zeros_like(smalls)
    for k in range(CONV + 1):
        smalls[k : k + 1, :] = jnp.sum(csums[8 * k : 8 * k + 8, :], axis=0, keepdims=True)
    for k in range(2):
        smalls[CONV + 1 + k : CONV + 2 + k, :inner] = jnp.sum(sums[8 * k : 8 * k + 8, :], axis=0, keepdims=True)
        smalls[7:8, k * LANES : (k + 1) * LANES] = jnp.sum(dsums[8 * k : 8 * k + 8, :], axis=0, keepdims=True)
    for k in range(features // inner):
        smalls[8 + k : 9 + k, :inner] = jnp.sum(colacc[:, k * inner : (k + 1) * inner], axis=0, keepdims=True)
    for i in range(1, n):
        rows_copy(i).start()
    for i in range(1, size):
        dp_copy(i).start()

    later[0].wait()
    shard = dwz.shape[0]
    z_scatter = Scatter(
        ring, lambda r: z_grads.at[pl.ds(pl.multiple_of(r * shard, shard), shard), :], z_cores, z_parts, z_wholes,
        (z_core_send, z_core_recv, z_ring_send, z_ring_recv),
    )
    x_scatter = Scatter(
        ring, lambda r: x_grads.at[pl.ds(pl.multiple_of(r * shard, shard), shard), :], x_cores, x_parts, x_wholes,
        (x_core_send, x_core_recv, x_ring_send, x_ring_recv),
    )

    def weight(j, right, grads):
        for c in range(0, 2 * shard, shard):
            rows = pl.ds(pl.multiple_of(j * 2 * shard + c, shard), shard)
            left = v_normed[:, rows]
            for at, w in tiles(grads.shape[1], 512):
                grads[rows, at : at + w] = mm_tn(left, right[:, at : at + w]).astype(bf16)

    def z_weight(j, carry):
        weight(j, v_gate, z_grads)
        z_scatter.start(j)

        @pl.when(j % 2 == 1)
        def _():
            line.inject(6 + j // 2)
            line.forward(1 + j // 2, 1)

        return carry

    lax.fori_loop(0, 4, z_weight, 0)
    line.forward(0, 2)

    def x_weight(j, carry):
        weight(j, v_xd, x_grads)
        x_scatter.start(j)

        @pl.when(j == 1)
        def _():
            z_scatter.first()

        @pl.when(j % 2 == 1)
        def _():
            line.inject(8 + j // 2)
            line.forward(3 + j // 2, 1)
            line.forward(1 + j // 2, 2)

        return carry

    lax.fori_loop(0, 4, x_weight, 0)
    z_scatter.second()
    line.inject(10)
    line.inject(11)
    x_scatter.first()

    for i in range(1, size):
        dp_copy(i).wait()
    smalls[...] += functools.reduce(lambda a, b: a + b, [dp_in[i] for i in range(size - 1)])
    for i in range(1, n):
        bc_copy(i).start()
        gain_copy(i).start()
    line.forward(5, 1)
    line.forward(3, 2)
    z_scatter.finish(dwz)
    for i in range(1, n):
        rows_copy(i).wait()
    rows_own[...] += functools.reduce(lambda a, b: a + b, [rows_in[i] for i in range(n - 1)])
    x_scatter.second()
    line.forward(6, 1)
    line.forward(7, 1)
    for i in range(1, n):
        bc_copy(i).wait()
        gain_copy(i).wait()
    smalls[0:8, inner:] += functools.reduce(lambda a, b: a + b, [bc_in[i] for i in range(n - 1)])
    smalls[8:16, :inner] += functools.reduce(lambda a, b: a + b, [gain_in[i] for i in range(n - 1)])
    x_scatter.finish(dwxd)
    later[1].wait()

    def last(t, carry):
        line.finish(t)
        rows = line.rows(t)
        mean = jnp.broadcast_to(rows_own[0:1, rows] / features, (LANES, BLOCK)).T
        for c in range(0, own, LANES):
            columns = pl.ds(pl.multiple_of(z * own + c, LANES), LANES)
            hat = v_tok[rows, columns].astype(f32) * inverse[rows, :]
            change = inverse[rows, :] * (total[:, c : c + LANES] * gain[:, columns] - hat * mean)
            grad[rows, c : c + LANES] = (v_cot[rows, c : c + LANES].astype(f32) + change).astype(bf16)
        return carry

    lax.fori_loop(0, line.blocks, last, 0)
    line.drain()


def gate_back_kernel(gate, ssd, x_low, gnorm, crow, stat, gn, low_gate, gs, sums, *, width):
    gate_backward(gate, ssd, x_low, gnorm, crow, stat, width, gn, low_gate, gs, sums)


def call(kernel, outs, scratch, smem, *operands, places=None, sems=(), collective=None):
    spaces = {"s": pltpu.SMEM, "v": pltpu.VMEM, "a": pl.ANY}
    if places is None:
        places = "s" * smem + "v" * (len(operands) - smem)
    extra = {} if collective is None else dict(collective_id=collective, has_side_effects=True)
    return pl.pallas_call(
        kernel,
        out_shape=[jax.ShapeDtypeStruct(shape, kind) for shape, kind in outs],
        in_specs=[pl.BlockSpec(memory_space=spaces[c]) for c in places],
        out_specs=[pl.BlockSpec(memory_space=pltpu.VMEM)] * len(outs),
        scratch_shapes=[pltpu.VMEM(shape, kind) for shape, kind in scratch]
        + [pltpu.SemaphoreType.DMA(shape) for shape in sems],
        compiler_params=pltpu.CompilerParams(vmem_limit_bytes=VMEM_LIMIT, **extra),
    )(*operands)


def per_device(
    tokens, cotangent, doc_lengths, w_z, w_x, w_bc, w_dt, w_out, conv_x, conv_x_bias, conv_bc,
    conv_bc_bias, dt_bias, a_rate, d_skip, input_norm_gain, out_gain,
):
    group = lax.axis_size("mp")
    rank = lax.axis_index("mp")
    T, D = tokens.shape
    inner, heads = w_x.shape[1], w_dt.shape[1]
    pair = 2 * STATE
    width = inner + pair
    wide = width + LANES
    own = D // group

    lengths = doc_lengths[0]
    starts = jnp.cumsum(lengths) - lengths
    packed = jnp.concatenate([w_bc, conv_bc, conv_bc_bias[None, :]], axis=0)
    packed = lax.all_gather(packed, "mp", axis=1, tiled=True)
    shard = w_bc.shape[0]
    w_bc_all, taps_bc = packed[:shard], packed[shard:]
    wxd = jnp.concatenate(
        [w_x.astype(bf16), w_bc_all.astype(bf16), w_dt.astype(bf16), jnp.zeros((shard, LANES - heads), bf16)],
        axis=1,
    )
    wxd = lax.all_gather(wxd, "dp", axis=0, tiled=True)
    wz = lax.all_gather(w_z.astype(bf16), "dp", axis=0, tiled=True)
    wout = lax.all_gather(w_out.astype(bf16), "dp", axis=1, tiled=True)
    taps = jnp.concatenate([jnp.concatenate([conv_x, conv_x_bias[None, :]], axis=0), taps_bc], axis=1)
    taps = jnp.pad(taps, ((0, 8 - CONV - 1), (0, 0)))
    crow = jnp.pad(jnp.stack([out_gain, jnp.repeat(d_skip, HEADDIM)]), ((0, 6), (0, 0)))
    dpar = jnp.pad(jnp.stack([dt_bias, a_rate]), ((0, 6), (0, LANES - heads)))
    gain = input_norm_gain[None, :]

    blocks = T // BLOCK
    (
        normed, inverse, xin, slope, gate, x_low, bc_low, step, sgdt, step_low, decay_low, ssd, states,
    ) = call(
        forward_kernel,
        [
            ((T, D), bf16), ((T, LANES), f32), ((T + 8, width), f32), ((T, width), bf16), ((T, inner), f32),
            ((T, inner), bf16), ((T, pair), bf16), ((T, LANES), f32), ((T, LANES), f32),
            ((T, LANES), bf16), ((T, LANES), bf16), ((T, inner), bf16), ((blocks, STATE, inner), bf16),
        ],
        [
            ((T, LANES), jnp.int32), ((LANES, inner), bf16), ((T, LANES), f32), ((STATE, inner), f32),
            ((BLOCK, inner), bf16), ((BLOCK, inner), f32), ((BLOCK, BLOCK), f32),
        ],
        1, starts, tokens, gain, wxd, wz, taps, dpar,
    )
    gnorm, stat = call(
        gate_kernel,
        [((T, inner), f32), ((T, LANES), f32)],
        [],
        0, cotangent, wout, gate, ssd, x_low, crow,
    )
    stat = jnp.pad(lax.psum(stat[:, :8], "mp"), ((0, 0), (0, LANES - 8)))
    if lax.axis_size("dp") == 8 and group == 4:
        gn, low_gate, gs, sums = call(
            functools.partial(gate_back_kernel, width=inner * group),
            [((T, inner), bf16), ((T, inner), bf16), ((T, inner), bf16), ((16, inner), f32)],
            [],
            0, gate, ssd, x_low, gnorm, crow, stat,
        )
        columns = D // lax.axis_size("dp")
        messages = blocks * (group - 1)
        output, w_out_grad, low_xd, csums, dsums = call(
            output_kernel,
            [
                ((T, own), bf16), ((inner, columns), f32), ((T, wide), bf16), ((8 * CONV + 8, width), f32),
                ((16, LANES), f32),
            ],
            [
                ((T, inner), bf16), ((inner, D), bf16), ((2, T, 2 * columns), bf16), ((T, inner), bf16),
                ((T, inner), bf16), ((blocks, STATE, inner), bf16), ((T, inner), bf16), ((T, width), bf16),
                ((T + 8, width), f32),
                ((T, D), bf16), ((2, messages, BLOCK, own), bf16),
                ((4, inner, columns), bf16), ((2, inner // 2, columns), bf16), ((2, inner, columns), bf16),
                ((T, LANES), jnp.int32), ((T, LANES), jnp.int32), ((LANES, inner), bf16), ((T + 8, width), f32),
                ((STATE, inner), f32), ((BLOCK, inner), bf16), ((BLOCK, inner), f32), ((BLOCK, BLOCK), f32),
                ((BLOCK, BLOCK), f32),
            ],
            0, starts, tokens, gn, wout, cotangent, x_low, ssd, states, gs, slope, xin, bc_low, step, sgdt,
            step_low, decay_low, taps, crow, dpar,
            places="s" + "a" * 10 + "v" * 8,
            sems=[(9,), (2,), (2, messages), (2, messages), (4,), (4,), (4,), (4,)],
            collective=1,
        )
        size = lax.axis_size("dp")
        input_grad, w_z_grad, dwxd_own, smalls = call(
            input_kernel,
            [((T, own), bf16), ((shard, inner), f32), ((shard, wide), f32), ((16, width), f32)],
            [
                ((T, D), bf16), ((T, D), bf16), ((T, inner), bf16), ((T, wide), bf16), ((D, inner), bf16),
                ((D, wide), bf16), ((T, own), bf16),
                ((T, D), bf16), ((2, messages, BLOCK, own), bf16), ((BLOCK, own), f32),
                ((D, inner), bf16), ((4, shard, inner), bf16), ((2, shard // 2, inner), bf16), ((2, shard, inner), bf16),
                ((D, wide), bf16), ((4, shard, wide), bf16), ((2, shard // 2, wide), bf16), ((2, shard, wide), bf16),
                ((T, LANES), f32), ((8, T), f32), ((group - 1, 8, T), f32), ((8, D), f32),
                ((size - 1, 16, width), f32), ((group - 1, 8, pair), f32), ((group - 1, 8, inner), f32),
            ],
            0, tokens, inverse, gain, normed, low_gate, low_xd, wz, wxd, cotangent, csums, sums, dsums,
            places="avvaaaaaavvv",
            sems=[
                (7,), (2, messages), (2, messages), (4,), (4,), (4,), (4,), (4,), (4,), (4,), (4,),
                (group - 1,), (group - 1,), (size - 1,), (size - 1,), (2 * group - 2,), (2 * group - 2,),
            ],
            collective=2,
        )
        bc = lax.dynamic_slice_in_dim(smalls[: CONV + 1, inner:], rank * (pair // group), pair // group, 1)
        in_gain = lax.dynamic_slice_in_dim(smalls[8 : 8 + D // inner, :inner].reshape(D), rank * own, own, 0)
        w_bc_grad = lax.psum_scatter(
            dwxd_own[:, inner:width].astype(bf16), "mp", scatter_dimension=1, tiled=True
        ).astype(f32)
        return (
            output, input_grad, w_z_grad, dwxd_own[:, :inner], w_bc_grad, dwxd_own[:, width : width + heads],
            w_out_grad, smalls[:CONV, :inner], smalls[CONV, :inner], bc[:CONV], bc[CONV],
            smalls[7, :heads], smalls[7, LANES : LANES + heads],
            jnp.sum(smalls[6, :inner].reshape(heads, HEADDIM), axis=1), in_gain, smalls[5, :inner],
        )
    branch, dwout, dwz, low_gate, gs, sums = call(
        functools.partial(middle_kernel, width=inner * group),
        [
            ((T, D), bf16), ((inner, D), bf16), ((D, inner), bf16), ((T, inner), bf16), ((T, inner), bf16),
            ((16, inner), f32),
        ],
        [((T, inner), bf16)],
        0, cotangent, wout, normed, gate, x_low, ssd, gnorm, crow, stat,
    )
    low_xd, csums, dsums = call(
        backward_kernel,
        [((T, wide), bf16), ((8 * CONV + 8, width), f32), ((16, LANES), f32)],
        [
            ((T, LANES), jnp.int32), ((T, LANES), jnp.int32), ((LANES, inner), bf16), ((T + 8, width), f32),
            ((STATE, inner), f32), ((BLOCK, inner), bf16), ((BLOCK, inner), f32), ((BLOCK, BLOCK), f32),
            ((BLOCK, BLOCK), f32),
        ],
        1, starts, xin, slope, x_low, bc_low, step, sgdt, step_low, decay_low, ssd, states, gs, taps, crow,
        dpar,
    )
    dwxd, gfull, rowdot = call(
        last_kernel,
        [((D, wide), bf16), ((T, D), bf16), ((T, LANES), f32)],
        [],
        0, tokens, inverse, gain, normed, low_gate, low_xd, wz, wxd,
    )

    def scatter(v, axis, dim):
        return lax.psum_scatter(v, axis, scatter_dimension=dim, tiled=True)

    token_own = lax.dynamic_slice_in_dim(tokens, rank * own, own, 1).astype(f32)
    output = (token_own + scatter(branch, "mp", 1).astype(f32)).astype(bf16)
    w_out_grad = scatter(dwout, "dp", 1).astype(f32)
    w_z_grad = scatter(dwz, "dp", 0).astype(f32)
    dwxd_own = scatter(dwxd, "dp", 0)
    w_x_grad = dwxd_own[:, :inner].astype(f32)
    w_dt_grad = dwxd_own[:, width : width + heads].astype(f32)
    w_bc_grad = scatter(dwxd_own[:, inner:width], "mp", 1).astype(f32)

    g_own = scatter(gfull, "mp", 1).astype(f32)
    gain_own = lax.dynamic_slice_in_dim(input_norm_gain, rank * own, own, 0)
    row_mean = (lax.psum(rowdot[:, 0], "mp") / D)[:, None]
    inv = inverse[:, :1]
    hat = token_own * inv
    cot_own = lax.dynamic_slice_in_dim(cotangent, rank * own, own, 1).astype(f32)
    input_grad = (cot_own + inv * (g_own * gain_own - hat * row_mean)).astype(bf16)
    in_gain = jnp.sum(g_own * hat, axis=0)

    csums = jnp.sum(csums.reshape(CONV + 1, 8, width), axis=1)
    sums = jnp.sum(sums.reshape(2, 8, inner), axis=1)
    dsums = jnp.sum(dsums.reshape(2, 8, LANES), axis=1)[:, :heads]
    csums_bc = scatter(csums[:, inner:], "mp", 1)
    conv_grad, conv_bc_grad, sums, dsums, in_gain = lax.psum(
        (csums[:, :inner], csums_bc, sums, dsums, in_gain), "dp"
    )
    d_skip_grad = jnp.sum(sums[1].reshape(heads, HEADDIM), axis=1)
    return (
        output, input_grad, w_z_grad, w_x_grad, w_bc_grad, w_dt_grad, w_out_grad,
        conv_grad[:CONV], conv_grad[CONV], conv_bc_grad[:CONV], conv_bc_grad[CONV],
        dsums[0], dsums[1], d_skip_grad, in_gain, sums[0],
    )


def solution(mesh):
    row, block, column = P("dp", None), P("dp", "mp"), P("mp")
    return jax.shard_map(
        per_device,
        mesh=mesh,
        in_specs=(
            row, row, row, block, block, block, block, P("mp", "dp"), P(None, "mp"), column,
            P(None, "mp"), column, column, column, column, P(), column,
        ),
        out_specs=(
            block, block, block, block, block, block, P("mp", "dp"), P(None, "mp"), column,
            P(None, "mp"), column, column, column, column, column, column,
        ),
        check_vma=False,
    )
```

```python
import functools

import jax
import jax.numpy as jnp
from jax import lax
from jax.experimental import pallas as pl
from jax.experimental.pallas import tpu as pltpu
from jax.sharding import PartitionSpec as P

HEADDIM = 64
STATE = 128
CONV = 4
BLOCK = 256
DOCS = 5
LANES = 128
EPS = 1e-05
f32 = jnp.float32
bf16 = jnp.bfloat16
VMEM_LIMIT = 62 * 2**20


def mm(a, b):
    return jnp.dot(a, b, preferred_element_type=f32)


def mm_nt(a, b):
    return lax.dot_general(a, b, (((1,), (1,)), ((), ())), preferred_element_type=f32)


def mm_tn(a, b):
    return lax.dot_general(a, b, (((0,), (0,)), ((), ())), preferred_element_type=f32)


def halves(v):
    high = v.astype(bf16)
    return high, (v - high.astype(f32)).astype(bf16)


def expand(v, spread):
    high, rest = halves(v)
    return mm(high, spread) + mm(rest, spread)


def gather_heads(v, spread):
    high, rest = halves(v)
    return mm_nt(high, spread) + mm_nt(rest, spread)


def logistic(v):
    return 1.0 / (1.0 + jnp.exp(-v))


def tiles(total, size):
    return [(at, min(size, total - at)) for at in range(0, total, size)]


def fold(v):
    return jnp.sum(v.reshape(v.shape[0] // 8, 8, v.shape[1]), axis=0)


def doc_of(starts, place):
    count = (place >= starts[0]).astype(jnp.int32)
    for k in range(1, DOCS):
        count = count + (place >= starts[k]).astype(jnp.int32)
    return count


def fill_spread(spread):
    rows, columns = spread.shape
    head = lax.broadcasted_iota(jnp.int32, (rows, columns), 0)
    channel = lax.broadcasted_iota(jnp.int32, (rows, columns), 1)
    low = head * HEADDIM
    spread[...] = jnp.where((channel >= low) & (channel < low + HEADDIM), 1.0, 0.0).astype(bf16)


def fill_positions(starts, pos, rpos):
    length = pos.shape[0]

    def body(i, carry):
        at = pl.multiple_of(i * BLOCK, BLOCK)
        place = lax.broadcasted_iota(jnp.int32, (BLOCK, LANES), 0) + at
        begin = jnp.zeros_like(place)
        end = jnp.full_like(place, length)
        for k in range(DOCS):
            begin = jnp.maximum(begin, jnp.where(place >= starts[k], starts[k], 0))
            end = jnp.minimum(end, jnp.where(place < starts[k], starts[k], length))
        pos[pl.ds(at, BLOCK), :] = place - begin
        if rpos is not None:
            rpos[pl.ds(at, BLOCK), :] = end - 1 - place
        return carry

    lax.fori_loop(0, length // BLOCK, body, 0)


def normalize(tok, gain, normed, stat):
    step = 64

    def body(i, carry):
        rows = pl.ds(pl.multiple_of(i * step, step), step)
        v = tok[rows, :].astype(f32)
        inverse = lax.rsqrt(jnp.mean(v * v, axis=1, keepdims=True) + EPS)
        normed[rows, :] = (v * inverse * gain[...]).astype(bf16)
        stat[rows, :] = jnp.broadcast_to(inverse, (step, LANES))
        return carry

    lax.fori_loop(0, tok.shape[0] // step, body, 0)


def project_x(normed, wxd, xin, dtin):
    length, width = normed.shape[0], xin.shape[1]
    xin[pl.ds(0, 8), :] = jnp.zeros((8, width), f32)
    rows = 512

    def body(i, carry):
        at = pl.multiple_of(i * rows, rows)
        left = normed[pl.ds(at, rows), :]
        for c, w in tiles(width, 512):
            xin[pl.ds(at + 8, rows), c : c + w] = mm(left, wxd[:, c : c + w])
        dtin[pl.ds(at, rows), :] = mm(left, wxd[:, width : width + LANES])
        return carry

    lax.fori_loop(0, length // rows, body, 0)


def convolve(xin, taps, pos, slope, x_low, bc_low):
    width, inner = xin.shape[1], x_low.shape[1]

    def tile(b, c, out, at):
        rows = pl.ds(pl.multiple_of(b * BLOCK, BLOCK), BLOCK)
        x = xin[pl.ds(pl.multiple_of(b * BLOCK, BLOCK), BLOCK + 8), pl.ds(c, LANES)]
        place = pos[rows, :]
        tap = taps[:, pl.ds(c, LANES)]
        pre = tap[CONV : CONV + 1] + tap[CONV - 1 : CONV] * x[8:]
        for lag in range(1, CONV):
            earlier = pltpu.roll(x, lag, 0)[8:]
            pre = pre + tap[CONV - 1 - lag : CONV - lag] * jnp.where(place >= lag, earlier, 0.0)
        sg = logistic(pre)
        slope[rows, pl.ds(c, LANES)] = (sg * (1.0 + pre * (1.0 - sg))).astype(bf16)
        out[rows, pl.ds(at, LANES)] = (pre * sg).astype(bf16)

    blocks = x_low.shape[0] // BLOCK
    xcols, bcols = inner // LANES, (width - inner) // LANES

    def x_body(i, carry):
        c = pl.multiple_of((i % xcols) * LANES, LANES)
        tile(i // xcols, c, x_low, c)
        return carry

    def bc_body(i, carry):
        c = pl.multiple_of((i % bcols) * LANES, LANES)
        tile(i // bcols, inner + c, bc_low, c)
        return carry

    lax.fori_loop(0, blocks * xcols, x_body, 0)
    lax.fori_loop(0, blocks * bcols, bc_body, 0)


def steps(dtin, dpar, step, sgdt, step_low, decay_low):
    def body(i, carry):
        rows = pl.ds(pl.multiple_of(i * BLOCK, BLOCK), BLOCK)
        v = dtin[rows, :] + dpar[0:1, :]
        soft = jnp.maximum(v, 0.0) + jnp.log1p(jnp.exp(-jnp.abs(v)))
        step[rows, :] = soft
        sgdt[rows, :] = logistic(v)
        step_low[rows, :] = soft.astype(bf16)
        decay_low[rows, :] = (-dpar[1:2, :] * soft).astype(bf16)
        return carry

    lax.fori_loop(0, dtin.shape[0] // BLOCK, body, 0)


def block_marks(starts, b):
    at = b * BLOCK
    column = doc_of(starts, lax.broadcasted_iota(jnp.int32, (BLOCK, 1), 0) + at)
    row = doc_of(starts, lax.broadcasted_iota(jnp.int32, (1, BLOCK), 1) + at)
    before = doc_of(starts, at - 1)
    last = doc_of(starts, at + BLOCK - 1)
    return column, row, before, last


def block_decays(b, starts, decay_low, step_low, spread):
    rows = pl.ds(pl.multiple_of(b * BLOCK, BLOCK), BLOCK)
    column, row, before, last = block_marks(starts, b)
    i0 = lax.broadcasted_iota(jnp.int32, (BLOCK, BLOCK), 0)
    i1 = lax.broadcasted_iota(jnp.int32, (BLOCK, BLOCK), 1)
    lower = jnp.where(i0 >= i1, 1.0, 0.0).astype(bf16)
    cum = mm(lower, decay_low[rows, :])
    step_e = mm(step_low[rows, :], spread[...])
    cum_e = expand(jnp.exp(cum), spread[...])
    kept_e = jnp.where(before == last, cum_e[BLOCK - 1 : BLOCK], 0.0)
    in_e = jnp.where(column == before, cum_e, 0.0)
    out_e = expand(jnp.exp(cum[BLOCK - 1 : BLOCK] - cum), spread[...])
    out_e = jnp.where(column == last, out_e, 0.0)
    return cum, step_e, kept_e, in_e, out_e, column, row


def scan_forward(
    starts, x_low, bc_low, step_low, decay_low, ssd, states, spread, state, xs, yin, cbm, tick=None
):
    length, inner = x_low.shape
    state[...] = jnp.zeros_like(state)

    def body(b, carry):
        rows = pl.ds(pl.multiple_of(b * BLOCK, BLOCK), BLOCK)
        cum, step_e, kept_e, in_e, out_e, column, row = block_decays(
            b, starts, decay_low, step_low, spread
        )
        bm, cm = bc_low[rows, :STATE], bc_low[rows, STATE:]
        i0 = lax.broadcasted_iota(jnp.int32, (BLOCK, BLOCK), 0)
        i1 = lax.broadcasted_iota(jnp.int32, (BLOCK, BLOCK), 1)
        cbm[...] = jnp.where((column == row) & (i0 >= i1), mm_nt(cm, bm), 0.0)
        stepped = x_low[rows, :].astype(f32) * step_e
        xs[...] = stepped.astype(bf16)
        entering = state[...].astype(bf16)
        states[b] = entering
        yin[...] = in_e * mm(cm, entering)
        state[...] = kept_e * state[...] + mm_tn(bm, (stepped * out_e).astype(bf16))
        cum_t = cum.T
        first = lax.broadcasted_iota(jnp.int32, (BLOCK, LANES), 1) < HEADDIM
        for j in range(inner // LANES):
            cols = slice(j * LANES, (j + 1) * LANES)
            pair = xs[:, cols]
            part = []
            for h in (2 * j, 2 * j + 1):
                span = jnp.minimum(cum[:, h : h + 1] - cum_t[h : h + 1, :], 0.0)
                part.append(mm((jnp.exp(span) * cbm[...]).astype(bf16), pair))
            y = jnp.where(first, part[0], part[1]) + yin[:, cols]
            ssd[rows, cols] = y.astype(bf16)
        if tick is not None:
            tick(b)
        return carry

    lax.fori_loop(0, length // BLOCK, body, 0)


def project_rows(left, right, out, rows=512, columns=512):
    def body(i, carry):
        at = pl.ds(pl.multiple_of(i * rows, rows), rows)
        part = left[at, :]
        for c, w in tiles(out.shape[1], columns):
            out[at, c : c + w] = mm(part, right[:, c : c + w]).astype(out.dtype)
        return carry

    lax.fori_loop(0, out.shape[0] // rows, body, 0)


def back_rows(left, right, out, rows=512, columns=512):
    def body(i, carry):
        at = pl.ds(pl.multiple_of(i * rows, rows), rows)
        part = left[at, :]
        for c, w in tiles(out.shape[1], columns):
            out[at, c : c + w] = mm_nt(part, right[c : c + w, :]).astype(out.dtype)
        return carry

    lax.fori_loop(0, out.shape[0] // rows, body, 0)


def weight_rows(left, right, out, rows=256, columns=512):
    def body(i, carry):
        at = pl.ds(pl.multiple_of(i * rows, rows), rows)
        part = left[:, at]
        for c, w in tiles(out.shape[1], columns):
            out[at, c : c + w] = mm_tn(part, right[:, c : c + w]).astype(out.dtype)
        return carry

    lax.fori_loop(0, out.shape[0] // rows, body, 0)


def gate_sums(gate, ssd, x_low, gnorm, crow, stat):
    step, inner = 64, gate.shape[1]

    def body(i, carry):
        rows = pl.ds(pl.multiple_of(i * step, step), step)
        squares = jnp.zeros((step, 256), f32)
        crosses = jnp.zeros((step, 256), f32)
        for c in range(0, inner, 256):
            cols = slice(c, c + 256)
            g = gate[rows, cols]
            mixed = ssd[rows, cols].astype(f32) + crow[1:2, cols] * x_low[rows, cols].astype(f32)
            gated = mixed * (g * logistic(g))
            squares = squares + gated * gated
            crosses = crosses + gnorm[rows, cols] * crow[0:1, cols] * gated
        lane = lax.broadcasted_iota(jnp.int32, (step, LANES), 1)
        s1 = jnp.sum(squares, axis=1, keepdims=True)
        s2 = jnp.sum(crosses, axis=1, keepdims=True)
        stat[rows, :] = jnp.where(lane == 0, s1, jnp.where(lane == 1, s2, 0.0))
        return carry

    lax.fori_loop(0, gate.shape[0] // step, body, 0)


def forward_kernel(
    starts, tok, gain, wxd, wz, taps, dpar,
    normed, inverse, xin, slope, gate, x_low, bc_low, step, sgdt, step_low, decay_low, ssd, states,
    pos, spread, dtin, state, xs, yin, cbm,
):
    fill_spread(spread)
    fill_positions(starts, pos, None)
    normalize(tok, gain, normed, inverse)
    project_x(normed, wxd, xin, dtin)
    convolve(xin, taps, pos, slope, x_low, bc_low)
    steps(dtin, dpar, step, sgdt, step_low, decay_low)
    scan_forward(starts, x_low, bc_low, step_low, decay_low, ssd, states, spread, state, xs, yin, cbm)
    project_rows(normed, wz, gate)


def gate_kernel(cot, wout, gate, ssd, x_low, crow, gnorm, stat):
    back_rows(cot, wout, gnorm)
    gate_sums(gate, ssd, x_low, gnorm, crow, stat)


def gate_backward(gate, ssd, x_low, gnorm, crow, stat, width, gn, low_gate, gs, sums):
    step, inner = 64, gate.shape[1]
    sums[...] = jnp.zeros_like(sums)

    def body(i, carry):
        rows = pl.ds(pl.multiple_of(i * step, step), step)
        inverse = lax.rsqrt(stat[rows, 0:1] / width + EPS)
        mean = inverse * stat[rows, 1:2] / width
        for c in range(0, inner, 256):
            cols = slice(c, c + 256)
            g = gate[rows, cols]
            x = x_low[rows, cols].astype(f32)
            mixed = ssd[rows, cols].astype(f32) + crow[1:2, cols] * x
            sg = logistic(g)
            act = g * sg
            hat = mixed * act * inverse
            gn[rows, cols] = (hat * crow[0:1, cols]).astype(bf16)
            gnorm_here = gnorm[rows, cols]
            grad = inverse * (gnorm_here * crow[0:1, cols] - hat * mean)
            grad_mixed = grad * act
            low_gate[rows, cols] = (grad * mixed * (sg * (1.0 + g * (1.0 - sg)))).astype(bf16)
            gs[rows, cols] = grad_mixed.astype(bf16)
            sums[0:8, cols] += fold(gnorm_here * hat)
            sums[8:16, cols] += fold(grad_mixed * x)
        return carry

    lax.fori_loop(0, gate.shape[0] // step, body, 0)


def middle_kernel(
    cot, wout, normed, gate, x_low, ssd, gnorm, crow, stat,
    branch, dwout, dwz, low_gate, gs, sums,
    gn, *, width,
):
    gate_backward(gate, ssd, x_low, gnorm, crow, stat, width, gn, low_gate, gs, sums)
    project_rows(gn, wout, branch)
    weight_rows(gn, cot, dwout)
    weight_rows(normed, low_gate, dwz)


def scan_backward(
    starts, x_low, bc_low, step_low, decay_low, ssd, states, gs, slope, crow, step, sgdt, dpar,
    gpre, low_xd, dsums, spread, dstate, xs, gx, cbm, acc, tick=None,
):
    length, inner = x_low.shape
    width = gpre.shape[1]
    blocks = length // BLOCK
    dstate[...] = jnp.zeros_like(dstate)
    dsums[...] = jnp.zeros_like(dsums)
    gpre[pl.ds(length, 8), :] = jnp.zeros((8, width), f32)

    def body(i, carry):
        b = blocks - 1 - i
        rows = pl.ds(pl.multiple_of(b * BLOCK, BLOCK), BLOCK)
        cum, step_e, kept_e, in_e, out_e, column, row = block_decays(
            b, starts, decay_low, step_low, spread
        )
        bm, cm = bc_low[rows, :STATE], bc_low[rows, STATE:]
        i0 = lax.broadcasted_iota(jnp.int32, (BLOCK, BLOCK), 0)
        i1 = lax.broadcasted_iota(jnp.int32, (BLOCK, BLOCK), 1)
        linked = (column == row) & (i0 <= i1)
        cbm[...] = jnp.where(linked, mm_nt(bm, cm), 0.0)
        x = x_low[rows, :].astype(f32)
        stepped = x * step_e
        xs[...] = stepped.astype(bf16)
        cum_t = cum.T
        first = lax.broadcasted_iota(jnp.int32, (BLOCK, LANES), 1) < HEADDIM
        acc[...] = jnp.zeros_like(acc)
        for j in range(inner // LANES):
            cols = slice(j * LANES, (j + 1) * LANES)
            xpair, gpair = xs[:, cols], gs[rows, cols]
            none = jnp.zeros_like(xpair)
            part, total = [], None
            for k in range(2):
                h = 2 * j + k
                kernel = jnp.exp(jnp.minimum(cum_t[h : h + 1, :] - cum[:, h : h + 1], 0.0))
                part.append(mm((kernel * cbm[...]).astype(bf16), gpair))
                own = jnp.where(first, xpair, none) if k == 0 else jnp.where(first, none, xpair)
                here = kernel * mm_nt(own, gpair)
                total = here if total is None else total + here
            acc[...] += total
            gx[:, cols] = jnp.where(first, part[0], part[1])
        dstate_low = dstate[...].astype(bf16)
        entering = states[b]
        leaving = states[jnp.minimum(b + 1, blocks - 1)]
        end = jnp.sum(dstate[...] * leaving.astype(f32), axis=0, keepdims=True)
        g = gs[rows, :].astype(f32)
        g_in = (in_e * g).astype(bf16)
        raw = gx[...] + out_e * mm(bm, dstate_low)
        grad_x = (step_e * raw).astype(bf16).astype(f32)
        gpre[rows, :inner] = (grad_x + crow[1:2, :] * g) * slope[rows, :inner]
        pairs = jnp.where(linked, acc[...], 0.0).astype(bf16)
        db = mm(pairs, cm) + mm_nt((stepped * out_e).astype(bf16), dstate_low)
        dc = mm_tn(pairs, bm) + mm_nt(g_in, entering)
        gpre[rows, inner : inner + STATE] = db * slope[rows, inner : inner + STATE]
        gpre[rows, inner + STATE :] = dc * slope[rows, inner + STATE :]
        raw_x = x * raw
        grad_step = gather_heads(raw_x, spread[...]).astype(bf16).astype(f32)
        dcum = gather_heads(g * ssd[rows, :].astype(f32) - step_e * raw_x, spread[...])
        tail = gather_heads(jnp.broadcast_to(end, (8, inner)), spread[...])[0:1]
        upper = jnp.where(i0 <= i1, 1.0, 0.0).astype(bf16)
        high, rest = halves(dcum)
        later = mm(upper, high) + mm(upper, rest) + tail
        grad_decay = later.astype(bf16).astype(f32)
        total_step = grad_step - dpar[1:2, :] * grad_decay
        grad_dt = total_step * sgdt[rows, :]
        low_xd[rows, width:] = grad_dt.astype(bf16)
        dsums[0:8, :] += fold(grad_dt)
        dsums[8:16, :] -= fold(grad_decay * step[rows, :])
        dstate[...] = kept_e * dstate[...] + mm_tn(cm, g_in)
        if tick is not None:
            tick(i)
        return carry

    lax.fori_loop(0, blocks, body, 0)


def convolve_back(xin, gpre, taps, pos, rpos, low_xd, csums):
    width = gpre.shape[1]
    columns = width // LANES
    csums[...] = jnp.zeros_like(csums)

    def body(i, carry):
        at = pl.multiple_of((i // columns) * BLOCK, BLOCK)
        cols = pl.ds(pl.multiple_of((i % columns) * LANES, LANES), LANES)
        rows = pl.ds(at, BLOCK)
        x = xin[pl.ds(at, BLOCK + 8), cols]
        g = gpre[pl.ds(at, BLOCK + 8), cols]
        here = g[:BLOCK]
        place, ahead = pos[rows, :], rpos[rows, :]
        tap = taps[:, cols]
        grad = tap[CONV - 1 : CONV] * here
        csums[pl.ds(8 * CONV, 8), cols] += fold(here)
        csums[pl.ds(8 * (CONV - 1), 8), cols] += fold(here * x[8:])
        for lag in range(1, CONV):
            k = CONV - 1 - lag
            later = pltpu.roll(g, BLOCK + 8 - lag, 0)[:BLOCK]
            earlier = pltpu.roll(x, lag, 0)[8:]
            grad = grad + tap[k : k + 1] * jnp.where(ahead >= lag, later, 0.0)
            csums[pl.ds(8 * k, 8), cols] += fold(here * jnp.where(place >= lag, earlier, 0.0))
        low_xd[rows, cols] = grad.astype(bf16)
        return carry

    lax.fori_loop(0, (xin.shape[0] - 8) // BLOCK * columns, body, 0)


def backward_kernel(
    starts, xin, slope, x_low, bc_low, step, sgdt, step_low, decay_low, ssd, states, gs, taps, crow, dpar,
    low_xd, csums, dsums,
    pos, rpos, spread, gpre, dstate, xs, gx, cbm, acc,
):
    fill_spread(spread)
    fill_positions(starts, pos, rpos)
    scan_backward(
        starts, x_low, bc_low, step_low, decay_low, ssd, states, gs, slope, crow, step, sgdt, dpar,
        gpre, low_xd, dsums, spread, dstate, xs, gx, cbm, acc,
    )
    convolve_back(xin, gpre, taps, pos, rpos, low_xd, csums)


def last_kernel(tok, inverse, gain, normed, low_gate, low_xd, wz, wxd, dwxd, gfull, rowdot):
    weight_rows(normed, low_xd, dwxd)
    rows = 256

    def body(i, carry):
        at = pl.ds(pl.multiple_of(i * rows, rows), rows)
        total = jnp.zeros((rows, 1), f32)
        for c, w in tiles(gfull.shape[1], 512):
            cols = slice(c, c + w)
            part = mm_nt(low_gate[at, :], wz[cols, :]) + mm_nt(low_xd[at, :], wxd[cols, :])
            gfull[at, cols] = part.astype(bf16)
            total = total + jnp.sum(part * gain[:, cols] * tok[at, cols].astype(f32), axis=1, keepdims=True)
        rowdot[at, :] = total * inverse[at, :]
        return carry

    lax.fori_loop(0, gfull.shape[0] // rows, body, 0)


MESH = pl.DeviceIdType.MESH


def remote(source, target, send, receive, **where):
    return pltpu.make_async_remote_copy(
        src_ref=source, dst_ref=target, send_sem=send, recv_sem=receive, device_id=where, device_id_type=MESH
    )


def add_into(target, source, rows=64):
    def body(i, carry):
        at = pl.ds(pl.multiple_of(i * rows, rows), rows)
        target[at, :] = (target[at, :].astype(f32) + source[at, :].astype(f32)).astype(target.dtype)
        return carry

    lax.fori_loop(0, target.shape[0] // rows, body, 0)


class Ring:
    def __init__(self):
        self.me = lax.axis_index("dp")
        self.core = self.me % 2
        chip = self.me // 2
        y = chip // 2
        self.pos = 2 * y + (chip + y) % 2
        self.partner = self.me + 1 - 2 * self.core
        self.right = self.at(self.pos + 1)
        self.left = self.at(self.pos + 3)
        self.across = self.at(self.pos + 2)

    def at(self, pos):
        pos = pos % 4
        y = pos // 2
        return (2 * y + (pos + y) % 2) * 2 + self.core


def greet(ring, everyone):
    barrier = pltpu.get_barrier_semaphore()
    n, z = lax.axis_size("mp"), lax.axis_index("mp")
    if everyone:
        size = lax.axis_size("dp")
        close = [(ring.me + i) % size for i in range(1, size)]
    else:
        close = [ring.partner, ring.right, ring.left]
    for other in close:
        pl.semaphore_signal(barrier, inc=1, device_id={"dp": other}, device_id_type=MESH)
    for i in range(1, n):
        pl.semaphore_signal(barrier, inc=1, device_id={"mp": (z + i) % n}, device_id_type=MESH)
    pl.semaphore_wait(barrier, len(close) + n - 1)


class Scatter:
    def __init__(self, ring, shard, cores, parts, wholes, sems):
        self.ring, self.shard = ring, shard
        self.cores, self.parts, self.wholes = cores, parts, wholes
        self.core_send, self.core_recv, self.ring_send, self.ring_recv = sems
        self.half = cores.shape[1] // 2

    def upper(self, r):
        return self.shard(r).at[pl.ds(0, self.half), :]

    def lower(self, r):
        return self.shard(r).at[pl.ds(self.half, self.half), :]

    def core_copy(self, chip):
        ring = self.ring
        return remote(
            self.shard(2 * chip + 1 - ring.core), self.cores.at[chip],
            self.core_send.at[chip], self.core_recv.at[chip], dp=ring.partner,
        )

    def ring_copy(self, k):
        ring = self.ring
        source = (self.upper(ring.across), self.lower(ring.across), self.shard(ring.right), self.shard(ring.left))[k]
        target = (self.parts.at[0], self.parts.at[1], self.wholes.at[0], self.wholes.at[1])[k]
        return remote(
            source, target, self.ring_send.at[k], self.ring_recv.at[k], dp=(ring.right, ring.left)[k % 2]
        )

    def start(self, chip):
        self.core_copy(chip).start()

    def first(self):
        def body(chip, carry):
            self.core_copy(chip).wait_recv()
            add_into(self.shard(2 * chip + self.ring.core), self.cores.at[chip])
            return carry

        lax.fori_loop(0, 4, body, 0)
        self.ring_copy(0).start()
        self.ring_copy(1).start()

    def second(self):
        self.ring_copy(0).wait_recv()
        add_into(self.upper(self.ring.right), self.parts.at[0])
        self.ring_copy(2).start()
        self.ring_copy(1).wait_recv()
        add_into(self.lower(self.ring.left), self.parts.at[1])
        self.ring_copy(3).start()

    def finish(self, out, rows=64):
        self.ring_copy(2).wait_recv()
        self.ring_copy(3).wait_recv()
        own = self.shard(self.ring.me)

        def body(i, carry):
            at = pl.ds(pl.multiple_of(i * rows, rows), rows)
            out[at, :] = own[at, :].astype(f32) + self.wholes[0, at, :].astype(f32) + self.wholes[1, at, :].astype(f32)
            return carry

        lax.fori_loop(0, out.shape[0] // rows, body, 0)

        def done(chip, carry):
            self.core_copy(chip).wait_send()
            return carry

        lax.fori_loop(0, 4, done, 0)
        for k in range(4):
            self.ring_copy(k).wait_send()


class Line:
    def __init__(self, part, slots, sems, total):
        self.part, self.slots, self.total = part, slots, total
        self.send, self.recv = sems
        self.n, self.z = lax.axis_size("mp"), lax.axis_index("mp")
        self.blocks = part.shape[0] // BLOCK
        self.own = part.shape[1] // self.n
        self.place = (self.z, self.n - 1 - self.z)
        self.count = self.blocks * (self.n - 1)

    def rows(self, t):
        return pl.ds(pl.multiple_of(t * BLOCK, BLOCK), BLOCK)

    def columns(self, q):
        return pl.ds(pl.multiple_of(q * self.own, self.own), self.own)

    def copy(self, side, k):
        d = k // self.blocks
        q = self.n - 1 - d if side == 0 else d
        source = self.part.at[self.rows(k - d * self.blocks), self.columns(q)]
        return remote(
            source, self.slots.at[side, k], self.send.at[side, k], self.recv.at[side, k],
            mp=self.z + 1 if side == 0 else self.z - 1,
        ), source

    def inject(self, k):
        for side in range(2):
            @pl.when(self.place[side] == 0)
            def _():
                self.copy(side, k)[0].start()

    def forward(self, k, hop):
        for side in range(2):
            @pl.when(self.place[side] == hop)
            def _():
                copy, source = self.copy(side, k)
                copy.wait_recv()
                add_into(source, self.slots.at[side, k])
                copy.start()

    def finish(self, t):
        self.total[...] = self.part[self.rows(t), self.columns(self.z)].astype(f32)
        for side in range(2):
            @pl.when(self.place[side] >= 1)
            def _():
                k = (self.n - 1 - self.place[side]) * self.blocks + t
                self.copy(side, k)[0].wait_recv()
                self.total[...] += self.slots[side, k].astype(f32)

    def drain(self):
        def body(k, carry):
            for side in range(2):
                @pl.when(self.place[side] + k // self.blocks <= self.n - 2)
                def _():
                    self.copy(side, k)[0].wait_send()
            return carry

        lax.fori_loop(0, self.count, body, 0)

    def order(self, i):
        z = self.z
        far = jnp.where(z < 2, 3 - i, i)
        near = z + 1 - 2 * (z % 2)
        return jnp.where(i < 2, far, jnp.where(i == 2, near, z))


class Loads:
    def __init__(self, sems):
        self.sems, self.pairs = sems, []

    def start(self, source, target):
        i = len(self.pairs)
        copy = pltpu.make_async_copy(source, target, self.sems.at[i])
        copy.start()
        self.pairs.append(copy)
        return copy


class Gather:
    def __init__(self, ring, shard, rows, sems):
        self.ring, self.shard, self.half = ring, shard, rows // 2
        self.ring_send, self.ring_recv, self.core_send, self.core_recv = sems
        self.other = 1 - 2 * ring.core

    def ring_copy(self, k, source):
        ring = self.ring
        piece = self.shard(source)
        if k >= 2:
            piece = piece.at[pl.ds((k - 2) * self.half, self.half), :]
        return remote(
            piece, piece, self.ring_send.at[k], self.ring_recv.at[k], dp=(ring.right, ring.left)[k % 2]
        )

    def core_copy(self, k, source):
        return remote(
            self.shard(source), self.shard(source), self.core_send.at[k], self.core_recv.at[k], dp=self.ring.partner
        )

    def start(self):
        me = self.ring.me
        self.ring_copy(0, me).start()
        self.ring_copy(1, me).start()
        self.core_copy(0, me).start()

    def second(self):
        left, right = self.ring.left, self.ring.right
        self.ring_copy(0, left).wait_recv()
        self.ring_copy(2, left).start()
        self.core_copy(1, left).start()
        self.ring_copy(1, right).wait_recv()
        self.ring_copy(3, right).start()
        self.core_copy(2, right).start()

    def third(self):
        across = self.ring.across
        self.ring_copy(2, across).wait_recv()
        self.ring_copy(3, across).wait_recv()
        self.core_copy(3, across).start()

    def arrived(self, k):
        ring = self.ring
        source = (ring.me, ring.left, ring.right, ring.across)[k] + self.other
        self.core_copy(k, source).wait_recv()

    def drain(self):
        ring = self.ring
        for k, source in enumerate((ring.me, ring.me, ring.left, ring.right)):
            self.ring_copy(k, source).wait_send()
        for k, source in enumerate((ring.me, ring.left, ring.right, ring.across)):
            self.core_copy(k, source).wait_send()


def cast_into(target, source, rows=64):
    def body(i, carry):
        at = pl.ds(pl.multiple_of(i * rows, rows), rows)
        target[at, :] = source[at, :].astype(target.dtype)
        return carry

    lax.fori_loop(0, target.shape[0] // rows, body, 0)


def gather_kernel(
    lengths, tok, cot, w_x, w_z, w_out, w_bc, w_dt, conv_x, conv_x_bias, conv_bc, conv_bc_bias, dt_bias, a_rate,
    d_skip, gain, out_gain,
    normed_o, xin_o, slope_o, x_low_o, ssd_o, states_o, wxd_o, wz_o, wout_o, gn_o, low_gate_o, gs_o,
    bc_low, step, sgdt, step_low, decay_low, inverse, sums, taps, crow, dpar,
    v_tc, stage_a, stage_b, normed, xin, slope, x_low, ssd, states, wxd, wz, wout, gate, gnorm,
    bc_slots, tap_slots, row_slots, wide, stat, turned,
    pos, spread, dtin, state, xs, yin, cbm,
    load_sems, store_sems, ring_send, ring_recv, core_send, core_recv, mp_send, mp_recv,
):
    ring = Ring()
    n, z = lax.axis_size("mp"), lax.axis_index("mp")
    length, features = normed.shape
    inner, width = gate.shape[1], xin.shape[1]
    shard, column_shard = stage_a.shape[0], stage_b.shape[1]
    heads, per = w_dt.shape[1], w_bc.shape[1]
    loads, stores = Loads(load_sems), Loads(store_sems)
    load_x = loads.start(w_x, stage_a)
    load_tok = loads.start(tok, v_tc)
    load_out = loads.start(w_out, stage_b)
    starts = [jnp.int32(0)]
    for k in range(DOCS - 1):
        starts.append(starts[-1] + lengths[0, k])

    wide[...] = jnp.zeros_like(wide)
    wide[:, :per] = w_bc[...]
    bc_slots[0] = wide[...].astype(bf16)
    tap_slots[0] = jnp.zeros_like(tap_slots[0])
    tap_slots[0, :CONV, :per] = conv_bc[...]
    tap_slots[0, CONV : CONV + 1, :per] = conv_bc_bias[...]
    wide[...] = jnp.zeros_like(wide)
    wide[:, :heads] = w_dt[...]
    own_rows = pl.ds(pl.multiple_of(ring.me * shard, shard), shard)
    wxd[own_rows, width:] = wide[...].astype(bf16)
    dpar[...] = jnp.zeros_like(dpar)
    dpar[0:1, :heads] = dt_bias[...]
    dpar[1:2, :heads] = a_rate[...]
    dpar[2:3, :heads] = d_skip[...]

    greet(ring, False)

    def exchange(k, i):
        slots = (bc_slots, tap_slots, row_slots)[k]
        at = k * (n - 1) + i - 1
        return remote(slots.at[0], slots.at[i], mp_send.at[at], mp_recv.at[at], mp=(z + i) % n)

    def rows_of(ref, low, high):
        def shard_of(r):
            return ref.at[pl.ds(pl.multiple_of(r * shard, shard), shard), pl.ds(low, high - low)]

        return shard_of

    def columns_of(r):
        return wout.at[:, pl.ds(pl.multiple_of(r * column_shard, column_shard), column_shard)]

    sems = [tuple(group.at[k] for group in (ring_send, ring_recv, core_send, core_recv)) for k in range(4)]
    get_x = Gather(ring, rows_of(wxd, 0, inner), shard, sems[0])
    get_bd = Gather(ring, rows_of(wxd, inner, wxd.shape[1]), shard, sems[1])
    get_z = Gather(ring, rows_of(wz, 0, inner), shard, sems[2])
    get_out = Gather(ring, columns_of, inner, sems[3])

    load_x.wait()
    cast_into(get_x.shard(ring.me), stage_a)
    get_x.start()
    for k in range(2):
        for i in range(1, n):
            exchange(k, i).start()
    load_z = loads.start(w_z, stage_a)
    fill_spread(spread)
    fill_positions(starts, pos, None)
    crow[0:1, :] = out_gain[...]
    crow[1:2, :] = expand(dpar[...], spread[...])[2:3]
    load_tok.wait()
    normalize(tok=v_tc, gain=gain, normed=normed, stat=inverse)
    load_cot = loads.start(cot, v_tc)
    store_normed = stores.start(normed, normed_o)
    for k in range(2):
        for i in range(1, n):
            exchange(k, i).wait()
    first = lax.broadcasted_iota(jnp.int32, (shard, LANES), 1) < per
    for j in range((width - inner) // LANES):
        low, high = (z - 2 * j + n) % n, (z - 2 * j - 1 + n) % n
        columns = slice(inner + j * LANES, inner + (j + 1) * LANES)
        pair = jnp.where(first, bc_slots[low].astype(f32), pltpu.roll(bc_slots[high].astype(f32), per, 1))
        wxd[own_rows, columns] = pair.astype(bf16)
        taps[:, columns] = jnp.where(first[:8], tap_slots[low], pltpu.roll(tap_slots[high], per, 1))
    get_bd.start()
    taps[:, :inner] = jnp.zeros((8, inner), f32)
    taps[:CONV, :inner] = conv_x[...]
    taps[CONV : CONV + 1, :inner] = conv_x_bias[...]
    load_z.wait()
    cast_into(get_z.shard(ring.me), stage_a)
    load_out.wait()
    cast_into(get_out.shard(ring.me), stage_b)
    xin[pl.ds(0, 8), :] = jnp.zeros((8, width), f32)

    def project_chip(k, source):
        get_x.arrived(k)
        get_bd.arrived(k)
        part = pl.ds(pl.multiple_of((source // 2) * 2 * shard, 2 * shard), 2 * shard)

        def body(i, carry):
            at = pl.multiple_of(i * 512, 512)
            left = normed[pl.ds(at, 512), part]
            for c, w in tiles(wxd.shape[1], 512):
                here = mm(left, wxd[part, c : c + w])
                w_x_part = min(w, width - c)
                if k == 0:
                    xin[pl.ds(at + 8, 512), c : c + w_x_part] = here[:, :w_x_part]
                else:
                    xin[pl.ds(at + 8, 512), c : c + w_x_part] += here[:, :w_x_part]
                if w_x_part < w:
                    if k == 0:
                        dtin[pl.ds(at, 512), :] = here[:, w_x_part:]
                    else:
                        dtin[pl.ds(at, 512), :] += here[:, w_x_part:]
            return carry

        lax.fori_loop(0, length // 512, body, 0)

    project_chip(0, ring.me)
    get_x.second()
    get_bd.second()
    get_z.start()
    project_chip(1, ring.left)
    project_chip(2, ring.right)
    get_x.third()
    get_bd.third()
    project_chip(3, ring.across)
    for source, target in ((xin, xin_o), (wxd, wxd_o)):
        stores.start(source, target)
    steps(dtin, dpar, step, sgdt, step_low, decay_low)
    convolve(xin, taps, pos, slope, x_low, bc_low)
    get_z.second()
    get_out.start()
    for source, target in ((slope, slope_o), (x_low, x_low_o)):
        stores.start(source, target)

    def scan_tick(b):
        @pl.when(b == 1)
        def _():
            get_z.third()

    scan_forward(
        starts, x_low, bc_low, step_low, decay_low, ssd, states, spread, state, xs, yin, cbm, scan_tick
    )
    for source, target in ((ssd, ssd_o), (states, states_o)):
        stores.start(source, target)
    get_out.second()
    for k in range(4):
        get_z.arrived(k)
    project_rows(normed, wz, gate)
    stores.start(wz, wz_o)
    load_cot.wait()

    def back_chip(k, source):
        get_out.arrived(k)
        part = pl.ds(pl.multiple_of((source // 2) * 2 * column_shard, 2 * column_shard), 2 * column_shard)

        def body(i, carry):
            at = pl.ds(pl.multiple_of(i * 512, 512), 512)
            left = v_tc[at, part]
            for c, w in tiles(inner, 512):
                here = mm_nt(left, wout[c : c + w, part])
                if k == 0:
                    gnorm[at, c : c + w] = here
                else:
                    gnorm[at, c : c + w] += here
            return carry

        lax.fori_loop(0, length // 512, body, 0)

    back_chip(0, ring.me)
    back_chip(1, ring.left)
    back_chip(2, ring.right)
    get_out.third()
    back_chip(3, ring.across)
    stores.start(wout, wout_o)
    gate_sums(gate, ssd, x_low, gnorm, crow, stat)
    for b in range(length // BLOCK):
        columns = slice(b * BLOCK, (b + 1) * BLOCK)
        row_slots[0, :, columns] = stat[columns, :].T[:8]
    for i in range(1, n):
        exchange(2, i).start()
    store_normed.wait()
    turned[...] = jnp.zeros_like(turned)
    for i in range(1, n):
        exchange(2, i).wait()
    for b in range(length // BLOCK):
        columns = slice(b * BLOCK, (b + 1) * BLOCK)
        turned[0:8, :] = functools.reduce(lambda p, q: p + q, [row_slots[i, :, columns] for i in range(n)])
        stat[columns, :] = turned[...].T
    gn = v_tc.at[:, pl.ds(0, inner)]
    low_gate = v_tc.at[:, pl.ds(inner, inner)]
    gs = normed.at[:, pl.ds(0, inner)]
    gate_backward(gate, ssd, x_low, gnorm, crow, stat, inner * n, gn, low_gate, gs, sums)
    for source, target in ((gn, gn_o), (low_gate, low_gate_o), (gs, gs_o)):
        stores.start(source, target)
    for each in (get_x, get_bd, get_z, get_out):
        each.drain()
    for copy in stores.pairs[1:]:
        copy.wait()


def output_kernel(
    lengths, tok, gn, wout, cot, x_low, ssd, states, gs, slope, xin, bc_low, step, sgdt, step_low, decay_low,
    taps, crow, dpar,
    out, dwout, low_xd, csums, dsums,
    v_gn, v_wout, v_cot, v_x, v_ssd, v_states, v_gs, v_slope, v_xin,
    part, slots, cores, parts, wholes,
    pos, rpos, spread, gpre, dstate, xs, gx, cbm, acc,
    load_sems, cot_sems, line_send, line_recv, core_send, core_recv, ring_send, ring_recv,
):
    ring = Ring()
    starts = [jnp.int32(0)]
    for k in range(DOCS - 1):
        starts.append(starts[-1] + lengths[0, k])
    loads = Loads(load_sems)
    n = lax.axis_size("mp")
    z = lax.axis_index("mp")
    own = part.shape[1] // n
    load_gn = loads.start(gn, v_gn)
    load_wout = loads.start(wout, v_wout)
    later = [
        loads.start(source, target)
        for source, target in (
            (x_low, v_x), (ssd, v_ssd), (states, v_states), (gs, v_gs), (slope, v_slope), (xin, v_xin),
        )
    ]
    greet(ring, False)
    total = gx.at[:, pl.ds(0, own)]
    line = Line(part, slots, (line_send, line_recv), total)
    chunk = v_cot.shape[2]
    shard = dwout.shape[1]

    def cot_copy(j):
        return pltpu.make_async_copy(
            cot.at[:, pl.ds(pl.multiple_of(j * chunk, chunk), chunk)], v_cot.at[j % 2], cot_sems.at[j % 2]
        )

    cot_copy(0).start()
    fill_spread(spread)
    fill_positions(starts, pos, rpos)
    load_gn.wait()
    load_wout.wait()

    def quarter(i, carry):
        q = line.order(i)
        columns = line.columns(q)
        for r in range(0, part.shape[0], 512):
            part[r : r + 512, columns] = mm(v_gn[r : r + 512, :], v_wout[:, columns]).astype(bf16)

        @pl.when(i == 0)
        def _():
            line.inject(0)
            line.inject(1)

        line.inject(i + 2)
        return carry

    lax.fori_loop(0, n, quarter, 0)

    grads = v_wout
    scatter = Scatter(
        ring, lambda r: grads.at[:, pl.ds(pl.multiple_of(r * shard, shard), shard)], cores, parts, wholes,
        (core_send, core_recv, ring_send, ring_recv),
    )

    def weight(j, carry):
        @pl.when(j < 3)
        def _():
            cot_copy(j + 1).start()

        cot_copy(j).wait()
        columns = pl.ds(pl.multiple_of(j * chunk, chunk), chunk)
        for r in range(0, grads.shape[0], 256):
            grads[r : r + 256, columns] = mm_tn(v_gn[:, r : r + 256], v_cot[j % 2]).astype(bf16)
        scatter.start(j)

        @pl.when(j == 2)
        def _():
            line.forward(0, 1)
            line.inject(6)

        return carry

    lax.fori_loop(0, 4, weight, 0)
    v_tok = v_cot.at[0]
    load_tok = loads.start(tok.at[:, pl.ds(pl.multiple_of(z * own, own), own)], v_tok)
    for copy in later[:5]:
        copy.wait()

    def scan_tick(i):
        @pl.when(i == 0)
        def _():
            scatter.first()

        @pl.when(i == 1)
        def _():
            scatter.second()

        line.forward(i + 1, 1)
        line.forward(i, 2)
        line.inject(i + 7)

    scan_backward(
        starts, v_x, bc_low, step_low, decay_low, v_ssd, v_states, v_gs, v_slope, crow, step, sgdt, dpar,
        gpre, low_xd, dsums, spread, dstate, xs, gx, cbm, acc, scan_tick,
    )
    line.inject(11)
    line.forward(5, 1)
    scatter.finish(dwout)
    later[5].wait()
    convolve_back(v_xin, gpre, taps, pos, rpos, low_xd, csums)
    line.forward(6, 1)
    line.forward(7, 1)
    load_tok.wait()

    def last(t, carry):
        line.finish(t)
        out[line.rows(t), :] = (v_tok[line.rows(t), :].astype(f32) + total[...]).astype(bf16)
        return carry

    lax.fori_loop(0, line.blocks, last, 0)
    line.drain()


def input_kernel(
    tok, inverse, gain, normed, low_gate, low_xd, wz, wxd, cot, csums, sums, dsums,
    grad, dwz, dwx, dwbc, dwdt, conv_x, conv_x_bias, conv_bc, conv_bc_bias, dt_bias, a_rate, d_skip, in_gain, out_gain,
    dwxd, smalls, spread, bc_own, bc_slots,
    v_tok, v_normed, v_gate, v_xd, v_wz, v_wxd, v_cot,
    part, slots, total, z_grads, z_cores, z_parts, z_wholes, x_grads, x_cores, x_parts, x_wholes,
    rowacc, rows_own, rows_in, colacc, dp_in, bc_in, gain_in,
    load_sems, line_send, line_recv, z_core_send, z_core_recv, z_ring_send, z_ring_recv,
    x_core_send, x_core_recv, x_ring_send, x_ring_recv,
    rows_send, rows_recv, dp_send, dp_recv, mp_send, mp_recv, bc_send, bc_recv,
):
    ring = Ring()
    loads = Loads(load_sems)
    n = lax.axis_size("mp")
    z = lax.axis_index("mp")
    size = lax.axis_size("dp")
    length, features = part.shape
    inner = v_gate.shape[1]
    width = smalls.shape[1]
    heads, per = dwdt.shape[1], dwbc.shape[1]
    first = [
        loads.start(source, target)
        for source, target in ((low_gate, v_gate), (wz, v_wz), (low_xd, v_xd), (wxd, v_wxd), (tok, v_tok))
    ]
    own = features // n
    own_columns = pl.ds(pl.multiple_of(z * own, own), own)
    later = [
        loads.start(source, target)
        for source, target in ((normed, v_normed), (cot.at[:, own_columns], v_cot))
    ]
    greet(ring, True)
    line = Line(part, slots, (line_send, line_recv), total)
    rowacc[...] = jnp.zeros_like(rowacc)
    for copy in first:
        copy.wait()

    def quarter(i, carry):
        columns = line.columns(line.order(i))
        for r in range(0, length, 256):
            rows = slice(r, r + 256)
            here = mm_nt(v_gate[rows, :], v_wz[columns, :]) + mm_nt(v_xd[rows, :], v_wxd[columns, :])
            part[rows, columns] = here.astype(bf16)
            along = here * (v_tok[rows, columns].astype(f32) * inverse[rows, :1])
            folded = fold(along)
            if r == 0:
                colacc[:, columns] = folded
            else:
                colacc[:, columns] += folded
            along = along * gain[:, columns]
            sum_lanes = along[:, :LANES]
            for c in range(LANES, own, LANES):
                sum_lanes = sum_lanes + along[:, c : c + LANES]
            rowacc[rows, :] += sum_lanes

        @pl.when(i == 0)
        def _():
            line.inject(0)
            line.inject(1)

        line.inject(i + 2)
        return carry

    lax.fori_loop(0, n, quarter, 0)
    line.forward(0, 1)

    for b in range(length // BLOCK):
        columns = slice(b * BLOCK, (b + 1) * BLOCK)
        line_sum = jnp.sum(rowacc[columns, :].T, axis=0, keepdims=True)
        rows_own[:, columns] = jnp.broadcast_to(line_sum, (8, BLOCK))

    def rows_copy(i):
        return remote(
            rows_own, rows_in.at[i - 1], rows_send.at[i - 1], rows_recv.at[i - 1], mp=(z + i) % n
        )

    def dp_copy(i):
        return remote(
            smalls, dp_in.at[i - 1], dp_send.at[i - 1], dp_recv.at[i - 1], dp=(ring.me + i) % size
        )

    def bc_copy(i):
        return remote(
            smalls.at[pl.ds(0, 8), pl.ds(inner, width - inner)], bc_in.at[i - 1],
            mp_send.at[i - 1], mp_recv.at[i - 1], mp=(z + i) % n,
        )

    def gain_copy(i):
        return remote(
            smalls.at[pl.ds(8, 8), pl.ds(0, inner)], gain_in.at[i - 1],
            mp_send.at[n + i - 2], mp_recv.at[n + i - 2], mp=(z + i) % n,
        )

    smalls[...] = jnp.zeros_like(smalls)
    for k in range(CONV + 1):
        smalls[k : k + 1, :] = jnp.sum(csums[8 * k : 8 * k + 8, :], axis=0, keepdims=True)
    for k in range(2):
        smalls[CONV + 1 + k : CONV + 2 + k, :inner] = jnp.sum(sums[8 * k : 8 * k + 8, :], axis=0, keepdims=True)
        smalls[7:8, k * LANES : (k + 1) * LANES] = jnp.sum(dsums[8 * k : 8 * k + 8, :], axis=0, keepdims=True)
    for k in range(features // inner):
        smalls[8 + k : 9 + k, :inner] = jnp.sum(colacc[:, k * inner : (k + 1) * inner], axis=0, keepdims=True)
    for i in range(1, n):
        rows_copy(i).start()
    for i in range(1, size):
        dp_copy(i).start()

    later[0].wait()
    shard = dwz.shape[0]
    z_scatter = Scatter(
        ring, lambda r: z_grads.at[pl.ds(pl.multiple_of(r * shard, shard), shard), :], z_cores, z_parts, z_wholes,
        (z_core_send, z_core_recv, z_ring_send, z_ring_recv),
    )
    x_scatter = Scatter(
        ring, lambda r: x_grads.at[pl.ds(pl.multiple_of(r * shard, shard), shard), :], x_cores, x_parts, x_wholes,
        (x_core_send, x_core_recv, x_ring_send, x_ring_recv),
    )

    def weight(j, right, grads):
        for c in range(0, 2 * shard, shard):
            rows = pl.ds(pl.multiple_of(j * 2 * shard + c, shard), shard)
            left = v_normed[:, rows]
            for at, w in tiles(grads.shape[1], 512):
                grads[rows, at : at + w] = mm_tn(left, right[:, at : at + w]).astype(bf16)

    def z_weight(j, carry):
        weight(j, v_gate, z_grads)
        z_scatter.start(j)

        @pl.when(j % 2 == 1)
        def _():
            line.inject(6 + j // 2)
            line.forward(1 + j // 2, 1)

        return carry

    lax.fori_loop(0, 4, z_weight, 0)
    line.forward(0, 2)

    def x_weight(j, carry):
        weight(j, v_xd, x_grads)
        x_scatter.start(j)

        @pl.when(j == 1)
        def _():
            z_scatter.first()

        @pl.when(j % 2 == 1)
        def _():
            line.inject(8 + j // 2)
            line.forward(3 + j // 2, 1)
            line.forward(1 + j // 2, 2)

        return carry

    lax.fori_loop(0, 4, x_weight, 0)
    z_scatter.second()
    line.inject(10)
    line.inject(11)
    x_scatter.first()

    for i in range(1, size):
        dp_copy(i).wait()
    smalls[...] += functools.reduce(lambda a, b: a + b, [dp_in[i] for i in range(size - 1)])
    for i in range(1, n):
        bc_copy(i).start()
        gain_copy(i).start()
    line.forward(5, 1)
    line.forward(3, 2)
    z_scatter.finish(dwz)
    for i in range(1, n):
        rows_copy(i).wait()
    rows_own[...] += functools.reduce(lambda a, b: a + b, [rows_in[i] for i in range(n - 1)])
    x_scatter.second()
    line.forward(6, 1)
    line.forward(7, 1)
    for i in range(1, n):
        bc_copy(i).wait()
        gain_copy(i).wait()
    smalls[0:8, inner:] += functools.reduce(lambda a, b: a + b, [bc_in[i] for i in range(n - 1)])
    smalls[8:16, :inner] += functools.reduce(lambda a, b: a + b, [gain_in[i] for i in range(n - 1)])
    x_scatter.finish(dwxd)
    share = LANES // per

    def mine(v):
        turns = [v] + [pltpu.roll(v, LANES - k * per, 1) for k in range(1, share)]
        which = jnp.full(v.shape, z % share, jnp.int32)
        return functools.reduce(lambda a, k: jnp.where(which == k, turns[k], a), range(1, share), turns[0])

    for j in range((width - inner) // LANES):
        bc_own[j] = dwxd[:, inner + j * LANES : inner + (j + 1) * LANES].astype(bf16)

    def weight_copy(i):
        other = (z + i) % n
        return remote(
            bc_own.at[other // share], bc_slots.at[i - 1], bc_send.at[i - 1], bc_recv.at[i - 1], mp=other
        )

    for i in range(1, n):
        weight_copy(i).start()
    cast_into(dwx, dwxd.at[:, pl.ds(0, inner)])
    dwdt[...] = dwxd[:, width : width + heads]
    lanes = pl.ds(pl.multiple_of(inner + (z // share) * LANES, LANES), LANES)
    conv_x[...] = smalls[:CONV, :inner]
    conv_x_bias[...] = smalls[CONV : CONV + 1, :inner]
    taps = mine(smalls[:8, lanes])
    conv_bc[...] = taps[:CONV, :per]
    conv_bc_bias[...] = taps[CONV : CONV + 1, :per]
    out_gain[...] = smalls[5:6, :inner]
    fill_spread(spread)
    d_skip[...] = gather_heads(smalls[0:8, :inner], spread[...])[6:7, :heads]
    dt_bias[...] = smalls[7:8, :heads]
    a_rate[...] = smalls[7:8, LANES : LANES + heads]
    fits = inner // own
    in_gain[...] = smalls[pl.ds(8 + z // fits, 1), pl.ds(pl.multiple_of((z % fits) * own, own), own)]
    for i in range(1, n):
        weight_copy(i).wait()
    here = functools.reduce(lambda a, b: a + b, [bc_slots[i].astype(f32) for i in range(n - 1)], dwxd[:, lanes])
    dwbc[...] = mine(here)[:, :per]
    later[1].wait()

    def last(t, carry):
        line.finish(t)
        rows = line.rows(t)
        mean = jnp.broadcast_to(rows_own[0:1, rows] / features, (LANES, BLOCK)).T
        for c in range(0, own, LANES):
            columns = pl.ds(pl.multiple_of(z * own + c, LANES), LANES)
            hat = v_tok[rows, columns].astype(f32) * inverse[rows, :]
            change = inverse[rows, :] * (total[:, c : c + LANES] * gain[:, columns] - hat * mean)
            grad[rows, c : c + LANES] = (v_cot[rows, c : c + LANES].astype(f32) + change).astype(bf16)
        return carry

    lax.fori_loop(0, line.blocks, last, 0)
    line.drain()


def call(kernel, outs, scratch, smem, *operands, places=None, sems=(), collective=None, far=0):
    spaces = {"s": pltpu.SMEM, "v": pltpu.VMEM, "a": pl.ANY}
    if places is None:
        places = "s" * smem + "v" * (len(operands) - smem)
    extra = {} if collective is None else dict(collective_id=collective, has_side_effects=True)
    return pl.pallas_call(
        kernel,
        out_shape=[jax.ShapeDtypeStruct(shape, kind) for shape, kind in outs],
        in_specs=[pl.BlockSpec(memory_space=spaces[c]) for c in places],
        out_specs=[pl.BlockSpec(memory_space=pl.ANY if i < far else pltpu.VMEM) for i in range(len(outs))],
        scratch_shapes=[pltpu.VMEM(shape, kind) for shape, kind in scratch]
        + [pltpu.SemaphoreType.DMA(shape) for shape in sems],
        compiler_params=pltpu.CompilerParams(vmem_limit_bytes=VMEM_LIMIT, **extra),
    )(*operands)


def per_device_any(
    tokens, cotangent, doc_lengths, w_z, w_x, w_bc, w_dt, w_out, conv_x, conv_x_bias, conv_bc,
    conv_bc_bias, dt_bias, a_rate, d_skip, input_norm_gain, out_gain,
):
    group = lax.axis_size("mp")
    rank = lax.axis_index("mp")
    T, D = tokens.shape
    inner, heads = w_x.shape[1], w_dt.shape[1]
    pair = 2 * STATE
    width = inner + pair
    wide = width + LANES
    own = D // group

    lengths = doc_lengths[0]
    starts = jnp.cumsum(lengths) - lengths
    packed = jnp.concatenate([w_bc, conv_bc, conv_bc_bias[None, :]], axis=0)
    packed = lax.all_gather(packed, "mp", axis=1, tiled=True)
    shard = w_bc.shape[0]
    w_bc_all, taps_bc = packed[:shard], packed[shard:]
    wxd = jnp.concatenate(
        [w_x.astype(bf16), w_bc_all.astype(bf16), w_dt.astype(bf16), jnp.zeros((shard, LANES - heads), bf16)],
        axis=1,
    )
    wxd = lax.all_gather(wxd, "dp", axis=0, tiled=True)
    wz = lax.all_gather(w_z.astype(bf16), "dp", axis=0, tiled=True)
    wout = lax.all_gather(w_out.astype(bf16), "dp", axis=1, tiled=True)
    taps = jnp.concatenate([jnp.concatenate([conv_x, conv_x_bias[None, :]], axis=0), taps_bc], axis=1)
    taps = jnp.pad(taps, ((0, 8 - CONV - 1), (0, 0)))
    crow = jnp.pad(jnp.stack([out_gain, jnp.repeat(d_skip, HEADDIM)]), ((0, 6), (0, 0)))
    dpar = jnp.pad(jnp.stack([dt_bias, a_rate]), ((0, 6), (0, LANES - heads)))
    gain = input_norm_gain[None, :]

    blocks = T // BLOCK
    (
        normed, inverse, xin, slope, gate, x_low, bc_low, step, sgdt, step_low, decay_low, ssd, states,
    ) = call(
        forward_kernel,
        [
            ((T, D), bf16), ((T, LANES), f32), ((T + 8, width), f32), ((T, width), bf16), ((T, inner), f32),
            ((T, inner), bf16), ((T, pair), bf16), ((T, LANES), f32), ((T, LANES), f32),
            ((T, LANES), bf16), ((T, LANES), bf16), ((T, inner), bf16), ((blocks, STATE, inner), bf16),
        ],
        [
            ((T, LANES), jnp.int32), ((LANES, inner), bf16), ((T, LANES), f32), ((STATE, inner), f32),
            ((BLOCK, inner), bf16), ((BLOCK, inner), f32), ((BLOCK, BLOCK), f32),
        ],
        1, starts, tokens, gain, wxd, wz, taps, dpar,
    )
    gnorm, stat = call(
        gate_kernel,
        [((T, inner), f32), ((T, LANES), f32)],
        [],
        0, cotangent, wout, gate, ssd, x_low, crow,
    )
    stat = jnp.pad(lax.psum(stat[:, :8], "mp"), ((0, 0), (0, LANES - 8)))
    branch, dwout, dwz, low_gate, gs, sums = call(
        functools.partial(middle_kernel, width=inner * group),
        [
            ((T, D), bf16), ((inner, D), bf16), ((D, inner), bf16), ((T, inner), bf16), ((T, inner), bf16),
            ((16, inner), f32),
        ],
        [((T, inner), bf16)],
        0, cotangent, wout, normed, gate, x_low, ssd, gnorm, crow, stat,
    )
    low_xd, csums, dsums = call(
        backward_kernel,
        [((T, wide), bf16), ((8 * CONV + 8, width), f32), ((16, LANES), f32)],
        [
            ((T, LANES), jnp.int32), ((T, LANES), jnp.int32), ((LANES, inner), bf16), ((T + 8, width), f32),
            ((STATE, inner), f32), ((BLOCK, inner), bf16), ((BLOCK, inner), f32), ((BLOCK, BLOCK), f32),
            ((BLOCK, BLOCK), f32),
        ],
        1, starts, xin, slope, x_low, bc_low, step, sgdt, step_low, decay_low, ssd, states, gs, taps, crow,
        dpar,
    )
    dwxd, gfull, rowdot = call(
        last_kernel,
        [((D, wide), bf16), ((T, D), bf16), ((T, LANES), f32)],
        [],
        0, tokens, inverse, gain, normed, low_gate, low_xd, wz, wxd,
    )

    def scatter(v, axis, dim):
        return lax.psum_scatter(v, axis, scatter_dimension=dim, tiled=True)

    token_own = lax.dynamic_slice_in_dim(tokens, rank * own, own, 1).astype(f32)
    output = (token_own + scatter(branch, "mp", 1).astype(f32)).astype(bf16)
    w_out_grad = scatter(dwout, "dp", 1).astype(f32)
    w_z_grad = scatter(dwz, "dp", 0).astype(f32)
    dwxd_own = scatter(dwxd, "dp", 0)
    w_x_grad = dwxd_own[:, :inner].astype(f32)
    w_dt_grad = dwxd_own[:, width : width + heads].astype(f32)
    w_bc_grad = scatter(dwxd_own[:, inner:width], "mp", 1).astype(f32)

    g_own = scatter(gfull, "mp", 1).astype(f32)
    gain_own = lax.dynamic_slice_in_dim(input_norm_gain, rank * own, own, 0)
    row_mean = (lax.psum(rowdot[:, 0], "mp") / D)[:, None]
    inv = inverse[:, :1]
    hat = token_own * inv
    cot_own = lax.dynamic_slice_in_dim(cotangent, rank * own, own, 1).astype(f32)
    input_grad = (cot_own + inv * (g_own * gain_own - hat * row_mean)).astype(bf16)
    in_gain = jnp.sum(g_own * hat, axis=0)

    csums = jnp.sum(csums.reshape(CONV + 1, 8, width), axis=1)
    sums = jnp.sum(sums.reshape(2, 8, inner), axis=1)
    dsums = jnp.sum(dsums.reshape(2, 8, LANES), axis=1)[:, :heads]
    csums_bc = scatter(csums[:, inner:], "mp", 1)
    conv_grad, conv_bc_grad, sums, dsums, in_gain = lax.psum(
        (csums[:, :inner], csums_bc, sums, dsums, in_gain), "dp"
    )
    d_skip_grad = jnp.sum(sums[1].reshape(heads, HEADDIM), axis=1)
    return (
        output, input_grad, w_z_grad, w_x_grad, w_bc_grad, w_dt_grad, w_out_grad,
        conv_grad[:CONV], conv_grad[CONV], conv_bc_grad[:CONV], conv_bc_grad[CONV],
        dsums[0], dsums[1], d_skip_grad, in_gain, sums[0],
    )


def per_device(
    tokens, cotangent, doc_lengths, w_z, w_x, w_bc, w_dt, w_out, conv_x, conv_x_bias, conv_bc,
    conv_bc_bias, dt_bias, a_rate, d_skip, input_norm_gain, out_gain,
):
    group, size = lax.axis_size("mp"), lax.axis_size("dp")
    T, D = tokens.shape
    shard, inner = w_x.shape
    heads, per = w_dt.shape[1], w_bc.shape[1]
    pair = per * group
    width = inner + pair
    wide = width + LANES
    own = D // group
    columns = w_out.shape[1]
    blocks = T // BLOCK
    messages = blocks * (group - 1)

    def row(v):
        return v[None, :]

    (
        normed, xin, slope, x_low, ssd, states, wxd, wz, wout, gn, low_gate, gs,
        bc_low, step, sgdt, step_low, decay_low, inverse, sums, taps, crow, dpar,
    ) = call(
        gather_kernel,
        [
            ((T, D), bf16), ((T + 8, width), f32), ((T, width), bf16), ((T, inner), bf16), ((T, inner), bf16),
            ((blocks, STATE, inner), bf16), ((D, wide), bf16), ((D, inner), bf16), ((inner, D), bf16),
            ((T, inner), bf16), ((T, inner), bf16), ((T, inner), bf16),
            ((T, pair), bf16), ((T, LANES), f32), ((T, LANES), f32), ((T, LANES), bf16), ((T, LANES), bf16),
            ((T, LANES), f32), ((16, inner), f32), ((8, width), f32), ((8, inner), f32), ((8, LANES), f32),
        ],
        [
            ((T, D), bf16), ((shard, inner), f32), ((inner, columns), f32), ((T, D), bf16), ((T + 8, width), f32),
            ((T, width), bf16), ((T, inner), bf16), ((T, inner), bf16), ((blocks, STATE, inner), bf16),
            ((D, wide), bf16), ((D, inner), bf16), ((inner, D), bf16), ((T, inner), f32), ((T, inner), f32),
            ((group, shard, LANES), bf16), ((group, 8, LANES), f32), ((group, 8, T), f32), ((shard, LANES), f32),
            ((T, LANES), f32), ((LANES, BLOCK), f32),
            ((T, LANES), jnp.int32), ((LANES, inner), bf16), ((T, LANES), f32), ((STATE, inner), f32),
            ((BLOCK, inner), bf16), ((BLOCK, inner), f32), ((BLOCK, BLOCK), f32),
        ],
        0, doc_lengths, tokens, cotangent, w_x, w_z, w_out, w_bc, w_dt, conv_x, row(conv_x_bias), conv_bc,
        row(conv_bc_bias), row(dt_bias), row(a_rate), row(d_skip), row(input_norm_gain), row(out_gain),
        places="s" + "a" * 5 + "v" * 11,
        sems=[(5,), (12,), (4, 4), (4, 4), (4, 4), (4, 4), (3 * group - 3,), (3 * group - 3,)],
        collective=0,
        far=12,
    )
    output, w_out_grad, low_xd, csums, dsums = call(
        output_kernel,
        [
            ((T, own), bf16), ((inner, columns), f32), ((T, wide), bf16), ((8 * CONV + 8, width), f32),
            ((16, LANES), f32),
        ],
        [
            ((T, inner), bf16), ((inner, D), bf16), ((2, T, 2 * columns), bf16), ((T, inner), bf16),
            ((T, inner), bf16), ((blocks, STATE, inner), bf16), ((T, inner), bf16), ((T, width), bf16),
            ((T + 8, width), f32),
            ((T, D), bf16), ((2, messages, BLOCK, own), bf16),
            ((4, inner, columns), bf16), ((2, inner // 2, columns), bf16), ((2, inner, columns), bf16),
            ((T, LANES), jnp.int32), ((T, LANES), jnp.int32), ((LANES, inner), bf16), ((T + 8, width), f32),
            ((STATE, inner), f32), ((BLOCK, inner), bf16), ((BLOCK, inner), f32), ((BLOCK, BLOCK), f32),
            ((BLOCK, BLOCK), f32),
        ],
        0, doc_lengths, tokens, gn, wout, cotangent, x_low, ssd, states, gs, slope, xin, bc_low, step, sgdt,
        step_low, decay_low, taps, crow, dpar,
        places="s" + "a" * 10 + "v" * 8,
        sems=[(9,), (2,), (2, messages), (2, messages), (4,), (4,), (4,), (4,)],
        collective=1,
    )
    (
        input_grad, w_z_grad, w_x_grad, w_bc_grad, w_dt_grad, conv_x_grad, conv_x_bias_grad, conv_bc_grad,
        conv_bc_bias_grad, dt_bias_grad, a_rate_grad, d_skip_grad, in_gain_grad, out_gain_grad,
    ) = call(
        input_kernel,
        [
            ((T, own), bf16), ((shard, inner), f32), ((shard, inner), f32), ((shard, per), f32),
            ((shard, heads), f32), ((CONV, inner), f32), ((1, inner), f32), ((CONV, per), f32), ((1, per), f32),
            ((1, heads), f32), ((1, heads), f32), ((1, heads), f32), ((1, own), f32), ((1, inner), f32),
        ],
        [
            ((shard, wide), f32), ((16, width), f32), ((LANES, inner), bf16), ((pair // LANES, shard, LANES), bf16),
            ((group - 1, shard, LANES), bf16),
            ((T, D), bf16), ((T, D), bf16), ((T, inner), bf16), ((T, wide), bf16), ((D, inner), bf16),
            ((D, wide), bf16), ((T, own), bf16),
            ((T, D), bf16), ((2, messages, BLOCK, own), bf16), ((BLOCK, own), f32),
            ((D, inner), bf16), ((4, shard, inner), bf16), ((2, shard // 2, inner), bf16), ((2, shard, inner), bf16),
            ((D, wide), bf16), ((4, shard, wide), bf16), ((2, shard // 2, wide), bf16), ((2, shard, wide), bf16),
            ((T, LANES), f32), ((8, T), f32), ((group - 1, 8, T), f32), ((8, D), f32),
            ((size - 1, 16, width), f32), ((group - 1, 8, pair), f32), ((group - 1, 8, inner), f32),
        ],
        0, tokens, inverse, row(input_norm_gain), normed, low_gate, low_xd, wz, wxd, cotangent, csums, sums, dsums,
        places="avvaaaaaavvv",
        sems=[
            (7,), (2, messages), (2, messages), (4,), (4,), (4,), (4,), (4,), (4,), (4,), (4,),
            (group - 1,), (group - 1,), (size - 1,), (size - 1,), (2 * group - 2,), (2 * group - 2,),
            (group - 1,), (group - 1,),
        ],
        collective=2,
    )
    return (
        output, input_grad, w_z_grad, w_x_grad, w_bc_grad, w_dt_grad, w_out_grad,
        conv_x_grad, conv_x_bias_grad[0], conv_bc_grad, conv_bc_bias_grad[0], dt_bias_grad[0], a_rate_grad[0],
        d_skip_grad[0], in_gain_grad[0], out_gain_grad[0],
    )


def solution(mesh):
    row, block, column = P("dp", None), P("dp", "mp"), P("mp")
    return jax.shard_map(
        per_device if (mesh.shape["dp"], mesh.shape["mp"]) == (8, 4) else per_device_any,
        mesh=mesh,
        in_specs=(
            row, row, row, block, block, block, block, P("mp", "dp"), P(None, "mp"), column,
            P(None, "mp"), column, column, column, column, P(), column,
        ),
        out_specs=(
            block, block, block, block, block, block, P("mp", "dp"), P(None, "mp"), column,
            P(None, "mp"), column, column, column, column, column, column,
        ),
        check_vma=False,
    )
```

```python
import functools

import jax
import jax.numpy as jnp
from jax import lax
from jax.experimental import pallas as pl
from jax.experimental.pallas import tpu as pltpu
from jax.sharding import PartitionSpec as P

HEADDIM = 64
STATE = 128
CONV = 4
BLOCK = 256
DOCS = 5
LANES = 128
EPS = 1e-05
f32 = jnp.float32
bf16 = jnp.bfloat16
VMEM_LIMIT = 62 * 2**20


def mm(a, b):
    return jnp.dot(a, b, preferred_element_type=f32)


def mm_nt(a, b):
    return lax.dot_general(a, b, (((1,), (1,)), ((), ())), preferred_element_type=f32)


def mm_tn(a, b):
    return lax.dot_general(a, b, (((0,), (0,)), ((), ())), preferred_element_type=f32)


def halves(v):
    high = v.astype(bf16)
    return high, (v - high.astype(f32)).astype(bf16)


def expand(v, spread):
    high, rest = halves(v)
    return mm(high, spread) + mm(rest, spread)


def gather_heads(v, spread):
    high, rest = halves(v)
    return mm_nt(high, spread) + mm_nt(rest, spread)


def logistic(v):
    return 1.0 / (1.0 + jnp.exp(-v))


def tiles(total, size):
    return [(at, min(size, total - at)) for at in range(0, total, size)]


def fold(v):
    return jnp.sum(v.reshape(v.shape[0] // 8, 8, v.shape[1]), axis=0)


def doc_of(starts, place):
    count = (place >= starts[0]).astype(jnp.int32)
    for k in range(1, DOCS):
        count = count + (place >= starts[k]).astype(jnp.int32)
    return count


def fill_spread(spread):
    rows, columns = spread.shape
    head = lax.broadcasted_iota(jnp.int32, (rows, columns), 0)
    channel = lax.broadcasted_iota(jnp.int32, (rows, columns), 1)
    low = head * HEADDIM
    spread[...] = jnp.where((channel >= low) & (channel < low + HEADDIM), 1.0, 0.0).astype(bf16)


def fill_positions(starts, pos, rpos):
    length = pos.shape[0]

    def body(i, carry):
        at = pl.multiple_of(i * BLOCK, BLOCK)
        place = lax.broadcasted_iota(jnp.int32, (BLOCK, LANES), 0) + at
        begin = jnp.zeros_like(place)
        end = jnp.full_like(place, length)
        for k in range(DOCS):
            begin = jnp.maximum(begin, jnp.where(place >= starts[k], starts[k], 0))
            end = jnp.minimum(end, jnp.where(place < starts[k], starts[k], length))
        pos[pl.ds(at, BLOCK), :] = place - begin
        if rpos is not None:
            rpos[pl.ds(at, BLOCK), :] = end - 1 - place
        return carry

    lax.fori_loop(0, length // BLOCK, body, 0)


def normalize(tok, gain, normed, stat):
    step = 64

    def body(i, carry):
        rows = pl.ds(pl.multiple_of(i * step, step), step)
        v = tok[rows, :].astype(f32)
        inverse = lax.rsqrt(jnp.mean(v * v, axis=1, keepdims=True) + EPS)
        normed[rows, :] = (v * inverse * gain[...]).astype(bf16)
        stat[rows, :] = jnp.broadcast_to(inverse, (step, LANES))
        return carry

    lax.fori_loop(0, tok.shape[0] // step, body, 0)


def project_x(normed, wxd, xin, dtin):
    length, width = normed.shape[0], xin.shape[1]
    xin[pl.ds(0, 8), :] = jnp.zeros((8, width), f32)
    rows = 512

    def body(i, carry):
        at = pl.multiple_of(i * rows, rows)
        left = normed[pl.ds(at, rows), :]
        for c, w in tiles(width, 512):
            xin[pl.ds(at + 8, rows), c : c + w] = mm(left, wxd[:, c : c + w])
        dtin[pl.ds(at, rows), :] = mm(left, wxd[:, width : width + LANES])
        return carry

    lax.fori_loop(0, length // rows, body, 0)


def convolve(xin, taps, pos, slope, x_low, bc_low):
    width, inner = xin.shape[1], x_low.shape[1]

    def tile(b, c, out, at):
        rows = pl.ds(pl.multiple_of(b * BLOCK, BLOCK), BLOCK)
        x = xin[pl.ds(pl.multiple_of(b * BLOCK, BLOCK), BLOCK + 8), pl.ds(c, LANES)]
        place = pos[rows, :]
        tap = taps[:, pl.ds(c, LANES)]
        pre = tap[CONV : CONV + 1] + tap[CONV - 1 : CONV] * x[8:]
        for lag in range(1, CONV):
            earlier = pltpu.roll(x, lag, 0)[8:]
            pre = pre + tap[CONV - 1 - lag : CONV - lag] * jnp.where(place >= lag, earlier, 0.0)
        sg = logistic(pre)
        slope[rows, pl.ds(c, LANES)] = (sg * (1.0 + pre * (1.0 - sg))).astype(bf16)
        out[rows, pl.ds(at, LANES)] = (pre * sg).astype(bf16)

    blocks = x_low.shape[0] // BLOCK
    xcols, bcols = inner // LANES, (width - inner) // LANES

    def x_body(i, carry):
        c = pl.multiple_of((i % xcols) * LANES, LANES)
        tile(i // xcols, c, x_low, c)
        return carry

    def bc_body(i, carry):
        c = pl.multiple_of((i % bcols) * LANES, LANES)
        tile(i // bcols, inner + c, bc_low, c)
        return carry

    lax.fori_loop(0, blocks * xcols, x_body, 0)
    lax.fori_loop(0, blocks * bcols, bc_body, 0)


def steps(dtin, dpar, step, sgdt, step_low, decay_low):
    def body(i, carry):
        rows = pl.ds(pl.multiple_of(i * BLOCK, BLOCK), BLOCK)
        v = dtin[rows, :] + dpar[0:1, :]
        soft = jnp.maximum(v, 0.0) + jnp.log1p(jnp.exp(-jnp.abs(v)))
        step[rows, :] = soft
        sgdt[rows, :] = logistic(v)
        step_low[rows, :] = soft.astype(bf16)
        decay_low[rows, :] = (-dpar[1:2, :] * soft).astype(bf16)
        return carry

    lax.fori_loop(0, dtin.shape[0] // BLOCK, body, 0)


def block_marks(starts, b):
    at = b * BLOCK
    column = doc_of(starts, lax.broadcasted_iota(jnp.int32, (BLOCK, 1), 0) + at)
    row = doc_of(starts, lax.broadcasted_iota(jnp.int32, (1, BLOCK), 1) + at)
    before = doc_of(starts, at - 1)
    last = doc_of(starts, at + BLOCK - 1)
    return column, row, before, last


def block_decays(b, starts, decay_low, step_low, spread):
    rows = pl.ds(pl.multiple_of(b * BLOCK, BLOCK), BLOCK)
    column, row, before, last = block_marks(starts, b)
    i0 = lax.broadcasted_iota(jnp.int32, (BLOCK, BLOCK), 0)
    i1 = lax.broadcasted_iota(jnp.int32, (BLOCK, BLOCK), 1)
    lower = jnp.where(i0 >= i1, 1.0, 0.0).astype(bf16)
    cum = mm(lower, decay_low[rows, :])
    step_e = mm(step_low[rows, :], spread[...])
    cum_e = expand(jnp.exp(cum), spread[...])
    kept_e = jnp.where(before == last, cum_e[BLOCK - 1 : BLOCK], 0.0)
    in_e = jnp.where(column == before, cum_e, 0.0)
    out_e = expand(jnp.exp(cum[BLOCK - 1 : BLOCK] - cum), spread[...])
    out_e = jnp.where(column == last, out_e, 0.0)
    return cum, step_e, kept_e, in_e, out_e, column, row


def scan_forward(
    starts, x_low, bc_low, step_low, decay_low, ssd, states, spread, state, xs, yin, cbm, tick=None
):
    length, inner = x_low.shape
    state[...] = jnp.zeros_like(state)

    def body(b, carry):
        rows = pl.ds(pl.multiple_of(b * BLOCK, BLOCK), BLOCK)
        cum, step_e, kept_e, in_e, out_e, column, row = block_decays(
            b, starts, decay_low, step_low, spread
        )
        bm, cm = bc_low[rows, :STATE], bc_low[rows, STATE:]
        i0 = lax.broadcasted_iota(jnp.int32, (BLOCK, BLOCK), 0)
        i1 = lax.broadcasted_iota(jnp.int32, (BLOCK, BLOCK), 1)
        cbm[...] = jnp.where((column == row) & (i0 >= i1), mm_nt(cm, bm), 0.0)
        stepped = x_low[rows, :].astype(f32) * step_e
        xs[...] = stepped.astype(bf16)
        entering = state[...].astype(bf16)
        states[b] = entering
        yin[...] = in_e * mm(cm, entering)
        state[...] = kept_e * state[...] + mm_tn(bm, (stepped * out_e).astype(bf16))
        cum_t = cum.T
        first = lax.broadcasted_iota(jnp.int32, (BLOCK, LANES), 1) < HEADDIM
        for j in range(inner // LANES):
            cols = slice(j * LANES, (j + 1) * LANES)
            pair = xs[:, cols]
            part = []
            for h in (2 * j, 2 * j + 1):
                span = jnp.minimum(cum[:, h : h + 1] - cum_t[h : h + 1, :], 0.0)
                part.append(mm((jnp.exp(span) * cbm[...]).astype(bf16), pair))
            y = jnp.where(first, part[0], part[1]) + yin[:, cols]
            ssd[rows, cols] = y.astype(bf16)
        if tick is not None:
            tick(b)
        return carry

    lax.fori_loop(0, length // BLOCK, body, 0)


def project_rows(left, right, out, rows=512, columns=512):
    def body(i, carry):
        at = pl.ds(pl.multiple_of(i * rows, rows), rows)
        part = left[at, :]
        for c, w in tiles(out.shape[1], columns):
            out[at, c : c + w] = mm(part, right[:, c : c + w]).astype(out.dtype)
        return carry

    lax.fori_loop(0, out.shape[0] // rows, body, 0)


def back_rows(left, right, out, rows=512, columns=512):
    def body(i, carry):
        at = pl.ds(pl.multiple_of(i * rows, rows), rows)
        part = left[at, :]
        for c, w in tiles(out.shape[1], columns):
            out[at, c : c + w] = mm_nt(part, right[c : c + w, :]).astype(out.dtype)
        return carry

    lax.fori_loop(0, out.shape[0] // rows, body, 0)


def weight_rows(left, right, out, rows=256, columns=512):
    def body(i, carry):
        at = pl.ds(pl.multiple_of(i * rows, rows), rows)
        part = left[:, at]
        for c, w in tiles(out.shape[1], columns):
            out[at, c : c + w] = mm_tn(part, right[:, c : c + w]).astype(out.dtype)
        return carry

    lax.fori_loop(0, out.shape[0] // rows, body, 0)


def gate_sums(gate, ssd, x_low, gnorm, crow, stat):
    step, inner = 64, gate.shape[1]

    def body(i, carry):
        rows = pl.ds(pl.multiple_of(i * step, step), step)
        squares = jnp.zeros((step, 256), f32)
        crosses = jnp.zeros((step, 256), f32)
        for c in range(0, inner, 256):
            cols = slice(c, c + 256)
            g = gate[rows, cols]
            mixed = ssd[rows, cols].astype(f32) + crow[1:2, cols] * x_low[rows, cols].astype(f32)
            gated = mixed * (g * logistic(g))
            squares = squares + gated * gated
            crosses = crosses + gnorm[rows, cols] * crow[0:1, cols] * gated
        lane = lax.broadcasted_iota(jnp.int32, (step, LANES), 1)
        s1 = jnp.sum(squares, axis=1, keepdims=True)
        s2 = jnp.sum(crosses, axis=1, keepdims=True)
        stat[rows, :] = jnp.where(lane == 0, s1, jnp.where(lane == 1, s2, 0.0))
        return carry

    lax.fori_loop(0, gate.shape[0] // step, body, 0)


def gate_squares(gate, ssd, x_low, crow, gated, stat):
    step, inner = 64, gate.shape[1]

    def body(i, carry):
        rows = pl.ds(pl.multiple_of(i * step, step), step)
        squares = jnp.zeros((step, 256), f32)
        for c in range(0, inner, 256):
            cols = slice(c, c + 256)
            g = gate[rows, cols]
            mixed = ssd[rows, cols].astype(f32) + crow[1:2, cols] * x_low[rows, cols].astype(f32)
            value = mixed * (g * logistic(g))
            gated[rows, cols] = value
            squares = squares + value * value
        stat[rows, :] = jnp.broadcast_to(jnp.sum(squares, axis=1, keepdims=True), (step, LANES))
        return carry

    lax.fori_loop(0, gate.shape[0] // step, body, 0)


def scale_rows(gated, inverse_out, crow, gn):
    step, inner = 64, gated.shape[1]

    def body(i, carry):
        rows = pl.ds(pl.multiple_of(i * step, step), step)
        inverse = inverse_out[rows, :1]
        for c in range(0, inner, 256):
            cols = slice(c, c + 256)
            gn[rows, cols] = (gated[rows, cols] * inverse * crow[0:1, cols]).astype(bf16)
        return carry

    lax.fori_loop(0, gated.shape[0] // step, body, 0)


def cross_sums(gnorm, gn, stat):
    step, inner = 64, gn.shape[1]

    def body(i, carry):
        rows = pl.ds(pl.multiple_of(i * step, step), step)
        total = jnp.zeros((step, 256), f32)
        for c in range(0, inner, 256):
            cols = slice(c, c + 256)
            total = total + gnorm[rows, cols] * gn[rows, cols].astype(f32)
        stat[rows, :] = jnp.broadcast_to(jnp.sum(total, axis=1, keepdims=True), (step, LANES))
        return carry

    lax.fori_loop(0, gn.shape[0] // step, body, 0)


def forward_kernel(
    starts, tok, gain, wxd, wz, taps, dpar,
    normed, inverse, xin, slope, gate, x_low, bc_low, step, sgdt, step_low, decay_low, ssd, states,
    pos, spread, dtin, state, xs, yin, cbm,
):
    fill_spread(spread)
    fill_positions(starts, pos, None)
    normalize(tok, gain, normed, inverse)
    project_x(normed, wxd, xin, dtin)
    convolve(xin, taps, pos, slope, x_low, bc_low)
    steps(dtin, dpar, step, sgdt, step_low, decay_low)
    scan_forward(starts, x_low, bc_low, step_low, decay_low, ssd, states, spread, state, xs, yin, cbm)
    project_rows(normed, wz, gate)


def gate_kernel(cot, wout, gate, ssd, x_low, crow, gnorm, stat):
    back_rows(cot, wout, gnorm)
    gate_sums(gate, ssd, x_low, gnorm, crow, stat)


def gate_backward(gate, ssd, x_low, gnorm, crow, stat, width, gn, low_gate, gs, sums, known=None):
    step, inner = 64, ssd.shape[1]
    sums[...] = jnp.zeros_like(sums)

    def body(i, carry):
        rows = pl.ds(pl.multiple_of(i * step, step), step)
        if known is None:
            inverse = lax.rsqrt(stat[rows, 0:1] / width + EPS)
            mean = inverse * stat[rows, 1:2] / width
        else:
            inverse, mean = known[rows, :1], stat[rows, :1]
        for c in range(0, inner, 256):
            cols = slice(c, c + 256)
            g = gate[rows, cols]
            x = x_low[rows, cols].astype(f32)
            mixed = ssd[rows, cols].astype(f32) + crow[1:2, cols] * x
            sg = logistic(g)
            act = g * sg
            hat = mixed * act * inverse
            if gn is not None:
                gn[rows, cols] = (hat * crow[0:1, cols]).astype(bf16)
            gnorm_here = gnorm[rows, cols]
            grad = inverse * (gnorm_here * crow[0:1, cols] - hat * mean)
            grad_mixed = grad * act
            low_gate[rows, cols] = (grad * mixed * (sg * (1.0 + g * (1.0 - sg)))).astype(bf16)
            gs[rows, cols] = grad_mixed.astype(bf16)
            sums[0:8, cols] += fold(gnorm_here * hat)
            sums[8:16, cols] += fold(grad_mixed * x)
        return carry

    lax.fori_loop(0, ssd.shape[0] // step, body, 0)


def middle_kernel(
    cot, wout, normed, gate, x_low, ssd, gnorm, crow, stat,
    branch, dwout, dwz, low_gate, gs, sums,
    gn, *, width,
):
    gate_backward(gate, ssd, x_low, gnorm, crow, stat, width, gn, low_gate, gs, sums)
    project_rows(gn, wout, branch)
    weight_rows(gn, cot, dwout)
    weight_rows(normed, low_gate, dwz)


def scan_backward(
    starts, x_low, bc_low, step_low, decay_low, ssd, states, gs, slope, crow, step, sgdt, dpar,
    gpre, low_xd, dsums, spread, dstate, xs, gx, cbm, acc, tick=None,
):
    length, inner = x_low.shape
    width = gpre.shape[1]
    blocks = length // BLOCK
    dstate[...] = jnp.zeros_like(dstate)
    dsums[...] = jnp.zeros_like(dsums)
    gpre[pl.ds(length, 8), :] = jnp.zeros((8, width), f32)

    def body(i, carry):
        b = blocks - 1 - i
        rows = pl.ds(pl.multiple_of(b * BLOCK, BLOCK), BLOCK)
        cum, step_e, kept_e, in_e, out_e, column, row = block_decays(
            b, starts, decay_low, step_low, spread
        )
        bm, cm = bc_low[rows, :STATE], bc_low[rows, STATE:]
        i0 = lax.broadcasted_iota(jnp.int32, (BLOCK, BLOCK), 0)
        i1 = lax.broadcasted_iota(jnp.int32, (BLOCK, BLOCK), 1)
        linked = (column == row) & (i0 <= i1)
        cbm[...] = jnp.where(linked, mm_nt(bm, cm), 0.0)
        x = x_low[rows, :].astype(f32)
        stepped = x * step_e
        xs[...] = stepped.astype(bf16)
        cum_t = cum.T
        first = lax.broadcasted_iota(jnp.int32, (BLOCK, LANES), 1) < HEADDIM
        acc[...] = jnp.zeros_like(acc)
        for j in range(inner // LANES):
            cols = slice(j * LANES, (j + 1) * LANES)
            xpair, gpair = xs[:, cols], gs[rows, cols]
            none = jnp.zeros_like(xpair)
            part, total = [], None
            for k in range(2):
                h = 2 * j + k
                kernel = jnp.exp(jnp.minimum(cum_t[h : h + 1, :] - cum[:, h : h + 1], 0.0))
                part.append(mm((kernel * cbm[...]).astype(bf16), gpair))
                own = jnp.where(first, xpair, none) if k == 0 else jnp.where(first, none, xpair)
                here = kernel * mm_nt(own, gpair)
                total = here if total is None else total + here
            acc[...] += total
            gx[:, cols] = jnp.where(first, part[0], part[1])
        dstate_low = dstate[...].astype(bf16)
        entering = states[b]
        leaving = states[jnp.minimum(b + 1, blocks - 1)]
        end = jnp.sum(dstate[...] * leaving.astype(f32), axis=0, keepdims=True)
        g = gs[rows, :].astype(f32)
        g_in = (in_e * g).astype(bf16)
        raw = gx[...] + out_e * mm(bm, dstate_low)
        grad_x = (step_e * raw).astype(bf16).astype(f32)
        gpre[rows, :inner] = (grad_x + crow[1:2, :] * g) * slope[rows, :inner]
        pairs = jnp.where(linked, acc[...], 0.0).astype(bf16)
        db = mm(pairs, cm) + mm_nt((stepped * out_e).astype(bf16), dstate_low)
        dc = mm_tn(pairs, bm) + mm_nt(g_in, entering)
        gpre[rows, inner : inner + STATE] = db * slope[rows, inner : inner + STATE]
        gpre[rows, inner + STATE :] = dc * slope[rows, inner + STATE :]
        raw_x = x * raw
        grad_step = gather_heads(raw_x, spread[...]).astype(bf16).astype(f32)
        dcum = gather_heads(g * ssd[rows, :].astype(f32) - step_e * raw_x, spread[...])
        tail = gather_heads(jnp.broadcast_to(end, (8, inner)), spread[...])[0:1]
        upper = jnp.where(i0 <= i1, 1.0, 0.0).astype(bf16)
        high, rest = halves(dcum)
        later = mm(upper, high) + mm(upper, rest) + tail
        grad_decay = later.astype(bf16).astype(f32)
        total_step = grad_step - dpar[1:2, :] * grad_decay
        grad_dt = total_step * sgdt[rows, :]
        low_xd[rows, width:] = grad_dt.astype(bf16)
        dsums[0:8, :] += fold(grad_dt)
        dsums[8:16, :] -= fold(grad_decay * step[rows, :])
        dstate[...] = kept_e * dstate[...] + mm_tn(cm, g_in)
        if tick is not None:
            tick(i)
        return carry

    lax.fori_loop(0, blocks, body, 0)


def convolve_back(xin, gpre, taps, pos, rpos, low_xd, csums, tick=None):
    width = gpre.shape[1]
    columns = width // LANES
    csums[...] = jnp.zeros_like(csums)

    def body(b, j):
        at = pl.multiple_of(b * BLOCK, BLOCK)
        cols = pl.ds(pl.multiple_of(j * LANES, LANES), LANES)
        rows = pl.ds(at, BLOCK)
        x = xin[pl.ds(at, BLOCK + 8), cols]
        g = gpre[pl.ds(at, BLOCK + 8), cols]
        here = g[:BLOCK]
        place, ahead = pos[rows, :], rpos[rows, :]
        tap = taps[:, cols]
        grad = tap[CONV - 1 : CONV] * here
        csums[pl.ds(8 * CONV, 8), cols] += fold(here)
        csums[pl.ds(8 * (CONV - 1), 8), cols] += fold(here * x[8:])
        for lag in range(1, CONV):
            k = CONV - 1 - lag
            later = pltpu.roll(g, BLOCK + 8 - lag, 0)[:BLOCK]
            earlier = pltpu.roll(x, lag, 0)[8:]
            grad = grad + tap[k : k + 1] * jnp.where(ahead >= lag, later, 0.0)
            csums[pl.ds(8 * k, 8), cols] += fold(here * jnp.where(place >= lag, earlier, 0.0))
        low_xd[rows, cols] = grad.astype(bf16)

    def block(b, carry):
        lax.fori_loop(0, columns, lambda j, c: (body(b, j), c)[1], 0)
        if tick is not None:
            tick(b)
        return carry

    lax.fori_loop(0, (xin.shape[0] - 8) // BLOCK, block, 0)


def backward_kernel(
    starts, xin, slope, x_low, bc_low, step, sgdt, step_low, decay_low, ssd, states, gs, taps, crow, dpar,
    low_xd, csums, dsums,
    pos, rpos, spread, gpre, dstate, xs, gx, cbm, acc,
):
    fill_spread(spread)
    fill_positions(starts, pos, rpos)
    scan_backward(
        starts, x_low, bc_low, step_low, decay_low, ssd, states, gs, slope, crow, step, sgdt, dpar,
        gpre, low_xd, dsums, spread, dstate, xs, gx, cbm, acc,
    )
    convolve_back(xin, gpre, taps, pos, rpos, low_xd, csums)


def last_kernel(tok, inverse, gain, normed, low_gate, low_xd, wz, wxd, dwxd, gfull, rowdot):
    weight_rows(normed, low_xd, dwxd)
    rows = 256

    def body(i, carry):
        at = pl.ds(pl.multiple_of(i * rows, rows), rows)
        total = jnp.zeros((rows, 1), f32)
        for c, w in tiles(gfull.shape[1], 512):
            cols = slice(c, c + w)
            part = mm_nt(low_gate[at, :], wz[cols, :]) + mm_nt(low_xd[at, :], wxd[cols, :])
            gfull[at, cols] = part.astype(bf16)
            total = total + jnp.sum(part * gain[:, cols] * tok[at, cols].astype(f32), axis=1, keepdims=True)
        rowdot[at, :] = total * inverse[at, :]
        return carry

    lax.fori_loop(0, gfull.shape[0] // rows, body, 0)


MESH = pl.DeviceIdType.MESH


def remote(source, target, send, receive, **where):
    return pltpu.make_async_remote_copy(
        src_ref=source, dst_ref=target, send_sem=send, recv_sem=receive, device_id=where, device_id_type=MESH
    )


def add_into(target, source, rows=64):
    def body(i, carry):
        at = pl.ds(pl.multiple_of(i * rows, rows), rows)
        target[at, :] = (target[at, :].astype(f32) + source[at, :].astype(f32)).astype(target.dtype)
        return carry

    lax.fori_loop(0, target.shape[0] // rows, body, 0)


class Ring:
    def __init__(self):
        self.me = lax.axis_index("dp")
        self.core = self.me % 2
        chip = self.me // 2
        y = chip // 2
        self.pos = 2 * y + (chip + y) % 2
        self.partner = self.me + 1 - 2 * self.core
        self.right = self.at(self.pos + 1)
        self.left = self.at(self.pos + 3)
        self.across = self.at(self.pos + 2)

    def at(self, pos):
        pos = pos % 4
        y = pos // 2
        return (2 * y + (pos + y) % 2) * 2 + self.core


def greet(ring, everyone):
    barrier = pltpu.get_barrier_semaphore()
    n, z = lax.axis_size("mp"), lax.axis_index("mp")
    if everyone:
        size = lax.axis_size("dp")
        close = [(ring.me + i) % size for i in range(1, size)]
    else:
        close = [ring.partner, ring.right, ring.left]
    for other in close:
        pl.semaphore_signal(barrier, inc=1, device_id={"dp": other}, device_id_type=MESH)
    for i in range(1, n):
        pl.semaphore_signal(barrier, inc=1, device_id={"mp": (z + i) % n}, device_id_type=MESH)
    pl.semaphore_wait(barrier, len(close) + n - 1)


class Scatter:
    def __init__(self, ring, shard, cores, parts, wholes, sems):
        self.ring, self.shard = ring, shard
        self.cores, self.parts, self.wholes = cores, parts, wholes
        self.core_send, self.core_recv, self.ring_send, self.ring_recv = sems
        self.half = cores.shape[1] // 2

    def upper(self, r):
        return self.shard(r).at[pl.ds(0, self.half), :]

    def lower(self, r):
        return self.shard(r).at[pl.ds(self.half, self.half), :]

    def core_copy(self, chip):
        ring = self.ring
        return remote(
            self.shard(2 * chip + 1 - ring.core), self.cores.at[chip],
            self.core_send.at[chip], self.core_recv.at[chip], dp=ring.partner,
        )

    def ring_copy(self, k):
        ring = self.ring
        source = (self.upper(ring.across), self.lower(ring.across), self.shard(ring.right), self.shard(ring.left))[k]
        target = (self.parts.at[0], self.parts.at[1], self.wholes.at[0], self.wholes.at[1])[k]
        return remote(
            source, target, self.ring_send.at[k], self.ring_recv.at[k], dp=(ring.right, ring.left)[k % 2]
        )

    def start(self, chip):
        self.core_copy(chip).start()

    def first(self):
        def body(chip, carry):
            self.core_copy(chip).wait_recv()
            add_into(self.shard(2 * chip + self.ring.core), self.cores.at[chip])
            return carry

        lax.fori_loop(0, 4, body, 0)
        self.ring_copy(0).start()
        self.ring_copy(1).start()

    def second(self):
        self.ring_copy(0).wait_recv()
        add_into(self.upper(self.ring.right), self.parts.at[0])
        self.ring_copy(2).start()
        self.ring_copy(1).wait_recv()
        add_into(self.lower(self.ring.left), self.parts.at[1])
        self.ring_copy(3).start()

    def finish(self, out, rows=64):
        self.ring_copy(2).wait_recv()
        self.ring_copy(3).wait_recv()
        own = self.shard(self.ring.me)

        def body(i, carry):
            at = pl.ds(pl.multiple_of(i * rows, rows), rows)
            out[at, :] = own[at, :].astype(f32) + self.wholes[0, at, :].astype(f32) + self.wholes[1, at, :].astype(f32)
            return carry

        lax.fori_loop(0, out.shape[0] // rows, body, 0)

        def done(chip, carry):
            self.core_copy(chip).wait_send()
            return carry

        lax.fori_loop(0, 4, done, 0)
        for k in range(4):
            self.ring_copy(k).wait_send()


class Line:
    def __init__(self, part, slots, sems, total):
        self.part, self.slots, self.total = part, slots, total
        self.send, self.recv = sems
        self.n, self.z = lax.axis_size("mp"), lax.axis_index("mp")
        self.blocks = part.shape[0] // BLOCK
        self.own = part.shape[1] // self.n
        self.place = (self.z, self.n - 1 - self.z)
        self.count = self.blocks * (self.n - 1)

    def rows(self, t):
        return pl.ds(pl.multiple_of(t * BLOCK, BLOCK), BLOCK)

    def columns(self, q):
        return pl.ds(pl.multiple_of(q * self.own, self.own), self.own)

    def copy(self, side, k):
        d = k // self.blocks
        q = self.n - 1 - d if side == 0 else d
        source = self.part.at[self.rows(k - d * self.blocks), self.columns(q)]
        return remote(
            source, self.slots.at[side, k], self.send.at[side, k], self.recv.at[side, k],
            mp=self.z + 1 if side == 0 else self.z - 1,
        ), source

    def inject(self, k):
        for side in range(2):
            @pl.when(self.place[side] == 0)
            def _():
                @pl.when(jnp.int32(k) >= 2)
                def _():
                    self.copy(side, jnp.maximum(k - 2, 0))[0].wait_send()

                self.copy(side, k)[0].start()

    def forward(self, k, hop):
        for side in range(2):
            @pl.when(self.place[side] == hop)
            def _():
                copy, source = self.copy(side, k)
                copy.wait_recv()
                add_into(source, self.slots.at[side, k])
                copy.start()

    def finish(self, t):
        self.total[...] = self.part[self.rows(t), self.columns(self.z)].astype(f32)
        for side in range(2):
            @pl.when(self.place[side] >= 1)
            def _():
                k = (self.n - 1 - self.place[side]) * self.blocks + t
                self.copy(side, k)[0].wait_recv()
                self.total[...] += self.slots[side, k].astype(f32)

    def drain(self):
        def body(k, carry):
            for side in range(2):
                started = self.place[side] + k // self.blocks <= self.n - 2

                @pl.when(started & ((self.place[side] > 0) | (k >= self.count - 2)))
                def _():
                    self.copy(side, k)[0].wait_send()
            return carry

        lax.fori_loop(0, self.count, body, 0)

    def order(self, i):
        z = self.z
        far = jnp.where(z < 2, 3 - i, i)
        near = z + 1 - 2 * (z % 2)
        return jnp.where(i < 2, far, jnp.where(i == 2, near, z))


class Loads:
    def __init__(self, sems):
        self.sems, self.pairs = sems, []

    def start(self, source, target):
        i = len(self.pairs)
        copy = pltpu.make_async_copy(source, target, self.sems.at[i])
        copy.start()
        self.pairs.append(copy)
        return copy


class Gather:
    def __init__(self, ring, shard, rows, sems):
        self.ring, self.shard, self.half = ring, shard, rows // 2
        self.ring_send, self.ring_recv, self.core_send, self.core_recv = sems
        self.other = 1 - 2 * ring.core

    def ring_copy(self, k, source):
        ring = self.ring
        piece = self.shard(source)
        if k >= 2:
            piece = piece.at[pl.ds((k - 2) * self.half, self.half), :]
        return remote(
            piece, piece, self.ring_send.at[k], self.ring_recv.at[k], dp=(ring.right, ring.left)[k % 2]
        )

    def core_copy(self, k, source):
        return remote(
            self.shard(source), self.shard(source), self.core_send.at[k], self.core_recv.at[k], dp=self.ring.partner
        )

    def start(self):
        me = self.ring.me
        self.ring_copy(0, me).start()
        self.ring_copy(1, me).start()
        self.core_copy(0, me).start()

    def second(self):
        left, right = self.ring.left, self.ring.right
        self.ring_copy(0, left).wait_recv()
        self.ring_copy(2, left).start()
        self.core_copy(1, left).start()
        self.ring_copy(1, right).wait_recv()
        self.ring_copy(3, right).start()
        self.core_copy(2, right).start()

    def third(self):
        across = self.ring.across
        self.ring_copy(2, across).wait_recv()
        self.ring_copy(3, across).wait_recv()
        self.core_copy(3, across).start()

    def arrived(self, k):
        ring = self.ring
        source = (ring.me, ring.left, ring.right, ring.across)[k] + self.other
        self.core_copy(k, source).wait_recv()

    def drain(self):
        ring = self.ring
        for k, source in enumerate((ring.me, ring.me, ring.left, ring.right)):
            self.ring_copy(k, source).wait_send()
        for k, source in enumerate((ring.me, ring.left, ring.right, ring.across)):
            self.core_copy(k, source).wait_send()


def cast_into(target, source, rows=64):
    def body(i, carry):
        at = pl.ds(pl.multiple_of(i * rows, rows), rows)
        target[at, :] = source[at, :].astype(target.dtype)
        return carry

    lax.fori_loop(0, target.shape[0] // rows, body, 0)


def gather_kernel(
    lengths, tok, cot, w_x, w_z, w_out, w_bc, w_dt, conv_x, conv_x_bias, conv_bc, conv_bc_bias, dt_bias, a_rate,
    d_skip, gain, out_gain,
    normed_o, xin_o, slope_o, x_low_o, ssd_o, states_o, wxd_o, wz_o, wout_o, gn_o, gate_o, gnorm_o,
    bc_low_o, step_o, sgdt_o, step_low_o, decay_low_o, inverse_o, inverse_out_o,
    taps, crow, dpar, rows,
    v_tok, stage_a, stage_b, normed, xin, slope, x_low, ssd, states, wxd, wz, wout, gate, gated, gnorm,
    bc_low, step, sgdt, step_low, decay_low, inverse, inverse_out,
    bc_slots, tap_slots, row_slots, stat, turned,
    pos, spread, dtin, state, xs, yin, cbm,
    load_sems, store_sems, ring_send, ring_recv, core_send, core_recv, mp_send, mp_recv,
):
    ring = Ring()
    n, z = lax.axis_size("mp"), lax.axis_index("mp")
    length, features = normed.shape
    inner, width = gate.shape[1], xin.shape[1]
    shard, column_shard = stage_a.shape[0], stage_b.shape[1]
    heads, per = w_dt.shape[0], w_bc.shape[0]
    loads, stores = Loads(load_sems), Loads(store_sems)
    load_x = loads.start(w_x, stage_a)
    load_tok = loads.start(tok, v_tok)
    load_out = loads.start(w_out, stage_b)
    starts = [jnp.int32(0)]
    for k in range(DOCS - 1):
        starts.append(starts[-1] + lengths[0, k])

    turned[...] = jnp.zeros_like(turned)
    turned[:per, :] = w_bc[...]
    bc_slots[0] = turned[...].T.astype(bf16)
    tap_slots[0] = jnp.zeros_like(tap_slots[0])
    tap_slots[0, :CONV, :per] = conv_bc[...]
    tap_slots[0, CONV : CONV + 1, :per] = conv_bc_bias[...]
    turned[...] = jnp.zeros_like(turned)
    turned[:heads, :] = w_dt[...]
    own_rows = pl.ds(pl.multiple_of(ring.me * shard, shard), shard)
    wxd[own_rows, width:] = turned[...].T.astype(bf16)
    dpar[...] = jnp.zeros_like(dpar)
    dpar[0:1, :heads] = dt_bias[...]
    dpar[1:2, :heads] = a_rate[...]
    dpar[2:3, :heads] = d_skip[...]

    greet(ring, False)

    def exchange(k, i):
        slots = (bc_slots, tap_slots, row_slots)[k]
        at = k * (n - 1) + i - 1
        return remote(slots.at[0], slots.at[i], mp_send.at[at], mp_recv.at[at], mp=(z + i) % n)

    def rows_of(ref, low, high):
        def shard_of(r):
            return ref.at[pl.ds(pl.multiple_of(r * shard, shard), shard), pl.ds(low, high - low)]

        return shard_of

    def columns_of(r):
        return wout.at[:, pl.ds(pl.multiple_of(r * column_shard, column_shard), column_shard)]

    sems = [tuple(group.at[k] for group in (ring_send, ring_recv, core_send, core_recv)) for k in range(4)]
    get_x = Gather(ring, rows_of(wxd, 0, inner), shard, sems[0])
    get_bd = Gather(ring, rows_of(wxd, inner, wxd.shape[1]), shard, sems[1])
    get_z = Gather(ring, rows_of(wz, 0, inner), shard, sems[2])
    get_out = Gather(ring, columns_of, inner, sems[3])

    load_x.wait()
    cast_into(get_x.shard(ring.me), stage_a)
    get_x.start()
    for k in range(2):
        for i in range(1, n):
            exchange(k, i).start()
    load_z = loads.start(w_z, stage_a)
    fill_spread(spread)
    fill_positions(starts, pos, None)
    crow[0:1, :] = out_gain[...]
    crow[1:2, :] = expand(dpar[...], spread[...])[2:3]
    load_tok.wait()
    normalize(v_tok, gain, normed, inverse)
    load_cot = loads.start(cot, v_tok)
    store_normed = stores.start(normed, normed_o)
    stores.start(inverse, inverse_o)
    for k in range(2):
        for i in range(1, n):
            exchange(k, i).wait()
    first = lax.broadcasted_iota(jnp.int32, (shard, LANES), 1) < per
    for j in range((width - inner) // LANES):
        low, high = (z - 2 * j + n) % n, (z - 2 * j - 1 + n) % n
        columns = slice(inner + j * LANES, inner + (j + 1) * LANES)
        pair = jnp.where(first, bc_slots[low].astype(f32), pltpu.roll(bc_slots[high].astype(f32), per, 1))
        wxd[own_rows, columns] = pair.astype(bf16)
        taps[:, columns] = jnp.where(first[:8], tap_slots[low], pltpu.roll(tap_slots[high], per, 1))
    get_bd.start()
    taps[:, :inner] = jnp.zeros((8, inner), f32)
    taps[:CONV, :inner] = conv_x[...]
    taps[CONV : CONV + 1, :inner] = conv_x_bias[...]
    load_z.wait()
    cast_into(get_z.shard(ring.me), stage_a)
    load_out.wait()
    cast_into(get_out.shard(ring.me), stage_b)
    xin[pl.ds(0, 8), :] = jnp.zeros((8, width), f32)

    def project_chip(k, source):
        get_x.arrived(k)
        get_bd.arrived(k)
        part = pl.ds(pl.multiple_of((source // 2) * 2 * shard, 2 * shard), 2 * shard)

        def body(i, carry):
            at = pl.multiple_of(i * 512, 512)
            left = normed[pl.ds(at, 512), part]
            for c, w in tiles(wxd.shape[1], 512):
                here = mm(left, wxd[part, c : c + w])
                w_x_part = min(w, width - c)
                if k == 0:
                    xin[pl.ds(at + 8, 512), c : c + w_x_part] = here[:, :w_x_part]
                else:
                    xin[pl.ds(at + 8, 512), c : c + w_x_part] += here[:, :w_x_part]
                if w_x_part < w:
                    if k == 0:
                        dtin[pl.ds(at, 512), :] = here[:, w_x_part:]
                    else:
                        dtin[pl.ds(at, 512), :] += here[:, w_x_part:]
            return carry

        lax.fori_loop(0, length // 512, body, 0)

    project_chip(0, ring.me)
    get_x.second()
    get_bd.second()
    get_z.start()
    project_chip(1, ring.left)
    project_chip(2, ring.right)
    get_x.third()
    get_bd.third()
    project_chip(3, ring.across)
    for source, target in ((xin, xin_o), (wxd, wxd_o)):
        stores.start(source, target)
    steps(dtin, dpar, step, sgdt, step_low, decay_low)
    convolve(xin, taps, pos, slope, x_low, bc_low)
    get_z.second()
    get_out.start()
    for source, target in (
        (slope, slope_o), (x_low, x_low_o), (bc_low, bc_low_o), (step, step_o), (sgdt, sgdt_o),
        (step_low, step_low_o), (decay_low, decay_low_o),
    ):
        stores.start(source, target)

    def scan_tick(b):
        @pl.when(b == 1)
        def _():
            get_z.third()

    scan_forward(
        starts, x_low, bc_low, step_low, decay_low, ssd, states, spread, state, xs, yin, cbm, scan_tick
    )
    for source, target in ((ssd, ssd_o), (states, states_o)):
        stores.start(source, target)
    for k in range(4):
        get_z.arrived(k)
    project_rows(normed, wz, gate)
    stores.start(wz, wz_o)
    stores.start(gate, gate_o)
    gate_squares(gate, ssd, x_low, crow, gated, stat)
    for b in range(length // BLOCK):
        columns = slice(b * BLOCK, (b + 1) * BLOCK)
        row_slots[0, :, columns] = stat[columns, :].T[:8]
    for i in range(1, n):
        exchange(2, i).start()

    load_cot.wait()

    def back_chip(k, source):
        get_out.arrived(k)
        part = pl.ds(pl.multiple_of((source // 2) * 2 * column_shard, 2 * column_shard), 2 * column_shard)
        stores.start(wout.at[:, part], wout_o.at[:, part])

        def body(i, carry):
            at = pl.ds(pl.multiple_of(i * 512, 512), 512)
            left = v_tok[at, part]
            for c, w in tiles(inner, 512):
                here = mm_nt(left, wout[c : c + w, part])
                if k == 0:
                    gnorm[at, c : c + w] = here
                else:
                    gnorm[at, c : c + w] += here
            return carry

        lax.fori_loop(0, length // 512, body, 0)

    back_chip(0, ring.me)
    get_out.second()
    for i in range(1, n):
        exchange(2, i).wait()
    for b in range(length // BLOCK):
        columns = slice(b * BLOCK, (b + 1) * BLOCK)
        total = functools.reduce(lambda p, q: p + q, [row_slots[i, 0:1, columns] for i in range(n)])
        turned[...] = jnp.broadcast_to(lax.rsqrt(total / (inner * n) + EPS), turned.shape)
        inverse_out[columns, :] = turned[...].T
    store_normed.wait()
    gn = normed.at[:, pl.ds(0, inner)]
    scale_rows(gated, inverse_out, crow, gn)
    stores.start(gn, gn_o)
    stores.start(inverse_out, inverse_out_o)
    back_chip(1, ring.left)
    back_chip(2, ring.right)
    get_out.third()
    back_chip(3, ring.across)
    stores.start(gnorm, gnorm_o)
    cross_sums(gnorm, gn, stat)
    for b in range(length // BLOCK):
        columns = slice(b * BLOCK, (b + 1) * BLOCK)
        rows[:, columns] = stat[columns, :].T[:8]
    for each in (get_x, get_bd, get_z, get_out):
        each.drain()
    for copy in stores.pairs:
        if copy is not store_normed:
            copy.wait()


def output_kernel(
    lengths, rows_own, tok, gn, wout, cot, gate, gnorm_o, x_low, ssd, states, slope, xin, bc_low, step, sgdt,
    step_low, decay_low, inverse_out, taps, crow, dpar,
    low_gate, low_xd, out, dwout_o, csums, dsums, sums,
    v_gn, v_wout, v_cot, v_x, v_ssd, v_states, gs, v_slope, first_wide, second_wide, v_xd, dwout,
    v_bc, v_step, v_sgdt, v_step_low, v_decay_low, v_inverse,
    part, slots, cores, parts, wholes, row_slots, turned, stat,
    pos, rpos, spread, dstate, xs, gx, cbm, acc,
    load_sems, wout_sems, cot_sems, line_send, line_recv, core_send, core_recv, ring_send, ring_recv, mp_send, mp_recv,
):
    ring = Ring()
    starts = [jnp.int32(0)]
    for k in range(DOCS - 1):
        starts.append(starts[-1] + lengths[0, k])
    loads = Loads(load_sems)
    n = lax.axis_size("mp")
    z = lax.axis_index("mp")
    length, inner = v_gn.shape
    own = part.shape[1] // n
    v_gate = first_wide.at[pl.ds(0, length), pl.ds(0, inner)]
    gnorm = second_wide.at[pl.ds(0, length), pl.ds(0, inner)]
    total = gx.at[:, pl.ds(0, own)]
    line = Line(part, slots, (line_send, line_recv), total)

    def wout_copy(i):
        columns = line.columns(line.order(i))
        return pltpu.make_async_copy(wout.at[:, columns], v_wout.at[:, columns], wout_sems.at[i])

    load_gn = loads.start(gn, v_gn)
    wout_copy(0).start()
    row_slots[0] = rows_own[...]
    greet(ring, False)

    def exchange(i):
        return remote(
            row_slots.at[0], row_slots.at[i], mp_send.at[i - 1], mp_recv.at[i - 1], mp=(z + i) % n
        )

    for i in range(1, n):
        exchange(i).start()
    chunk = v_cot.shape[2]
    shard = dwout.shape[1]

    def cot_copy(j):
        return pltpu.make_async_copy(
            cot.at[:, pl.ds(pl.multiple_of(j * chunk, chunk), chunk)], v_cot.at[j % 2], cot_sems.at[j % 2]
        )

    load_gn.wait()
    for i in range(1, n):
        wout_copy(i).start()
    cot_copy(0).start()
    early = [
        loads.start(source, target)
        for source, target in (
            (gate, v_gate), (gnorm_o, gnorm), (x_low, v_x), (ssd, v_ssd), (inverse_out, v_inverse),
        )
    ]
    later = [
        loads.start(source, target)
        for source, target in (
            (states, v_states), (slope, v_slope), (bc_low, v_bc), (step, v_step), (sgdt, v_sgdt),
            (step_low, v_step_low), (decay_low, v_decay_low),
        )
    ]

    def quarter(i, carry):
        columns = line.columns(line.order(i))
        wout_copy(i).wait()
        for r in range(0, length, 512):
            part[r : r + 512, columns] = mm(v_gn[r : r + 512, :], v_wout[:, columns]).astype(bf16)

        @pl.when(i == 0)
        def _():
            line.inject(0)
            line.inject(1)

        return carry

    lax.fori_loop(0, n, quarter, 0)
    line.inject(2)
    grads = v_wout
    scatter = Scatter(
        ring, lambda r: grads.at[:, pl.ds(pl.multiple_of(r * shard, shard), shard)], cores, parts, wholes,
        (core_send, core_recv, ring_send, ring_recv),
    )

    def weight(j, carry):
        @pl.when(j < 3)
        def _():
            cot_copy(j + 1).start()

        cot_copy(j).wait()
        columns = pl.ds(pl.multiple_of(j * chunk, chunk), chunk)
        for r in range(0, inner, 256):
            grads[r : r + 256, columns] = mm_tn(v_gn[:, r : r + 256], v_cot[j % 2]).astype(bf16)
        scatter.start(j)
        return carry

    lax.fori_loop(0, 4, weight, 0)
    line.inject(3)
    line.forward(0, 1)
    v_tok, v_out = v_cot.at[0], v_cot.at[1]
    load_tok = loads.start(tok.at[:, pl.ds(pl.multiple_of(z * own, own), own)], v_tok)
    fill_spread(spread)
    fill_positions(starts, pos, rpos)
    for copy in early:
        copy.wait()
    for i in range(1, n):
        exchange(i).wait()
    for b in range(length // BLOCK):
        columns = slice(b * BLOCK, (b + 1) * BLOCK)
        row = functools.reduce(lambda p, q: p + q, [row_slots[i, 0:1, columns] for i in range(n)])
        turned[...] = jnp.broadcast_to(row / (inner * n), turned.shape)
        stat[columns, :] = turned[...].T
    gate_backward(
        v_gate, v_ssd, v_x, gnorm, crow, stat, inner * n, None, v_gn, gs, sums, known=v_inverse
    )
    load_xin = loads.start(xin, second_wide)
    store_gate = loads.start(v_gn, low_gate)
    line.inject(4)
    line.forward(1, 1)
    line.forward(0, 2)
    scatter.first()
    for copy in later:
        copy.wait()

    def scan_tick(i):
        line.inject(i + 5)
        line.forward(i + 2, 1)

        @pl.when(i < 3)
        def _():
            line.forward(i + 1, 2)

        @pl.when(i == 1)
        def _():
            scatter.second()

    gpre = first_wide
    scan_backward(
        starts, v_x, v_bc, v_step_low, v_decay_low, v_ssd, v_states, gs, v_slope, crow, v_step, v_sgdt, dpar,
        gpre, v_xd, dsums, spread, dstate, xs, gx, cbm, acc, scan_tick,
    )
    scatter.finish(dwout)
    store_dwout = loads.start(dwout, dwout_o)
    load_xin.wait()

    def conv_tick(b):
        @pl.when(b % 2 == 1)
        def _():
            line.inject(9 + b // 2)
            line.forward(6 + b // 2, 1)

    convolve_back(second_wide, gpre, taps, pos, rpos, v_xd, csums, conv_tick)
    line.inject(11)
    store_xd = loads.start(v_xd, low_xd)
    load_tok.wait()

    def last(t, carry):
        line.finish(t)
        v_out[line.rows(t), :] = (v_tok[line.rows(t), :].astype(f32) + total[...]).astype(bf16)
        return carry

    lax.fori_loop(0, line.blocks, last, 0)
    store_out = loads.start(v_out, out)
    line.drain()
    for copy in (store_gate, store_dwout, store_xd, store_out):
        copy.wait()


def input_kernel(
    tok, inverse, gain, normed, low_gate, low_xd, wz, wxd, cot, csums, sums, dsums,
    dwz_o, dwx_o, grad, dwbc, dwdt, conv_x, conv_x_bias, conv_bc, conv_bc_bias, dt_bias, a_rate, d_skip, in_gain, out_gain,
    dwz, dwxd, smalls, spread, bc_own, bc_slots,
    v_tok, v_normed, v_gate, v_xd, v_wz, v_wxd, v_cot,
    part, slots, total, z_grads, z_cores, z_parts, z_wholes, x_grads, x_cores, x_parts, x_wholes,
    rowacc, rows_own, rows_in, colacc, dp_in, bc_in, gain_in,
    load_sems, quarter_sems, line_send, line_recv, z_core_send, z_core_recv, z_ring_send, z_ring_recv,
    x_core_send, x_core_recv, x_ring_send, x_ring_recv,
    rows_send, rows_recv, dp_send, dp_recv, mp_send, mp_recv, bc_send, bc_recv,
):
    ring = Ring()
    loads = Loads(load_sems)
    n = lax.axis_size("mp")
    z = lax.axis_index("mp")
    size = lax.axis_size("dp")
    length, features = part.shape
    inner = v_gate.shape[1]
    width = smalls.shape[1]
    heads, per = dwdt.shape[0], dwbc.shape[0]
    own = features // n
    own_columns = pl.ds(pl.multiple_of(z * own, own), own)
    line = Line(part, slots, (line_send, line_recv), total)

    def quarter_loads(i):
        columns = line.columns(line.order(i))
        return [
            pltpu.make_async_copy(source, target, quarter_sems.at[i, k])
            for k, (source, target) in enumerate((
                (wz.at[columns, :], v_wz.at[columns, :]),
                (wxd.at[columns, :], v_wxd.at[columns, :]),
                (tok.at[:, columns], v_tok.at[:, columns]),
            ))
        ]

    first = [loads.start(source, target) for source, target in ((low_gate, v_gate), (low_xd, v_xd))]
    for copy in quarter_loads(0):
        copy.start()
    greet(ring, True)
    rowacc[...] = jnp.zeros_like(rowacc)
    for copy in first:
        copy.wait()
    for i in range(1, n):
        for copy in quarter_loads(i):
            copy.start()
    later = [
        loads.start(source, target)
        for source, target in ((normed, v_normed), (cot.at[:, own_columns], v_cot))
    ]

    def quarter(i, carry):
        columns = line.columns(line.order(i))
        for copy in quarter_loads(i):
            copy.wait()
        for r in range(0, length, 256):
            rows = slice(r, r + 256)
            here = mm_nt(v_gate[rows, :], v_wz[columns, :]) + mm_nt(v_xd[rows, :], v_wxd[columns, :])
            part[rows, columns] = here.astype(bf16)
            along = here * (v_tok[rows, columns].astype(f32) * inverse[rows, :1])
            folded = fold(along)
            if r == 0:
                colacc[:, columns] = folded
            else:
                colacc[:, columns] += folded
            along = along * gain[:, columns]
            sum_lanes = along[:, :LANES]
            for c in range(LANES, own, LANES):
                sum_lanes = sum_lanes + along[:, c : c + LANES]
            rowacc[rows, :] += sum_lanes

        @pl.when(i == 0)
        def _():
            line.inject(0)
            line.inject(1)

        @pl.when(i == 2)
        def _():
            line.inject(2)

        return carry

    lax.fori_loop(0, n, quarter, 0)
    line.inject(3)
    line.forward(0, 1)

    for b in range(length // BLOCK):
        columns = slice(b * BLOCK, (b + 1) * BLOCK)
        line_sum = jnp.sum(rowacc[columns, :].T, axis=0, keepdims=True)
        rows_own[:, columns] = jnp.broadcast_to(line_sum, (8, BLOCK))

    def rows_copy(i):
        return remote(
            rows_own, rows_in.at[i - 1], rows_send.at[i - 1], rows_recv.at[i - 1], mp=(z + i) % n
        )

    def dp_copy(i):
        return remote(
            smalls, dp_in.at[i - 1], dp_send.at[i - 1], dp_recv.at[i - 1], dp=(ring.me + i) % size
        )

    def bc_copy(i):
        return remote(
            smalls.at[pl.ds(0, 8), pl.ds(inner, width - inner)], bc_in.at[i - 1],
            mp_send.at[i - 1], mp_recv.at[i - 1], mp=(z + i) % n,
        )

    def gain_copy(i):
        return remote(
            smalls.at[pl.ds(8, 8), pl.ds(0, inner)], gain_in.at[i - 1],
            mp_send.at[n + i - 2], mp_recv.at[n + i - 2], mp=(z + i) % n,
        )

    smalls[...] = jnp.zeros_like(smalls)
    for k in range(CONV + 1):
        smalls[k : k + 1, :] = jnp.sum(csums[8 * k : 8 * k + 8, :], axis=0, keepdims=True)
    for k in range(2):
        smalls[CONV + 1 + k : CONV + 2 + k, :inner] = jnp.sum(sums[8 * k : 8 * k + 8, :], axis=0, keepdims=True)
        smalls[7:8, k * LANES : (k + 1) * LANES] = jnp.sum(dsums[8 * k : 8 * k + 8, :], axis=0, keepdims=True)
    for k in range(features // inner):
        smalls[8 + k : 9 + k, :inner] = jnp.sum(colacc[:, k * inner : (k + 1) * inner], axis=0, keepdims=True)
    for i in range(1, n):
        rows_copy(i).start()
    for i in range(1, size):
        dp_copy(i).start()

    later[0].wait()
    shard = dwz.shape[0]
    z_scatter = Scatter(
        ring, lambda r: z_grads.at[pl.ds(pl.multiple_of(r * shard, shard), shard), :], z_cores, z_parts, z_wholes,
        (z_core_send, z_core_recv, z_ring_send, z_ring_recv),
    )
    x_scatter = Scatter(
        ring, lambda r: x_grads.at[pl.ds(pl.multiple_of(r * shard, shard), shard), :], x_cores, x_parts, x_wholes,
        (x_core_send, x_core_recv, x_ring_send, x_ring_recv),
    )

    def weight(j, right, grads):
        for c in range(0, 2 * shard, shard):
            rows = pl.ds(pl.multiple_of(j * 2 * shard + c, shard), shard)
            left = v_normed[:, rows]
            for at, w in tiles(grads.shape[1], 512):
                grads[rows, at : at + w] = mm_tn(left, right[:, at : at + w]).astype(bf16)

    def z_weight(j, carry):
        weight(j, v_gate, z_grads)
        z_scatter.start(j)
        return carry

    lax.fori_loop(0, 4, z_weight, 0)
    line.inject(4)
    line.forward(1, 1)
    line.forward(0, 2)

    def x_weight(j, carry):
        weight(j, v_xd, x_grads)
        x_scatter.start(j)

        @pl.when(j == 1)
        def _():
            z_scatter.first()

        @pl.when(j % 2 == 1)
        def _():
            line.inject(5 + j // 2)
            line.forward(2 + j // 2, 1)

        return carry

    lax.fori_loop(0, 4, x_weight, 0)
    line.forward(1, 2)
    x_scatter.first()
    z_scatter.second()
    line.inject(7)
    line.forward(4, 1)
    line.forward(2, 2)

    for i in range(1, size):
        dp_copy(i).wait()
    smalls[...] += functools.reduce(lambda a, b: a + b, [dp_in[i] for i in range(size - 1)])
    for i in range(1, n):
        bc_copy(i).start()
        gain_copy(i).start()
    x_scatter.second()
    line.inject(8)
    line.forward(5, 1)
    line.forward(3, 2)
    z_scatter.finish(dwz)
    store_z = loads.start(dwz, dwz_o)
    line.inject(9)
    line.forward(6, 1)
    for i in range(1, n):
        rows_copy(i).wait()
    rows_own[...] += functools.reduce(lambda a, b: a + b, [rows_in[i] for i in range(n - 1)])
    line.inject(10)
    line.forward(7, 1)
    for i in range(1, n):
        bc_copy(i).wait()
        gain_copy(i).wait()
    smalls[0:8, inner:] += functools.reduce(lambda a, b: a + b, [bc_in[i] for i in range(n - 1)])
    smalls[8:16, :inner] += functools.reduce(lambda a, b: a + b, [gain_in[i] for i in range(n - 1)])
    line.inject(11)
    x_scatter.finish(dwxd)
    share = LANES // per

    def mine(v):
        turns = [v] + [pltpu.roll(v, LANES - k * per, 1) for k in range(1, share)]
        which = jnp.full(v.shape, z % share, jnp.int32)
        return functools.reduce(lambda a, k: jnp.where(which == k, turns[k], a), range(1, share), turns[0])

    for j in range((width - inner) // LANES):
        bc_own[j] = dwxd[:, inner + j * LANES : inner + (j + 1) * LANES].astype(bf16)

    def weight_copy(i):
        other = (z + i) % n
        return remote(
            bc_own.at[other // share], bc_slots.at[i - 1], bc_send.at[i - 1], bc_recv.at[i - 1], mp=other
        )

    for i in range(1, n):
        weight_copy(i).start()
    store_x = loads.start(dwxd.at[:, pl.ds(0, inner)], dwx_o)
    dwdt[...] = dwxd[:, width:].T[:heads]
    lanes = pl.ds(pl.multiple_of(inner + (z // share) * LANES, LANES), LANES)
    conv_x[...] = smalls[:CONV, :inner]
    conv_x_bias[...] = smalls[CONV : CONV + 1, :inner]
    taps = mine(smalls[:8, lanes])
    conv_bc[...] = taps[:CONV, :per]
    conv_bc_bias[...] = taps[CONV : CONV + 1, :per]
    out_gain[...] = smalls[5:6, :inner]
    fill_spread(spread)
    d_skip[...] = gather_heads(smalls[0:8, :inner], spread[...])[6:7, :heads]
    dt_bias[...] = smalls[7:8, :heads]
    a_rate[...] = smalls[7:8, LANES : LANES + heads]
    fits = inner // own
    in_gain[...] = smalls[pl.ds(8 + z // fits, 1), pl.ds(pl.multiple_of((z % fits) * own, own), own)]
    for i in range(1, n):
        weight_copy(i).wait()
    here = functools.reduce(lambda a, b: a + b, [bc_slots[i].astype(f32) for i in range(n - 1)], dwxd[:, lanes])
    dwbc[...] = mine(here).T[:per]
    later[1].wait()

    def last(t, carry):
        line.finish(t)
        rows = line.rows(t)
        mean = jnp.broadcast_to(rows_own[0:1, rows] / features, (LANES, BLOCK)).T
        for c in range(0, own, LANES):
            columns = pl.ds(pl.multiple_of(z * own + c, LANES), LANES)
            hat = v_tok[rows, columns].astype(f32) * inverse[rows, :]
            change = inverse[rows, :] * (total[:, c : c + LANES] * gain[:, columns] - hat * mean)
            grad[rows, c : c + LANES] = (v_cot[rows, c : c + LANES].astype(f32) + change).astype(bf16)
        return carry

    lax.fori_loop(0, line.blocks, last, 0)
    line.drain()
    store_z.wait()
    store_x.wait()


def hand_on_kernel(*refs):
    count = (len(refs) - 2) // 3
    sources, targets, buffers = refs[:count], refs[count : 2 * count], refs[2 * count : 3 * count]
    into, out = refs[-2:]
    there = [pltpu.make_async_copy(sources[k], buffers[k], into.at[k]) for k in range(count)]
    back = [pltpu.make_async_copy(buffers[k], targets[k], out.at[k]) for k in range(count)]
    for copy in there:
        copy.start()
    for k in range(count):
        there[k].wait()
        back[k].start()
    for copy in back:
        copy.wait()


def hand_on(*arrays):
    kinds = [(v.shape, v.dtype) for v in arrays]
    return call(
        hand_on_kernel, kinds, kinds, 0, *arrays,
        places="a" * len(arrays), sems=[(len(arrays),)] * 2, far=len(arrays),
    )


def call(kernel, outs, scratch, smem, *operands, places=None, sems=(), collective=None, far=0):
    spaces = {"s": pltpu.SMEM, "v": pltpu.VMEM, "a": pl.ANY}
    if places is None:
        places = "s" * smem + "v" * (len(operands) - smem)
    extra = {} if collective is None else dict(collective_id=collective, has_side_effects=True)
    return pl.pallas_call(
        kernel,
        out_shape=[jax.ShapeDtypeStruct(shape, kind) for shape, kind in outs],
        in_specs=[pl.BlockSpec(memory_space=spaces[c]) for c in places],
        out_specs=[pl.BlockSpec(memory_space=pl.ANY if i < far else pltpu.VMEM) for i in range(len(outs))],
        scratch_shapes=[pltpu.VMEM(shape, kind) for shape, kind in scratch]
        + [pltpu.SemaphoreType.DMA(shape) for shape in sems],
        compiler_params=pltpu.CompilerParams(vmem_limit_bytes=VMEM_LIMIT, **extra),
    )(*operands)


def per_device_any(
    tokens, cotangent, doc_lengths, w_z, w_x, w_bc, w_dt, w_out, conv_x, conv_x_bias, conv_bc,
    conv_bc_bias, dt_bias, a_rate, d_skip, input_norm_gain, out_gain,
):
    group = lax.axis_size("mp")
    rank = lax.axis_index("mp")
    T, D = tokens.shape
    inner, heads = w_x.shape[1], w_dt.shape[1]
    pair = 2 * STATE
    width = inner + pair
    wide = width + LANES
    own = D // group

    lengths = doc_lengths[0]
    starts = jnp.cumsum(lengths) - lengths
    packed = jnp.concatenate([w_bc, conv_bc, conv_bc_bias[None, :]], axis=0)
    packed = lax.all_gather(packed, "mp", axis=1, tiled=True)
    shard = w_bc.shape[0]
    w_bc_all, taps_bc = packed[:shard], packed[shard:]
    wxd = jnp.concatenate(
        [w_x.astype(bf16), w_bc_all.astype(bf16), w_dt.astype(bf16), jnp.zeros((shard, LANES - heads), bf16)],
        axis=1,
    )
    wxd = lax.all_gather(wxd, "dp", axis=0, tiled=True)
    wz = lax.all_gather(w_z.astype(bf16), "dp", axis=0, tiled=True)
    wout = lax.all_gather(w_out.astype(bf16), "dp", axis=1, tiled=True)
    taps = jnp.concatenate([jnp.concatenate([conv_x, conv_x_bias[None, :]], axis=0), taps_bc], axis=1)
    taps = jnp.pad(taps, ((0, 8 - CONV - 1), (0, 0)))
    crow = jnp.pad(jnp.stack([out_gain, jnp.repeat(d_skip, HEADDIM)]), ((0, 6), (0, 0)))
    dpar = jnp.pad(jnp.stack([dt_bias, a_rate]), ((0, 6), (0, LANES - heads)))
    gain = input_norm_gain[None, :]

    blocks = T // BLOCK
    (
        normed, inverse, xin, slope, gate, x_low, bc_low, step, sgdt, step_low, decay_low, ssd, states,
    ) = call(
        forward_kernel,
        [
            ((T, D), bf16), ((T, LANES), f32), ((T + 8, width), f32), ((T, width), bf16), ((T, inner), f32),
            ((T, inner), bf16), ((T, pair), bf16), ((T, LANES), f32), ((T, LANES), f32),
            ((T, LANES), bf16), ((T, LANES), bf16), ((T, inner), bf16), ((blocks, STATE, inner), bf16),
        ],
        [
            ((T, LANES), jnp.int32), ((LANES, inner), bf16), ((T, LANES), f32), ((STATE, inner), f32),
            ((BLOCK, inner), bf16), ((BLOCK, inner), f32), ((BLOCK, BLOCK), f32),
        ],
        1, starts, tokens, gain, wxd, wz, taps, dpar,
    )
    gnorm, stat = call(
        gate_kernel,
        [((T, inner), f32), ((T, LANES), f32)],
        [],
        0, cotangent, wout, gate, ssd, x_low, crow,
    )
    stat = jnp.pad(lax.psum(stat[:, :8], "mp"), ((0, 0), (0, LANES - 8)))
    branch, dwout, dwz, low_gate, gs, sums = call(
        functools.partial(middle_kernel, width=inner * group),
        [
            ((T, D), bf16), ((inner, D), bf16), ((D, inner), bf16), ((T, inner), bf16), ((T, inner), bf16),
            ((16, inner), f32),
        ],
        [((T, inner), bf16)],
        0, cotangent, wout, normed, gate, x_low, ssd, gnorm, crow, stat,
    )
    low_xd, csums, dsums = call(
        backward_kernel,
        [((T, wide), bf16), ((8 * CONV + 8, width), f32), ((16, LANES), f32)],
        [
            ((T, LANES), jnp.int32), ((T, LANES), jnp.int32), ((LANES, inner), bf16), ((T + 8, width), f32),
            ((STATE, inner), f32), ((BLOCK, inner), bf16), ((BLOCK, inner), f32), ((BLOCK, BLOCK), f32),
            ((BLOCK, BLOCK), f32),
        ],
        1, starts, xin, slope, x_low, bc_low, step, sgdt, step_low, decay_low, ssd, states, gs, taps, crow,
        dpar,
    )
    dwxd, gfull, rowdot = call(
        last_kernel,
        [((D, wide), bf16), ((T, D), bf16), ((T, LANES), f32)],
        [],
        0, tokens, inverse, gain, normed, low_gate, low_xd, wz, wxd,
    )

    def scatter(v, axis, dim):
        return lax.psum_scatter(v, axis, scatter_dimension=dim, tiled=True)

    token_own = lax.dynamic_slice_in_dim(tokens, rank * own, own, 1).astype(f32)
    output = (token_own + scatter(branch, "mp", 1).astype(f32)).astype(bf16)
    w_out_grad = scatter(dwout, "dp", 1).astype(f32)
    w_z_grad = scatter(dwz, "dp", 0).astype(f32)
    dwxd_own = scatter(dwxd, "dp", 0)
    w_x_grad = dwxd_own[:, :inner].astype(f32)
    w_dt_grad = dwxd_own[:, width : width + heads].astype(f32)
    w_bc_grad = scatter(dwxd_own[:, inner:width], "mp", 1).astype(f32)

    g_own = scatter(gfull, "mp", 1).astype(f32)
    gain_own = lax.dynamic_slice_in_dim(input_norm_gain, rank * own, own, 0)
    row_mean = (lax.psum(rowdot[:, 0], "mp") / D)[:, None]
    inv = inverse[:, :1]
    hat = token_own * inv
    cot_own = lax.dynamic_slice_in_dim(cotangent, rank * own, own, 1).astype(f32)
    input_grad = (cot_own + inv * (g_own * gain_own - hat * row_mean)).astype(bf16)
    in_gain = jnp.sum(g_own * hat, axis=0)

    csums = jnp.sum(csums.reshape(CONV + 1, 8, width), axis=1)
    sums = jnp.sum(sums.reshape(2, 8, inner), axis=1)
    dsums = jnp.sum(dsums.reshape(2, 8, LANES), axis=1)[:, :heads]
    csums_bc = scatter(csums[:, inner:], "mp", 1)
    conv_grad, conv_bc_grad, sums, dsums, in_gain = lax.psum(
        (csums[:, :inner], csums_bc, sums, dsums, in_gain), "dp"
    )
    d_skip_grad = jnp.sum(sums[1].reshape(heads, HEADDIM), axis=1)
    return (
        output, input_grad, w_z_grad, w_x_grad, w_bc_grad, w_dt_grad, w_out_grad,
        conv_grad[:CONV], conv_grad[CONV], conv_bc_grad[:CONV], conv_bc_grad[CONV],
        dsums[0], dsums[1], d_skip_grad, in_gain, sums[0],
    )


def per_device(
    tokens, cotangent, doc_lengths, w_z, w_x, w_bc, w_dt, w_out, conv_x, conv_x_bias, conv_bc,
    conv_bc_bias, dt_bias, a_rate, d_skip, input_norm_gain, out_gain,
):
    group, size = lax.axis_size("mp"), lax.axis_size("dp")
    T, D = tokens.shape
    shard, inner = w_x.shape
    heads, per = w_dt.shape[1], w_bc.shape[1]
    pair = per * group
    width = inner + pair
    wide = width + LANES
    own = D // group
    columns = w_out.shape[1]
    blocks = T // BLOCK
    messages = blocks * (group - 1)

    def row(v):
        return v[None, :]

    (
        normed, xin, slope, x_low, ssd, states, wxd, wz, wout, gn, gate, gnorm,
        bc_low, step, sgdt, step_low, decay_low, inverse, inverse_out, taps, crow, dpar, rows,
    ) = call(
        gather_kernel,
        [
            ((T, D), bf16), ((T + 8, width), f32), ((T, width), bf16), ((T, inner), bf16), ((T, inner), bf16),
            ((blocks, STATE, inner), bf16), ((D, wide), bf16), ((D, inner), bf16), ((inner, D), bf16),
            ((T, inner), bf16), ((T, inner), f32), ((T, inner), f32),
            ((T, pair), bf16), ((T, LANES), f32), ((T, LANES), f32), ((T, LANES), bf16), ((T, LANES), bf16),
            ((T, LANES), f32), ((T, LANES), f32),
            ((8, width), f32), ((8, inner), f32), ((8, LANES), f32), ((8, T), f32),
        ],
        [
            ((T, D), bf16), ((shard, inner), f32), ((inner, columns), f32), ((T, D), bf16), ((T + 8, width), f32),
            ((T, width), bf16), ((T, inner), bf16), ((T, inner), bf16), ((blocks, STATE, inner), bf16),
            ((D, wide), bf16), ((D, inner), bf16), ((inner, D), bf16), ((T, inner), f32), ((T, inner), f32),
            ((T, inner), f32),
            ((T, pair), bf16), ((T, LANES), f32), ((T, LANES), f32), ((T, LANES), bf16), ((T, LANES), bf16),
            ((T, LANES), f32), ((T, LANES), f32),
            ((group, shard, LANES), bf16), ((group, 8, LANES), f32), ((group, 8, T), f32),
            ((T, LANES), f32), ((LANES, BLOCK), f32),
            ((T, LANES), jnp.int32), ((LANES, inner), bf16), ((T, LANES), f32), ((STATE, inner), f32),
            ((BLOCK, inner), bf16), ((BLOCK, inner), f32), ((BLOCK, BLOCK), f32),
        ],
        0, doc_lengths, tokens, cotangent, w_x, w_z, w_out, w_bc.T, w_dt.T, conv_x, row(conv_x_bias), conv_bc,
        row(conv_bc_bias), row(dt_bias), row(a_rate), row(d_skip), row(input_norm_gain), row(out_gain),
        places="s" + "a" * 5 + "v" * 11,
        sems=[(5,), (23,), (4, 4), (4, 4), (4, 4), (4, 4), (3 * group - 3,), (3 * group - 3,)],
        collective=0,
        far=19,
    )
    low_gate, low_xd, output, w_out_grad, csums, dsums, sums = call(
        output_kernel,
        [
            ((T, inner), bf16), ((T, wide), bf16),
            ((T, own), bf16), ((inner, columns), f32), ((8 * CONV + 8, width), f32), ((16, LANES), f32),
            ((16, inner), f32),
        ],
        [
            ((T, inner), bf16), ((inner, D), bf16), ((2, T, 2 * columns), bf16), ((T, inner), bf16),
            ((T, inner), bf16), ((blocks, STATE, inner), bf16), ((T, inner), bf16), ((T, width), bf16),
            ((T + 8, width), f32), ((T + 8, width), f32), ((T, wide), bf16), ((inner, columns), f32),
            ((T, pair), bf16), ((T, LANES), f32), ((T, LANES), f32), ((T, LANES), bf16), ((T, LANES), bf16),
            ((T, LANES), f32),
            ((T, D), bf16), ((2, messages, BLOCK, own), bf16),
            ((4, inner, columns), bf16), ((2, inner // 2, columns), bf16), ((2, inner, columns), bf16),
            ((group, 8, T), f32), ((LANES, BLOCK), f32), ((T, LANES), f32),
            ((T, LANES), jnp.int32), ((T, LANES), jnp.int32), ((LANES, inner), bf16),
            ((STATE, inner), f32), ((BLOCK, inner), bf16), ((BLOCK, inner), f32), ((BLOCK, BLOCK), f32),
            ((BLOCK, BLOCK), f32),
        ],
        0, doc_lengths, rows, tokens, gn, wout, cotangent, gate, gnorm, x_low, ssd, states, slope, xin, bc_low,
        step, sgdt, step_low, decay_low, inverse_out, taps, crow, dpar,
        places="sv" + "a" * 17 + "v" * 3,
        sems=[(19,), (group,), (2,), (2, messages), (2, messages), (4,), (4,), (4,), (4,), (group - 1,), (group - 1,)],
        collective=1,
        far=4,
    )
    w_z_grad, w_x_grad, input_grad, w_bc_grad, w_dt_grad, *small_grads = call(
        input_kernel,
        [
            ((shard, inner), f32), ((shard, inner), f32), ((T, own), bf16), ((per, shard), f32),
            ((heads, shard), f32), ((CONV, inner), f32), ((1, inner), f32), ((CONV, per), f32), ((1, per), f32),
            ((1, heads), f32), ((1, heads), f32), ((1, heads), f32), ((1, own), f32), ((1, inner), f32),
        ],
        [
            ((shard, inner), f32), ((shard, wide), f32), ((16, width), f32), ((LANES, inner), bf16),
            ((pair // LANES, shard, LANES), bf16), ((group - 1, shard, LANES), bf16),
            ((T, D), bf16), ((T, D), bf16), ((T, inner), bf16), ((T, wide), bf16), ((D, inner), bf16),
            ((D, wide), bf16), ((T, own), bf16),
            ((T, D), bf16), ((2, messages, BLOCK, own), bf16), ((BLOCK, own), f32),
            ((D, inner), bf16), ((4, shard, inner), bf16), ((2, shard // 2, inner), bf16), ((2, shard, inner), bf16),
            ((D, wide), bf16), ((4, shard, wide), bf16), ((2, shard // 2, wide), bf16), ((2, shard, wide), bf16),
            ((T, LANES), f32), ((8, T), f32), ((group - 1, 8, T), f32), ((8, D), f32),
            ((size - 1, 16, width), f32), ((group - 1, 8, pair), f32), ((group - 1, 8, inner), f32),
        ],
        0, tokens, inverse, row(input_norm_gain), normed, low_gate, low_xd, wz, wxd, cotangent, csums, sums, dsums,
        places="avvaaaaaavvv",
        sems=[
            (6,), (group, 3), (2, messages), (2, messages), (4,), (4,), (4,), (4,), (4,), (4,), (4,), (4,),
            (group - 1,), (group - 1,), (size - 1,), (size - 1,), (2 * group - 2,), (2 * group - 2,),
            (group - 1,), (group - 1,),
        ],
        collective=2,
        far=2,
    )
    (
        output, input_grad, w_z_grad, w_x_grad, w_bc_grad, w_dt_grad, w_out_grad, conv_x_grad, conv_x_bias_grad,
        conv_bc_grad, conv_bc_bias_grad, dt_bias_grad, a_rate_grad, d_skip_grad, in_gain_grad, out_gain_grad,
    ) = hand_on(output, input_grad, w_z_grad, w_x_grad, w_bc_grad, w_dt_grad, w_out_grad, *small_grads)
    return (
        output, input_grad, w_z_grad, w_x_grad, w_bc_grad.T, w_dt_grad.T, w_out_grad,
        conv_x_grad, conv_x_bias_grad[0], conv_bc_grad, conv_bc_bias_grad[0], dt_bias_grad[0], a_rate_grad[0],
        d_skip_grad[0], in_gain_grad[0], out_gain_grad[0],
    )


def solution(mesh):
    row, block, column = P("dp", None), P("dp", "mp"), P("mp")
    return jax.shard_map(
        per_device if (mesh.shape["dp"], mesh.shape["mp"]) == (8, 4) else per_device_any,
        mesh=mesh,
        in_specs=(
            row, row, row, block, block, block, block, P("mp", "dp"), P(None, "mp"), column,
            P(None, "mp"), column, column, column, column, P(), column,
        ),
        out_specs=(
            block, block, block, block, block, block, P("mp", "dp"), P(None, "mp"), column,
            P(None, "mp"), column, column, column, column, column, column,
        ),
        check_vma=False,
    )
```

```python
import functools

import jax
import jax.numpy as jnp
from jax import lax
from jax.experimental import pallas as pl
from jax.experimental.pallas import tpu as pltpu
from jax.sharding import PartitionSpec as P

HEADDIM = 64
STATE = 128
CONV = 4
BLOCK = 256
DOCS = 5
LANES = 128
EPS = 1e-05
f32 = jnp.float32
bf16 = jnp.bfloat16
VMEM_LIMIT = 127 * 2**19


def mm(a, b):
    return jnp.dot(a, b, preferred_element_type=f32)


def mm_nt(a, b):
    return lax.dot_general(a, b, (((1,), (1,)), ((), ())), preferred_element_type=f32)


def mm_tn(a, b):
    return lax.dot_general(a, b, (((0,), (0,)), ((), ())), preferred_element_type=f32)


def halves(v):
    high = v.astype(bf16)
    return high, (v - high.astype(f32)).astype(bf16)


def expand(v, spread):
    high, rest = halves(v)
    return mm(high, spread) + mm(rest, spread)


def gather_heads(v, spread):
    high, rest = halves(v)
    return mm_nt(high, spread) + mm_nt(rest, spread)


def logistic(v):
    return 1.0 / (1.0 + jnp.exp(-v))


def tiles(total, size):
    return [(at, min(size, total - at)) for at in range(0, total, size)]


def fold(v):
    return jnp.sum(v.reshape(v.shape[0] // 8, 8, v.shape[1]), axis=0)


def doc_of(starts, place):
    count = (place >= starts[0]).astype(jnp.int32)
    for k in range(1, DOCS):
        count = count + (place >= starts[k]).astype(jnp.int32)
    return count


def fill_spread(spread):
    rows, columns = spread.shape
    head = lax.broadcasted_iota(jnp.int32, (rows, columns), 0)
    channel = lax.broadcasted_iota(jnp.int32, (rows, columns), 1)
    low = head * HEADDIM
    spread[...] = jnp.where((channel >= low) & (channel < low + HEADDIM), 1.0, 0.0).astype(bf16)


def fill_positions(starts, pos, rpos):
    length = pos.shape[0]

    def body(i, carry):
        at = pl.multiple_of(i * BLOCK, BLOCK)
        place = lax.broadcasted_iota(jnp.int32, (BLOCK, LANES), 0) + at
        begin = jnp.zeros_like(place)
        end = jnp.full_like(place, length)
        for k in range(DOCS):
            begin = jnp.maximum(begin, jnp.where(place >= starts[k], starts[k], 0))
            end = jnp.minimum(end, jnp.where(place < starts[k], starts[k], length))
        pos[pl.ds(at, BLOCK), :] = place - begin
        if rpos is not None:
            rpos[pl.ds(at, BLOCK), :] = end - 1 - place
        return carry

    lax.fori_loop(0, length // BLOCK, body, 0)


def normalize(tok, gain, normed, stat):
    step = 64

    def body(i, carry):
        rows = pl.ds(pl.multiple_of(i * step, step), step)
        v = tok[rows, :].astype(f32)
        inverse = lax.rsqrt(jnp.mean(v * v, axis=1, keepdims=True) + EPS)
        normed[rows, :] = (v * inverse * gain[...]).astype(bf16)
        stat[rows, :] = jnp.broadcast_to(inverse, (step, LANES))
        return carry

    lax.fori_loop(0, tok.shape[0] // step, body, 0)


def project_x(normed, wxd, xin, dtin):
    length, width = normed.shape[0], xin.shape[1]
    xin[pl.ds(0, 8), :] = jnp.zeros((8, width), f32)
    rows = 512

    def body(i, carry):
        at = pl.multiple_of(i * rows, rows)
        left = normed[pl.ds(at, rows), :]
        for c, w in tiles(width, 512):
            xin[pl.ds(at + 8, rows), c : c + w] = mm(left, wxd[:, c : c + w])
        dtin[pl.ds(at, rows), :] = mm(left, wxd[:, width : width + LANES])
        return carry

    lax.fori_loop(0, length // rows, body, 0)


def convolve(xin, taps, pos, slope, x_low, bc_low):
    width, inner = xin.shape[1], x_low.shape[1]

    def tile(b, c, out, at):
        rows = pl.ds(pl.multiple_of(b * BLOCK, BLOCK), BLOCK)
        x = xin[pl.ds(pl.multiple_of(b * BLOCK, BLOCK), BLOCK + 8), pl.ds(c, LANES)]
        place = pos[rows, :]
        tap = taps[:, pl.ds(c, LANES)]
        pre = tap[CONV : CONV + 1] + tap[CONV - 1 : CONV] * x[8:]
        for lag in range(1, CONV):
            earlier = pltpu.roll(x, lag, 0)[8:]
            pre = pre + tap[CONV - 1 - lag : CONV - lag] * jnp.where(place >= lag, earlier, 0.0)
        sg = logistic(pre)
        slope[rows, pl.ds(c, LANES)] = (sg * (1.0 + pre * (1.0 - sg))).astype(bf16)
        out[rows, pl.ds(at, LANES)] = (pre * sg).astype(bf16)

    blocks = x_low.shape[0] // BLOCK
    xcols, bcols = inner // LANES, (width - inner) // LANES

    def x_body(i, carry):
        c = pl.multiple_of((i % xcols) * LANES, LANES)
        tile(i // xcols, c, x_low, c)
        return carry

    def bc_body(i, carry):
        c = pl.multiple_of((i % bcols) * LANES, LANES)
        tile(i // bcols, inner + c, bc_low, c)
        return carry

    lax.fori_loop(0, blocks * xcols, x_body, 0)
    lax.fori_loop(0, blocks * bcols, bc_body, 0)


def softplus(v):
    return jnp.maximum(v, 0.0) + jnp.log1p(jnp.exp(-jnp.abs(v)))


def steps(dtin, dpar, step, sgdt, step_low, decay_low):
    def body(i, carry):
        rows = pl.ds(pl.multiple_of(i * BLOCK, BLOCK), BLOCK)
        v = dtin[rows, :] + dpar[0:1, :]
        soft = softplus(v)
        if step is not None:
            step[rows, :] = soft
            sgdt[rows, :] = logistic(v)
        step_low[rows, :] = soft.astype(bf16)
        decay_low[rows, :] = (-dpar[1:2, :] * soft).astype(bf16)
        return carry

    lax.fori_loop(0, dtin.shape[0] // BLOCK, body, 0)


def block_marks(starts, b):
    at = b * BLOCK
    column = doc_of(starts, lax.broadcasted_iota(jnp.int32, (BLOCK, 1), 0) + at)
    row = doc_of(starts, lax.broadcasted_iota(jnp.int32, (1, BLOCK), 1) + at)
    before = doc_of(starts, at - 1)
    last = doc_of(starts, at + BLOCK - 1)
    return column, row, before, last


def block_decays(b, starts, decay_low, step_low, spread):
    rows = pl.ds(pl.multiple_of(b * BLOCK, BLOCK), BLOCK)
    column, row, before, last = block_marks(starts, b)
    i0 = lax.broadcasted_iota(jnp.int32, (BLOCK, BLOCK), 0)
    i1 = lax.broadcasted_iota(jnp.int32, (BLOCK, BLOCK), 1)
    lower = jnp.where(i0 >= i1, 1.0, 0.0).astype(bf16)
    cum = mm(lower, decay_low[rows, :])
    step_e = mm(step_low[rows, :], spread[...])
    cum_e = expand(jnp.exp(cum), spread[...])
    kept_e = jnp.where(before == last, cum_e[BLOCK - 1 : BLOCK], 0.0)
    in_e = jnp.where(column == before, cum_e, 0.0)
    out_e = expand(jnp.exp(cum[BLOCK - 1 : BLOCK] - cum), spread[...])
    out_e = jnp.where(column == last, out_e, 0.0)
    return cum, step_e, kept_e, in_e, out_e, column, row


def scan_forward(
    starts, x_low, bc_low, step_low, decay_low, ssd, states, spread, state, xs, yin, cbm, tick=None
):
    length, inner = x_low.shape
    state[...] = jnp.zeros_like(state)

    def body(b, carry):
        rows = pl.ds(pl.multiple_of(b * BLOCK, BLOCK), BLOCK)
        cum, step_e, kept_e, in_e, out_e, column, row = block_decays(
            b, starts, decay_low, step_low, spread
        )
        bm, cm = bc_low[rows, :STATE], bc_low[rows, STATE:]
        i0 = lax.broadcasted_iota(jnp.int32, (BLOCK, BLOCK), 0)
        i1 = lax.broadcasted_iota(jnp.int32, (BLOCK, BLOCK), 1)
        cbm[...] = jnp.where((column == row) & (i0 >= i1), mm_nt(cm, bm), 0.0)
        stepped = x_low[rows, :].astype(f32) * step_e
        xs[...] = stepped.astype(bf16)
        entering = state[...].astype(bf16)
        states[b] = entering
        yin[...] = in_e * mm(cm, entering)
        state[...] = kept_e * state[...] + mm_tn(bm, (stepped * out_e).astype(bf16))
        cum_t = cum.T
        first = lax.broadcasted_iota(jnp.int32, (BLOCK, LANES), 1) < HEADDIM
        for j in range(inner // LANES):
            cols = slice(j * LANES, (j + 1) * LANES)
            pair = xs[:, cols]
            part = []
            for h in (2 * j, 2 * j + 1):
                span = jnp.minimum(cum[:, h : h + 1] - cum_t[h : h + 1, :], 0.0)
                part.append(mm((jnp.exp(span) * cbm[...]).astype(bf16), pair))
            y = jnp.where(first, part[0], part[1]) + yin[:, cols]
            ssd[rows, cols] = y.astype(bf16)
        if tick is not None:
            tick(b)
        return carry

    lax.fori_loop(0, length // BLOCK, body, 0)


def project_rows(left, right, out, rows=512, columns=512):
    def body(i, carry):
        at = pl.ds(pl.multiple_of(i * rows, rows), rows)
        part = left[at, :]
        for c, w in tiles(out.shape[1], columns):
            out[at, c : c + w] = mm(part, right[:, c : c + w]).astype(out.dtype)
        return carry

    lax.fori_loop(0, out.shape[0] // rows, body, 0)


def back_rows(left, right, out, rows=512, columns=512):
    def body(i, carry):
        at = pl.ds(pl.multiple_of(i * rows, rows), rows)
        part = left[at, :]
        for c, w in tiles(out.shape[1], columns):
            out[at, c : c + w] = mm_nt(part, right[c : c + w, :]).astype(out.dtype)
        return carry

    lax.fori_loop(0, out.shape[0] // rows, body, 0)


def weight_rows(left, right, out, rows=256, columns=512):
    def body(i, carry):
        at = pl.ds(pl.multiple_of(i * rows, rows), rows)
        part = left[:, at]
        for c, w in tiles(out.shape[1], columns):
            out[at, c : c + w] = mm_tn(part, right[:, c : c + w]).astype(out.dtype)
        return carry

    lax.fori_loop(0, out.shape[0] // rows, body, 0)


def gate_sums(gate, ssd, x_low, gnorm, crow, stat):
    step, inner = 64, gate.shape[1]

    def body(i, carry):
        rows = pl.ds(pl.multiple_of(i * step, step), step)
        squares = jnp.zeros((step, 256), f32)
        crosses = jnp.zeros((step, 256), f32)
        for c in range(0, inner, 256):
            cols = slice(c, c + 256)
            g = gate[rows, cols]
            mixed = ssd[rows, cols].astype(f32) + crow[1:2, cols] * x_low[rows, cols].astype(f32)
            gated = mixed * (g * logistic(g))
            squares = squares + gated * gated
            crosses = crosses + gnorm[rows, cols] * crow[0:1, cols] * gated
        lane = lax.broadcasted_iota(jnp.int32, (step, LANES), 1)
        s1 = jnp.sum(squares, axis=1, keepdims=True)
        s2 = jnp.sum(crosses, axis=1, keepdims=True)
        stat[rows, :] = jnp.where(lane == 0, s1, jnp.where(lane == 1, s2, 0.0))
        return carry

    lax.fori_loop(0, gate.shape[0] // step, body, 0)


def gate_squares(gate, ssd, x_low, crow, stat):
    step, inner = 64, gate.shape[1]

    def body(i, carry):
        rows = pl.ds(pl.multiple_of(i * step, step), step)
        squares = jnp.zeros((step, 256), f32)
        for c in range(0, inner, 256):
            cols = slice(c, c + 256)
            g = gate[rows, cols]
            mixed = ssd[rows, cols].astype(f32) + crow[1:2, cols] * x_low[rows, cols].astype(f32)
            value = mixed * (g * logistic(g))
            squares = squares + value * value
        stat[rows, :] = jnp.broadcast_to(jnp.sum(squares, axis=1, keepdims=True), (step, LANES))
        return carry

    lax.fori_loop(0, gate.shape[0] // step, body, 0)


def gate_norm(gate, ssd, x_low, inverse_out, crow, gn):
    step, inner = 64, gate.shape[1]

    def body(i, carry):
        rows = pl.ds(pl.multiple_of(i * step, step), step)
        inverse = inverse_out[rows, :1]
        for c in range(0, inner, 256):
            cols = slice(c, c + 256)
            g = gate[rows, cols]
            mixed = ssd[rows, cols].astype(f32) + crow[1:2, cols] * x_low[rows, cols].astype(f32)
            gn[rows, cols] = (mixed * (g * logistic(g)) * inverse * crow[0:1, cols]).astype(bf16)
        return carry

    lax.fori_loop(0, gate.shape[0] // step, body, 0)


def cross_sums(gnorm, gn, stat):
    step, inner = 64, gn.shape[1]

    def body(i, carry):
        rows = pl.ds(pl.multiple_of(i * step, step), step)
        total = jnp.zeros((step, 256), f32)
        for c in range(0, inner, 256):
            cols = slice(c, c + 256)
            total = total + gnorm[rows, cols] * gn[rows, cols].astype(f32)
        stat[rows, :] = jnp.broadcast_to(jnp.sum(total, axis=1, keepdims=True), (step, LANES))
        return carry

    lax.fori_loop(0, gn.shape[0] // step, body, 0)


def forward_kernel(
    starts, tok, gain, wxd, wz, taps, dpar,
    normed, inverse, xin, slope, gate, x_low, bc_low, step, sgdt, step_low, decay_low, ssd, states,
    pos, spread, dtin, state, xs, yin, cbm,
):
    fill_spread(spread)
    fill_positions(starts, pos, None)
    normalize(tok, gain, normed, inverse)
    project_x(normed, wxd, xin, dtin)
    convolve(xin, taps, pos, slope, x_low, bc_low)
    steps(dtin, dpar, step, sgdt, step_low, decay_low)
    scan_forward(starts, x_low, bc_low, step_low, decay_low, ssd, states, spread, state, xs, yin, cbm)
    project_rows(normed, wz, gate)


def gate_kernel(cot, wout, gate, ssd, x_low, crow, gnorm, stat):
    back_rows(cot, wout, gnorm)
    gate_sums(gate, ssd, x_low, gnorm, crow, stat)


def gate_backward(gate, ssd, x_low, gnorm, crow, stat, width, gn, low_gate, gs, sums, known=None):
    step, inner = 64, ssd.shape[1]
    sums[...] = jnp.zeros_like(sums)

    def body(i, carry):
        rows = pl.ds(pl.multiple_of(i * step, step), step)
        if known is None:
            inverse = lax.rsqrt(stat[rows, 0:1] / width + EPS)
            mean = inverse * stat[rows, 1:2] / width
        else:
            inverse, mean = known[rows, :1], stat[rows, :1]
        for c in range(0, inner, 256):
            cols = slice(c, c + 256)
            g = gate[rows, cols]
            x = x_low[rows, cols].astype(f32)
            mixed = ssd[rows, cols].astype(f32) + crow[1:2, cols] * x
            sg = logistic(g)
            act = g * sg
            hat = mixed * act * inverse
            if gn is not None:
                gn[rows, cols] = (hat * crow[0:1, cols]).astype(bf16)
            gnorm_here = gnorm[rows, cols]
            grad = inverse * (gnorm_here * crow[0:1, cols] - hat * mean)
            grad_mixed = grad * act
            low_gate[rows, cols] = (grad * mixed * (sg * (1.0 + g * (1.0 - sg)))).astype(bf16)
            gs[rows, cols] = grad_mixed.astype(bf16)
            sums[0:8, cols] += fold(gnorm_here * hat)
            sums[8:16, cols] += fold(grad_mixed * x)
        return carry

    lax.fori_loop(0, ssd.shape[0] // step, body, 0)


def middle_kernel(
    cot, wout, normed, gate, x_low, ssd, gnorm, crow, stat,
    branch, dwout, dwz, low_gate, gs, sums,
    gn, *, width,
):
    gate_backward(gate, ssd, x_low, gnorm, crow, stat, width, gn, low_gate, gs, sums)
    project_rows(gn, wout, branch)
    weight_rows(gn, cot, dwout)
    weight_rows(normed, low_gate, dwz)


def scan_backward(
    starts, x_low, bc_low, step_low, decay_low, ssd, states, gs, slope, crow, step, sgdt, dpar,
    gpre, low_xd, dsums, spread, dstate, xs, gx, cbm, acc, tick=None,
):
    length, inner = x_low.shape
    width = gpre.shape[1]
    blocks = length // BLOCK
    dstate[...] = jnp.zeros_like(dstate)
    dsums[...] = jnp.zeros_like(dsums)
    gpre[pl.ds(length, 8), :] = jnp.zeros((8, width), f32)

    def body(i, carry):
        b = blocks - 1 - i
        rows = pl.ds(pl.multiple_of(b * BLOCK, BLOCK), BLOCK)
        cum, step_e, kept_e, in_e, out_e, column, row = block_decays(
            b, starts, decay_low, step_low, spread
        )
        bm, cm = bc_low[rows, :STATE], bc_low[rows, STATE:]
        i0 = lax.broadcasted_iota(jnp.int32, (BLOCK, BLOCK), 0)
        i1 = lax.broadcasted_iota(jnp.int32, (BLOCK, BLOCK), 1)
        linked = (column == row) & (i0 <= i1)
        cbm[...] = jnp.where(linked, mm_nt(bm, cm), 0.0)
        x = x_low[rows, :].astype(f32)
        stepped = x * step_e
        xs[...] = stepped.astype(bf16)
        cum_t = cum.T
        first = lax.broadcasted_iota(jnp.int32, (BLOCK, LANES), 1) < HEADDIM
        acc[...] = jnp.zeros_like(acc)
        for j in range(inner // LANES):
            cols = slice(j * LANES, (j + 1) * LANES)
            xpair, gpair = xs[:, cols], gs[rows, cols]
            none = jnp.zeros_like(xpair)
            part, total = [], None
            for k in range(2):
                h = 2 * j + k
                kernel = jnp.exp(jnp.minimum(cum_t[h : h + 1, :] - cum[:, h : h + 1], 0.0))
                part.append(mm((kernel * cbm[...]).astype(bf16), gpair))
                own = jnp.where(first, xpair, none) if k == 0 else jnp.where(first, none, xpair)
                here = kernel * mm_nt(own, gpair)
                total = here if total is None else total + here
            acc[...] += total
            gx[:, cols] = jnp.where(first, part[0], part[1])
        dstate_low = dstate[...].astype(bf16)
        entering = states[b]
        leaving = states[jnp.minimum(b + 1, blocks - 1)]
        end = jnp.sum(dstate[...] * leaving.astype(f32), axis=0, keepdims=True)
        g = gs[rows, :].astype(f32)
        g_in = (in_e * g).astype(bf16)
        raw = gx[...] + out_e * mm(bm, dstate_low)
        grad_x = (step_e * raw).astype(bf16).astype(f32)
        gpre[rows, :inner] = (grad_x + crow[1:2, :] * g) * slope[rows, :inner]
        pairs = jnp.where(linked, acc[...], 0.0).astype(bf16)
        db = mm(pairs, cm) + mm_nt((stepped * out_e).astype(bf16), dstate_low)
        dc = mm_tn(pairs, bm) + mm_nt(g_in, entering)
        gpre[rows, inner : inner + STATE] = db * slope[rows, inner : inner + STATE]
        gpre[rows, inner + STATE :] = dc * slope[rows, inner + STATE :]
        raw_x = x * raw
        grad_step = gather_heads(raw_x, spread[...]).astype(bf16).astype(f32)
        dcum = gather_heads(g * ssd[rows, :].astype(f32) - step_e * raw_x, spread[...])
        tail = gather_heads(jnp.broadcast_to(end, (8, inner)), spread[...])[0:1]
        upper = jnp.where(i0 <= i1, 1.0, 0.0).astype(bf16)
        high, rest = halves(dcum)
        later = mm(upper, high) + mm(upper, rest) + tail
        grad_decay = later.astype(bf16).astype(f32)
        total_step = grad_step - dpar[1:2, :] * grad_decay
        if sgdt is None:
            before_step = step[rows, :] + dpar[0:1, :]
            slope_here, step_here = logistic(before_step), softplus(before_step)
        else:
            slope_here, step_here = sgdt[rows, :], step[rows, :]
        grad_dt = total_step * slope_here
        low_xd[rows, width:] = grad_dt.astype(bf16)
        dsums[0:8, :] += fold(grad_dt)
        dsums[8:16, :] -= fold(grad_decay * step_here)
        dstate[...] = kept_e * dstate[...] + mm_tn(cm, g_in)
        if tick is not None:
            tick(i)
        return carry

    lax.fori_loop(0, blocks, body, 0)


def convolve_back(xin, gpre, taps, pos, rpos, low_xd, csums, tick=None):
    width = gpre.shape[1]
    columns = width // LANES
    csums[...] = jnp.zeros_like(csums)

    def body(b, j):
        at = pl.multiple_of(b * BLOCK, BLOCK)
        cols = pl.ds(pl.multiple_of(j * LANES, LANES), LANES)
        rows = pl.ds(at, BLOCK)
        x = xin[pl.ds(at, BLOCK + 8), cols]
        g = gpre[pl.ds(at, BLOCK + 8), cols]
        here = g[:BLOCK]
        place, ahead = pos[rows, :], rpos[rows, :]
        tap = taps[:, cols]
        grad = tap[CONV - 1 : CONV] * here
        csums[pl.ds(8 * CONV, 8), cols] += fold(here)
        csums[pl.ds(8 * (CONV - 1), 8), cols] += fold(here * x[8:])
        for lag in range(1, CONV):
            k = CONV - 1 - lag
            later = pltpu.roll(g, BLOCK + 8 - lag, 0)[:BLOCK]
            earlier = pltpu.roll(x, lag, 0)[8:]
            grad = grad + tap[k : k + 1] * jnp.where(ahead >= lag, later, 0.0)
            csums[pl.ds(8 * k, 8), cols] += fold(here * jnp.where(place >= lag, earlier, 0.0))
        low_xd[rows, cols] = grad.astype(bf16)

    def block(b, carry):
        lax.fori_loop(0, columns, lambda j, c: (body(b, j), c)[1], 0)
        if tick is not None:
            tick(b)
        return carry

    lax.fori_loop(0, (xin.shape[0] - 8) // BLOCK, block, 0)


def backward_kernel(
    starts, xin, slope, x_low, bc_low, step, sgdt, step_low, decay_low, ssd, states, gs, taps, crow, dpar,
    low_xd, csums, dsums,
    pos, rpos, spread, gpre, dstate, xs, gx, cbm, acc,
):
    fill_spread(spread)
    fill_positions(starts, pos, rpos)
    scan_backward(
        starts, x_low, bc_low, step_low, decay_low, ssd, states, gs, slope, crow, step, sgdt, dpar,
        gpre, low_xd, dsums, spread, dstate, xs, gx, cbm, acc,
    )
    convolve_back(xin, gpre, taps, pos, rpos, low_xd, csums)


def last_kernel(tok, inverse, gain, normed, low_gate, low_xd, wz, wxd, dwxd, gfull, rowdot):
    weight_rows(normed, low_xd, dwxd)
    rows = 256

    def body(i, carry):
        at = pl.ds(pl.multiple_of(i * rows, rows), rows)
        total = jnp.zeros((rows, 1), f32)
        for c, w in tiles(gfull.shape[1], 512):
            cols = slice(c, c + w)
            part = mm_nt(low_gate[at, :], wz[cols, :]) + mm_nt(low_xd[at, :], wxd[cols, :])
            gfull[at, cols] = part.astype(bf16)
            total = total + jnp.sum(part * gain[:, cols] * tok[at, cols].astype(f32), axis=1, keepdims=True)
        rowdot[at, :] = total * inverse[at, :]
        return carry

    lax.fori_loop(0, gfull.shape[0] // rows, body, 0)


MESH = pl.DeviceIdType.MESH


def remote(source, target, send, receive, **where):
    return pltpu.make_async_remote_copy(
        src_ref=source, dst_ref=target, send_sem=send, recv_sem=receive, device_id=where, device_id_type=MESH
    )


def add_into(target, source, rows=64):
    def body(i, carry):
        at = pl.ds(pl.multiple_of(i * rows, rows), rows)
        target[at, :] = (target[at, :].astype(f32) + source[at, :].astype(f32)).astype(target.dtype)
        return carry

    lax.fori_loop(0, target.shape[0] // rows, body, 0)


class Ring:
    def __init__(self):
        self.me = lax.axis_index("dp")
        self.core = self.me % 2
        chip = self.me // 2
        y = chip // 2
        self.pos = 2 * y + (chip + y) % 2
        self.partner = self.me + 1 - 2 * self.core
        self.right = self.at(self.pos + 1)
        self.left = self.at(self.pos + 3)
        self.across = self.at(self.pos + 2)

    def at(self, pos):
        pos = pos % 4
        y = pos // 2
        return (2 * y + (pos + y) % 2) * 2 + self.core


def greet(ring, everyone):
    barrier = pltpu.get_barrier_semaphore()
    n, z = lax.axis_size("mp"), lax.axis_index("mp")
    if everyone:
        size = lax.axis_size("dp")
        close = [(ring.me + i) % size for i in range(1, size)]
    else:
        close = [ring.partner, ring.right, ring.left]
    for other in close:
        pl.semaphore_signal(barrier, inc=1, device_id={"dp": other}, device_id_type=MESH)
    for i in range(1, n):
        pl.semaphore_signal(barrier, inc=1, device_id={"mp": (z + i) % n}, device_id_type=MESH)
    pl.semaphore_wait(barrier, len(close) + n - 1)


class Scatter:
    def __init__(self, ring, shard, cores, parts, wholes, sems):
        self.ring, self.shard = ring, shard
        self.cores, self.parts, self.wholes = cores, parts, wholes
        self.core_send, self.core_recv, self.ring_send, self.ring_recv = sems
        self.half = cores.shape[1] // 2

    def upper(self, r):
        return self.shard(r).at[pl.ds(0, self.half), :]

    def lower(self, r):
        return self.shard(r).at[pl.ds(self.half, self.half), :]

    def core_copy(self, chip):
        ring = self.ring
        return remote(
            self.shard(2 * chip + 1 - ring.core), self.cores.at[chip],
            self.core_send.at[chip], self.core_recv.at[chip], dp=ring.partner,
        )

    def ring_copy(self, k):
        ring = self.ring
        source = (self.upper(ring.across), self.lower(ring.across), self.shard(ring.right), self.shard(ring.left))[k]
        target = (self.parts.at[0], self.parts.at[1], self.wholes.at[0], self.wholes.at[1])[k]
        return remote(
            source, target, self.ring_send.at[k], self.ring_recv.at[k], dp=(ring.right, ring.left)[k % 2]
        )

    def start(self, chip):
        self.core_copy(chip).start()

    def first(self):
        def body(chip, carry):
            self.core_copy(chip).wait_recv()
            add_into(self.shard(2 * chip + self.ring.core), self.cores.at[chip])
            return carry

        lax.fori_loop(0, 4, body, 0)
        self.ring_copy(0).start()
        self.ring_copy(1).start()

    def second(self):
        self.ring_copy(0).wait_recv()
        add_into(self.upper(self.ring.right), self.parts.at[0])
        self.ring_copy(2).start()
        self.ring_copy(1).wait_recv()
        add_into(self.lower(self.ring.left), self.parts.at[1])
        self.ring_copy(3).start()

    def finish(self, out, rows=64):
        self.ring_copy(2).wait_recv()
        self.ring_copy(3).wait_recv()
        own = self.shard(self.ring.me)

        def body(i, carry):
            at = pl.ds(pl.multiple_of(i * rows, rows), rows)
            out[at, :] = own[at, :].astype(f32) + self.wholes[0, at, :].astype(f32) + self.wholes[1, at, :].astype(f32)
            return carry

        lax.fori_loop(0, out.shape[0] // rows, body, 0)

        def done(chip, carry):
            self.core_copy(chip).wait_send()
            return carry

        lax.fori_loop(0, 4, done, 0)
        for k in range(4):
            self.ring_copy(k).wait_send()


class Line:
    def __init__(self, piece, slot, blocks, sems, total):
        self.piece, self.slot, self.blocks, self.total = piece, slot, blocks, total
        self.send, self.recv = sems
        self.n, self.z = lax.axis_size("mp"), lax.axis_index("mp")
        self.place = (self.z, self.n - 1 - self.z)

    def rows(self, t):
        return pl.ds(pl.multiple_of(t * BLOCK, BLOCK), BLOCK)

    def source(self, side, k):
        d = k // self.blocks
        return self.piece(k - d * self.blocks, self.n - 1 - d if side == 0 else d)

    def copy(self, side, place, k):
        return remote(
            self.source(side, k), self.slot(side, place + 1, k), self.send.at[side, k], self.recv.at[side, k],
            mp=self.z + 1 if side == 0 else self.z - 1,
        )

    def arrived(self, side, place, k):
        target = self.slot(side, place, k)
        remote(target, target, self.send.at[side, k], self.recv.at[side, k], mp=self.z).wait_recv()
        return target

    def inject(self, k):
        for side in range(2):
            @pl.when(self.place[side] == 0)
            def _():
                @pl.when(jnp.int32(k) >= 2)
                def _():
                    self.copy(side, 0, jnp.maximum(k - 2, 0)).wait_send()

                self.copy(side, 0, k).start()

    def forward(self, k, hop):
        for side in range(2):
            @pl.when(self.place[side] == hop)
            def _():
                add_into(self.source(side, k), self.arrived(side, hop, k))
                self.copy(side, hop, k).start()

    def finish(self, t):
        self.total[...] = self.piece(t, self.z)[...].astype(f32)
        for side in range(2):
            for place in range(1, self.n):
                @pl.when(self.place[side] == place)
                def _():
                    self.total[...] += self.arrived(side, place, (self.n - 1 - place) * self.blocks + t)[...].astype(f32)

    def drain(self):
        for side in range(2):
            for place in range(self.n - 1):
                count = (self.n - 1 - place) * self.blocks

                @pl.when(self.place[side] == place)
                def _():
                    def body(k, carry):
                        self.copy(side, place, k).wait_send()
                        return carry

                    lax.fori_loop(count - 2 if place == 0 else 0, count, body, 0)

    def order(self, i):
        z = self.z
        far = jnp.where(z < 2, 3 - i, i)
        near = z + 1 - 2 * (z % 2)
        return jnp.where(i < 2, far, jnp.where(i == 2, near, z))


class Loads:
    def __init__(self, sems):
        self.sems, self.pairs = sems, []

    def start(self, source, target):
        i = len(self.pairs)
        copy = pltpu.make_async_copy(source, target, self.sems.at[i])
        copy.start()
        self.pairs.append(copy)
        return copy


class Gather:
    def __init__(self, ring, shard, rows, sems):
        self.ring, self.shard, self.half = ring, shard, rows // 2
        self.ring_send, self.ring_recv, self.core_send, self.core_recv = sems
        self.other = 1 - 2 * ring.core

    def ring_copy(self, k, source):
        ring = self.ring
        piece = self.shard(source)
        if k >= 2:
            piece = piece.at[pl.ds((k - 2) * self.half, self.half), :]
        return remote(
            piece, piece, self.ring_send.at[k], self.ring_recv.at[k], dp=(ring.right, ring.left)[k % 2]
        )

    def core_copy(self, k, source):
        return remote(
            self.shard(source), self.shard(source), self.core_send.at[k], self.core_recv.at[k], dp=self.ring.partner
        )

    def start(self):
        me = self.ring.me
        self.ring_copy(0, me).start()
        self.ring_copy(1, me).start()
        self.core_copy(0, me).start()

    def second(self):
        left, right = self.ring.left, self.ring.right
        self.ring_copy(0, left).wait_recv()
        self.ring_copy(2, left).start()
        self.core_copy(1, left).start()
        self.ring_copy(1, right).wait_recv()
        self.ring_copy(3, right).start()
        self.core_copy(2, right).start()

    def third(self):
        across = self.ring.across
        self.ring_copy(2, across).wait_recv()
        self.ring_copy(3, across).wait_recv()
        self.core_copy(3, across).start()

    def arrived(self, k):
        ring = self.ring
        source = (ring.me, ring.left, ring.right, ring.across)[k] + self.other
        self.core_copy(k, source).wait_recv()

    def drain(self):
        ring = self.ring
        for k, source in enumerate((ring.me, ring.me, ring.left, ring.right)):
            self.ring_copy(k, source).wait_send()
        for k, source in enumerate((ring.me, ring.left, ring.right, ring.across)):
            self.core_copy(k, source).wait_send()


def cast_into(target, source, rows=64):
    def body(i, carry):
        at = pl.ds(pl.multiple_of(i * rows, rows), rows)
        target[at, :] = source[at, :].astype(target.dtype)
        return carry

    lax.fori_loop(0, target.shape[0] // rows, body, 0)


def trunk_kernel(
    lengths, tok, cot, w_x, w_z, w_out, w_bc, w_dt, conv_x, conv_x_bias, conv_bc, conv_bc_bias, dt_bias, a_rate,
    d_skip, gain, out_gain,
    normed_o, xin_o, wxd_o, wz_o, low_gate_o, low_xd_o, out_o, dwout_o, inverse_o,
    csums, dsums, sums,
    v_tok, stage_b, normed, xin, first_wide, slope, x_low, ssd, states, wxd, wz, wout,
    bc_low, step_low, decay_low, inverse_out, taps, crow, dpar,
    bc_slots, tap_slots, row_slots, cross_slots, stat, turned,
    pos, rpos, spread, dtin, state, xs, wide, cbm, acc, near, cores, parts, wholes,
    load_sems, store_sems, ring_send, ring_recv, core_send, core_recv, mp_send, mp_recv, line_send, line_recv,
    scatter_core_send, scatter_core_recv, scatter_ring_send, scatter_ring_recv,
):
    ring = Ring()
    n, z = lax.axis_size("mp"), lax.axis_index("mp")
    length, features = normed.shape
    stage_a = wide
    inverse = inverse_out
    inner, width = x_low.shape[1], xin.shape[1]
    own = features // n
    shard, column_shard = stage_a.shape[0], stage_b.shape[1]
    heads, per = w_dt.shape[0], w_bc.shape[0]
    loads, stores = Loads(load_sems), Loads(store_sems)
    load_x = loads.start(w_x, stage_a)
    load_tok = loads.start(tok, v_tok)
    load_out = loads.start(w_out, stage_b)
    starts = [jnp.int32(0)]
    for k in range(DOCS - 1):
        starts.append(starts[-1] + lengths[0, k])

    turned[...] = jnp.zeros_like(turned)
    turned[:per, :] = w_bc[...]
    bc_slots[0] = turned[...].T.astype(bf16)
    tap_slots[0] = jnp.zeros_like(tap_slots[0])
    tap_slots[0, :CONV, :per] = conv_bc[...]
    tap_slots[0, CONV : CONV + 1, :per] = conv_bc_bias[...]
    turned[...] = jnp.zeros_like(turned)
    turned[:heads, :] = w_dt[...]
    own_rows = pl.ds(pl.multiple_of(ring.me * shard, shard), shard)
    wxd[own_rows, width:] = turned[...].T.astype(bf16)
    dpar[...] = jnp.zeros_like(dpar)
    dpar[0:1, :heads] = dt_bias[...]
    dpar[1:2, :heads] = a_rate[...]
    dpar[2:3, :heads] = d_skip[...]

    greet(ring, False)

    def exchange(k, i):
        slots = (bc_slots, tap_slots, row_slots, cross_slots)[k]
        at = k * (n - 1) + i - 1
        return remote(slots.at[0], slots.at[i], mp_send.at[at], mp_recv.at[at], mp=(z + i) % n)

    def rows_of(ref, low, high):
        def shard_of(r):
            return ref.at[pl.ds(pl.multiple_of(r * shard, shard), shard), pl.ds(low, high - low)]

        return shard_of

    def columns_of(r):
        return wout.at[:, pl.ds(pl.multiple_of(r * column_shard, column_shard), column_shard)]

    sems = [tuple(group.at[k] for group in (ring_send, ring_recv, core_send, core_recv)) for k in range(4)]
    get_x = Gather(ring, rows_of(wxd, 0, inner), shard, sems[0])
    get_bd = Gather(ring, rows_of(wxd, inner, wxd.shape[1]), shard, sems[1])
    get_z = Gather(ring, rows_of(wz, 0, inner), shard, sems[2])
    get_out = Gather(ring, columns_of, inner, sems[3])

    load_x.wait()
    cast_into(get_x.shard(ring.me), stage_a)
    get_x.start()
    for k in range(2):
        for i in range(1, n):
            exchange(k, i).start()
    load_z = loads.start(w_z, stage_a)
    fill_spread(spread)
    fill_positions(starts, pos, rpos)
    crow[0:1, :] = out_gain[...]
    crow[1:2, :] = expand(dpar[...], spread[...])[2:3]
    load_tok.wait()
    normalize(v_tok, gain, normed, inverse)
    load_cot = loads.start(cot, v_tok)
    store_normed = stores.start(normed, normed_o)
    store_inverse = stores.start(inverse, inverse_o)
    for k in range(2):
        for i in range(1, n):
            exchange(k, i).wait()
    first = lax.broadcasted_iota(jnp.int32, (shard, LANES), 1) < per
    for j in range((width - inner) // LANES):
        low, high = (z - 2 * j + n) % n, (z - 2 * j - 1 + n) % n
        columns = slice(inner + j * LANES, inner + (j + 1) * LANES)
        pair = jnp.where(first, bc_slots[low].astype(f32), pltpu.roll(bc_slots[high].astype(f32), per, 1))
        wxd[own_rows, columns] = pair.astype(bf16)
        taps[:, columns] = jnp.where(first[:8], tap_slots[low], pltpu.roll(tap_slots[high], per, 1))
    get_bd.start()
    taps[:, :inner] = jnp.zeros((8, inner), f32)
    taps[:CONV, :inner] = conv_x[...]
    taps[CONV : CONV + 1, :inner] = conv_x_bias[...]
    load_z.wait()
    cast_into(get_z.shard(ring.me), stage_a)
    load_out.wait()
    cast_into(get_out.shard(ring.me), stage_b)
    xin[pl.ds(0, 8), :] = jnp.zeros((8, width), f32)

    def project_chip(k, source):
        get_x.arrived(k)
        get_bd.arrived(k)
        part = pl.ds(pl.multiple_of((source // 2) * 2 * shard, 2 * shard), 2 * shard)

        def body(i, carry):
            at = pl.multiple_of(i * 512, 512)
            left = normed[pl.ds(at, 512), part]
            for c, w in tiles(wxd.shape[1], 512):
                here = mm(left, wxd[part, c : c + w])
                w_x_part = min(w, width - c)
                if k == 0:
                    xin[pl.ds(at + 8, 512), c : c + w_x_part] = here[:, :w_x_part]
                else:
                    xin[pl.ds(at + 8, 512), c : c + w_x_part] += here[:, :w_x_part]
                if w_x_part < w:
                    if k == 0:
                        dtin[pl.ds(at, 512), :] = here[:, w_x_part:]
                    else:
                        dtin[pl.ds(at, 512), :] += here[:, w_x_part:]
            return carry

        lax.fori_loop(0, length // 512, body, 0)

    project_chip(0, ring.me)
    get_x.second()
    get_bd.second()
    get_z.start()
    project_chip(1, ring.left)
    project_chip(2, ring.right)
    get_x.third()
    get_bd.third()
    project_chip(3, ring.across)
    store_xin = stores.start(xin, xin_o)
    store_wxd = stores.start(wxd, wxd_o)
    steps(dtin, dpar, None, None, step_low, decay_low)
    convolve(xin, taps, pos, slope, x_low, bc_low)
    get_z.second()
    get_out.start()

    def forward_tick(b):
        @pl.when(b == 1)
        def _():
            get_z.third()

    scan_forward(
        starts, x_low, bc_low, step_low, decay_low, ssd, states, spread, state, xs, wide, cbm, forward_tick
    )
    for k in range(4):
        get_z.arrived(k)
    gate = first_wide.at[pl.ds(0, length), pl.ds(0, inner)]
    gnorm = xin.at[pl.ds(0, length), pl.ds(0, inner)]
    project_rows(normed, wz, gate)
    store_wz = stores.start(wz, wz_o)
    gate_squares(gate, ssd, x_low, crow, stat)

    def put_rows(slots):
        for b in range(length // BLOCK):
            columns = slice(b * BLOCK, (b + 1) * BLOCK)
            slots[0, :, columns] = stat[columns, :].T[:8]

    def sum_rows(slots, out, finish):
        for b in range(length // BLOCK):
            columns = slice(b * BLOCK, (b + 1) * BLOCK)
            total = functools.reduce(lambda p, q: p + q, [slots[i, 0:1, columns] for i in range(n)])
            turned[...] = jnp.broadcast_to(finish(total), turned.shape)
            out[columns, :] = turned[...].T

    put_rows(row_slots)
    get_x.drain()
    get_bd.drain()
    store_wxd.wait()
    for i in range(1, n):
        exchange(2, i).start()
    load_cot.wait()
    store_xin.wait()

    def back_chip(k, source):
        get_out.arrived(k)
        part = pl.ds(pl.multiple_of((source // 2) * 2 * column_shard, 2 * column_shard), 2 * column_shard)

        def body(i, carry):
            at = pl.ds(pl.multiple_of(i * 512, 512), 512)
            left = v_tok[at, part]
            for c, w in tiles(inner, 512):
                here = mm_nt(left, wout[c : c + w, part])
                if k == 0:
                    gnorm[at, c : c + w] = here
                else:
                    gnorm[at, c : c + w] += here
            return carry

        lax.fori_loop(0, length // 512, body, 0)

    back_chip(0, ring.me)
    get_out.second()
    for i in range(1, n):
        exchange(2, i).wait()
    store_inverse.wait()
    sum_rows(row_slots, inverse_out, lambda total: lax.rsqrt(total / (inner * n) + EPS))
    store_normed.wait()
    gn = normed.at[:, pl.ds(0, inner)]
    gs = normed.at[:, pl.ds(inner, inner)]
    gate_norm(gate, ssd, x_low, inverse_out, crow, gn)
    back_chip(1, ring.left)
    back_chip(2, ring.right)
    get_out.third()
    back_chip(3, ring.across)
    cross_sums(gnorm, gn, stat)
    put_rows(cross_slots)
    for i in range(1, n):
        exchange(3, i).start()
    get_z.drain()
    store_wz.wait()

    fold_columns = inner // own

    def piece(t, q):
        row = pl.multiple_of((q // fold_columns) * length + t * BLOCK, BLOCK)
        return wz.at[pl.ds(row, BLOCK), pl.ds(pl.multiple_of((q % fold_columns) * own, own), own)]

    def slot(side, place, k):
        if place == 2:
            return near.at[k]
        row = pl.multiple_of((k // fold_columns) * BLOCK, BLOCK)
        return wxd.at[pl.ds(row, BLOCK), pl.ds(pl.multiple_of((k % fold_columns) * own, own), own)]

    total = wide.at[:, pl.ds(0, own)]
    line = Line(piece, slot, length // BLOCK, (line_send, line_recv), total)

    def quarter(i, carry):
        q = line.order(i)
        columns = pl.ds(pl.multiple_of(q * own, own), own)
        for r in range(0, length, 512):
            at = pl.ds(pl.multiple_of((q // fold_columns) * length + r, 512), 512)
            cols = pl.ds(pl.multiple_of((q % fold_columns) * own, own), own)
            wz[at, cols] = mm(gn[r : r + 512, :], wout[:, columns]).astype(bf16)
            if r == 0:
                @pl.when(i == 0)
                def _():
                    line.inject(0)
                    line.inject(1)

        return carry

    lax.fori_loop(0, n, quarter, 0)
    line.inject(2)
    get_out.drain()
    grads = wout
    scatter = Scatter(
        ring, lambda r: grads.at[:, pl.ds(pl.multiple_of(r * column_shard, column_shard), column_shard)],
        cores, parts, wholes, (scatter_core_send, scatter_core_recv, scatter_ring_send, scatter_ring_recv),
    )
    chunk = 2 * column_shard

    def weight(j, carry):
        columns = pl.ds(pl.multiple_of(j * chunk, chunk), chunk)
        for r in range(0, inner, 256):
            grads[r : r + 256, columns] = mm_tn(gn[:, r : r + 256], v_tok[:, columns]).astype(bf16)
        scatter.start(j)
        return carry

    lax.fori_loop(0, 4, weight, 0)
    line.inject(3)
    line.forward(0, 1)
    xd = v_tok.at[:, pl.ds(0, wxd.shape[1])]
    token_own = v_tok.at[:, pl.ds(wxd.shape[1], own)]
    load_own = loads.start(tok.at[:, pl.ds(pl.multiple_of(z * own, own), own)], token_own)
    for i in range(1, n):
        exchange(3, i).wait()
    sum_rows(cross_slots, stat, lambda total: total / (inner * n))
    low_gate = gn
    gate_backward(gate, ssd, x_low, gnorm, crow, stat, inner * n, None, low_gate, gs, sums, known=inverse_out)
    load_xin = loads.start(xin_o, xin)
    stores.start(low_gate, low_gate_o)
    line.inject(4)
    line.forward(1, 1)
    line.forward(0, 2)
    scatter.first()

    def scan_tick(i):
        line.inject(i + 5)
        line.forward(i + 2, 1)

        @pl.when(i < 3)
        def _():
            line.forward(i + 1, 2)

        @pl.when(i == 1)
        def _():
            scatter.second()

    gpre = first_wide
    scan_backward(
        starts, x_low, bc_low, step_low, decay_low, ssd, states, gs, slope, crow, dtin, None, dpar,
        gpre, xd, dsums, spread, state, xs, wide, cbm, acc, scan_tick,
    )
    scatter.finish(stage_b)
    stores.start(stage_b, dwout_o)
    load_xin.wait()

    def conv_tick(b):
        @pl.when(b % 2 == 1)
        def _():
            line.inject(9 + b // 2)
            line.forward(6 + b // 2, 1)

    convolve_back(xin, gpre, taps, pos, rpos, xd, csums, conv_tick)
    line.inject(11)
    stores.start(xd, low_xd_o)
    load_own.wait()
    out = x_low.at[:, pl.ds(0, own)]

    def last(t, carry):
        line.finish(t)
        out[line.rows(t), :] = (token_own[line.rows(t), :].astype(f32) + total[...]).astype(bf16)
        return carry

    lax.fori_loop(0, line.blocks, last, 0)
    stores.start(out, out_o)
    line.drain()
    for copy in stores.pairs:
        if not any(copy is done for done in (store_normed, store_inverse, store_xin, store_wxd, store_wz)):
            copy.wait()


def input_kernel(
    tok, inverse, gain, normed, low_gate, low_xd, wz, wxd, cot, csums, sums, dsums,
    dwz_o, dwx_o, grad, dwbc, dwdt, conv_x, conv_x_bias, conv_bc, conv_bc_bias, dt_bias, a_rate, d_skip, in_gain, out_gain,
    dwz, dwxd, smalls, spread, bc_own, bc_slots,
    v_tok, v_normed, v_gate, v_xd, v_wz, v_wxd, v_cot,
    part, slots, total, z_grads, z_cores, z_parts, z_wholes, x_grads, x_cores, x_parts, x_wholes,
    rowacc, rows_own, rows_in, colacc, dp_in, bc_in, gain_in,
    load_sems, quarter_sems, line_send, line_recv, z_core_send, z_core_recv, z_ring_send, z_ring_recv,
    x_core_send, x_core_recv, x_ring_send, x_ring_recv,
    rows_send, rows_recv, dp_send, dp_recv, mp_send, mp_recv, bc_send, bc_recv,
):
    ring = Ring()
    loads = Loads(load_sems)
    n = lax.axis_size("mp")
    z = lax.axis_index("mp")
    size = lax.axis_size("dp")
    length, features = part.shape
    inner = v_gate.shape[1]
    width = smalls.shape[1]
    heads, per = dwdt.shape[0], dwbc.shape[0]
    own = features // n
    own_columns = pl.ds(pl.multiple_of(z * own, own), own)

    def quarter_columns(q):
        return pl.ds(pl.multiple_of(q * own, own), own)

    line = Line(
        lambda t, q: part.at[pl.ds(pl.multiple_of(t * BLOCK, BLOCK), BLOCK), quarter_columns(q)],
        lambda side, place, k: slots.at[side, k], length // BLOCK, (line_send, line_recv), total,
    )

    def quarter_loads(i):
        columns = quarter_columns(line.order(i))
        return [
            pltpu.make_async_copy(source, target, quarter_sems.at[i, k])
            for k, (source, target) in enumerate((
                (wz.at[columns, :], v_wz.at[columns, :]),
                (wxd.at[columns, :], v_wxd.at[columns, :]),
                (tok.at[:, columns], v_tok.at[:, columns]),
            ))
        ]

    first = [loads.start(source, target) for source, target in ((low_gate, v_gate), (low_xd, v_xd))]
    for copy in quarter_loads(0):
        copy.start()
    greet(ring, True)
    rowacc[...] = jnp.zeros_like(rowacc)
    for copy in first:
        copy.wait()
    for i in range(1, n):
        for copy in quarter_loads(i):
            copy.start()
    later = [
        loads.start(source, target)
        for source, target in ((normed, v_normed), (cot.at[:, own_columns], v_cot))
    ]

    def quarter(i, carry):
        columns = quarter_columns(line.order(i))
        for copy in quarter_loads(i):
            copy.wait()
        for r in range(0, length, 256):
            rows = slice(r, r + 256)
            here = mm_nt(v_gate[rows, :], v_wz[columns, :]) + mm_nt(v_xd[rows, :], v_wxd[columns, :])
            part[rows, columns] = here.astype(bf16)
            if r < 512:
                @pl.when(i == 0)
                def _():
                    line.inject(r // 256)

            along = here * (v_tok[rows, columns].astype(f32) * inverse[rows, :1])
            folded = fold(along)
            if r == 0:
                colacc[:, columns] = folded
            else:
                colacc[:, columns] += folded
            along = along * gain[:, columns]
            sum_lanes = along[:, :LANES]
            for c in range(LANES, own, LANES):
                sum_lanes = sum_lanes + along[:, c : c + LANES]
            rowacc[rows, :] += sum_lanes

        @pl.when(i == 1)
        def _():
            line.inject(2)

        return carry

    lax.fori_loop(0, n, quarter, 0)
    line.inject(3)
    line.forward(0, 1)

    for b in range(length // BLOCK):
        columns = slice(b * BLOCK, (b + 1) * BLOCK)
        line_sum = jnp.sum(rowacc[columns, :].T, axis=0, keepdims=True)
        rows_own[:, columns] = jnp.broadcast_to(line_sum, (8, BLOCK))

    def rows_copy(i):
        return remote(
            rows_own, rows_in.at[i - 1], rows_send.at[i - 1], rows_recv.at[i - 1], mp=(z + i) % n
        )

    def dp_copy(i):
        return remote(
            smalls, dp_in.at[i - 1], dp_send.at[i - 1], dp_recv.at[i - 1], dp=(ring.me + i) % size
        )

    def bc_copy(i):
        return remote(
            smalls.at[pl.ds(0, 8), pl.ds(inner, width - inner)], bc_in.at[i - 1],
            mp_send.at[i - 1], mp_recv.at[i - 1], mp=(z + i) % n,
        )

    def gain_copy(i):
        return remote(
            smalls.at[pl.ds(8, 8), pl.ds(0, inner)], gain_in.at[i - 1],
            mp_send.at[n + i - 2], mp_recv.at[n + i - 2], mp=(z + i) % n,
        )

    smalls[...] = jnp.zeros_like(smalls)
    for k in range(CONV + 1):
        smalls[k : k + 1, :] = jnp.sum(csums[8 * k : 8 * k + 8, :], axis=0, keepdims=True)
    for k in range(2):
        smalls[CONV + 1 + k : CONV + 2 + k, :inner] = jnp.sum(sums[8 * k : 8 * k + 8, :], axis=0, keepdims=True)
        smalls[7:8, k * LANES : (k + 1) * LANES] = jnp.sum(dsums[8 * k : 8 * k + 8, :], axis=0, keepdims=True)
    for k in range(features // inner):
        smalls[8 + k : 9 + k, :inner] = jnp.sum(colacc[:, k * inner : (k + 1) * inner], axis=0, keepdims=True)
    for i in range(1, n):
        rows_copy(i).start()
    for i in range(1, size):
        dp_copy(i).start()

    later[0].wait()
    shard = dwz.shape[0]
    z_scatter = Scatter(
        ring, lambda r: z_grads.at[pl.ds(pl.multiple_of(r * shard, shard), shard), :], z_cores, z_parts, z_wholes,
        (z_core_send, z_core_recv, z_ring_send, z_ring_recv),
    )
    x_scatter = Scatter(
        ring, lambda r: x_grads.at[pl.ds(pl.multiple_of(r * shard, shard), shard), :], x_cores, x_parts, x_wholes,
        (x_core_send, x_core_recv, x_ring_send, x_ring_recv),
    )

    def weight(j, right, grads):
        for c in range(0, 2 * shard, shard):
            rows = pl.ds(pl.multiple_of(j * 2 * shard + c, shard), shard)
            left = v_normed[:, rows]
            for at, w in tiles(grads.shape[1], 512):
                grads[rows, at : at + w] = mm_tn(left, right[:, at : at + w]).astype(bf16)

    def z_weight(j, carry):
        weight(j, v_gate, z_grads)
        z_scatter.start(j)
        return carry

    lax.fori_loop(0, 4, z_weight, 0)
    line.inject(4)
    line.forward(1, 1)
    line.forward(0, 2)

    def x_weight(j, carry):
        weight(j, v_xd, x_grads)
        x_scatter.start(j)

        @pl.when(j == 1)
        def _():
            z_scatter.first()

        @pl.when(j % 2 == 1)
        def _():
            line.inject(5 + j // 2)
            line.forward(2 + j // 2, 1)

        return carry

    lax.fori_loop(0, 4, x_weight, 0)
    line.forward(1, 2)
    x_scatter.first()
    z_scatter.second()
    line.inject(7)
    line.forward(4, 1)
    line.forward(2, 2)

    for i in range(1, size):
        dp_copy(i).wait()
    smalls[...] += functools.reduce(lambda a, b: a + b, [dp_in[i] for i in range(size - 1)])
    for i in range(1, n):
        bc_copy(i).start()
        gain_copy(i).start()
    x_scatter.second()
    line.inject(8)
    line.forward(5, 1)
    line.forward(3, 2)
    z_scatter.finish(dwz)
    store_z = loads.start(dwz, dwz_o)
    line.inject(9)
    line.forward(6, 1)
    line.inject(10)
    line.forward(7, 1)
    line.inject(11)
    x_scatter.finish(dwxd)
    share = LANES // per

    def mine(v):
        turns = [v] + [pltpu.roll(v, LANES - k * per, 1) for k in range(1, share)]
        which = jnp.full(v.shape, z % share, jnp.int32)
        return functools.reduce(lambda a, k: jnp.where(which == k, turns[k], a), range(1, share), turns[0])

    for j in range((width - inner) // LANES):
        bc_own[j] = dwxd[:, inner + j * LANES : inner + (j + 1) * LANES].astype(bf16)

    def weight_copy(i):
        other = (z + i) % n
        return remote(
            bc_own.at[other // share], bc_slots.at[i - 1], bc_send.at[i - 1], bc_recv.at[i - 1], mp=other
        )

    for i in range(1, n):
        weight_copy(i).start()
    for i in range(1, n):
        rows_copy(i).wait()
        bc_copy(i).wait()
        gain_copy(i).wait()
    rows_own[...] += functools.reduce(lambda a, b: a + b, [rows_in[i] for i in range(n - 1)])
    smalls[0:8, inner:] += functools.reduce(lambda a, b: a + b, [bc_in[i] for i in range(n - 1)])
    smalls[8:16, :inner] += functools.reduce(lambda a, b: a + b, [gain_in[i] for i in range(n - 1)])
    store_x = loads.start(dwxd.at[:, pl.ds(0, inner)], dwx_o)
    dwdt[...] = dwxd[:, width:].T[:heads]
    lanes = pl.ds(pl.multiple_of(inner + (z // share) * LANES, LANES), LANES)
    conv_x[...] = smalls[:CONV, :inner]
    conv_x_bias[...] = smalls[CONV : CONV + 1, :inner]
    taps = mine(smalls[:8, lanes])
    conv_bc[...] = taps[:CONV, :per]
    conv_bc_bias[...] = taps[CONV : CONV + 1, :per]
    out_gain[...] = smalls[5:6, :inner]
    fill_spread(spread)
    d_skip[...] = gather_heads(smalls[0:8, :inner], spread[...])[6:7, :heads]
    dt_bias[...] = smalls[7:8, :heads]
    a_rate[...] = smalls[7:8, LANES : LANES + heads]
    fits = inner // own
    in_gain[...] = smalls[pl.ds(8 + z // fits, 1), pl.ds(pl.multiple_of((z % fits) * own, own), own)]
    later[1].wait()

    def last(t, carry):
        line.finish(t)
        rows = line.rows(t)
        mean = jnp.broadcast_to(rows_own[0:1, rows] / features, (LANES, BLOCK)).T
        for c in range(0, own, LANES):
            columns = pl.ds(pl.multiple_of(z * own + c, LANES), LANES)
            hat = v_tok[rows, columns].astype(f32) * inverse[rows, :]
            change = inverse[rows, :] * (total[:, c : c + LANES] * gain[:, columns] - hat * mean)
            grad[rows, c : c + LANES] = (v_cot[rows, c : c + LANES].astype(f32) + change).astype(bf16)
        return carry

    lax.fori_loop(0, line.blocks, last, 0)
    for i in range(1, n):
        weight_copy(i).wait()
    here = functools.reduce(lambda a, b: a + b, [bc_slots[i].astype(f32) for i in range(n - 1)], dwxd[:, lanes])
    dwbc[...] = mine(here).T[:per]
    line.drain()
    store_z.wait()
    store_x.wait()


def hand_on_kernel(*refs):
    count = (len(refs) - 2) // 3
    sources, targets, buffers = refs[:count], refs[count : 2 * count], refs[2 * count : 3 * count]
    into, out = refs[-2:]
    there = [pltpu.make_async_copy(sources[k], buffers[k], into.at[k]) for k in range(count)]
    back = [pltpu.make_async_copy(buffers[k], targets[k], out.at[k]) for k in range(count)]
    for copy in there:
        copy.start()
    for k in range(count):
        there[k].wait()
        back[k].start()
    for copy in back:
        copy.wait()


def hand_on(*arrays):
    kinds = [(v.shape, v.dtype) for v in arrays]
    return call(
        hand_on_kernel, kinds, kinds, 0, *arrays,
        places="a" * len(arrays), sems=[(len(arrays),)] * 2, far=len(arrays),
    )


def call(kernel, outs, scratch, smem, *operands, places=None, sems=(), collective=None, far=0):
    spaces = {"s": pltpu.SMEM, "v": pltpu.VMEM, "a": pl.ANY}
    if places is None:
        places = "s" * smem + "v" * (len(operands) - smem)
    extra = {} if collective is None else dict(collective_id=collective, has_side_effects=True)
    return pl.pallas_call(
        kernel,
        out_shape=[jax.ShapeDtypeStruct(shape, kind) for shape, kind in outs],
        in_specs=[pl.BlockSpec(memory_space=spaces[c]) for c in places],
        out_specs=[pl.BlockSpec(memory_space=pl.ANY if i < far else pltpu.VMEM) for i in range(len(outs))],
        scratch_shapes=[pltpu.VMEM(shape, kind) for shape, kind in scratch]
        + [pltpu.SemaphoreType.DMA(shape) for shape in sems],
        compiler_params=pltpu.CompilerParams(vmem_limit_bytes=VMEM_LIMIT, **extra),
    )(*operands)


def per_device_any(
    tokens, cotangent, doc_lengths, w_z, w_x, w_bc, w_dt, w_out, conv_x, conv_x_bias, conv_bc,
    conv_bc_bias, dt_bias, a_rate, d_skip, input_norm_gain, out_gain,
):
    group = lax.axis_size("mp")
    rank = lax.axis_index("mp")
    T, D = tokens.shape
    inner, heads = w_x.shape[1], w_dt.shape[1]
    pair = 2 * STATE
    width = inner + pair
    wide = width + LANES
    own = D // group

    lengths = doc_lengths[0]
    starts = jnp.cumsum(lengths) - lengths
    packed = jnp.concatenate([w_bc, conv_bc, conv_bc_bias[None, :]], axis=0)
    packed = lax.all_gather(packed, "mp", axis=1, tiled=True)
    shard = w_bc.shape[0]
    w_bc_all, taps_bc = packed[:shard], packed[shard:]
    wxd = jnp.concatenate(
        [w_x.astype(bf16), w_bc_all.astype(bf16), w_dt.astype(bf16), jnp.zeros((shard, LANES - heads), bf16)],
        axis=1,
    )
    wxd = lax.all_gather(wxd, "dp", axis=0, tiled=True)
    wz = lax.all_gather(w_z.astype(bf16), "dp", axis=0, tiled=True)
    wout = lax.all_gather(w_out.astype(bf16), "dp", axis=1, tiled=True)
    taps = jnp.concatenate([jnp.concatenate([conv_x, conv_x_bias[None, :]], axis=0), taps_bc], axis=1)
    taps = jnp.pad(taps, ((0, 8 - CONV - 1), (0, 0)))
    crow = jnp.pad(jnp.stack([out_gain, jnp.repeat(d_skip, HEADDIM)]), ((0, 6), (0, 0)))
    dpar = jnp.pad(jnp.stack([dt_bias, a_rate]), ((0, 6), (0, LANES - heads)))
    gain = input_norm_gain[None, :]

    blocks = T // BLOCK
    (
        normed, inverse, xin, slope, gate, x_low, bc_low, step, sgdt, step_low, decay_low, ssd, states,
    ) = call(
        forward_kernel,
        [
            ((T, D), bf16), ((T, LANES), f32), ((T + 8, width), f32), ((T, width), bf16), ((T, inner), f32),
            ((T, inner), bf16), ((T, pair), bf16), ((T, LANES), f32), ((T, LANES), f32),
            ((T, LANES), bf16), ((T, LANES), bf16), ((T, inner), bf16), ((blocks, STATE, inner), bf16),
        ],
        [
            ((T, LANES), jnp.int32), ((LANES, inner), bf16), ((T, LANES), f32), ((STATE, inner), f32),
            ((BLOCK, inner), bf16), ((BLOCK, inner), f32), ((BLOCK, BLOCK), f32),
        ],
        1, starts, tokens, gain, wxd, wz, taps, dpar,
    )
    gnorm, stat = call(
        gate_kernel,
        [((T, inner), f32), ((T, LANES), f32)],
        [],
        0, cotangent, wout, gate, ssd, x_low, crow,
    )
    stat = jnp.pad(lax.psum(stat[:, :8], "mp"), ((0, 0), (0, LANES - 8)))
    branch, dwout, dwz, low_gate, gs, sums = call(
        functools.partial(middle_kernel, width=inner * group),
        [
            ((T, D), bf16), ((inner, D), bf16), ((D, inner), bf16), ((T, inner), bf16), ((T, inner), bf16),
            ((16, inner), f32),
        ],
        [((T, inner), bf16)],
        0, cotangent, wout, normed, gate, x_low, ssd, gnorm, crow, stat,
    )
    low_xd, csums, dsums = call(
        backward_kernel,
        [((T, wide), bf16), ((8 * CONV + 8, width), f32), ((16, LANES), f32)],
        [
            ((T, LANES), jnp.int32), ((T, LANES), jnp.int32), ((LANES, inner), bf16), ((T + 8, width), f32),
            ((STATE, inner), f32), ((BLOCK, inner), bf16), ((BLOCK, inner), f32), ((BLOCK, BLOCK), f32),
            ((BLOCK, BLOCK), f32),
        ],
        1, starts, xin, slope, x_low, bc_low, step, sgdt, step_low, decay_low, ssd, states, gs, taps, crow,
        dpar,
    )
    dwxd, gfull, rowdot = call(
        last_kernel,
        [((D, wide), bf16), ((T, D), bf16), ((T, LANES), f32)],
        [],
        0, tokens, inverse, gain, normed, low_gate, low_xd, wz, wxd,
    )

    def scatter(v, axis, dim):
        return lax.psum_scatter(v, axis, scatter_dimension=dim, tiled=True)

    token_own = lax.dynamic_slice_in_dim(tokens, rank * own, own, 1).astype(f32)
    output = (token_own + scatter(branch, "mp", 1).astype(f32)).astype(bf16)
    w_out_grad = scatter(dwout, "dp", 1).astype(f32)
    w_z_grad = scatter(dwz, "dp", 0).astype(f32)
    dwxd_own = scatter(dwxd, "dp", 0)
    w_x_grad = dwxd_own[:, :inner].astype(f32)
    w_dt_grad = dwxd_own[:, width : width + heads].astype(f32)
    w_bc_grad = scatter(dwxd_own[:, inner:width], "mp", 1).astype(f32)

    g_own = scatter(gfull, "mp", 1).astype(f32)
    gain_own = lax.dynamic_slice_in_dim(input_norm_gain, rank * own, own, 0)
    row_mean = (lax.psum(rowdot[:, 0], "mp") / D)[:, None]
    inv = inverse[:, :1]
    hat = token_own * inv
    cot_own = lax.dynamic_slice_in_dim(cotangent, rank * own, own, 1).astype(f32)
    input_grad = (cot_own + inv * (g_own * gain_own - hat * row_mean)).astype(bf16)
    in_gain = jnp.sum(g_own * hat, axis=0)

    csums = jnp.sum(csums.reshape(CONV + 1, 8, width), axis=1)
    sums = jnp.sum(sums.reshape(2, 8, inner), axis=1)
    dsums = jnp.sum(dsums.reshape(2, 8, LANES), axis=1)[:, :heads]
    csums_bc = scatter(csums[:, inner:], "mp", 1)
    conv_grad, conv_bc_grad, sums, dsums, in_gain = lax.psum(
        (csums[:, :inner], csums_bc, sums, dsums, in_gain), "dp"
    )
    d_skip_grad = jnp.sum(sums[1].reshape(heads, HEADDIM), axis=1)
    return (
        output, input_grad, w_z_grad, w_x_grad, w_bc_grad, w_dt_grad, w_out_grad,
        conv_grad[:CONV], conv_grad[CONV], conv_bc_grad[:CONV], conv_bc_grad[CONV],
        dsums[0], dsums[1], d_skip_grad, in_gain, sums[0],
    )


def per_device(
    tokens, cotangent, doc_lengths, w_z, w_x, w_bc, w_dt, w_out, conv_x, conv_x_bias, conv_bc,
    conv_bc_bias, dt_bias, a_rate, d_skip, input_norm_gain, out_gain,
):
    group, size = lax.axis_size("mp"), lax.axis_size("dp")
    T, D = tokens.shape
    shard, inner = w_x.shape
    heads, per = w_dt.shape[1], w_bc.shape[1]
    pair = per * group
    width = inner + pair
    wide = width + LANES
    own = D // group
    columns = w_out.shape[1]
    blocks = T // BLOCK
    messages = blocks * (group - 1)

    def row(v):
        return v[None, :]

    (
        normed, _, wxd, wz, low_gate, low_xd, output, w_out_grad, inverse, csums, dsums, sums,
    ) = call(
        trunk_kernel,
        [
            ((T, D), bf16), ((T + 8, width), f32), ((D, wide), bf16), ((D, inner), bf16), ((T, inner), bf16),
            ((T, wide), bf16), ((T, own), bf16), ((inner, columns), f32), ((T, LANES), f32),
            ((8 * CONV + 8, width), f32), ((16, LANES), f32), ((16, inner), f32),
        ],
        [
            ((T, D), bf16), ((inner, columns), f32), ((T, D), bf16), ((T + 8, width), f32),
            ((T + 8, width), f32), ((T, width), bf16), ((T, inner), bf16), ((T, inner), bf16),
            ((blocks, STATE, inner), bf16), ((D, wide), bf16), ((D, inner), bf16), ((inner, D), bf16),
            ((T, pair), bf16), ((T, LANES), bf16), ((T, LANES), bf16), ((T, LANES), f32),
            ((8, width), f32), ((8, inner), f32), ((8, LANES), f32),
            ((group, shard, LANES), bf16), ((group, 8, LANES), f32), ((group, 8, T), f32), ((group, 8, T), f32),
            ((T, LANES), f32), ((LANES, BLOCK), f32),
            ((T, LANES), jnp.int32), ((T, LANES), jnp.int32), ((LANES, inner), bf16), ((T, LANES), f32),
            ((STATE, inner), f32), ((BLOCK, inner), bf16), ((BLOCK, inner), f32), ((BLOCK, BLOCK), f32),
            ((BLOCK, BLOCK), f32), ((2 * blocks, BLOCK, own), bf16),
            ((4, inner, columns), bf16), ((2, inner // 2, columns), bf16), ((2, inner, columns), bf16),
        ],
        0, doc_lengths, tokens, cotangent, w_x, w_z, w_out, w_bc.T, w_dt.T, conv_x, row(conv_x_bias), conv_bc,
        row(conv_bc_bias), row(dt_bias), row(a_rate), row(d_skip), row(input_norm_gain), row(out_gain),
        places="s" + "a" * 5 + "v" * 11,
        sems=[
            (7,), (9,), (4, 4), (4, 4), (4, 4), (4, 4), (4 * group - 4,), (4 * group - 4,),
            (2, messages), (2, messages), (4,), (4,), (4,), (4,),
        ],
        collective=0,
        far=9,
    )
    w_z_grad, w_x_grad, input_grad, w_bc_grad, w_dt_grad, *small_grads = call(
        input_kernel,
        [
            ((shard, inner), f32), ((shard, inner), f32), ((T, own), bf16), ((per, shard), f32),
            ((heads, shard), f32), ((CONV, inner), f32), ((1, inner), f32), ((CONV, per), f32), ((1, per), f32),
            ((1, heads), f32), ((1, heads), f32), ((1, heads), f32), ((1, own), f32), ((1, inner), f32),
        ],
        [
            ((shard, inner), f32), ((shard, wide), f32), ((16, width), f32), ((LANES, inner), bf16),
            ((pair // LANES, shard, LANES), bf16), ((group - 1, shard, LANES), bf16),
            ((T, D), bf16), ((T, D), bf16), ((T, inner), bf16), ((T, wide), bf16), ((D, inner), bf16),
            ((D, wide), bf16), ((T, own), bf16),
            ((T, D), bf16), ((2, messages, BLOCK, own), bf16), ((BLOCK, own), f32),
            ((D, inner), bf16), ((4, shard, inner), bf16), ((2, shard // 2, inner), bf16), ((2, shard, inner), bf16),
            ((D, wide), bf16), ((4, shard, wide), bf16), ((2, shard // 2, wide), bf16), ((2, shard, wide), bf16),
            ((T, LANES), f32), ((8, T), f32), ((group - 1, 8, T), f32), ((8, D), f32),
            ((size - 1, 16, width), f32), ((group - 1, 8, pair), f32), ((group - 1, 8, inner), f32),
        ],
        0, tokens, inverse, row(input_norm_gain), normed, low_gate, low_xd, wz, wxd, cotangent, csums, sums, dsums,
        places="avvaaaaaavvv",
        sems=[
            (6,), (group, 3), (2, messages), (2, messages), (4,), (4,), (4,), (4,), (4,), (4,), (4,), (4,),
            (group - 1,), (group - 1,), (size - 1,), (size - 1,), (2 * group - 2,), (2 * group - 2,),
            (group - 1,), (group - 1,),
        ],
        collective=2,
        far=2,
    )
    (
        output, input_grad, w_z_grad, w_x_grad, w_bc_grad, w_dt_grad, w_out_grad, conv_x_grad, conv_x_bias_grad,
        conv_bc_grad, conv_bc_bias_grad, dt_bias_grad, a_rate_grad, d_skip_grad, in_gain_grad, out_gain_grad,
    ) = hand_on(output, input_grad, w_z_grad, w_x_grad, w_bc_grad, w_dt_grad, w_out_grad, *small_grads)
    return (
        output, input_grad, w_z_grad, w_x_grad, w_bc_grad.T, w_dt_grad.T, w_out_grad,
        conv_x_grad, conv_x_bias_grad[0], conv_bc_grad, conv_bc_bias_grad[0], dt_bias_grad[0], a_rate_grad[0],
        d_skip_grad[0], in_gain_grad[0], out_gain_grad[0],
    )


def solution(mesh):
    row, block, column = P("dp", None), P("dp", "mp"), P("mp")
    return jax.shard_map(
        per_device if (mesh.shape["dp"], mesh.shape["mp"]) == (8, 4) else per_device_any,
        mesh=mesh,
        in_specs=(
            row, row, row, block, block, block, block, P("mp", "dp"), P(None, "mp"), column,
            P(None, "mp"), column, column, column, column, P(), column,
        ),
        out_specs=(
            block, block, block, block, block, block, P("mp", "dp"), P(None, "mp"), column,
            P(None, "mp"), column, column, column, column, column, column,
        ),
        check_vma=False,
    )
```

```python
import functools

import jax
import jax.numpy as jnp
from jax import lax
from jax.experimental import pallas as pl
from jax.experimental.pallas import tpu as pltpu
from jax.sharding import PartitionSpec as P

HEADDIM = 64
STATE = 128
CONV = 4
BLOCK = 256
DOCS = 5
LANES = 128
EPS = 1e-05
f32 = jnp.float32
bf16 = jnp.bfloat16
VMEM_LIMIT = 127 * 2**19


def mm(a, b):
    return jnp.dot(a, b, preferred_element_type=f32)


def mm_nt(a, b):
    return lax.dot_general(a, b, (((1,), (1,)), ((), ())), preferred_element_type=f32)


def mm_tn(a, b):
    return lax.dot_general(a, b, (((0,), (0,)), ((), ())), preferred_element_type=f32)


def halves(v):
    high = v.astype(bf16)
    return high, (v - high.astype(f32)).astype(bf16)


def expand(v, spread):
    high, rest = halves(v)
    return mm(high, spread) + mm(rest, spread)


def gather_heads(v, spread):
    high, rest = halves(v)
    return mm_nt(high, spread) + mm_nt(rest, spread)


def logistic(v):
    return 1.0 / (1.0 + jnp.exp(-v))


def tiles(total, size):
    return [(at, min(size, total - at)) for at in range(0, total, size)]


def fold(v):
    return jnp.sum(v.reshape(v.shape[0] // 8, 8, v.shape[1]), axis=0)


def doc_of(starts, place):
    count = (place >= starts[0]).astype(jnp.int32)
    for k in range(1, DOCS):
        count = count + (place >= starts[k]).astype(jnp.int32)
    return count


def fill_spread(spread):
    rows, columns = spread.shape
    head = lax.broadcasted_iota(jnp.int32, (rows, columns), 0)
    channel = lax.broadcasted_iota(jnp.int32, (rows, columns), 1)
    low = head * HEADDIM
    spread[...] = jnp.where((channel >= low) & (channel < low + HEADDIM), 1.0, 0.0).astype(bf16)


def fill_positions(starts, pos, rpos):
    length = pos.shape[0]

    def body(i, carry):
        at = pl.multiple_of(i * BLOCK, BLOCK)
        place = lax.broadcasted_iota(jnp.int32, (BLOCK, LANES), 0) + at
        begin = jnp.zeros_like(place)
        end = jnp.full_like(place, length)
        for k in range(DOCS):
            begin = jnp.maximum(begin, jnp.where(place >= starts[k], starts[k], 0))
            end = jnp.minimum(end, jnp.where(place < starts[k], starts[k], length))
        pos[pl.ds(at, BLOCK), :] = place - begin
        if rpos is not None:
            rpos[pl.ds(at, BLOCK), :] = end - 1 - place
        return carry

    lax.fori_loop(0, length // BLOCK, body, 0)


def normalize(tok, gain, normed, stat):
    step = 64

    def body(i, carry):
        rows = pl.ds(pl.multiple_of(i * step, step), step)
        v = tok[rows, :].astype(f32)
        inverse = lax.rsqrt(jnp.mean(v * v, axis=1, keepdims=True) + EPS)
        normed[rows, :] = (v * inverse * gain[...]).astype(bf16)
        stat[rows, :] = jnp.broadcast_to(inverse, (step, LANES))
        return carry

    lax.fori_loop(0, tok.shape[0] // step, body, 0)


def project_x(normed, wxd, xin, dtin):
    length, width = normed.shape[0], xin.shape[1]
    xin[pl.ds(0, 8), :] = jnp.zeros((8, width), f32)
    rows = 512

    def body(i, carry):
        at = pl.multiple_of(i * rows, rows)
        left = normed[pl.ds(at, rows), :]
        for c, w in tiles(width, 512):
            xin[pl.ds(at + 8, rows), c : c + w] = mm(left, wxd[:, c : c + w])
        dtin[pl.ds(at, rows), :] = mm(left, wxd[:, width : width + LANES])
        return carry

    lax.fori_loop(0, length // rows, body, 0)


def convolve(xin, taps, pos, slope, x_low, bc_low):
    width, inner = xin.shape[1], x_low.shape[1]

    def tile(b, c, out, at):
        rows = pl.ds(pl.multiple_of(b * BLOCK, BLOCK), BLOCK)
        x = xin[pl.ds(pl.multiple_of(b * BLOCK, BLOCK), BLOCK + 8), pl.ds(c, LANES)]
        place = pos[rows, :]
        tap = taps[:, pl.ds(c, LANES)]
        pre = tap[CONV : CONV + 1] + tap[CONV - 1 : CONV] * x[8:]
        for lag in range(1, CONV):
            earlier = pltpu.roll(x, lag, 0)[8:]
            pre = pre + tap[CONV - 1 - lag : CONV - lag] * jnp.where(place >= lag, earlier, 0.0)
        sg = logistic(pre)
        slope[rows, pl.ds(c, LANES)] = (sg * (1.0 + pre * (1.0 - sg))).astype(bf16)
        out[rows, pl.ds(at, LANES)] = (pre * sg).astype(bf16)

    blocks = x_low.shape[0] // BLOCK
    xcols, bcols = inner // LANES, (width - inner) // LANES

    def x_body(i, carry):
        c = pl.multiple_of((i % xcols) * LANES, LANES)
        tile(i // xcols, c, x_low, c)
        return carry

    def bc_body(i, carry):
        c = pl.multiple_of((i % bcols) * LANES, LANES)
        tile(i // bcols, inner + c, bc_low, c)
        return carry

    lax.fori_loop(0, blocks * xcols, x_body, 0)
    lax.fori_loop(0, blocks * bcols, bc_body, 0)


def softplus(v):
    return jnp.maximum(v, 0.0) + jnp.log1p(jnp.exp(-jnp.abs(v)))


def steps(dtin, dpar, step, sgdt, step_low, decay_low):
    def body(i, carry):
        rows = pl.ds(pl.multiple_of(i * BLOCK, BLOCK), BLOCK)
        v = dtin[rows, :] + dpar[0:1, :]
        soft = softplus(v)
        if step is not None:
            step[rows, :] = soft
            sgdt[rows, :] = logistic(v)
        step_low[rows, :] = soft.astype(bf16)
        decay_low[rows, :] = (-dpar[1:2, :] * soft).astype(bf16)
        return carry

    lax.fori_loop(0, dtin.shape[0] // BLOCK, body, 0)


def block_marks(starts, b):
    at = b * BLOCK
    column = doc_of(starts, lax.broadcasted_iota(jnp.int32, (BLOCK, 1), 0) + at)
    row = doc_of(starts, lax.broadcasted_iota(jnp.int32, (1, BLOCK), 1) + at)
    before = doc_of(starts, at - 1)
    last = doc_of(starts, at + BLOCK - 1)
    return column, row, before, last


def block_decays(b, starts, decay_low, step_low, spread):
    rows = pl.ds(pl.multiple_of(b * BLOCK, BLOCK), BLOCK)
    column, row, before, last = block_marks(starts, b)
    i0 = lax.broadcasted_iota(jnp.int32, (BLOCK, BLOCK), 0)
    i1 = lax.broadcasted_iota(jnp.int32, (BLOCK, BLOCK), 1)
    lower = jnp.where(i0 >= i1, 1.0, 0.0).astype(bf16)
    cum = mm(lower, decay_low[rows, :])
    step_e = mm(step_low[rows, :], spread[...])
    cum_e = expand(jnp.exp(cum), spread[...])
    kept_e = jnp.where(before == last, cum_e[BLOCK - 1 : BLOCK], 0.0)
    in_e = jnp.where(column == before, cum_e, 0.0)
    out_e = expand(jnp.exp(cum[BLOCK - 1 : BLOCK] - cum), spread[...])
    out_e = jnp.where(column == last, out_e, 0.0)
    return cum, step_e, kept_e, in_e, out_e, column, row


def scan_forward(
    starts, x_low, bc_low, step_low, decay_low, ssd, states, spread, state, xs, yin, cbm, tick=None
):
    length, inner = x_low.shape
    state[...] = jnp.zeros_like(state)

    def body(b, carry):
        rows = pl.ds(pl.multiple_of(b * BLOCK, BLOCK), BLOCK)
        cum, step_e, kept_e, in_e, out_e, column, row = block_decays(
            b, starts, decay_low, step_low, spread
        )
        bm, cm = bc_low[rows, :STATE], bc_low[rows, STATE:]
        i0 = lax.broadcasted_iota(jnp.int32, (BLOCK, BLOCK), 0)
        i1 = lax.broadcasted_iota(jnp.int32, (BLOCK, BLOCK), 1)
        cbm[...] = jnp.where((column == row) & (i0 >= i1), mm_nt(cm, bm), 0.0)
        stepped = x_low[rows, :].astype(f32) * step_e
        xs[...] = stepped.astype(bf16)
        entering = state[...].astype(bf16)
        states[b] = entering
        yin[...] = in_e * mm(cm, entering)
        state[...] = kept_e * state[...] + mm_tn(bm, (stepped * out_e).astype(bf16))
        cum_t = cum.T
        first = lax.broadcasted_iota(jnp.int32, (BLOCK, LANES), 1) < HEADDIM
        for j in range(inner // LANES):
            cols = slice(j * LANES, (j + 1) * LANES)
            pair = xs[:, cols]
            part = []
            for h in (2 * j, 2 * j + 1):
                span = jnp.minimum(cum[:, h : h + 1] - cum_t[h : h + 1, :], 0.0)
                part.append(mm((jnp.exp(span) * cbm[...]).astype(bf16), pair))
            y = jnp.where(first, part[0], part[1]) + yin[:, cols]
            ssd[rows, cols] = y.astype(bf16)
        if tick is not None:
            tick(b)
        return carry

    lax.fori_loop(0, length // BLOCK, body, 0)


def project_rows(left, right, out, rows=512, columns=512):
    def body(i, carry):
        at = pl.ds(pl.multiple_of(i * rows, rows), rows)
        part = left[at, :]
        for c, w in tiles(out.shape[1], columns):
            out[at, c : c + w] = mm(part, right[:, c : c + w]).astype(out.dtype)
        return carry

    lax.fori_loop(0, out.shape[0] // rows, body, 0)


def back_rows(left, right, out, rows=512, columns=512):
    def body(i, carry):
        at = pl.ds(pl.multiple_of(i * rows, rows), rows)
        part = left[at, :]
        for c, w in tiles(out.shape[1], columns):
            out[at, c : c + w] = mm_nt(part, right[c : c + w, :]).astype(out.dtype)
        return carry

    lax.fori_loop(0, out.shape[0] // rows, body, 0)


def weight_rows(left, right, out, rows=256, columns=512):
    def body(i, carry):
        at = pl.ds(pl.multiple_of(i * rows, rows), rows)
        part = left[:, at]
        for c, w in tiles(out.shape[1], columns):
            out[at, c : c + w] = mm_tn(part, right[:, c : c + w]).astype(out.dtype)
        return carry

    lax.fori_loop(0, out.shape[0] // rows, body, 0)


def gate_sums(gate, ssd, x_low, gnorm, crow, stat):
    step, inner = 64, gate.shape[1]

    def body(i, carry):
        rows = pl.ds(pl.multiple_of(i * step, step), step)
        squares = jnp.zeros((step, 256), f32)
        crosses = jnp.zeros((step, 256), f32)
        for c in range(0, inner, 256):
            cols = slice(c, c + 256)
            g = gate[rows, cols]
            mixed = ssd[rows, cols].astype(f32) + crow[1:2, cols] * x_low[rows, cols].astype(f32)
            gated = mixed * (g * logistic(g))
            squares = squares + gated * gated
            crosses = crosses + gnorm[rows, cols] * crow[0:1, cols] * gated
        lane = lax.broadcasted_iota(jnp.int32, (step, LANES), 1)
        s1 = jnp.sum(squares, axis=1, keepdims=True)
        s2 = jnp.sum(crosses, axis=1, keepdims=True)
        stat[rows, :] = jnp.where(lane == 0, s1, jnp.where(lane == 1, s2, 0.0))
        return carry

    lax.fori_loop(0, gate.shape[0] // step, body, 0)


def gate_squares(gate, ssd, x_low, crow, stat):
    step, inner = 64, gate.shape[1]

    def body(i, carry):
        rows = pl.ds(pl.multiple_of(i * step, step), step)
        squares = jnp.zeros((step, 256), f32)
        for c in range(0, inner, 256):
            cols = slice(c, c + 256)
            g = gate[rows, cols]
            mixed = ssd[rows, cols].astype(f32) + crow[1:2, cols] * x_low[rows, cols].astype(f32)
            value = mixed * (g * logistic(g))
            squares = squares + value * value
        stat[rows, :] = squares[:, :LANES] + squares[:, LANES:]
        return carry

    lax.fori_loop(0, gate.shape[0] // step, body, 0)


def gate_norm(gate, ssd, x_low, inverse_out, crow, gn):
    step, inner = 64, gate.shape[1]

    def body(i, carry):
        rows = pl.ds(pl.multiple_of(i * step, step), step)
        inverse = inverse_out[rows, :1]
        for c in range(0, inner, 256):
            cols = slice(c, c + 256)
            g = gate[rows, cols]
            mixed = ssd[rows, cols].astype(f32) + crow[1:2, cols] * x_low[rows, cols].astype(f32)
            gn[rows, cols] = (mixed * (g * logistic(g)) * inverse * crow[0:1, cols]).astype(bf16)
        return carry

    lax.fori_loop(0, gate.shape[0] // step, body, 0)


def cross_sums(gnorm, gn, stat):
    step, inner = 64, gn.shape[1]

    def body(i, carry):
        rows = pl.ds(pl.multiple_of(i * step, step), step)
        total = jnp.zeros((step, 256), f32)
        for c in range(0, inner, 256):
            cols = slice(c, c + 256)
            total = total + gnorm[rows, cols] * gn[rows, cols].astype(f32)
        stat[rows, :] = total[:, :LANES] + total[:, LANES:]
        return carry

    lax.fori_loop(0, gn.shape[0] // step, body, 0)


def forward_kernel(
    starts, tok, gain, wxd, wz, taps, dpar,
    normed, inverse, xin, slope, gate, x_low, bc_low, step, sgdt, step_low, decay_low, ssd, states,
    pos, spread, dtin, state, xs, yin, cbm,
):
    fill_spread(spread)
    fill_positions(starts, pos, None)
    normalize(tok, gain, normed, inverse)
    project_x(normed, wxd, xin, dtin)
    convolve(xin, taps, pos, slope, x_low, bc_low)
    steps(dtin, dpar, step, sgdt, step_low, decay_low)
    scan_forward(starts, x_low, bc_low, step_low, decay_low, ssd, states, spread, state, xs, yin, cbm)
    project_rows(normed, wz, gate)


def gate_kernel(cot, wout, gate, ssd, x_low, crow, gnorm, stat):
    back_rows(cot, wout, gnorm)
    gate_sums(gate, ssd, x_low, gnorm, crow, stat)


def gate_backward(gate, ssd, x_low, gnorm, crow, stat, width, gn, low_gate, gs, sums, known=None):
    step, inner = 64, ssd.shape[1]
    sums[...] = jnp.zeros_like(sums)

    def body(i, carry):
        rows = pl.ds(pl.multiple_of(i * step, step), step)
        if known is None:
            inverse = lax.rsqrt(stat[rows, 0:1] / width + EPS)
            mean = inverse * stat[rows, 1:2] / width
        else:
            inverse, mean = known[rows, :1], stat[rows, :1]
        for c in range(0, inner, 256):
            cols = slice(c, c + 256)
            g = gate[rows, cols]
            x = x_low[rows, cols].astype(f32)
            mixed = ssd[rows, cols].astype(f32) + crow[1:2, cols] * x
            sg = logistic(g)
            act = g * sg
            hat = mixed * act * inverse
            if gn is not None:
                gn[rows, cols] = (hat * crow[0:1, cols]).astype(bf16)
            gnorm_here = gnorm[rows, cols]
            grad = inverse * (gnorm_here * crow[0:1, cols] - hat * mean)
            grad_mixed = grad * act
            low_gate[rows, cols] = (grad * mixed * (sg * (1.0 + g * (1.0 - sg)))).astype(bf16)
            gs[rows, cols] = grad_mixed.astype(bf16)
            sums[0:8, cols] += fold(gnorm_here * hat)
            sums[8:16, cols] += fold(grad_mixed * x)
        return carry

    lax.fori_loop(0, ssd.shape[0] // step, body, 0)


def middle_kernel(
    cot, wout, normed, gate, x_low, ssd, gnorm, crow, stat,
    branch, dwout, dwz, low_gate, gs, sums,
    gn, *, width,
):
    gate_backward(gate, ssd, x_low, gnorm, crow, stat, width, gn, low_gate, gs, sums)
    project_rows(gn, wout, branch)
    weight_rows(gn, cot, dwout)
    weight_rows(normed, low_gate, dwz)


def scan_backward(
    starts, x_low, bc_low, step_low, decay_low, ssd, states, gs, slope, crow, step, sgdt, dpar,
    gpre, low_xd, dsums, spread, dstate, xs, gx, cbm, acc, tick=None,
):
    length, inner = x_low.shape
    width = gpre.shape[1]
    blocks = length // BLOCK
    dstate[...] = jnp.zeros_like(dstate)
    dsums[...] = jnp.zeros_like(dsums)
    gpre[pl.ds(length, 8), :] = jnp.zeros((8, width), f32)

    def body(i, carry):
        b = blocks - 1 - i
        rows = pl.ds(pl.multiple_of(b * BLOCK, BLOCK), BLOCK)
        cum, step_e, kept_e, in_e, out_e, column, row = block_decays(
            b, starts, decay_low, step_low, spread
        )
        bm, cm = bc_low[rows, :STATE], bc_low[rows, STATE:]
        i0 = lax.broadcasted_iota(jnp.int32, (BLOCK, BLOCK), 0)
        i1 = lax.broadcasted_iota(jnp.int32, (BLOCK, BLOCK), 1)
        linked = (column == row) & (i0 <= i1)
        cbm[...] = jnp.where(linked, mm_nt(bm, cm), 0.0)
        x = x_low[rows, :].astype(f32)
        stepped = x * step_e
        xs[...] = stepped.astype(bf16)
        cum_t = cum.T
        first = lax.broadcasted_iota(jnp.int32, (BLOCK, LANES), 1) < HEADDIM
        acc[...] = jnp.zeros_like(acc)
        for j in range(inner // LANES):
            cols = slice(j * LANES, (j + 1) * LANES)
            xpair, gpair = xs[:, cols], gs[rows, cols]
            none = jnp.zeros_like(xpair)
            part, total = [], None
            for k in range(2):
                h = 2 * j + k
                kernel = jnp.exp(jnp.minimum(cum_t[h : h + 1, :] - cum[:, h : h + 1], 0.0))
                part.append(mm((kernel * cbm[...]).astype(bf16), gpair))
                own = jnp.where(first, xpair, none) if k == 0 else jnp.where(first, none, xpair)
                here = kernel * mm_nt(own, gpair)
                total = here if total is None else total + here
            acc[...] += total
            gx[:, cols] = jnp.where(first, part[0], part[1])
        dstate_low = dstate[...].astype(bf16)
        entering = states[b]
        leaving = states[jnp.minimum(b + 1, blocks - 1)]
        end = jnp.sum(dstate[...] * leaving.astype(f32), axis=0, keepdims=True)
        g = gs[rows, :].astype(f32)
        g_in = (in_e * g).astype(bf16)
        raw = gx[...] + out_e * mm(bm, dstate_low)
        grad_x = (step_e * raw).astype(bf16).astype(f32)
        gpre[rows, :inner] = (grad_x + crow[1:2, :] * g) * slope[rows, :inner]
        pairs = jnp.where(linked, acc[...], 0.0).astype(bf16)
        db = mm(pairs, cm) + mm_nt((stepped * out_e).astype(bf16), dstate_low)
        dc = mm_tn(pairs, bm) + mm_nt(g_in, entering)
        gpre[rows, inner : inner + STATE] = db * slope[rows, inner : inner + STATE]
        gpre[rows, inner + STATE :] = dc * slope[rows, inner + STATE :]
        raw_x = x * raw
        grad_step = gather_heads(raw_x, spread[...]).astype(bf16).astype(f32)
        dcum = gather_heads(g * ssd[rows, :].astype(f32) - step_e * raw_x, spread[...])
        tail = gather_heads(jnp.broadcast_to(end, (8, inner)), spread[...])[0:1]
        upper = jnp.where(i0 <= i1, 1.0, 0.0).astype(bf16)
        high, rest = halves(dcum)
        later = mm(upper, high) + mm(upper, rest) + tail
        grad_decay = later.astype(bf16).astype(f32)
        total_step = grad_step - dpar[1:2, :] * grad_decay
        if sgdt is None:
            before_step = step[rows, :] + dpar[0:1, :]
            slope_here, step_here = logistic(before_step), softplus(before_step)
        else:
            slope_here, step_here = sgdt[rows, :], step[rows, :]
        grad_dt = total_step * slope_here
        low_xd[rows, width:] = grad_dt.astype(bf16)
        dsums[0:8, :] += fold(grad_dt)
        dsums[8:16, :] -= fold(grad_decay * step_here)
        dstate[...] = kept_e * dstate[...] + mm_tn(cm, g_in)
        if tick is not None:
            tick(i)
        return carry

    lax.fori_loop(0, blocks, body, 0)


def convolve_back(xin, gpre, taps, pos, rpos, low_xd, csums, tick=None):
    width = gpre.shape[1]
    columns = width // LANES
    csums[...] = jnp.zeros_like(csums)

    def body(b, j):
        at = pl.multiple_of(b * BLOCK, BLOCK)
        cols = pl.ds(pl.multiple_of(j * LANES, LANES), LANES)
        rows = pl.ds(at, BLOCK)
        x = xin[pl.ds(at, BLOCK + 8), cols]
        g = gpre[pl.ds(at, BLOCK + 8), cols]
        here = g[:BLOCK]
        place, ahead = pos[rows, :], rpos[rows, :]
        tap = taps[:, cols]
        grad = tap[CONV - 1 : CONV] * here
        csums[pl.ds(8 * CONV, 8), cols] += fold(here)
        csums[pl.ds(8 * (CONV - 1), 8), cols] += fold(here * x[8:])
        for lag in range(1, CONV):
            k = CONV - 1 - lag
            later = pltpu.roll(g, BLOCK + 8 - lag, 0)[:BLOCK]
            earlier = pltpu.roll(x, lag, 0)[8:]
            grad = grad + tap[k : k + 1] * jnp.where(ahead >= lag, later, 0.0)
            csums[pl.ds(8 * k, 8), cols] += fold(here * jnp.where(place >= lag, earlier, 0.0))
        low_xd[rows, cols] = grad.astype(bf16)

    def block(b, carry):
        lax.fori_loop(0, columns, lambda j, c: (body(b, j), c)[1], 0)
        if tick is not None:
            tick(b)
        return carry

    lax.fori_loop(0, (xin.shape[0] - 8) // BLOCK, block, 0)


def backward_kernel(
    starts, xin, slope, x_low, bc_low, step, sgdt, step_low, decay_low, ssd, states, gs, taps, crow, dpar,
    low_xd, csums, dsums,
    pos, rpos, spread, gpre, dstate, xs, gx, cbm, acc,
):
    fill_spread(spread)
    fill_positions(starts, pos, rpos)
    scan_backward(
        starts, x_low, bc_low, step_low, decay_low, ssd, states, gs, slope, crow, step, sgdt, dpar,
        gpre, low_xd, dsums, spread, dstate, xs, gx, cbm, acc,
    )
    convolve_back(xin, gpre, taps, pos, rpos, low_xd, csums)


def last_kernel(tok, inverse, gain, normed, low_gate, low_xd, wz, wxd, dwxd, gfull, rowdot):
    weight_rows(normed, low_xd, dwxd)
    rows = 256

    def body(i, carry):
        at = pl.ds(pl.multiple_of(i * rows, rows), rows)
        total = jnp.zeros((rows, 1), f32)
        for c, w in tiles(gfull.shape[1], 512):
            cols = slice(c, c + w)
            part = mm_nt(low_gate[at, :], wz[cols, :]) + mm_nt(low_xd[at, :], wxd[cols, :])
            gfull[at, cols] = part.astype(bf16)
            total = total + jnp.sum(part * gain[:, cols] * tok[at, cols].astype(f32), axis=1, keepdims=True)
        rowdot[at, :] = total * inverse[at, :]
        return carry

    lax.fori_loop(0, gfull.shape[0] // rows, body, 0)


MESH = pl.DeviceIdType.MESH


def remote(source, target, send, receive, **where):
    return pltpu.make_async_remote_copy(
        src_ref=source, dst_ref=target, send_sem=send, recv_sem=receive, device_id=where, device_id_type=MESH
    )


def add_into(target, source, rows=64):
    def body(i, carry):
        at = pl.ds(pl.multiple_of(i * rows, rows), rows)
        target[at, :] = (target[at, :].astype(f32) + source[at, :].astype(f32)).astype(target.dtype)
        return carry

    lax.fori_loop(0, target.shape[0] // rows, body, 0)


class Ring:
    def __init__(self):
        self.me = lax.axis_index("dp")
        self.core = self.me % 2
        chip = self.me // 2
        y = chip // 2
        self.pos = 2 * y + (chip + y) % 2
        self.partner = self.me + 1 - 2 * self.core
        self.right = self.at(self.pos + 1)
        self.left = self.at(self.pos + 3)
        self.across = self.at(self.pos + 2)

    def at(self, pos):
        pos = pos % 4
        y = pos // 2
        return (2 * y + (pos + y) % 2) * 2 + self.core


def greet(ring, everyone):
    barrier = pltpu.get_barrier_semaphore()
    n, z = lax.axis_size("mp"), lax.axis_index("mp")
    if everyone:
        size = lax.axis_size("dp")
        close = [(ring.me + i) % size for i in range(1, size)]
    else:
        close = [ring.partner, ring.right, ring.left]
    for other in close:
        pl.semaphore_signal(barrier, inc=1, device_id={"dp": other}, device_id_type=MESH)
    for i in range(1, n):
        pl.semaphore_signal(barrier, inc=1, device_id={"mp": (z + i) % n}, device_id_type=MESH)
    return lambda: pl.semaphore_wait(barrier, len(close) + n - 1)


class Scatter:
    def __init__(self, ring, shard, cores, parts, wholes, sems):
        self.ring, self.shard = ring, shard
        self.cores, self.parts, self.wholes = cores, parts, wholes
        self.core_send, self.core_recv, self.ring_send, self.ring_recv = sems
        self.half = cores.shape[1] // 2

    def upper(self, r):
        return self.shard(r).at[pl.ds(0, self.half), :]

    def lower(self, r):
        return self.shard(r).at[pl.ds(self.half, self.half), :]

    def core_copy(self, chip):
        ring = self.ring
        return remote(
            self.shard(2 * chip + 1 - ring.core), self.cores.at[chip],
            self.core_send.at[chip], self.core_recv.at[chip], dp=ring.partner,
        )

    def ring_copy(self, k):
        ring = self.ring
        source = (self.upper(ring.across), self.lower(ring.across), self.shard(ring.right), self.shard(ring.left))[k]
        target = (self.parts.at[0], self.parts.at[1], self.wholes.at[0], self.wholes.at[1])[k]
        return remote(
            source, target, self.ring_send.at[k], self.ring_recv.at[k], dp=(ring.right, ring.left)[k % 2]
        )

    def start(self, chip):
        self.core_copy(chip).start()

    def first(self):
        def body(chip, carry):
            self.core_copy(chip).wait_recv()
            add_into(self.shard(2 * chip + self.ring.core), self.cores.at[chip])
            return carry

        lax.fori_loop(0, 4, body, 0)
        self.ring_copy(0).start()
        self.ring_copy(1).start()

    def second(self):
        self.ring_copy(0).wait_recv()
        add_into(self.upper(self.ring.right), self.parts.at[0])
        self.ring_copy(2).start()
        self.ring_copy(1).wait_recv()
        add_into(self.lower(self.ring.left), self.parts.at[1])
        self.ring_copy(3).start()

    def finish(self, out, rows=64):
        self.ring_copy(2).wait_recv()
        self.ring_copy(3).wait_recv()
        own = self.shard(self.ring.me)

        def body(i, carry):
            at = pl.ds(pl.multiple_of(i * rows, rows), rows)
            out[at, :] = own[at, :].astype(f32) + self.wholes[0, at, :].astype(f32) + self.wholes[1, at, :].astype(f32)
            return carry

        lax.fori_loop(0, out.shape[0] // rows, body, 0)

        def done(chip, carry):
            self.core_copy(chip).wait_send()
            return carry

        lax.fori_loop(0, 4, done, 0)
        for k in range(4):
            self.ring_copy(k).wait_send()


class Line:
    def __init__(self, piece, slot, blocks, sems, total, depth):
        self.piece, self.slot, self.blocks, self.total, self.depth = piece, slot, blocks, total, depth
        self.send, self.recv = sems
        self.n, self.z = lax.axis_size("mp"), lax.axis_index("mp")
        self.place = (self.z, self.n - 1 - self.z)

    def rows(self, t):
        return pl.ds(pl.multiple_of(t * BLOCK, BLOCK), BLOCK)

    def source(self, side, k):
        d = k // self.blocks
        return self.piece(k - d * self.blocks, self.n - 1 - d if side == 0 else d)

    def copy(self, side, place, k):
        return remote(
            self.source(side, k), self.slot(side, place + 1, k), self.send.at[side, k], self.recv.at[side, k],
            mp=self.z + 1 if side == 0 else self.z - 1,
        )

    def arrived(self, side, place, k):
        target = self.slot(side, place, k)
        remote(target, target, self.send.at[side, k], self.recv.at[side, k], mp=self.z).wait_recv()
        return target

    def inject(self, k):
        for side in range(2):
            @pl.when(self.place[side] == 0)
            def _():
                @pl.when(jnp.int32(k) >= self.depth)
                def _():
                    self.copy(side, 0, jnp.maximum(k - self.depth, 0)).wait_send()

                self.copy(side, 0, k).start()

    def forward(self, k, hop):
        for side in range(2):
            @pl.when(self.place[side] == hop)
            def _():
                add_into(self.source(side, k), self.arrived(side, hop, k))
                self.copy(side, hop, k).start()

    def finish(self, t):
        self.total[...] = self.piece(t, self.z)[...].astype(f32)
        for side in range(2):
            for place in range(1, self.n):
                @pl.when(self.place[side] == place)
                def _():
                    self.total[...] += self.arrived(side, place, (self.n - 1 - place) * self.blocks + t)[...].astype(f32)

    def drain(self):
        for side in range(2):
            for place in range(self.n - 1):
                count = (self.n - 1 - place) * self.blocks

                @pl.when(self.place[side] == place)
                def _():
                    def body(k, carry):
                        self.copy(side, place, k).wait_send()
                        return carry

                    lax.fori_loop(count - self.depth if place == 0 else 0, count, body, 0)

    def order(self, i):
        z = self.z
        far = jnp.where(z < 2, 3 - i, i)
        near = z + 1 - 2 * (z % 2)
        return jnp.where(i < 2, far, jnp.where(i == 2, near, z))


class Loads:
    def __init__(self, sems):
        self.sems, self.pairs = sems, []

    def start(self, source, target):
        i = len(self.pairs)
        copy = pltpu.make_async_copy(source, target, self.sems.at[i])
        copy.start()
        self.pairs.append(copy)
        return copy


class Gather:
    def __init__(self, ring, shard, rows, sems):
        self.ring, self.shard, self.half = ring, shard, rows // 2
        self.ring_send, self.ring_recv, self.core_send, self.core_recv = sems
        self.other = 1 - 2 * ring.core

    def ring_copy(self, k, source):
        ring = self.ring
        piece = self.shard(source)
        if k >= 2:
            piece = piece.at[pl.ds((k - 2) * self.half, self.half), :]
        return remote(
            piece, piece, self.ring_send.at[k], self.ring_recv.at[k], dp=(ring.right, ring.left)[k % 2]
        )

    def core_copy(self, k, source):
        return remote(
            self.shard(source), self.shard(source), self.core_send.at[k], self.core_recv.at[k], dp=self.ring.partner
        )

    def start(self):
        me = self.ring.me
        self.ring_copy(0, me).start()
        self.ring_copy(1, me).start()
        self.core_copy(0, me).start()

    def second(self):
        left, right = self.ring.left, self.ring.right
        self.ring_copy(0, left).wait_recv()
        self.ring_copy(2, left).start()
        self.core_copy(1, left).start()
        self.ring_copy(1, right).wait_recv()
        self.ring_copy(3, right).start()
        self.core_copy(2, right).start()

    def third(self):
        across = self.ring.across
        self.ring_copy(2, across).wait_recv()
        self.ring_copy(3, across).wait_recv()
        self.core_copy(3, across).start()

    def arrived(self, k):
        ring = self.ring
        source = (ring.me, ring.left, ring.right, ring.across)[k] + self.other
        self.core_copy(k, source).wait_recv()

    def drain(self):
        ring = self.ring
        for k, source in enumerate((ring.me, ring.me, ring.left, ring.right)):
            self.ring_copy(k, source).wait_send()
        for k, source in enumerate((ring.me, ring.left, ring.right, ring.across)):
            self.core_copy(k, source).wait_send()


def cast_into(target, source, rows=64):
    def body(i, carry):
        at = pl.ds(pl.multiple_of(i * rows, rows), rows)
        target[at, :] = source[at, :].astype(target.dtype)
        return carry

    lax.fori_loop(0, target.shape[0] // rows, body, 0)


def trunk_kernel(
    lengths, tok, cot, w_x, w_z, w_out, w_bc, w_dt, conv_x, conv_x_bias, conv_bc, conv_bc_bias, dt_bias, a_rate,
    d_skip, gain, out_gain,
    normed_o, xin_o, wxd_o, wz_o, low_gate_o, low_xd_o, out_o, dwout_o, inverse_o, part_o,
    csums, dsums, sums, rows_o, colacc,
    v_tok, stage_b, normed, xin, first_wide, slope, both, states, wxd, wz, wout,
    bc_low, step_low, decay_low, inverse_out, taps, crow, dpar,
    bc_slots, tap_slots, row_slots, cross_slots, stat, turned,
    pos, rpos, spread, dtin, state, xs, wide, cbm, acc, near, cores, parts, wholes,
    load_sems, store_sems, token_sems, part_sems, ring_send, ring_recv, core_send, core_recv, mp_send, mp_recv, line_send, line_recv,
    scatter_core_send, scatter_core_recv, scatter_ring_send, scatter_ring_recv,
):
    ring = Ring()
    met = greet(ring, False)
    n, z = lax.axis_size("mp"), lax.axis_index("mp")
    length, features = normed.shape
    x_low, ssd = both.at[pl.ds(0, length), :], both.at[pl.ds(length, length), :]
    stage_a = wide
    inverse = inverse_out
    inner, width = x_low.shape[1], xin.shape[1]
    own = features // n
    shard, column_shard = stage_a.shape[0], stage_b.shape[1]
    heads, per = w_dt.shape[0], w_bc.shape[0]
    loads, stores = Loads(load_sems), Loads(store_sems)
    load_x = loads.start(w_x, stage_a)
    load_tok = loads.start(tok, v_tok)
    load_out = loads.start(w_out, stage_b)
    starts = [jnp.int32(0)]
    for k in range(DOCS - 1):
        starts.append(starts[-1] + lengths[0, k])

    def exchange(k, i):
        slots = (bc_slots, tap_slots, row_slots, cross_slots)[k]
        at = k * (n - 1) + i - 1
        return remote(slots.at[0], slots.at[i], mp_send.at[at], mp_recv.at[at], mp=(z + i) % n)

    def rows_of(ref, low, high):
        def shard_of(r):
            return ref.at[pl.ds(pl.multiple_of(r * shard, shard), shard), pl.ds(low, high - low)]

        return shard_of

    def columns_of(r):
        return wout.at[:, pl.ds(pl.multiple_of(r * column_shard, column_shard), column_shard)]

    sems = [tuple(group.at[k] for group in (ring_send, ring_recv, core_send, core_recv)) for k in range(4)]
    get_x = Gather(ring, rows_of(wxd, 0, inner), shard, sems[0])
    get_bd = Gather(ring, rows_of(wxd, inner, wxd.shape[1]), shard, sems[1])
    get_z = Gather(ring, rows_of(wz, 0, inner), shard, sems[2])
    get_out = Gather(ring, columns_of, inner, sems[3])

    load_x.wait()
    cast_into(get_x.shard(ring.me), stage_a)
    met()
    get_x.start()
    turned[...] = jnp.zeros_like(turned)
    turned[:per, :] = w_bc[...]
    bc_slots[0] = turned[...].T.astype(bf16)
    tap_slots[0] = jnp.zeros_like(tap_slots[0])
    tap_slots[0, :CONV, :per] = conv_bc[...]
    tap_slots[0, CONV : CONV + 1, :per] = conv_bc_bias[...]
    turned[...] = jnp.zeros_like(turned)
    turned[:heads, :] = w_dt[...]
    own_rows = pl.ds(pl.multiple_of(ring.me * shard, shard), shard)
    wxd[own_rows, width:] = turned[...].T.astype(bf16)
    dpar[...] = jnp.zeros_like(dpar)
    dpar[0:1, :heads] = dt_bias[...]
    dpar[1:2, :heads] = a_rate[...]
    dpar[2:3, :heads] = d_skip[...]
    for k in range(2):
        for i in range(1, n):
            exchange(k, i).start()
    load_z = loads.start(w_z, stage_a)
    fill_spread(spread)
    fill_positions(starts, pos, rpos)
    crow[0:1, :] = out_gain[...]
    crow[1:2, :] = expand(dpar[...], spread[...])[2:3]
    load_tok.wait()
    normalize(v_tok, gain, normed, inverse)
    load_cot = loads.start(cot, v_tok)
    store_normed = stores.start(normed, normed_o)
    store_inverse = stores.start(inverse, inverse_o)
    for k in range(2):
        for i in range(1, n):
            exchange(k, i).wait()
    first = lax.broadcasted_iota(jnp.int32, (shard, LANES), 1) < per
    for j in range((width - inner) // LANES):
        low, high = (z - 2 * j + n) % n, (z - 2 * j - 1 + n) % n
        columns = slice(inner + j * LANES, inner + (j + 1) * LANES)
        pair = jnp.where(first, bc_slots[low].astype(f32), pltpu.roll(bc_slots[high].astype(f32), per, 1))
        wxd[own_rows, columns] = pair.astype(bf16)
        taps[:, columns] = jnp.where(first[:8], tap_slots[low], pltpu.roll(tap_slots[high], per, 1))
    get_bd.start()
    taps[:, :inner] = jnp.zeros((8, inner), f32)
    taps[:CONV, :inner] = conv_x[...]
    taps[CONV : CONV + 1, :inner] = conv_x_bias[...]
    load_z.wait()
    cast_into(get_z.shard(ring.me), stage_a)
    load_out.wait()
    cast_into(get_out.shard(ring.me), stage_b)
    xin[pl.ds(0, 8), :] = jnp.zeros((8, width), f32)

    def project_chip(k, source):
        get_x.arrived(k)
        get_bd.arrived(k)
        part = pl.ds(pl.multiple_of((source // 2) * 2 * shard, 2 * shard), 2 * shard)

        def body(i, carry):
            at = pl.multiple_of(i * 512, 512)
            left = normed[pl.ds(at, 512), part]
            for c, w in tiles(wxd.shape[1], 512):
                here = mm(left, wxd[part, c : c + w])
                w_x_part = min(w, width - c)
                if k == 0:
                    xin[pl.ds(at + 8, 512), c : c + w_x_part] = here[:, :w_x_part]
                else:
                    xin[pl.ds(at + 8, 512), c : c + w_x_part] += here[:, :w_x_part]
                if w_x_part < w:
                    if k == 0:
                        dtin[pl.ds(at, 512), :] = here[:, w_x_part:]
                    else:
                        dtin[pl.ds(at, 512), :] += here[:, w_x_part:]
            return carry

        lax.fori_loop(0, length // 512, body, 0)

    project_chip(0, ring.me)
    get_x.second()
    get_bd.second()
    get_z.start()
    project_chip(1, ring.left)
    project_chip(2, ring.right)
    get_x.third()
    get_bd.third()
    project_chip(3, ring.across)
    store_xin = stores.start(xin, xin_o)
    store_wxd = stores.start(wxd, wxd_o)
    steps(dtin, dpar, None, None, step_low, decay_low)
    convolve(xin, taps, pos, slope, x_low, bc_low)
    get_z.second()
    get_out.start()

    def forward_tick(b):
        @pl.when(b == 1)
        def _():
            get_z.third()

    scan_forward(
        starts, x_low, bc_low, step_low, decay_low, ssd, states, spread, state, xs, wide, cbm, forward_tick
    )
    for k in range(4):
        get_z.arrived(k)
    gate = first_wide.at[pl.ds(0, length), pl.ds(0, inner)]
    gnorm = xin.at[pl.ds(0, length), pl.ds(0, inner)]
    project_rows(normed, wz, gate)
    store_wz = stores.start(wz, wz_o)
    gate_squares(gate, ssd, x_low, crow, stat)

    def put_rows(target):
        for b in range(length // BLOCK):
            line_sum = jnp.sum(stat[b * BLOCK : (b + 1) * BLOCK, :].T, axis=0, keepdims=True)
            for j in range(BLOCK // LANES):
                at = b * (BLOCK // LANES) + j
                target[at : at + 1, :] = line_sum[:, j * LANES : (j + 1) * LANES]

    def sum_rows(slots, out, finish):
        sums_here = finish(functools.reduce(lambda p, q: p + q, [slots[i] for i in range(n)]))
        for b in range(length // BLOCK):
            at = b * (BLOCK // LANES)
            row = jnp.concatenate([sums_here[at + j : at + j + 1] for j in range(BLOCK // LANES)], axis=1)
            turned[...] = jnp.broadcast_to(row, turned.shape)
            out[b * BLOCK : (b + 1) * BLOCK, :] = turned[...].T

    put_rows(row_slots.at[0])
    get_x.drain()
    get_bd.drain()
    store_wxd.wait()
    for i in range(1, n):
        exchange(2, i).start()
    load_cot.wait()
    store_xin.wait()

    def back_chip(k, source):
        get_out.arrived(k)
        part = pl.ds(pl.multiple_of((source // 2) * 2 * column_shard, 2 * column_shard), 2 * column_shard)

        def body(i, carry):
            at = pl.ds(pl.multiple_of(i * 512, 512), 512)
            left = v_tok[at, part]
            for c, w in tiles(inner, 512):
                here = mm_nt(left, wout[c : c + w, part])
                if k == 0:
                    gnorm[at, c : c + w] = here
                else:
                    gnorm[at, c : c + w] += here
            return carry

        lax.fori_loop(0, length // 512, body, 0)

    get_out.second()
    back_chip(0, ring.me)
    back_chip(1, ring.left)
    back_chip(2, ring.right)
    for i in range(1, n):
        exchange(2, i).wait()
    store_inverse.wait()
    sum_rows(row_slots, inverse_out, lambda total: lax.rsqrt(total / (inner * n) + EPS))
    get_out.third()
    store_normed.wait()
    gn = normed.at[:, pl.ds(0, inner)]
    gs = normed.at[:, pl.ds(inner, inner)]
    gate_norm(gate, ssd, x_low, inverse_out, crow, gn)
    back_chip(3, ring.across)
    cross_sums(gnorm, gn, stat)
    put_rows(cross_slots.at[0])
    for i in range(1, n):
        exchange(3, i).start()
    get_z.drain()
    store_wz.wait()

    fold_columns = inner // own

    def piece(t, q):
        row = pl.multiple_of((q // fold_columns) * length + t * BLOCK, BLOCK)
        return wz.at[pl.ds(row, BLOCK), pl.ds(pl.multiple_of((q % fold_columns) * own, own), own)]

    def slot(side, place, k):
        if place == 2:
            return near.at[k]
        row = pl.multiple_of((k // fold_columns) * BLOCK, BLOCK)
        return wxd.at[pl.ds(row, BLOCK), pl.ds(pl.multiple_of((k % fold_columns) * own, own), own)]

    total = wide.at[:, pl.ds(0, own)]
    line = Line(piece, slot, length // BLOCK, (line_send, line_recv), total, 4)

    def quarter(i, carry):
        q = line.order(i)
        columns = pl.ds(pl.multiple_of(q * own, own), own)
        for r in range(0, length, 512):
            at = pl.ds(pl.multiple_of((q // fold_columns) * length + r, 512), 512)
            cols = pl.ds(pl.multiple_of((q % fold_columns) * own, own), own)
            wz[at, cols] = mm(gn[r : r + 512, :], wout[:, columns]).astype(bf16)
            if r == 0:
                @pl.when(i == 0)
                def _():
                    line.inject(0)
                    line.inject(1)

        return carry

    lax.fori_loop(0, n, quarter, 0)
    line.inject(2)
    line.inject(3)
    get_out.drain()
    grads = wout
    scatter = Scatter(
        ring, lambda r: grads.at[:, pl.ds(pl.multiple_of(r * column_shard, column_shard), column_shard)],
        cores, parts, wholes, (scatter_core_send, scatter_core_recv, scatter_ring_send, scatter_ring_recv),
    )
    chunk = 2 * column_shard

    def weight(j, carry):
        columns = pl.ds(pl.multiple_of(j * chunk, chunk), chunk)
        for r in range(0, inner, 256):
            grads[r : r + 256, columns] = mm_tn(gn[:, r : r + 256], v_tok[:, columns]).astype(bf16)
        scatter.start(j)
        return carry

    lax.fori_loop(0, 4, weight, 0)
    line.inject(4)
    line.forward(0, 1)
    xd = v_tok.at[:, pl.ds(0, wxd.shape[1])]
    token_own = v_tok.at[:, pl.ds(wxd.shape[1], own)]
    load_own = loads.start(tok.at[:, pl.ds(pl.multiple_of(z * own, own), own)], token_own)
    for i in range(1, n):
        exchange(3, i).wait()
    sum_rows(cross_slots, stat, lambda total: total / (inner * n))
    low_gate = gn
    gate_backward(gate, ssd, x_low, gnorm, crow, stat, inner * n, None, low_gate, gs, sums, known=inverse_out)
    load_xin = loads.start(xin_o, xin)
    stores.start(low_gate, low_gate_o)
    line.forward(1, 1)
    line.forward(0, 2)
    scatter.first()

    def scan_tick(i):
        line.inject(i + 5)
        line.forward(i + 2, 1)

        @pl.when(i < 3)
        def _():
            line.forward(i + 1, 2)

        @pl.when(i == 1)
        def _():
            scatter.second()

    gpre = first_wide
    scan_backward(
        starts, x_low, bc_low, step_low, decay_low, ssd, states, gs, slope, crow, dtin, None, dpar,
        gpre, xd, dsums, spread, state, xs, wide, cbm, acc, scan_tick,
    )
    bd = wxd.shape[1] - inner
    weight_loads = [loads.start(wz_o, both)]
    for h in range(2):
        rows_here = pl.ds(h * length, length)
        weight_loads.append(
            loads.start(wxd_o.at[rows_here, pl.ds(inner, bd)], slope.at[:, pl.ds(h * bd, bd)])
        )
    inverse_in = dtin
    weight_loads.append(loads.start(inverse_o, inverse_in))

    def token_copy(i):
        return pltpu.make_async_copy(
            tok.at[:, pl.ds(pl.multiple_of(line.order(i) * own, own), own)],
            normed.at[:, pl.ds(pl.multiple_of(inner + (i % 2) * own, own), own)], token_sems.at[i],
        )

    token_copy(0).start()
    token_copy(1).start()
    scatter.finish(stage_b)
    stores.start(stage_b, dwout_o)
    for h in range(2):
        weight_loads.append(
            loads.start(wxd_o.at[pl.ds(h * length, length), pl.ds(0, inner)], wout.at[:, pl.ds(h * inner, inner)])
        )
    load_xin.wait()

    def conv_tick(b):
        @pl.when(b % 2 == 1)
        def _():
            line.inject(9 + b // 2)
            line.forward(6 + b // 2, 1)

    convolve_back(xin, gpre, taps, pos, rpos, xd, csums, conv_tick)
    stores.start(xd, low_xd_o)
    for copy in weight_loads:
        copy.wait()
    stat[...] = jnp.zeros_like(stat)
    half = own // 2

    def part_copy(i, h):
        column = pl.multiple_of(line.order(i) * own + h * half, half)
        return pltpu.make_async_copy(
            cores.at[(i % 2) * 2 + h], part_o.at[:, pl.ds(column, half)], part_sems.at[i, h]
        )

    def grad_quarter(i, carry):
        q = line.order(i)
        columns = pl.ds(pl.multiple_of(q * own, own), own)
        low = pl.ds(pl.multiple_of((q % 2) * own, own), own)
        high = q // 2
        x_columns = pl.ds(pl.multiple_of(high * inner, inner), inner)
        bd_columns = pl.ds(pl.multiple_of(high * bd, LANES), bd)
        token_columns = pl.ds(pl.multiple_of(inner + (i % 2) * own, own), own)
        token_copy(i).wait()

        @pl.when(i >= 2)
        def _():
            for h in range(2):
                part_copy(jnp.maximum(i - 2, 0), h).wait()

        for r in range(0, length, 256):
            rows = slice(r, r + 256)
            here = mm_nt(low_gate[rows, :], both[columns, :])
            here = here + mm_nt(xd[rows, :inner], wout[low, x_columns])
            here = here + mm_nt(xd[rows, inner:], slope[low, bd_columns])
            for h in range(2):
                cores[(i % 2) * 2 + h, rows, :] = here[:, h * half : (h + 1) * half].astype(bf16)
            along = here * (normed[rows, token_columns].astype(f32) * inverse_in[rows, :1])
            folded = fold(along)
            if r == 0:
                colacc[:, columns] = folded
            else:
                colacc[:, columns] += folded
            along = along * gain[:, columns]
            sum_lanes = along[:, :LANES]
            for c in range(LANES, own, LANES):
                sum_lanes = sum_lanes + along[:, c : c + LANES]
            stat[rows, :] += sum_lanes
        for h in range(2):
            part_copy(i, h).start()

        @pl.when(i < 2)
        def _():
            token_copy(jnp.minimum(i + 2, n - 1)).start()

        @pl.when(i == 0)
        def _():
            line.inject(11)

        return carry

    lax.fori_loop(0, n, grad_quarter, 0)
    put_rows(rows_o)
    load_own.wait()

    def last(t, carry):
        line.finish(t)
        value = (token_own[line.rows(t), :].astype(f32) + total[...]).astype(bf16)
        for h in range(2):
            wholes[h, line.rows(t), :] = value[:, h * half : (h + 1) * half]
        return carry

    lax.fori_loop(0, line.blocks, last, 0)
    for h in range(2):
        stores.start(wholes.at[h], out_o.at[:, pl.ds(h * half, half)])
    line.drain()
    for i in range(2, n):
        for h in range(2):
            part_copy(i, h).wait()
    for copy in stores.pairs:
        if not any(copy is done for done in (store_normed, store_inverse, store_xin, store_wxd, store_wz)):
            copy.wait()


def input_kernel(
    tok, inverse, gain, normed, low_gate, low_xd, part_o, cot, rows_o, colacc, csums, sums, dsums,
    dwz_o, dwx_o, grad_o, dwbc, dwdt, conv_x, conv_x_bias, conv_bc, conv_bc_bias, dt_bias, a_rate, d_skip, in_gain,
    out_gain,
    dwz, dwxd, grad, smalls, spread, bc_turned, bc_own, bc_slots,
    v_inverse, v_normed, v_gate, v_xd, v_cot, v_tok, v_colacc, v_csums, v_sums, v_dsums,
    part, slots, total, z_grads, z_cores, z_parts, z_wholes, x_grads, x_cores, x_parts, x_wholes,
    rows_slots, dp_in, mp_in, turned,
    load_sems, part_sems, line_send, line_recv, z_core_send, z_core_recv, z_ring_send, z_ring_recv,
    x_core_send, x_core_recv, x_ring_send, x_ring_recv,
    rows_send, rows_recv, dp_send, dp_recv, mp_send, mp_recv, bc_send, bc_recv,
):
    ring = Ring()
    met = greet(ring, True)
    loads = Loads(load_sems)
    n = lax.axis_size("mp")
    z = lax.axis_index("mp")
    size = lax.axis_size("dp")
    length, features = part.shape
    inner = v_gate.shape[1]
    width = v_csums.shape[1]
    heads, per = dwdt.shape[0], dwbc.shape[0]
    own = features // n

    def quarter_columns(q):
        return pl.ds(pl.multiple_of(q * own, own), own)

    line = Line(
        lambda t, q: part.at[pl.ds(pl.multiple_of(t * BLOCK, BLOCK), BLOCK), quarter_columns(q)],
        lambda side, place, k: slots.at[side, k], length // BLOCK, (line_send, line_recv), total, 2,
    )

    def part_copy(i):
        columns = quarter_columns(line.order(i))
        return pltpu.make_async_copy(part_o.at[:, columns], part.at[:, columns], part_sems.at[i])

    load_rows = loads.start(rows_o, rows_slots.at[0])
    part_copy(0).start()

    def rows_copy(i):
        return remote(
            rows_slots.at[0], rows_slots.at[i], rows_send.at[i - 1], rows_recv.at[i - 1], mp=(z + i) % n
        )

    load_rows.wait()
    met()
    for i in range(1, n):
        rows_copy(i).start()
    part_copy(0).wait()
    line.inject(0)
    line.inject(1)
    for i in range(1, n):
        part_copy(i).start()
    load_gate, load_normed, load_xd = [
        loads.start(source, target) for source, target in ((low_gate, v_gate), (normed, v_normed), (low_xd, v_xd))
    ]
    load_sums = [
        loads.start(source, target)
        for source, target in ((colacc, v_colacc), (csums, v_csums), (sums, v_sums), (dsums, v_dsums))
    ]
    own_columns = quarter_columns(z)
    later = [
        loads.start(source, target)
        for source, target in (
            (cot.at[:, own_columns], v_cot), (tok.at[:, own_columns], v_tok), (inverse, v_inverse),
        )
    ]

    gain_width = features // 8

    def dp_copy(i):
        return remote(
            smalls, dp_in.at[i - 1], dp_send.at[i - 1], dp_recv.at[i - 1], dp=(ring.me + i) % size
        )

    def mp_copy(i):
        return remote(
            smalls.at[:, pl.ds(inner, width - inner + gain_width)], mp_in.at[i - 1],
            mp_send.at[i - 1], mp_recv.at[i - 1], mp=(z + i) % n,
        )

    for copy in load_sums:
        copy.wait()
    smalls[...] = jnp.zeros_like(smalls)
    for k in range(CONV + 1):
        smalls[k : k + 1, :width] = jnp.sum(v_csums[8 * k : 8 * k + 8, :], axis=0, keepdims=True)
    for k in range(2):
        smalls[CONV + 1 + k : CONV + 2 + k, :inner] = jnp.sum(v_sums[8 * k : 8 * k + 8, :], axis=0, keepdims=True)
        smalls[7:8, k * LANES : (k + 1) * LANES] = jnp.sum(v_dsums[8 * k : 8 * k + 8, :], axis=0, keepdims=True)
    for k in range(8):
        columns = slice(k * gain_width, (k + 1) * gain_width)
        smalls[k : k + 1, width:] = jnp.sum(v_colacc[:, columns], axis=0, keepdims=True)
    for i in range(1, size):
        dp_copy(i).start()
    shard = dwz.shape[0]
    z_scatter = Scatter(
        ring, lambda r: z_grads.at[pl.ds(pl.multiple_of(r * shard, shard), shard), :], z_cores, z_parts, z_wholes,
        (z_core_send, z_core_recv, z_ring_send, z_ring_recv),
    )
    x_scatter = Scatter(
        ring, lambda r: x_grads.at[pl.ds(pl.multiple_of(r * shard, shard), shard), :], x_cores, x_parts, x_wholes,
        (x_core_send, x_core_recv, x_ring_send, x_ring_recv),
    )

    def weight(j, right, grads):
        for c in range(0, 2 * shard, shard):
            rows = pl.ds(pl.multiple_of(j * 2 * shard + c, shard), shard)
            left = v_normed[:, rows]
            for at, w in tiles(grads.shape[1], 512):
                grads[rows, at : at + w] = mm_tn(left, right[:, at : at + w]).astype(bf16)

    load_gate.wait()
    load_normed.wait()

    def z_weight(j, carry):
        weight(j, v_gate, z_grads)
        z_scatter.start(j)
        return carry

    lax.fori_loop(0, 4, z_weight, 0)
    for i in range(1, n):
        part_copy(i).wait()
    line.inject(2)
    line.forward(0, 1)
    load_xd.wait()

    def x_weight(j, carry):
        weight(j, v_xd, x_grads)
        x_scatter.start(j)

        @pl.when(j == 1)
        def _():
            z_scatter.first()

        @pl.when(j % 2 == 1)
        def _():
            line.inject(3 + j // 2)
            line.forward(1 + j // 2, 1)

        return carry

    lax.fori_loop(0, 4, x_weight, 0)
    line.forward(0, 2)
    z_scatter.second()
    line.inject(5)
    line.forward(3, 1)
    line.forward(1, 2)
    x_scatter.first()
    line.inject(6)
    line.forward(4, 1)
    line.forward(2, 2)
    for i in range(1, size):
        dp_copy(i).wait()
    smalls[...] += functools.reduce(lambda a, b: a + b, [dp_in[i] for i in range(size - 1)])
    for i in range(1, n):
        mp_copy(i).start()
    line.inject(7)
    line.forward(5, 1)
    line.forward(3, 2)
    z_scatter.finish(dwz)
    store_z = loads.start(dwz, dwz_o)
    x_scatter.second()
    line.inject(8)
    line.forward(6, 1)
    line.inject(9)
    line.forward(7, 1)
    x_scatter.finish(dwxd)

    bc_turned[...] = dwxd[:, inner:width].T
    bc_own[...] = bc_turned[...].astype(bf16)

    def weight_copy(i):
        other = (z + i) % n
        return remote(
            bc_own.at[pl.ds(pl.multiple_of(other * per, per), per), :], bc_slots.at[i - 1],
            bc_send.at[i - 1], bc_recv.at[i - 1], mp=other,
        )

    for i in range(1, n):
        weight_copy(i).start()
    line.inject(10)
    store_x = loads.start(dwxd.at[:, pl.ds(0, inner)], dwx_o)
    dwdt[...] = dwxd[:, width:].T[:heads]
    for i in range(1, n):
        rows_copy(i).wait()
        mp_copy(i).wait()
    line.inject(11)
    smalls[:, inner:] += functools.reduce(lambda a, b: a + b, [mp_in[i] for i in range(n - 1)])
    share = LANES // per

    def mine(v):
        turns = [v] + [pltpu.roll(v, LANES - k * per, 1) for k in range(1, share)]
        which = jnp.full(v.shape, z % share, jnp.int32)
        return functools.reduce(lambda a, k: jnp.where(which == k, turns[k], a), range(1, share), turns[0])

    lanes = pl.ds(pl.multiple_of(inner + (z // share) * LANES, LANES), LANES)
    conv_x[...] = smalls[:CONV, :inner]
    conv_x_bias[...] = smalls[CONV : CONV + 1, :inner]
    taps = mine(smalls[:8, lanes])
    conv_bc[...] = taps[:CONV, :per]
    conv_bc_bias[...] = taps[CONV : CONV + 1, :per]
    out_gain[...] = smalls[5:6, :inner]
    fill_spread(spread)
    d_skip[...] = gather_heads(smalls[0:8, :inner], spread[...])[6:7, :heads]
    dt_bias[...] = smalls[7:8, :heads]
    a_rate[...] = smalls[7:8, LANES : LANES + heads]
    rows_own = own // gain_width
    for k in range(rows_own):
        in_gain[:, k * gain_width : (k + 1) * gain_width] = smalls[
            pl.ds(z * rows_own + k, 1), width : width + gain_width
        ]
    for copy in later:
        copy.wait()
    means = functools.reduce(lambda a, b: a + b, [rows_slots[i] for i in range(n)]) / features
    rows_slots[0] = means

    def last(t, carry):
        line.finish(t)
        rows = line.rows(t)
        lines = BLOCK // LANES
        row = jnp.concatenate([rows_slots[0, pl.ds(t * lines + j, 1), :] for j in range(lines)], axis=1)
        turned[...] = jnp.broadcast_to(row, turned.shape)
        mean = turned[...].T
        for c in range(0, own, LANES):
            columns = slice(c, c + LANES)
            hat = v_tok[rows, columns].astype(f32) * v_inverse[rows, :]
            gain_here = gain[:, pl.ds(pl.multiple_of(z * own + c, LANES), LANES)]
            change = v_inverse[rows, :] * (total[:, columns] * gain_here - hat * mean)
            grad[rows, columns] = (v_cot[rows, columns].astype(f32) + change).astype(bf16)
        return carry

    lax.fori_loop(0, line.blocks, last, 0)
    store_grad = loads.start(grad, grad_o)
    for i in range(1, n):
        weight_copy(i).wait()
    dwbc[...] = functools.reduce(
        lambda a, b: a + b, [bc_slots[i].astype(f32) for i in range(n - 1)],
        bc_turned[pl.ds(pl.multiple_of(z * per, per), per), :],
    )
    line.drain()
    for copy in (store_z, store_x, store_grad):
        copy.wait()


def hand_on_kernel(*refs):
    count = (len(refs) - 2) // 3
    sources, targets, buffers = refs[:count], refs[count : 2 * count], refs[2 * count : 3 * count]
    into, out = refs[-2:]
    there = [pltpu.make_async_copy(sources[k], buffers[k], into.at[k]) for k in range(count)]
    back = [pltpu.make_async_copy(buffers[k], targets[k], out.at[k]) for k in range(count)]
    for copy in there:
        copy.start()
    for k in range(count):
        there[k].wait()
        back[k].start()
    for copy in back:
        copy.wait()


def hand_on(*arrays):
    kinds = [(v.shape, v.dtype) for v in arrays]
    return call(
        hand_on_kernel, kinds, kinds, 0, *arrays,
        places="a" * len(arrays), sems=[(len(arrays),)] * 2, far=len(arrays),
    )


def call(kernel, outs, scratch, smem, *operands, places=None, sems=(), collective=None, far=0):
    spaces = {"s": pltpu.SMEM, "v": pltpu.VMEM, "a": pl.ANY}
    if places is None:
        places = "s" * smem + "v" * (len(operands) - smem)
    extra = {} if collective is None else dict(collective_id=collective, has_side_effects=True)
    return pl.pallas_call(
        kernel,
        out_shape=[jax.ShapeDtypeStruct(shape, kind) for shape, kind in outs],
        in_specs=[pl.BlockSpec(memory_space=spaces[c]) for c in places],
        out_specs=[pl.BlockSpec(memory_space=pl.ANY if i < far else pltpu.VMEM) for i in range(len(outs))],
        scratch_shapes=[pltpu.VMEM(shape, kind) for shape, kind in scratch]
        + [pltpu.SemaphoreType.DMA(shape) for shape in sems],
        compiler_params=pltpu.CompilerParams(vmem_limit_bytes=VMEM_LIMIT, **extra),
    )(*operands)


def per_device_any(
    tokens, cotangent, doc_lengths, w_z, w_x, w_bc, w_dt, w_out, conv_x, conv_x_bias, conv_bc,
    conv_bc_bias, dt_bias, a_rate, d_skip, input_norm_gain, out_gain,
):
    group = lax.axis_size("mp")
    rank = lax.axis_index("mp")
    T, D = tokens.shape
    inner, heads = w_x.shape[1], w_dt.shape[1]
    pair = 2 * STATE
    width = inner + pair
    wide = width + LANES
    own = D // group

    lengths = doc_lengths[0]
    starts = jnp.cumsum(lengths) - lengths
    packed = jnp.concatenate([w_bc, conv_bc, conv_bc_bias[None, :]], axis=0)
    packed = lax.all_gather(packed, "mp", axis=1, tiled=True)
    shard = w_bc.shape[0]
    w_bc_all, taps_bc = packed[:shard], packed[shard:]
    wxd = jnp.concatenate(
        [w_x.astype(bf16), w_bc_all.astype(bf16), w_dt.astype(bf16), jnp.zeros((shard, LANES - heads), bf16)],
        axis=1,
    )
    wxd = lax.all_gather(wxd, "dp", axis=0, tiled=True)
    wz = lax.all_gather(w_z.astype(bf16), "dp", axis=0, tiled=True)
    wout = lax.all_gather(w_out.astype(bf16), "dp", axis=1, tiled=True)
    taps = jnp.concatenate([jnp.concatenate([conv_x, conv_x_bias[None, :]], axis=0), taps_bc], axis=1)
    taps = jnp.pad(taps, ((0, 8 - CONV - 1), (0, 0)))
    crow = jnp.pad(jnp.stack([out_gain, jnp.repeat(d_skip, HEADDIM)]), ((0, 6), (0, 0)))
    dpar = jnp.pad(jnp.stack([dt_bias, a_rate]), ((0, 6), (0, LANES - heads)))
    gain = input_norm_gain[None, :]

    blocks = T // BLOCK
    (
        normed, inverse, xin, slope, gate, x_low, bc_low, step, sgdt, step_low, decay_low, ssd, states,
    ) = call(
        forward_kernel,
        [
            ((T, D), bf16), ((T, LANES), f32), ((T + 8, width), f32), ((T, width), bf16), ((T, inner), f32),
            ((T, inner), bf16), ((T, pair), bf16), ((T, LANES), f32), ((T, LANES), f32),
            ((T, LANES), bf16), ((T, LANES), bf16), ((T, inner), bf16), ((blocks, STATE, inner), bf16),
        ],
        [
            ((T, LANES), jnp.int32), ((LANES, inner), bf16), ((T, LANES), f32), ((STATE, inner), f32),
            ((BLOCK, inner), bf16), ((BLOCK, inner), f32), ((BLOCK, BLOCK), f32),
        ],
        1, starts, tokens, gain, wxd, wz, taps, dpar,
    )
    gnorm, stat = call(
        gate_kernel,
        [((T, inner), f32), ((T, LANES), f32)],
        [],
        0, cotangent, wout, gate, ssd, x_low, crow,
    )
    stat = jnp.pad(lax.psum(stat[:, :8], "mp"), ((0, 0), (0, LANES - 8)))
    branch, dwout, dwz, low_gate, gs, sums = call(
        functools.partial(middle_kernel, width=inner * group),
        [
            ((T, D), bf16), ((inner, D), bf16), ((D, inner), bf16), ((T, inner), bf16), ((T, inner), bf16),
            ((16, inner), f32),
        ],
        [((T, inner), bf16)],
        0, cotangent, wout, normed, gate, x_low, ssd, gnorm, crow, stat,
    )
    low_xd, csums, dsums = call(
        backward_kernel,
        [((T, wide), bf16), ((8 * CONV + 8, width), f32), ((16, LANES), f32)],
        [
            ((T, LANES), jnp.int32), ((T, LANES), jnp.int32), ((LANES, inner), bf16), ((T + 8, width), f32),
            ((STATE, inner), f32), ((BLOCK, inner), bf16), ((BLOCK, inner), f32), ((BLOCK, BLOCK), f32),
            ((BLOCK, BLOCK), f32),
        ],
        1, starts, xin, slope, x_low, bc_low, step, sgdt, step_low, decay_low, ssd, states, gs, taps, crow,
        dpar,
    )
    dwxd, gfull, rowdot = call(
        last_kernel,
        [((D, wide), bf16), ((T, D), bf16), ((T, LANES), f32)],
        [],
        0, tokens, inverse, gain, normed, low_gate, low_xd, wz, wxd,
    )

    def scatter(v, axis, dim):
        return lax.psum_scatter(v, axis, scatter_dimension=dim, tiled=True)

    token_own = lax.dynamic_slice_in_dim(tokens, rank * own, own, 1).astype(f32)
    output = (token_own + scatter(branch, "mp", 1).astype(f32)).astype(bf16)
    w_out_grad = scatter(dwout, "dp", 1).astype(f32)
    w_z_grad = scatter(dwz, "dp", 0).astype(f32)
    dwxd_own = scatter(dwxd, "dp", 0)
    w_x_grad = dwxd_own[:, :inner].astype(f32)
    w_dt_grad = dwxd_own[:, width : width + heads].astype(f32)
    w_bc_grad = scatter(dwxd_own[:, inner:width], "mp", 1).astype(f32)

    g_own = scatter(gfull, "mp", 1).astype(f32)
    gain_own = lax.dynamic_slice_in_dim(input_norm_gain, rank * own, own, 0)
    row_mean = (lax.psum(rowdot[:, 0], "mp") / D)[:, None]
    inv = inverse[:, :1]
    hat = token_own * inv
    cot_own = lax.dynamic_slice_in_dim(cotangent, rank * own, own, 1).astype(f32)
    input_grad = (cot_own + inv * (g_own * gain_own - hat * row_mean)).astype(bf16)
    in_gain = jnp.sum(g_own * hat, axis=0)

    csums = jnp.sum(csums.reshape(CONV + 1, 8, width), axis=1)
    sums = jnp.sum(sums.reshape(2, 8, inner), axis=1)
    dsums = jnp.sum(dsums.reshape(2, 8, LANES), axis=1)[:, :heads]
    csums_bc = scatter(csums[:, inner:], "mp", 1)
    conv_grad, conv_bc_grad, sums, dsums, in_gain = lax.psum(
        (csums[:, :inner], csums_bc, sums, dsums, in_gain), "dp"
    )
    d_skip_grad = jnp.sum(sums[1].reshape(heads, HEADDIM), axis=1)
    return (
        output, input_grad, w_z_grad, w_x_grad, w_bc_grad, w_dt_grad, w_out_grad,
        conv_grad[:CONV], conv_grad[CONV], conv_bc_grad[:CONV], conv_bc_grad[CONV],
        dsums[0], dsums[1], d_skip_grad, in_gain, sums[0],
    )


def per_device(
    tokens, cotangent, doc_lengths, w_z, w_x, w_bc, w_dt, w_out, conv_x, conv_x_bias, conv_bc,
    conv_bc_bias, dt_bias, a_rate, d_skip, input_norm_gain, out_gain,
):
    group, size = lax.axis_size("mp"), lax.axis_size("dp")
    T, D = tokens.shape
    shard, inner = w_x.shape
    heads, per = w_dt.shape[1], w_bc.shape[1]
    pair = per * group
    width = inner + pair
    wide = width + LANES
    own = D // group
    columns = w_out.shape[1]
    blocks = T // BLOCK
    messages = blocks * (group - 1)

    def row(v):
        return v[None, :]

    (
        normed, _, _, _, low_gate, low_xd, output, w_out_grad, inverse, part, csums, dsums, sums, rows, colacc,
    ) = call(
        trunk_kernel,
        [
            ((T, D), bf16), ((T + 8, width), f32), ((D, wide), bf16), ((D, inner), bf16), ((T, inner), bf16),
            ((T, wide), bf16), ((T, own), bf16), ((inner, columns), f32), ((T, LANES), f32), ((T, D), bf16),
            ((8 * CONV + 8, width), f32), ((16, LANES), f32), ((16, inner), f32), ((T // LANES, LANES), f32),
            ((8, D), f32),
        ],
        [
            ((T, D), bf16), ((inner, columns), f32), ((T, D), bf16), ((T + 8, width), f32),
            ((T + 8, width), f32), ((T, width), bf16), ((2 * T, inner), bf16),
            ((blocks, STATE, inner), bf16), ((D, wide), bf16), ((D, inner), bf16), ((inner, D), bf16),
            ((T, pair), bf16), ((T, LANES), bf16), ((T, LANES), bf16), ((T, LANES), f32),
            ((8, width), f32), ((8, inner), f32), ((8, LANES), f32),
            ((group, shard, LANES), bf16), ((group, 8, LANES), f32), ((group, T // LANES, LANES), f32),
            ((group, T // LANES, LANES), f32), ((T, LANES), f32), ((LANES, BLOCK), f32),
            ((T, LANES), jnp.int32), ((T, LANES), jnp.int32), ((LANES, inner), bf16), ((T, LANES), f32),
            ((STATE, inner), f32), ((BLOCK, inner), bf16), ((BLOCK, inner), f32), ((BLOCK, BLOCK), f32),
            ((BLOCK, BLOCK), f32), ((2 * blocks, BLOCK, own), bf16),
            ((4, inner, columns), bf16), ((2, inner // 2, columns), bf16), ((2, inner, columns), bf16),
        ],
        0, doc_lengths, tokens, cotangent, w_x, w_z, w_out, w_bc.T, w_dt.T, conv_x, row(conv_x_bias), conv_bc,
        row(conv_bc_bias), row(dt_bias), row(a_rate), row(d_skip), row(input_norm_gain), row(out_gain),
        places="s" + "a" * 5 + "v" * 11,
        sems=[
            (13,), (10,), (group,), (group, 2), (4, 4), (4, 4), (4, 4), (4, 4), (4 * group - 4,), (4 * group - 4,),
            (2, messages), (2, messages), (4,), (4,), (4,), (4,),
        ],
        collective=0,
        far=10,
    )
    w_z_grad, w_x_grad, input_grad, w_bc_grad, w_dt_grad, *small_grads = call(
        input_kernel,
        [
            ((shard, inner), f32), ((shard, inner), f32), ((T, own), bf16), ((per, shard), f32),
            ((heads, shard), f32), ((CONV, inner), f32), ((1, inner), f32), ((CONV, per), f32), ((1, per), f32),
            ((1, heads), f32), ((1, heads), f32), ((1, heads), f32), ((1, own), f32), ((1, inner), f32),
        ],
        [
            ((shard, inner), f32), ((shard, wide), f32), ((T, own), bf16), ((8, width + D // 8), f32),
            ((LANES, inner), bf16), ((pair, shard), f32), ((pair, shard), bf16), ((group - 1, per, shard), bf16),
            ((T, LANES), f32), ((T, D), bf16), ((T, inner), bf16), ((T, wide), bf16), ((T, own), bf16),
            ((T, own), bf16), ((8, D), f32), ((8 * CONV + 8, width), f32), ((16, inner), f32), ((16, LANES), f32),
            ((T, D), bf16), ((2, messages, BLOCK, own), bf16), ((BLOCK, own), f32),
            ((D, inner), bf16), ((4, shard, inner), bf16), ((2, shard // 2, inner), bf16), ((2, shard, inner), bf16),
            ((D, wide), bf16), ((4, shard, wide), bf16), ((2, shard // 2, wide), bf16), ((2, shard, wide), bf16),
            ((group, T // LANES, LANES), f32), ((size - 1, 8, width + D // 8), f32),
            ((group - 1, 8, pair + D // 8), f32), ((LANES, BLOCK), f32),
        ],
        0, tokens, inverse, row(input_norm_gain), normed, low_gate, low_xd, part, cotangent, rows, colacc, csums,
        sums, dsums,
        places="aav" + "a" * 10,
        sems=[
            (14,), (group,), (2, messages), (2, messages), (4,), (4,), (4,), (4,), (4,), (4,), (4,), (4,),
            (group - 1,), (group - 1,), (size - 1,), (size - 1,), (group - 1,), (group - 1,),
            (group - 1,), (group - 1,),
        ],
        collective=2,
        far=3,
    )
    (
        output, input_grad, w_z_grad, w_x_grad, w_bc_grad, w_dt_grad, w_out_grad, conv_x_grad, conv_x_bias_grad,
        conv_bc_grad, conv_bc_bias_grad, dt_bias_grad, a_rate_grad, d_skip_grad, in_gain_grad, out_gain_grad,
    ) = hand_on(output, input_grad, w_z_grad, w_x_grad, w_bc_grad, w_dt_grad, w_out_grad, *small_grads)
    return (
        output, input_grad, w_z_grad, w_x_grad, w_bc_grad.T, w_dt_grad.T, w_out_grad,
        conv_x_grad, conv_x_bias_grad[0], conv_bc_grad, conv_bc_bias_grad[0], dt_bias_grad[0], a_rate_grad[0],
        d_skip_grad[0], in_gain_grad[0], out_gain_grad[0],
    )


def solution(mesh):
    row, block, column = P("dp", None), P("dp", "mp"), P("mp")
    return jax.shard_map(
        per_device if (mesh.shape["dp"], mesh.shape["mp"]) == (8, 4) else per_device_any,
        mesh=mesh,
        in_specs=(
            row, row, row, block, block, block, block, P("mp", "dp"), P(None, "mp"), column,
            P(None, "mp"), column, column, column, column, P(), column,
        ),
        out_specs=(
            block, block, block, block, block, block, P("mp", "dp"), P(None, "mp"), column,
            P(None, "mp"), column, column, column, column, column, column,
        ),
        check_vma=False,
    )
```

```python
import functools

import jax
import jax.numpy as jnp
from jax import lax
from jax.experimental import pallas as pl
from jax.experimental.pallas import tpu as pltpu
from jax.sharding import PartitionSpec as P

HEADDIM = 64
STATE = 128
CONV = 4
BLOCK = 256
DOCS = 5
LANES = 128
EPS = 1e-05
f32 = jnp.float32
bf16 = jnp.bfloat16
VMEM_LIMIT = 127 * 2**19


def mm(a, b):
    return jnp.dot(a, b, preferred_element_type=f32)


def mm_nt(a, b):
    return lax.dot_general(a, b, (((1,), (1,)), ((), ())), preferred_element_type=f32)


def mm_tn(a, b):
    return lax.dot_general(a, b, (((0,), (0,)), ((), ())), preferred_element_type=f32)


def halves(v):
    high = v.astype(bf16)
    return high, (v - high.astype(f32)).astype(bf16)


def expand(v, spread):
    high, rest = halves(v)
    return mm(high, spread) + mm(rest, spread)


def gather_heads(v, spread):
    high, rest = halves(v)
    return mm_nt(high, spread) + mm_nt(rest, spread)


def logistic(v):
    return 1.0 / (1.0 + jnp.exp(-v))


def tiles(total, size):
    return [(at, min(size, total - at)) for at in range(0, total, size)]


def fold(v):
    return jnp.sum(v.reshape(v.shape[0] // 8, 8, v.shape[1]), axis=0)


def doc_of(starts, place):
    count = (place >= starts[0]).astype(jnp.int32)
    for k in range(1, DOCS):
        count = count + (place >= starts[k]).astype(jnp.int32)
    return count


def fill_spread(spread):
    rows, columns = spread.shape
    head = lax.broadcasted_iota(jnp.int32, (rows, columns), 0)
    channel = lax.broadcasted_iota(jnp.int32, (rows, columns), 1)
    low = head * HEADDIM
    spread[...] = jnp.where((channel >= low) & (channel < low + HEADDIM), 1.0, 0.0).astype(bf16)


def fill_positions(starts, pos, rpos):
    length = pos.shape[0]

    def body(i, carry):
        at = pl.multiple_of(i * BLOCK, BLOCK)
        place = lax.broadcasted_iota(jnp.int32, (BLOCK, LANES), 0) + at
        begin = jnp.zeros_like(place)
        end = jnp.full_like(place, length)
        for k in range(DOCS):
            begin = jnp.maximum(begin, jnp.where(place >= starts[k], starts[k], 0))
            end = jnp.minimum(end, jnp.where(place < starts[k], starts[k], length))
        pos[pl.ds(at, BLOCK), :] = place - begin
        if rpos is not None:
            rpos[pl.ds(at, BLOCK), :] = end - 1 - place
        return carry

    lax.fori_loop(0, length // BLOCK, body, 0)


def normalize(tok, gain, normed, stat):
    step = 64

    def body(i, carry):
        rows = pl.ds(pl.multiple_of(i * step, step), step)
        v = tok[rows, :].astype(f32)
        inverse = lax.rsqrt(jnp.mean(v * v, axis=1, keepdims=True) + EPS)
        normed[rows, :] = (v * inverse * gain[...]).astype(bf16)
        stat[rows, :] = jnp.broadcast_to(inverse, (step, LANES))
        return carry

    lax.fori_loop(0, tok.shape[0] // step, body, 0)


def project_x(normed, wxd, xin, dtin):
    length, width = normed.shape[0], xin.shape[1]
    xin[pl.ds(0, 8), :] = jnp.zeros((8, width), f32)
    rows = 512

    def body(i, carry):
        at = pl.multiple_of(i * rows, rows)
        left = normed[pl.ds(at, rows), :]
        for c, w in tiles(width, 512):
            xin[pl.ds(at + 8, rows), c : c + w] = mm(left, wxd[:, c : c + w])
        dtin[pl.ds(at, rows), :] = mm(left, wxd[:, width : width + LANES])
        return carry

    lax.fori_loop(0, length // rows, body, 0)


def convolve(xin, taps, pos, slope, x_low, bc_low):
    width, inner = xin.shape[1], x_low.shape[1]

    def tile(b, c, out, at):
        rows = pl.ds(pl.multiple_of(b * BLOCK, BLOCK), BLOCK)
        x = xin[pl.ds(pl.multiple_of(b * BLOCK, BLOCK), BLOCK + 8), pl.ds(c, LANES)]
        place = pos[rows, :]
        tap = taps[:, pl.ds(c, LANES)]
        pre = tap[CONV : CONV + 1] + tap[CONV - 1 : CONV] * x[8:]
        for lag in range(1, CONV):
            earlier = pltpu.roll(x, lag, 0)[8:]
            pre = pre + tap[CONV - 1 - lag : CONV - lag] * jnp.where(place >= lag, earlier, 0.0)
        sg = logistic(pre)
        slope[rows, pl.ds(c, LANES)] = (sg * (1.0 + pre * (1.0 - sg))).astype(bf16)
        out[rows, pl.ds(at, LANES)] = (pre * sg).astype(bf16)

    blocks = x_low.shape[0] // BLOCK
    xcols, bcols = inner // LANES, (width - inner) // LANES

    def x_body(i, carry):
        c = pl.multiple_of((i % xcols) * LANES, LANES)
        tile(i // xcols, c, x_low, c)
        return carry

    def bc_body(i, carry):
        c = pl.multiple_of((i % bcols) * LANES, LANES)
        tile(i // bcols, inner + c, bc_low, c)
        return carry

    lax.fori_loop(0, blocks * xcols, x_body, 0)
    lax.fori_loop(0, blocks * bcols, bc_body, 0)


def softplus(v):
    return jnp.maximum(v, 0.0) + jnp.log1p(jnp.exp(-jnp.abs(v)))


def steps(dtin, dpar, step, sgdt, step_low, decay_low):
    def body(i, carry):
        rows = pl.ds(pl.multiple_of(i * BLOCK, BLOCK), BLOCK)
        v = dtin[rows, :] + dpar[0:1, :]
        soft = softplus(v)
        if step is not None:
            step[rows, :] = soft
            sgdt[rows, :] = logistic(v)
        step_low[rows, :] = soft.astype(bf16)
        decay_low[rows, :] = (-dpar[1:2, :] * soft).astype(bf16)
        return carry

    lax.fori_loop(0, dtin.shape[0] // BLOCK, body, 0)


def block_marks(starts, b):
    at = b * BLOCK
    column = doc_of(starts, lax.broadcasted_iota(jnp.int32, (BLOCK, 1), 0) + at)
    row = doc_of(starts, lax.broadcasted_iota(jnp.int32, (1, BLOCK), 1) + at)
    before = doc_of(starts, at - 1)
    last = doc_of(starts, at + BLOCK - 1)
    return column, row, before, last


def block_decays(b, starts, decay_low, step_low, spread):
    rows = pl.ds(pl.multiple_of(b * BLOCK, BLOCK), BLOCK)
    column, row, before, last = block_marks(starts, b)
    i0 = lax.broadcasted_iota(jnp.int32, (BLOCK, BLOCK), 0)
    i1 = lax.broadcasted_iota(jnp.int32, (BLOCK, BLOCK), 1)
    lower = jnp.where(i0 >= i1, 1.0, 0.0).astype(bf16)
    cum = mm(lower, decay_low[rows, :])
    step_e = mm(step_low[rows, :], spread[...])
    cum_e = expand(jnp.exp(cum), spread[...])
    kept_e = jnp.where(before == last, cum_e[BLOCK - 1 : BLOCK], 0.0)
    in_e = jnp.where(column == before, cum_e, 0.0)
    out_e = expand(jnp.exp(cum[BLOCK - 1 : BLOCK] - cum), spread[...])
    out_e = jnp.where(column == last, out_e, 0.0)
    return cum, step_e, kept_e, in_e, out_e, column, row


def scan_forward(
    starts, x_low, bc_low, step_low, decay_low, ssd, states, spread, state, xs, yin, cbm, tick=None
):
    length, inner = x_low.shape
    state[...] = jnp.zeros_like(state)

    def body(b, carry):
        rows = pl.ds(pl.multiple_of(b * BLOCK, BLOCK), BLOCK)
        cum, step_e, kept_e, in_e, out_e, column, row = block_decays(
            b, starts, decay_low, step_low, spread
        )
        bm, cm = bc_low[rows, :STATE], bc_low[rows, STATE:]
        i0 = lax.broadcasted_iota(jnp.int32, (BLOCK, BLOCK), 0)
        i1 = lax.broadcasted_iota(jnp.int32, (BLOCK, BLOCK), 1)
        cbm[...] = jnp.where((column == row) & (i0 >= i1), mm_nt(cm, bm), 0.0)
        stepped = x_low[rows, :].astype(f32) * step_e
        xs[...] = stepped.astype(bf16)
        entering = state[...].astype(bf16)
        states[b] = entering
        yin[...] = in_e * mm(cm, entering)
        state[...] = kept_e * state[...] + mm_tn(bm, (stepped * out_e).astype(bf16))
        cum_t = cum.T
        first = lax.broadcasted_iota(jnp.int32, (BLOCK, LANES), 1) < HEADDIM
        for j in range(inner // LANES):
            cols = slice(j * LANES, (j + 1) * LANES)
            pair = xs[:, cols]
            part = []
            for h in (2 * j, 2 * j + 1):
                span = jnp.minimum(cum[:, h : h + 1] - cum_t[h : h + 1, :], 0.0)
                part.append(mm((jnp.exp(span) * cbm[...]).astype(bf16), pair))
            y = jnp.where(first, part[0], part[1]) + yin[:, cols]
            ssd[rows, cols] = y.astype(bf16)
        if tick is not None:
            tick(b)
        return carry

    lax.fori_loop(0, length // BLOCK, body, 0)


def project_rows(left, right, out, rows=512, columns=512):
    def body(i, carry):
        at = pl.ds(pl.multiple_of(i * rows, rows), rows)
        part = left[at, :]
        for c, w in tiles(out.shape[1], columns):
            out[at, c : c + w] = mm(part, right[:, c : c + w]).astype(out.dtype)
        return carry

    lax.fori_loop(0, out.shape[0] // rows, body, 0)


def back_rows(left, right, out, rows=512, columns=512):
    def body(i, carry):
        at = pl.ds(pl.multiple_of(i * rows, rows), rows)
        part = left[at, :]
        for c, w in tiles(out.shape[1], columns):
            out[at, c : c + w] = mm_nt(part, right[c : c + w, :]).astype(out.dtype)
        return carry

    lax.fori_loop(0, out.shape[0] // rows, body, 0)


def weight_rows(left, right, out, rows=256, columns=512):
    def body(i, carry):
        at = pl.ds(pl.multiple_of(i * rows, rows), rows)
        part = left[:, at]
        for c, w in tiles(out.shape[1], columns):
            out[at, c : c + w] = mm_tn(part, right[:, c : c + w]).astype(out.dtype)
        return carry

    lax.fori_loop(0, out.shape[0] // rows, body, 0)


def gate_sums(gate, ssd, x_low, gnorm, crow, stat):
    step, inner = 64, gate.shape[1]

    def body(i, carry):
        rows = pl.ds(pl.multiple_of(i * step, step), step)
        squares = jnp.zeros((step, 256), f32)
        crosses = jnp.zeros((step, 256), f32)
        for c in range(0, inner, 256):
            cols = slice(c, c + 256)
            g = gate[rows, cols]
            mixed = ssd[rows, cols].astype(f32) + crow[1:2, cols] * x_low[rows, cols].astype(f32)
            gated = mixed * (g * logistic(g))
            squares = squares + gated * gated
            crosses = crosses + gnorm[rows, cols] * crow[0:1, cols] * gated
        lane = lax.broadcasted_iota(jnp.int32, (step, LANES), 1)
        s1 = jnp.sum(squares, axis=1, keepdims=True)
        s2 = jnp.sum(crosses, axis=1, keepdims=True)
        stat[rows, :] = jnp.where(lane == 0, s1, jnp.where(lane == 1, s2, 0.0))
        return carry

    lax.fori_loop(0, gate.shape[0] // step, body, 0)


def gate_squares(gate, ssd, x_low, crow, stat):
    step, inner = 64, gate.shape[1]

    def body(i, carry):
        rows = pl.ds(pl.multiple_of(i * step, step), step)
        squares = jnp.zeros((step, 256), f32)
        for c in range(0, inner, 256):
            cols = slice(c, c + 256)
            g = gate[rows, cols]
            mixed = ssd[rows, cols].astype(f32) + crow[1:2, cols] * x_low[rows, cols].astype(f32)
            value = mixed * (g * logistic(g))
            squares = squares + value * value
        stat[rows, :] = squares[:, :LANES] + squares[:, LANES:]
        return carry

    lax.fori_loop(0, gate.shape[0] // step, body, 0)


def gate_norm(gate, ssd, x_low, inverse_out, crow, gn):
    step, inner = 64, gate.shape[1]

    def body(i, carry):
        rows = pl.ds(pl.multiple_of(i * step, step), step)
        inverse = inverse_out[rows, :1]
        for c in range(0, inner, 256):
            cols = slice(c, c + 256)
            g = gate[rows, cols]
            mixed = ssd[rows, cols].astype(f32) + crow[1:2, cols] * x_low[rows, cols].astype(f32)
            gn[rows, cols] = (mixed * (g * logistic(g)) * inverse * crow[0:1, cols]).astype(bf16)
        return carry

    lax.fori_loop(0, gate.shape[0] // step, body, 0)


def cross_sums(gnorm, gn, stat):
    step, inner = 64, gn.shape[1]

    def body(i, carry):
        rows = pl.ds(pl.multiple_of(i * step, step), step)
        total = jnp.zeros((step, 256), f32)
        for c in range(0, inner, 256):
            cols = slice(c, c + 256)
            total = total + gnorm[rows, cols] * gn[rows, cols].astype(f32)
        stat[rows, :] = total[:, :LANES] + total[:, LANES:]
        return carry

    lax.fori_loop(0, gn.shape[0] // step, body, 0)


def forward_kernel(
    starts, tok, gain, wxd, wz, taps, dpar,
    normed, inverse, xin, slope, gate, x_low, bc_low, step, sgdt, step_low, decay_low, ssd, states,
    pos, spread, dtin, state, xs, yin, cbm,
):
    fill_spread(spread)
    fill_positions(starts, pos, None)
    normalize(tok, gain, normed, inverse)
    project_x(normed, wxd, xin, dtin)
    convolve(xin, taps, pos, slope, x_low, bc_low)
    steps(dtin, dpar, step, sgdt, step_low, decay_low)
    scan_forward(starts, x_low, bc_low, step_low, decay_low, ssd, states, spread, state, xs, yin, cbm)
    project_rows(normed, wz, gate)


def gate_kernel(cot, wout, gate, ssd, x_low, crow, gnorm, stat):
    back_rows(cot, wout, gnorm)
    gate_sums(gate, ssd, x_low, gnorm, crow, stat)


def gate_backward(gate, ssd, x_low, gnorm, crow, stat, width, gn, low_gate, gs, sums, known=None):
    step, inner = 64, ssd.shape[1]
    sums[...] = jnp.zeros_like(sums)

    def body(i, carry):
        rows = pl.ds(pl.multiple_of(i * step, step), step)
        if known is None:
            inverse = lax.rsqrt(stat[rows, 0:1] / width + EPS)
            mean = inverse * stat[rows, 1:2] / width
        else:
            inverse, mean = known[rows, :1], stat[rows, :1]
        for c in range(0, inner, 256):
            cols = slice(c, c + 256)
            g = gate[rows, cols]
            x = x_low[rows, cols].astype(f32)
            mixed = ssd[rows, cols].astype(f32) + crow[1:2, cols] * x
            sg = logistic(g)
            act = g * sg
            hat = mixed * act * inverse
            if gn is not None:
                gn[rows, cols] = (hat * crow[0:1, cols]).astype(bf16)
            gnorm_here = gnorm[rows, cols]
            grad = inverse * (gnorm_here * crow[0:1, cols] - hat * mean)
            grad_mixed = grad * act
            low_gate[rows, cols] = (grad * mixed * (sg * (1.0 + g * (1.0 - sg)))).astype(bf16)
            gs[rows, cols] = grad_mixed.astype(bf16)
            sums[0:8, cols] += fold(gnorm_here * hat)
            sums[8:16, cols] += fold(grad_mixed * x)
        return carry

    lax.fori_loop(0, ssd.shape[0] // step, body, 0)


def middle_kernel(
    cot, wout, normed, gate, x_low, ssd, gnorm, crow, stat,
    branch, dwout, dwz, low_gate, gs, sums,
    gn, *, width,
):
    gate_backward(gate, ssd, x_low, gnorm, crow, stat, width, gn, low_gate, gs, sums)
    project_rows(gn, wout, branch)
    weight_rows(gn, cot, dwout)
    weight_rows(normed, low_gate, dwz)


def scan_backward(
    starts, x_low, bc_low, step_low, decay_low, ssd, states, gs, slope, crow, step, sgdt, dpar,
    gpre, low_xd, dsums, spread, dstate, xs, gx, cbm, acc, tick=None,
):
    length, inner = x_low.shape
    width = gpre.shape[1]
    blocks = length // BLOCK
    dstate[...] = jnp.zeros_like(dstate)
    dsums[...] = jnp.zeros_like(dsums)
    gpre[pl.ds(length, 8), :] = jnp.zeros((8, width), f32)

    def body(i, carry):
        b = blocks - 1 - i
        rows = pl.ds(pl.multiple_of(b * BLOCK, BLOCK), BLOCK)
        cum, step_e, kept_e, in_e, out_e, column, row = block_decays(
            b, starts, decay_low, step_low, spread
        )
        bm, cm = bc_low[rows, :STATE], bc_low[rows, STATE:]
        i0 = lax.broadcasted_iota(jnp.int32, (BLOCK, BLOCK), 0)
        i1 = lax.broadcasted_iota(jnp.int32, (BLOCK, BLOCK), 1)
        linked = (column == row) & (i0 <= i1)
        cbm[...] = jnp.where(linked, mm_nt(bm, cm), 0.0)
        x = x_low[rows, :].astype(f32)
        stepped = x * step_e
        xs[...] = stepped.astype(bf16)
        cum_t = cum.T
        first = lax.broadcasted_iota(jnp.int32, (BLOCK, LANES), 1) < HEADDIM
        acc[...] = jnp.zeros_like(acc)
        for j in range(inner // LANES):
            cols = slice(j * LANES, (j + 1) * LANES)
            xpair, gpair = xs[:, cols], gs[rows, cols]
            none = jnp.zeros_like(xpair)
            part, total = [], None
            for k in range(2):
                h = 2 * j + k
                kernel = jnp.exp(jnp.minimum(cum_t[h : h + 1, :] - cum[:, h : h + 1], 0.0))
                part.append(mm((kernel * cbm[...]).astype(bf16), gpair))
                own = jnp.where(first, xpair, none) if k == 0 else jnp.where(first, none, xpair)
                here = kernel * mm_nt(own, gpair)
                total = here if total is None else total + here
            acc[...] += total
            gx[:, cols] = jnp.where(first, part[0], part[1])
        dstate_low = dstate[...].astype(bf16)
        entering = states[b]
        leaving = states[jnp.minimum(b + 1, blocks - 1)]
        end = jnp.sum(dstate[...] * leaving.astype(f32), axis=0, keepdims=True)
        g = gs[rows, :].astype(f32)
        g_in = (in_e * g).astype(bf16)
        raw = gx[...] + out_e * mm(bm, dstate_low)
        grad_x = (step_e * raw).astype(bf16).astype(f32)
        gpre[rows, :inner] = (grad_x + crow[1:2, :] * g) * slope[rows, :inner]
        pairs = jnp.where(linked, acc[...], 0.0).astype(bf16)
        db = mm(pairs, cm) + mm_nt((stepped * out_e).astype(bf16), dstate_low)
        dc = mm_tn(pairs, bm) + mm_nt(g_in, entering)
        gpre[rows, inner : inner + STATE] = db * slope[rows, inner : inner + STATE]
        gpre[rows, inner + STATE :] = dc * slope[rows, inner + STATE :]
        raw_x = x * raw
        grad_step = gather_heads(raw_x, spread[...]).astype(bf16).astype(f32)
        dcum = gather_heads(g * ssd[rows, :].astype(f32) - step_e * raw_x, spread[...])
        tail = gather_heads(jnp.broadcast_to(end, (8, inner)), spread[...])[0:1]
        upper = jnp.where(i0 <= i1, 1.0, 0.0).astype(bf16)
        high, rest = halves(dcum)
        later = mm(upper, high) + mm(upper, rest) + tail
        grad_decay = later.astype(bf16).astype(f32)
        total_step = grad_step - dpar[1:2, :] * grad_decay
        if sgdt is None:
            before_step = step[rows, :] + dpar[0:1, :]
            slope_here, step_here = logistic(before_step), softplus(before_step)
        else:
            slope_here, step_here = sgdt[rows, :], step[rows, :]
        grad_dt = total_step * slope_here
        low_xd[rows, width:] = grad_dt.astype(bf16)
        dsums[0:8, :] += fold(grad_dt)
        dsums[8:16, :] -= fold(grad_decay * step_here)
        dstate[...] = kept_e * dstate[...] + mm_tn(cm, g_in)
        if tick is not None:
            tick(i)
        return carry

    lax.fori_loop(0, blocks, body, 0)


def convolve_back(xin, gpre, taps, pos, rpos, low_xd, csums, tick=None):
    width = gpre.shape[1]
    columns = width // LANES
    csums[...] = jnp.zeros_like(csums)

    def body(b, j):
        at = pl.multiple_of(b * BLOCK, BLOCK)
        cols = pl.ds(pl.multiple_of(j * LANES, LANES), LANES)
        rows = pl.ds(at, BLOCK)
        x = xin[pl.ds(at, BLOCK + 8), cols]
        g = gpre[pl.ds(at, BLOCK + 8), cols]
        here = g[:BLOCK]
        place, ahead = pos[rows, :], rpos[rows, :]
        tap = taps[:, cols]
        grad = tap[CONV - 1 : CONV] * here
        csums[pl.ds(8 * CONV, 8), cols] += fold(here)
        csums[pl.ds(8 * (CONV - 1), 8), cols] += fold(here * x[8:])
        for lag in range(1, CONV):
            k = CONV - 1 - lag
            later = pltpu.roll(g, BLOCK + 8 - lag, 0)[:BLOCK]
            earlier = pltpu.roll(x, lag, 0)[8:]
            grad = grad + tap[k : k + 1] * jnp.where(ahead >= lag, later, 0.0)
            csums[pl.ds(8 * k, 8), cols] += fold(here * jnp.where(place >= lag, earlier, 0.0))
        low_xd[rows, cols] = grad.astype(bf16)

    def block(b, carry):
        lax.fori_loop(0, columns, lambda j, c: (body(b, j), c)[1], 0)
        if tick is not None:
            tick(b)
        return carry

    lax.fori_loop(0, (xin.shape[0] - 8) // BLOCK, block, 0)


def backward_kernel(
    starts, xin, slope, x_low, bc_low, step, sgdt, step_low, decay_low, ssd, states, gs, taps, crow, dpar,
    low_xd, csums, dsums,
    pos, rpos, spread, gpre, dstate, xs, gx, cbm, acc,
):
    fill_spread(spread)
    fill_positions(starts, pos, rpos)
    scan_backward(
        starts, x_low, bc_low, step_low, decay_low, ssd, states, gs, slope, crow, step, sgdt, dpar,
        gpre, low_xd, dsums, spread, dstate, xs, gx, cbm, acc,
    )
    convolve_back(xin, gpre, taps, pos, rpos, low_xd, csums)


def last_kernel(tok, inverse, gain, normed, low_gate, low_xd, wz, wxd, dwxd, gfull, rowdot):
    weight_rows(normed, low_xd, dwxd)
    rows = 256

    def body(i, carry):
        at = pl.ds(pl.multiple_of(i * rows, rows), rows)
        total = jnp.zeros((rows, 1), f32)
        for c, w in tiles(gfull.shape[1], 512):
            cols = slice(c, c + w)
            part = mm_nt(low_gate[at, :], wz[cols, :]) + mm_nt(low_xd[at, :], wxd[cols, :])
            gfull[at, cols] = part.astype(bf16)
            total = total + jnp.sum(part * gain[:, cols] * tok[at, cols].astype(f32), axis=1, keepdims=True)
        rowdot[at, :] = total * inverse[at, :]
        return carry

    lax.fori_loop(0, gfull.shape[0] // rows, body, 0)


MESH = pl.DeviceIdType.MESH


def remote(source, target, send, receive, **where):
    return pltpu.make_async_remote_copy(
        src_ref=source, dst_ref=target, send_sem=send, recv_sem=receive, device_id=where, device_id_type=MESH
    )


def add_into(target, source, rows=64):
    def body(i, carry):
        at = pl.ds(pl.multiple_of(i * rows, rows), rows)
        target[at, :] = (target[at, :].astype(f32) + source[at, :].astype(f32)).astype(target.dtype)
        return carry

    lax.fori_loop(0, target.shape[0] // rows, body, 0)


class Ring:
    def __init__(self):
        self.me = lax.axis_index("dp")
        self.core = self.me % 2
        chip = self.me // 2
        y = chip // 2
        self.pos = 2 * y + (chip + y) % 2
        self.partner = self.me + 1 - 2 * self.core
        self.right = self.at(self.pos + 1)
        self.left = self.at(self.pos + 3)
        self.across = self.at(self.pos + 2)

    def at(self, pos):
        pos = pos % 4
        y = pos // 2
        return (2 * y + (pos + y) % 2) * 2 + self.core


def greet(ring, everyone):
    barrier = pltpu.get_barrier_semaphore()
    n, z = lax.axis_size("mp"), lax.axis_index("mp")
    if everyone:
        size = lax.axis_size("dp")
        close = [(ring.me + i) % size for i in range(1, size)]
    else:
        close = [ring.partner, ring.right, ring.left]
    for other in close:
        pl.semaphore_signal(barrier, inc=1, device_id={"dp": other}, device_id_type=MESH)
    for i in range(1, n):
        pl.semaphore_signal(barrier, inc=1, device_id={"mp": (z + i) % n}, device_id_type=MESH)
    return lambda: pl.semaphore_wait(barrier, len(close) + n - 1)


class Scatter:
    def __init__(self, ring, shard, cores, parts, wholes, sems):
        self.ring, self.shard = ring, shard
        self.cores, self.parts, self.wholes = cores, parts, wholes
        self.core_send, self.core_recv, self.ring_send, self.ring_recv = sems
        self.half = cores.shape[1] // 2

    def upper(self, r):
        return self.shard(r).at[pl.ds(0, self.half), :]

    def lower(self, r):
        return self.shard(r).at[pl.ds(self.half, self.half), :]

    def core_copy(self, chip):
        ring = self.ring
        return remote(
            self.shard(2 * chip + 1 - ring.core), self.cores.at[chip],
            self.core_send.at[chip], self.core_recv.at[chip], dp=ring.partner,
        )

    def ring_copy(self, k):
        ring = self.ring
        source = (self.upper(ring.across), self.lower(ring.across), self.shard(ring.right), self.shard(ring.left))[k]
        target = (self.parts.at[0], self.parts.at[1], self.wholes.at[0], self.wholes.at[1])[k]
        return remote(
            source, target, self.ring_send.at[k], self.ring_recv.at[k], dp=(ring.right, ring.left)[k % 2]
        )

    def start(self, chip):
        self.core_copy(chip).start()

    def first(self):
        def body(chip, carry):
            self.core_copy(chip).wait_recv()
            add_into(self.shard(2 * chip + self.ring.core), self.cores.at[chip])
            return carry

        lax.fori_loop(0, 4, body, 0)
        self.ring_copy(0).start()
        self.ring_copy(1).start()

    def second(self):
        self.ring_copy(0).wait_recv()
        add_into(self.upper(self.ring.right), self.parts.at[0])
        self.ring_copy(2).start()
        self.ring_copy(1).wait_recv()
        add_into(self.lower(self.ring.left), self.parts.at[1])
        self.ring_copy(3).start()

    def finish(self, out, rows=64):
        self.ring_copy(2).wait_recv()
        self.ring_copy(3).wait_recv()
        own = self.shard(self.ring.me)

        def body(i, carry):
            at = pl.ds(pl.multiple_of(i * rows, rows), rows)
            out[at, :] = own[at, :].astype(f32) + self.wholes[0, at, :].astype(f32) + self.wholes[1, at, :].astype(f32)
            return carry

        lax.fori_loop(0, out.shape[0] // rows, body, 0)

        def done(chip, carry):
            self.core_copy(chip).wait_send()
            return carry

        lax.fori_loop(0, 4, done, 0)
        for k in range(4):
            self.ring_copy(k).wait_send()


class Line:
    def __init__(self, piece, slot, blocks, sems, total, depth):
        self.piece, self.slot, self.blocks, self.total, self.depth = piece, slot, blocks, total, depth
        self.send, self.recv = sems
        self.n, self.z = lax.axis_size("mp"), lax.axis_index("mp")
        self.place = (self.z, self.n - 1 - self.z)

    def rows(self, t):
        return pl.ds(pl.multiple_of(t * BLOCK, BLOCK), BLOCK)

    def source(self, side, k):
        d = k // self.blocks
        return self.piece(k - d * self.blocks, self.n - 1 - d if side == 0 else d)

    def copy(self, side, place, k):
        return remote(
            self.source(side, k), self.slot(side, place + 1, k), self.send.at[side, k], self.recv.at[side, k],
            mp=self.z + 1 if side == 0 else self.z - 1,
        )

    def arrived(self, side, place, k):
        target = self.slot(side, place, k)
        remote(target, target, self.send.at[side, k], self.recv.at[side, k], mp=self.z).wait_recv()
        return target

    def inject(self, k):
        for side in range(2):
            @pl.when(self.place[side] == 0)
            def _():
                @pl.when(jnp.int32(k) >= self.depth)
                def _():
                    self.copy(side, 0, jnp.maximum(k - self.depth, 0)).wait_send()

                self.copy(side, 0, k).start()

    def forward(self, k, hop):
        for side in range(2):
            @pl.when(self.place[side] == hop)
            def _():
                add_into(self.source(side, k), self.arrived(side, hop, k))
                self.copy(side, hop, k).start()

    def finish(self, t):
        self.total[...] = self.piece(t, self.z)[...].astype(f32)
        for side in range(2):
            for place in range(1, self.n):
                @pl.when(self.place[side] == place)
                def _():
                    self.total[...] += self.arrived(side, place, (self.n - 1 - place) * self.blocks + t)[...].astype(f32)

    def drain(self):
        for side in range(2):
            for place in range(self.n - 1):
                count = (self.n - 1 - place) * self.blocks

                @pl.when(self.place[side] == place)
                def _():
                    def body(k, carry):
                        self.copy(side, place, k).wait_send()
                        return carry

                    lax.fori_loop(count - self.depth if place == 0 else 0, count, body, 0)

    def order(self, i):
        z = self.z
        far = jnp.where(z < 2, 3 - i, i)
        near = z + 1 - 2 * (z % 2)
        return jnp.where(i < 2, far, jnp.where(i == 2, near, z))


class Loads:
    def __init__(self, sems):
        self.sems, self.pairs = sems, []

    def start(self, source, target):
        i = len(self.pairs)
        copy = pltpu.make_async_copy(source, target, self.sems.at[i])
        copy.start()
        self.pairs.append(copy)
        return copy


class Gather:
    def __init__(self, ring, shard, rows, sems):
        self.ring, self.shard, self.half = ring, shard, rows // 2
        self.ring_send, self.ring_recv, self.core_send, self.core_recv = sems
        self.other = 1 - 2 * ring.core

    def ring_copy(self, k, source):
        ring = self.ring
        half = (0, 1, 1, 0, 0, 1)[k]
        piece = self.shard(source).at[pl.ds(half * self.half, self.half), :]
        return remote(
            piece, piece, self.ring_send.at[k], self.ring_recv.at[k], dp=(ring.right, ring.left)[k % 2]
        )

    def core_copy(self, k, source):
        return remote(
            self.shard(source), self.shard(source), self.core_send.at[k], self.core_recv.at[k], dp=self.ring.partner
        )

    def start(self):
        me = self.ring.me
        for k in range(4):
            self.ring_copy(k, me).start()
        self.core_copy(0, me).start()

    def second(self):
        left, right = self.ring.left, self.ring.right
        self.ring_copy(0, left).wait_recv()
        self.ring_copy(4, left).start()
        self.ring_copy(1, right).wait_recv()
        self.ring_copy(5, right).start()

    def beside(self):
        left, right = self.ring.left, self.ring.right
        self.ring_copy(2, left).wait_recv()
        self.core_copy(1, left).start()
        self.ring_copy(3, right).wait_recv()
        self.core_copy(2, right).start()

    def third(self):
        across = self.ring.across
        self.ring_copy(4, across).wait_recv()
        self.ring_copy(5, across).wait_recv()
        self.core_copy(3, across).start()

    def arrived(self, k):
        ring = self.ring
        source = (ring.me, ring.left, ring.right, ring.across)[k] + self.other
        self.core_copy(k, source).wait_recv()

    def drain(self):
        ring = self.ring
        for k, source in enumerate((ring.me, ring.me, ring.me, ring.me, ring.left, ring.right)):
            self.ring_copy(k, source).wait_send()
        for k, source in enumerate((ring.me, ring.left, ring.right, ring.across)):
            self.core_copy(k, source).wait_send()


def cast_into(target, source, rows=64):
    def body(i, carry):
        at = pl.ds(pl.multiple_of(i * rows, rows), rows)
        target[at, :] = source[at, :].astype(target.dtype)
        return carry

    lax.fori_loop(0, target.shape[0] // rows, body, 0)


def trunk_kernel(
    lengths, tok, cot, w_x, w_z, w_out, w_bc, w_dt, conv_x, conv_x_bias, conv_bc, conv_bc_bias, dt_bias, a_rate,
    d_skip, gain, out_gain,
    normed_o, xin_o, wxd_o, wz_o, low_gate_o, low_xd_o, out_o, dwout_o, inverse_o, part_o,
    csums_o, dsums_o, sums_o, rows_o, colacc_o,
    csums, dsums, sums, rows, colacc, v_tok, stage_b, normed, xin, first_wide, slope, both, states, wxd, wz, wout,
    bc_low, step_low, decay_low, inverse_out, taps, crow, dpar,
    bc_slots, tap_slots, row_slots, cross_slots, stat, turned,
    pos, rpos, spread, dtin, state, xs, wide, cbm, acc, near, cores, parts, wholes,
    load_sems, store_sems, token_sems, part_sems, out_sems, ring_send, ring_recv, core_send, core_recv, mp_send, mp_recv, line_send, line_recv,
    scatter_core_send, scatter_core_recv, scatter_ring_send, scatter_ring_recv,
):
    ring = Ring()
    loads, stores = Loads(load_sems), Loads(store_sems)
    load_x = loads.start(w_x, wide)
    met = greet(ring, False)
    n, z = lax.axis_size("mp"), lax.axis_index("mp")
    length, features = normed.shape
    x_low, ssd = both.at[pl.ds(0, length), :], both.at[pl.ds(length, length), :]
    stage_a = wide
    inverse = inverse_out
    inner, width = x_low.shape[1], xin.shape[1]
    own = features // n
    shard, column_shard = stage_a.shape[0], stage_b.shape[1]
    heads, per = w_dt.shape[0], w_bc.shape[0]
    load_tok = loads.start(tok, v_tok)
    load_out = loads.start(w_out, stage_b)
    starts = [jnp.int32(0)]
    for k in range(DOCS - 1):
        starts.append(starts[-1] + lengths[0, k])

    def exchange(k, i):
        slots = (bc_slots, tap_slots, row_slots, cross_slots)[k]
        at = k * (n - 1) + i - 1
        return remote(slots.at[0], slots.at[i], mp_send.at[at], mp_recv.at[at], mp=(z + i) % n)

    def rows_of(ref, low, high):
        def shard_of(r):
            return ref.at[pl.ds(pl.multiple_of(r * shard, shard), shard), pl.ds(low, high - low)]

        return shard_of

    def columns_of(r):
        return wout.at[:, pl.ds(pl.multiple_of(r * column_shard, column_shard), column_shard)]

    sems = [tuple(group.at[k] for group in (ring_send, ring_recv, core_send, core_recv)) for k in range(4)]
    get_x = Gather(ring, rows_of(wxd, 0, inner), shard, sems[0])
    get_bd = Gather(ring, rows_of(wxd, inner, wxd.shape[1]), shard, sems[1])
    get_z = Gather(ring, rows_of(wz, 0, inner), shard, sems[2])
    get_out = Gather(ring, columns_of, inner, sems[3])

    load_x.wait()
    cast_into(get_x.shard(ring.me), stage_a)
    met()
    get_x.start()
    turned[...] = jnp.zeros_like(turned)
    turned[:per, :] = w_bc[...]
    bc_slots[0] = turned[...].T.astype(bf16)
    tap_slots[0] = jnp.zeros_like(tap_slots[0])
    tap_slots[0, :CONV, :per] = conv_bc[...]
    tap_slots[0, CONV : CONV + 1, :per] = conv_bc_bias[...]
    turned[...] = jnp.zeros_like(turned)
    turned[:heads, :] = w_dt[...]
    own_rows = pl.ds(pl.multiple_of(ring.me * shard, shard), shard)
    wxd[own_rows, width:] = turned[...].T.astype(bf16)
    dpar[...] = jnp.zeros_like(dpar)
    dpar[0:1, :heads] = dt_bias[...]
    dpar[1:2, :heads] = a_rate[...]
    dpar[2:3, :heads] = d_skip[...]
    for k in range(2):
        for i in range(1, n):
            exchange(k, i).start()
    load_z = loads.start(w_z, stage_a)
    fill_spread(spread)
    fill_positions(starts, pos, rpos)
    crow[0:1, :] = out_gain[...]
    crow[1:2, :] = expand(dpar[...], spread[...])[2:3]
    load_tok.wait()
    normalize(v_tok, gain, normed, inverse)
    load_cot = loads.start(cot, v_tok)
    store_normed = stores.start(normed, normed_o)
    store_inverse = stores.start(inverse, inverse_o)
    for k in range(2):
        for i in range(1, n):
            exchange(k, i).wait()
    first = lax.broadcasted_iota(jnp.int32, (shard, LANES), 1) < per
    for j in range((width - inner) // LANES):
        low, high = (z - 2 * j + n) % n, (z - 2 * j - 1 + n) % n
        columns = slice(inner + j * LANES, inner + (j + 1) * LANES)
        pair = jnp.where(first, bc_slots[low].astype(f32), pltpu.roll(bc_slots[high].astype(f32), per, 1))
        wxd[own_rows, columns] = pair.astype(bf16)
        taps[:, columns] = jnp.where(first[:8], tap_slots[low], pltpu.roll(tap_slots[high], per, 1))
    get_bd.start()
    taps[:, :inner] = jnp.zeros((8, inner), f32)
    taps[:CONV, :inner] = conv_x[...]
    taps[CONV : CONV + 1, :inner] = conv_x_bias[...]
    load_z.wait()
    cast_into(get_z.shard(ring.me), stage_a)
    load_out.wait()
    cast_into(get_out.shard(ring.me), stage_b)
    xin[pl.ds(0, 8), :] = jnp.zeros((8, width), f32)

    def project_chip(k, source):
        get_x.arrived(k)
        get_bd.arrived(k)
        part = pl.ds(pl.multiple_of((source // 2) * 2 * shard, 2 * shard), 2 * shard)

        def body(i, carry):
            at = pl.multiple_of(i * 512, 512)
            left = normed[pl.ds(at, 512), part]
            for c, w in tiles(wxd.shape[1], 512):
                here = mm(left, wxd[part, c : c + w])
                w_x_part = min(w, width - c)
                if k == 0:
                    xin[pl.ds(at + 8, 512), c : c + w_x_part] = here[:, :w_x_part]
                else:
                    xin[pl.ds(at + 8, 512), c : c + w_x_part] += here[:, :w_x_part]
                if w_x_part < w:
                    if k == 0:
                        dtin[pl.ds(at, 512), :] = here[:, w_x_part:]
                    else:
                        dtin[pl.ds(at, 512), :] += here[:, w_x_part:]
            return carry

        lax.fori_loop(0, length // 512, body, 0)

    get_x.second()
    project_chip(0, ring.me)
    get_x.beside()
    get_bd.second()
    get_z.start()
    get_bd.beside()
    project_chip(1, ring.left)
    project_chip(2, ring.right)
    get_x.third()
    get_bd.third()
    project_chip(3, ring.across)
    store_xin = stores.start(xin, xin_o)
    store_wxd = stores.start(wxd, wxd_o)
    steps(dtin, dpar, None, None, step_low, decay_low)
    convolve(xin, taps, pos, slope, x_low, bc_low)
    get_z.second()
    get_out.start()

    def forward_tick(b):
        @pl.when(b == 0)
        def _():
            get_z.beside()

        @pl.when(b == 3)
        def _():
            get_z.third()

    scan_forward(
        starts, x_low, bc_low, step_low, decay_low, ssd, states, spread, state, xs, wide, cbm, forward_tick
    )
    for k in range(4):
        get_z.arrived(k)
    gate = first_wide.at[pl.ds(0, length), pl.ds(0, inner)]
    gnorm = xin.at[pl.ds(0, length), pl.ds(0, inner)]
    project_rows(normed, wz, gate)
    store_wz = stores.start(wz, wz_o)
    get_out.second()
    gate_squares(gate, ssd, x_low, crow, stat)

    def put_rows(target):
        for b in range(length // BLOCK):
            line_sum = jnp.sum(stat[b * BLOCK : (b + 1) * BLOCK, :].T, axis=0, keepdims=True)
            for j in range(BLOCK // LANES):
                at = b * (BLOCK // LANES) + j
                target[at : at + 1, :] = line_sum[:, j * LANES : (j + 1) * LANES]

    def sum_rows(slots, out, finish):
        sums_here = finish(functools.reduce(lambda p, q: p + q, [slots[i] for i in range(n)]))
        for b in range(length // BLOCK):
            at = b * (BLOCK // LANES)
            row = jnp.concatenate([sums_here[at + j : at + j + 1] for j in range(BLOCK // LANES)], axis=1)
            turned[...] = jnp.broadcast_to(row, turned.shape)
            out[b * BLOCK : (b + 1) * BLOCK, :] = turned[...].T

    put_rows(row_slots.at[0])
    get_x.drain()
    get_bd.drain()
    store_wxd.wait()
    for i in range(1, n):
        exchange(2, i).start()
    load_cot.wait()
    store_xin.wait()

    def back_chip(k, source):
        if k < 3:
            get_out.arrived(k)
        part = pl.ds(pl.multiple_of((source // 2) * 2 * column_shard, 2 * column_shard), 2 * column_shard)

        def body(i, carry):
            at = pl.ds(pl.multiple_of(i * 512, 512), 512)
            left = v_tok[at, part]
            for c, w in tiles(inner, 512):
                here = mm_nt(left, wout[c : c + w, part])
                if k == 0:
                    gnorm[at, c : c + w] = here
                else:
                    gnorm[at, c : c + w] += here
            return carry

        lax.fori_loop(0, length // 512, body, 0)

    back_chip(0, ring.me)
    get_out.beside()
    back_chip(1, ring.left)
    back_chip(2, ring.right)
    for i in range(1, n):
        exchange(2, i).wait()
    store_inverse.wait()
    sum_rows(row_slots, inverse_out, lambda total: lax.rsqrt(total / (inner * n) + EPS))
    get_out.third()
    store_normed.wait()
    gn = normed.at[:, pl.ds(0, inner)]
    gs = normed.at[:, pl.ds(inner, inner)]
    get_z.drain()
    store_wz.wait()
    gate_norm(gate, ssd, x_low, inverse_out, crow, gn)
    get_out.arrived(3)

    fold_columns = inner // own

    def piece(t, q):
        row = pl.multiple_of((q // fold_columns) * length + t * BLOCK, BLOCK)
        return wz.at[pl.ds(row, BLOCK), pl.ds(pl.multiple_of((q % fold_columns) * own, own), own)]

    def slot(side, place, k):
        if place == 2:
            return near.at[k]
        row = pl.multiple_of((k // fold_columns) * BLOCK, BLOCK)
        return wxd.at[pl.ds(row, BLOCK), pl.ds(pl.multiple_of((k % fold_columns) * own, own), own)]

    total = wide.at[:, pl.ds(0, own)]
    line = Line(piece, slot, length // BLOCK, (line_send, line_recv), total, 4)

    def quarter(i, carry):
        q = line.order(i)
        columns = pl.ds(pl.multiple_of(q * own, own), own)
        for r in range(0, length, 512):
            at = pl.ds(pl.multiple_of((q // fold_columns) * length + r, 512), 512)
            cols = pl.ds(pl.multiple_of((q % fold_columns) * own, own), own)
            wz[at, cols] = mm(gn[r : r + 512, :], wout[:, columns]).astype(bf16)
            if r == 0:
                @pl.when(i == 0)
                def _():
                    line.inject(0)
                    line.inject(1)

        return carry

    quarter(0, 0)
    back_chip(3, ring.across)
    cross_sums(gnorm, gn, stat)
    put_rows(cross_slots.at[0])
    for i in range(1, n):
        exchange(3, i).start()
    line.inject(2)
    lax.fori_loop(1, n, quarter, 0)
    line.inject(3)
    get_out.drain()
    grads = wout
    scatter = Scatter(
        ring, lambda r: grads.at[:, pl.ds(pl.multiple_of(r * column_shard, column_shard), column_shard)],
        cores, parts, wholes, (scatter_core_send, scatter_core_recv, scatter_ring_send, scatter_ring_recv),
    )
    chunk = 2 * column_shard

    def weight(j, carry):
        columns = pl.ds(pl.multiple_of(j * chunk, chunk), chunk)
        for r in range(0, inner, 256):
            grads[r : r + 256, columns] = mm_tn(gn[:, r : r + 256], v_tok[:, columns]).astype(bf16)
        scatter.start(j)
        return carry

    lax.fori_loop(0, 4, weight, 0)
    line.inject(4)
    line.forward(0, 1)
    xd = v_tok.at[:, pl.ds(0, wxd.shape[1])]
    token_own = v_tok.at[:, pl.ds(wxd.shape[1], own)]
    load_own = loads.start(tok.at[:, pl.ds(pl.multiple_of(z * own, own), own)], token_own)
    for i in range(1, n):
        exchange(3, i).wait()
    sum_rows(cross_slots, stat, lambda total: total / (inner * n))
    low_gate = gn
    gate_backward(gate, ssd, x_low, gnorm, crow, stat, inner * n, None, low_gate, gs, sums, known=inverse_out)
    load_xin = loads.start(xin_o, xin)
    stores.start(low_gate, low_gate_o)
    stores.start(sums, sums_o)
    line.inject(5)
    line.forward(1, 1)
    line.forward(0, 2)
    scatter.first()

    def scan_tick(i):
        line.inject(i + 6)
        line.forward(i + 2, 1)

        @pl.when(i < 3)
        def _():
            line.forward(i + 1, 2)

        @pl.when(i == 1)
        def _():
            scatter.second()

    gpre = first_wide
    scan_backward(
        starts, x_low, bc_low, step_low, decay_low, ssd, states, gs, slope, crow, dtin, None, dpar,
        gpre, xd, dsums, spread, state, xs, wide, cbm, acc, scan_tick,
    )
    bd = wxd.shape[1] - inner
    weight_loads = [loads.start(wz_o, both)]
    for h in range(2):
        rows_here = pl.ds(h * length, length)
        weight_loads.append(
            loads.start(wxd_o.at[rows_here, pl.ds(inner, bd)], slope.at[:, pl.ds(h * bd, bd)])
        )
    inverse_in = dtin
    weight_loads.append(loads.start(inverse_o, inverse_in))

    def token_copy(i):
        return pltpu.make_async_copy(
            tok.at[:, pl.ds(pl.multiple_of(line.order(i) * own, own), own)],
            normed.at[:, pl.ds(pl.multiple_of(inner + (i % 2) * own, own), own)], token_sems.at[i],
        )

    token_copy(0).start()
    token_copy(1).start()
    scatter.finish(stage_b)
    stores.start(stage_b, dwout_o)
    for h in range(2):
        weight_loads.append(
            loads.start(wxd_o.at[pl.ds(h * length, length), pl.ds(0, inner)], wout.at[:, pl.ds(h * inner, inner)])
        )
    load_xin.wait()

    def conv_tick(b):
        @pl.when(b % 2 == 1)
        def _():
            line.inject(10 + b // 2)
            line.forward(6 + b // 2, 1)

    convolve_back(xin, gpre, taps, pos, rpos, xd, csums, conv_tick)
    for source, target in ((xd, low_xd_o), (csums, csums_o), (dsums, dsums_o)):
        stores.start(source, target)
    for copy in weight_loads:
        copy.wait()
    stat[...] = jnp.zeros_like(stat)
    half = own // 2

    def part_copy(i, h):
        column = pl.multiple_of(line.order(i) * own + h * half, half)
        return pltpu.make_async_copy(
            cores.at[(i % 2) * 2 + h], part_o.at[:, pl.ds(column, half)], part_sems.at[i, h]
        )

    def grad_quarter(i, carry):
        q = line.order(i)
        columns = pl.ds(pl.multiple_of(q * own, own), own)
        low = pl.ds(pl.multiple_of((q % 2) * own, own), own)
        high = q // 2
        x_columns = pl.ds(pl.multiple_of(high * inner, inner), inner)
        bd_columns = pl.ds(pl.multiple_of(high * bd, LANES), bd)
        token_columns = pl.ds(pl.multiple_of(inner + (i % 2) * own, own), own)
        token_copy(i).wait()

        @pl.when(i >= 2)
        def _():
            for h in range(2):
                part_copy(jnp.maximum(i - 2, 0), h).wait()

        for r in range(0, length, 256):
            at = slice(r, r + 256)
            here = mm_nt(low_gate[at, :], both[columns, :])
            here = here + mm_nt(xd[at, :inner], wout[low, x_columns])
            here = here + mm_nt(xd[at, inner:], slope[low, bd_columns])
            for h in range(2):
                cores[(i % 2) * 2 + h, at, :] = here[:, h * half : (h + 1) * half].astype(bf16)
            along = here * (normed[at, token_columns].astype(f32) * inverse_in[at, :1])
            folded = fold(along)
            if r == 0:
                colacc[:, columns] = folded
            else:
                colacc[:, columns] += folded
            along = along * gain[:, columns]
            sum_lanes = along[:, :LANES]
            for c in range(LANES, own, LANES):
                sum_lanes = sum_lanes + along[:, c : c + LANES]
            stat[at, :] += sum_lanes
        for h in range(2):
            part_copy(i, h).start()

        @pl.when(i < 2)
        def _():
            token_copy(jnp.minimum(i + 2, n - 1)).start()

        return carry

    lax.fori_loop(0, n, grad_quarter, 0)
    put_rows(rows)
    stores.start(rows, rows_o)
    stores.start(colacc, colacc_o)
    load_own.wait()

    def last(t, carry):
        line.finish(t)
        value = (token_own[line.rows(t), :].astype(f32) + total[...]).astype(bf16)
        for h in range(2):
            wholes[h, line.rows(t), :] = value[:, h * half : (h + 1) * half]
            out_copy(t, h).start()
        return carry

    def out_copy(t, h):
        return pltpu.make_async_copy(
            wholes.at[h, line.rows(t), :], out_o.at[line.rows(t), pl.ds(h * half, half)], out_sems.at[t, h]
        )

    lax.fori_loop(0, line.blocks, last, 0)
    line.drain()
    for t in range(line.blocks):
        for h in range(2):
            out_copy(t, h).wait()
    for i in range(2, n):
        for h in range(2):
            part_copy(i, h).wait()
    for copy in stores.pairs:
        if not any(copy is done for done in (store_normed, store_inverse, store_xin, store_wxd, store_wz)):
            copy.wait()


def input_kernel(
    tok, inverse, gain, normed, low_gate, low_xd, part_o, cot, rows_o, colacc, csums, sums, dsums,
    dwz_o, dwx_o, grad_o, dwbc, dwdt, conv_x, conv_x_bias, conv_bc, conv_bc_bias, dt_bias, a_rate, d_skip, in_gain,
    out_gain,
    dwz, dwxd, grad, smalls, spread, bc_turned, bc_own, bc_slots,
    v_inverse, v_normed, v_gate, v_xd, v_cot, v_tok, v_colacc, v_csums, v_sums, v_dsums,
    part, slots, total, z_grads, z_cores, z_parts, z_wholes, x_grads, x_cores, x_parts, x_wholes,
    rows_slots, dp_in, mp_in, turned,
    load_sems, part_sems, grad_sems, line_send, line_recv, z_core_send, z_core_recv, z_ring_send, z_ring_recv,
    x_core_send, x_core_recv, x_ring_send, x_ring_recv,
    rows_send, rows_recv, dp_send, dp_recv, mp_send, mp_recv, bc_send, bc_recv,
):
    ring = Ring()
    met = greet(ring, True)
    loads = Loads(load_sems)
    n = lax.axis_size("mp")
    z = lax.axis_index("mp")
    size = lax.axis_size("dp")
    length, features = part.shape
    inner = v_gate.shape[1]
    width = v_csums.shape[1]
    heads, per = dwdt.shape[0], dwbc.shape[0]
    own = features // n

    def quarter_columns(q):
        return pl.ds(pl.multiple_of(q * own, own), own)

    line = Line(
        lambda t, q: part.at[pl.ds(pl.multiple_of(t * BLOCK, BLOCK), BLOCK), quarter_columns(q)],
        lambda side, place, k: slots.at[side, k], length // BLOCK, (line_send, line_recv), total, 3,
    )

    def part_copy(i):
        columns = quarter_columns(line.order(i))
        return pltpu.make_async_copy(part_o.at[:, columns], part.at[:, columns], part_sems.at[i])

    load_rows = loads.start(rows_o, rows_slots.at[0])
    part_copy(0).start()

    def rows_copy(i):
        return remote(
            rows_slots.at[0], rows_slots.at[i], rows_send.at[i - 1], rows_recv.at[i - 1], mp=(z + i) % n
        )

    load_rows.wait()
    met()
    for i in range(1, n):
        rows_copy(i).start()
    part_copy(0).wait()
    line.inject(0)
    line.inject(1)
    for i in range(1, n):
        part_copy(i).start()
    load_gate, load_normed, load_xd = [
        loads.start(source, target) for source, target in ((low_gate, v_gate), (normed, v_normed), (low_xd, v_xd))
    ]
    load_sums = [
        loads.start(source, target)
        for source, target in ((colacc, v_colacc), (csums, v_csums), (sums, v_sums), (dsums, v_dsums))
    ]
    own_columns = quarter_columns(z)
    later = [
        loads.start(source, target)
        for source, target in (
            (cot.at[:, own_columns], v_cot), (tok.at[:, own_columns], v_tok), (inverse, v_inverse),
        )
    ]

    gain_width = features // 8

    def dp_copy(i):
        return remote(
            smalls, dp_in.at[i - 1], dp_send.at[i - 1], dp_recv.at[i - 1], dp=(ring.me + i) % size
        )

    def mp_copy(i):
        return remote(
            smalls.at[:, pl.ds(inner, width - inner + gain_width)], mp_in.at[i - 1],
            mp_send.at[i - 1], mp_recv.at[i - 1], mp=(z + i) % n,
        )

    for copy in load_sums:
        copy.wait()
    smalls[...] = jnp.zeros_like(smalls)
    for k in range(CONV + 1):
        smalls[k : k + 1, :width] = jnp.sum(v_csums[8 * k : 8 * k + 8, :], axis=0, keepdims=True)
    for k in range(2):
        smalls[CONV + 1 + k : CONV + 2 + k, :inner] = jnp.sum(v_sums[8 * k : 8 * k + 8, :], axis=0, keepdims=True)
        smalls[7:8, k * LANES : (k + 1) * LANES] = jnp.sum(v_dsums[8 * k : 8 * k + 8, :], axis=0, keepdims=True)
    for k in range(8):
        columns = slice(k * gain_width, (k + 1) * gain_width)
        smalls[k : k + 1, width:] = jnp.sum(v_colacc[:, columns], axis=0, keepdims=True)
    for i in range(1, size):
        dp_copy(i).start()
    shard = dwz.shape[0]
    z_scatter = Scatter(
        ring, lambda r: z_grads.at[pl.ds(pl.multiple_of(r * shard, shard), shard), :], z_cores, z_parts, z_wholes,
        (z_core_send, z_core_recv, z_ring_send, z_ring_recv),
    )
    x_scatter = Scatter(
        ring, lambda r: x_grads.at[pl.ds(pl.multiple_of(r * shard, shard), shard), :], x_cores, x_parts, x_wholes,
        (x_core_send, x_core_recv, x_ring_send, x_ring_recv),
    )

    def weight(j, right, grads):
        for c in range(0, 2 * shard, shard):
            rows = pl.ds(pl.multiple_of(j * 2 * shard + c, shard), shard)
            left = v_normed[:, rows]
            for at, w in tiles(grads.shape[1], 512):
                grads[rows, at : at + w] = mm_tn(left, right[:, at : at + w]).astype(bf16)

    load_gate.wait()
    load_normed.wait()

    def z_weight(j, carry):
        weight(j, v_gate, z_grads)
        z_scatter.start(j)
        return carry

    lax.fori_loop(0, 4, z_weight, 0)
    for i in range(1, n):
        part_copy(i).wait()
    line.inject(2)
    line.forward(0, 1)
    load_xd.wait()

    def x_weight(j, carry):
        weight(j, v_xd, x_grads)
        x_scatter.start(j)

        @pl.when(j == 1)
        def _():
            z_scatter.first()

        @pl.when(j % 2 == 1)
        def _():
            line.inject(3 + j // 2)
            line.forward(1 + j // 2, 1)

        return carry

    lax.fori_loop(0, 4, x_weight, 0)
    line.forward(0, 2)
    z_scatter.second()
    line.inject(5)
    line.forward(3, 1)
    line.forward(1, 2)
    x_scatter.first()
    line.inject(6)
    line.forward(4, 1)
    line.forward(2, 2)
    for i in range(1, size):
        dp_copy(i).wait()
    smalls[...] += functools.reduce(lambda a, b: a + b, [dp_in[i] for i in range(size - 1)])
    for i in range(1, n):
        mp_copy(i).start()
    line.inject(7)
    line.forward(5, 1)
    line.forward(3, 2)
    z_scatter.finish(dwz)
    store_z = loads.start(dwz, dwz_o)
    x_scatter.second()
    line.inject(8)
    line.forward(6, 1)
    line.inject(9)
    line.forward(7, 1)
    line.inject(10)
    x_scatter.finish(dwxd)

    bc_turned[...] = dwxd[:, inner:width].T
    bc_own[...] = bc_turned[...].astype(bf16)

    def weight_copy(i):
        other = (z + i) % n
        return remote(
            bc_own.at[pl.ds(pl.multiple_of(other * per, per), per), :], bc_slots.at[i - 1],
            bc_send.at[i - 1], bc_recv.at[i - 1], mp=other,
        )

    for i in range(1, n):
        weight_copy(i).start()
    line.inject(11)
    store_x = loads.start(dwxd.at[:, pl.ds(0, inner)], dwx_o)
    dwdt[...] = dwxd[:, width:].T[:heads]
    for i in range(1, n):
        rows_copy(i).wait()
        mp_copy(i).wait()
    smalls[:, inner:] += functools.reduce(lambda a, b: a + b, [mp_in[i] for i in range(n - 1)])
    share = LANES // per

    def mine(v):
        turns = [v] + [pltpu.roll(v, LANES - k * per, 1) for k in range(1, share)]
        which = jnp.full(v.shape, z % share, jnp.int32)
        return functools.reduce(lambda a, k: jnp.where(which == k, turns[k], a), range(1, share), turns[0])

    lanes = pl.ds(pl.multiple_of(inner + (z // share) * LANES, LANES), LANES)
    conv_x[...] = smalls[:CONV, :inner]
    conv_x_bias[...] = smalls[CONV : CONV + 1, :inner]
    taps = mine(smalls[:8, lanes])
    conv_bc[...] = taps[:CONV, :per]
    conv_bc_bias[...] = taps[CONV : CONV + 1, :per]
    out_gain[...] = smalls[5:6, :inner]
    fill_spread(spread)
    d_skip[...] = gather_heads(smalls[0:8, :inner], spread[...])[6:7, :heads]
    dt_bias[...] = smalls[7:8, :heads]
    a_rate[...] = smalls[7:8, LANES : LANES + heads]
    rows_own = own // gain_width
    for k in range(rows_own):
        in_gain[:, k * gain_width : (k + 1) * gain_width] = smalls[
            pl.ds(z * rows_own + k, 1), width : width + gain_width
        ]
    for copy in later:
        copy.wait()
    means = functools.reduce(lambda a, b: a + b, [rows_slots[i] for i in range(n)]) / features
    rows_slots[0] = means

    def last(t, carry):
        line.finish(t)
        rows = line.rows(t)
        lines = BLOCK // LANES
        row = jnp.concatenate([rows_slots[0, pl.ds(t * lines + j, 1), :] for j in range(lines)], axis=1)
        turned[...] = jnp.broadcast_to(row, turned.shape)
        mean = turned[...].T
        for c in range(0, own, LANES):
            columns = slice(c, c + LANES)
            hat = v_tok[rows, columns].astype(f32) * v_inverse[rows, :]
            gain_here = gain[:, pl.ds(pl.multiple_of(z * own + c, LANES), LANES)]
            change = v_inverse[rows, :] * (total[:, columns] * gain_here - hat * mean)
            grad[rows, columns] = (v_cot[rows, columns].astype(f32) + change).astype(bf16)
        grad_copy(t).start()
        return carry

    def grad_copy(t):
        return pltpu.make_async_copy(grad.at[line.rows(t), :], grad_o.at[line.rows(t), :], grad_sems.at[t])

    lax.fori_loop(0, line.blocks, last, 0)
    for i in range(1, n):
        weight_copy(i).wait()
    dwbc[...] = functools.reduce(
        lambda a, b: a + b, [bc_slots[i].astype(f32) for i in range(n - 1)],
        bc_turned[pl.ds(pl.multiple_of(z * per, per), per), :],
    )
    line.drain()
    for copy in (store_z, store_x):
        copy.wait()
    for t in range(line.blocks):
        grad_copy(t).wait()


def hand_on_kernel(*refs):
    count = (len(refs) - 2) // 3
    sources, targets, buffers = refs[:count], refs[count : 2 * count], refs[2 * count : 3 * count]
    into, out = refs[-2:]
    there = [pltpu.make_async_copy(sources[k], buffers[k], into.at[k]) for k in range(count)]
    back = [pltpu.make_async_copy(buffers[k], targets[k], out.at[k]) for k in range(count)]
    for copy in there:
        copy.start()
    for k in range(count):
        there[k].wait()
        back[k].start()
    for copy in back:
        copy.wait()


def hand_on(*arrays):
    kinds = [(v.shape, v.dtype) for v in arrays]
    count = len(arrays)
    return call(
        hand_on_kernel, kinds, kinds, 0, *arrays,
        places="a" * len(arrays), sems=[(count,)] * 2, far=len(arrays),
    )


def call(kernel, outs, scratch, smem, *operands, places=None, sems=(), collective=None, far=0):
    spaces = {"s": pltpu.SMEM, "v": pltpu.VMEM, "a": pl.ANY}
    if places is None:
        places = "s" * smem + "v" * (len(operands) - smem)
    extra = {} if collective is None else dict(collective_id=collective, has_side_effects=True)
    return pl.pallas_call(
        kernel,
        out_shape=[jax.ShapeDtypeStruct(shape, kind) for shape, kind in outs],
        in_specs=[pl.BlockSpec(memory_space=spaces[c]) for c in places],
        out_specs=[pl.BlockSpec(memory_space=pl.ANY if i < far else pltpu.VMEM) for i in range(len(outs))],
        scratch_shapes=[pltpu.VMEM(shape, kind) for shape, kind in scratch]
        + [pltpu.SemaphoreType.DMA(shape) for shape in sems],
        compiler_params=pltpu.CompilerParams(vmem_limit_bytes=VMEM_LIMIT, **extra),
    )(*operands)


def per_device_any(
    tokens, cotangent, doc_lengths, w_z, w_x, w_bc, w_dt, w_out, conv_x, conv_x_bias, conv_bc,
    conv_bc_bias, dt_bias, a_rate, d_skip, input_norm_gain, out_gain,
):
    group = lax.axis_size("mp")
    rank = lax.axis_index("mp")
    T, D = tokens.shape
    inner, heads = w_x.shape[1], w_dt.shape[1]
    pair = 2 * STATE
    width = inner + pair
    wide = width + LANES
    own = D // group

    lengths = doc_lengths[0]
    starts = jnp.cumsum(lengths) - lengths
    packed = jnp.concatenate([w_bc, conv_bc, conv_bc_bias[None, :]], axis=0)
    packed = lax.all_gather(packed, "mp", axis=1, tiled=True)
    shard = w_bc.shape[0]
    w_bc_all, taps_bc = packed[:shard], packed[shard:]
    wxd = jnp.concatenate(
        [w_x.astype(bf16), w_bc_all.astype(bf16), w_dt.astype(bf16), jnp.zeros((shard, LANES - heads), bf16)],
        axis=1,
    )
    wxd = lax.all_gather(wxd, "dp", axis=0, tiled=True)
    wz = lax.all_gather(w_z.astype(bf16), "dp", axis=0, tiled=True)
    wout = lax.all_gather(w_out.astype(bf16), "dp", axis=1, tiled=True)
    taps = jnp.concatenate([jnp.concatenate([conv_x, conv_x_bias[None, :]], axis=0), taps_bc], axis=1)
    taps = jnp.pad(taps, ((0, 8 - CONV - 1), (0, 0)))
    crow = jnp.pad(jnp.stack([out_gain, jnp.repeat(d_skip, HEADDIM)]), ((0, 6), (0, 0)))
    dpar = jnp.pad(jnp.stack([dt_bias, a_rate]), ((0, 6), (0, LANES - heads)))
    gain = input_norm_gain[None, :]

    blocks = T // BLOCK
    (
        normed, inverse, xin, slope, gate, x_low, bc_low, step, sgdt, step_low, decay_low, ssd, states,
    ) = call(
        forward_kernel,
        [
            ((T, D), bf16), ((T, LANES), f32), ((T + 8, width), f32), ((T, width), bf16), ((T, inner), f32),
            ((T, inner), bf16), ((T, pair), bf16), ((T, LANES), f32), ((T, LANES), f32),
            ((T, LANES), bf16), ((T, LANES), bf16), ((T, inner), bf16), ((blocks, STATE, inner), bf16),
        ],
        [
            ((T, LANES), jnp.int32), ((LANES, inner), bf16), ((T, LANES), f32), ((STATE, inner), f32),
            ((BLOCK, inner), bf16), ((BLOCK, inner), f32), ((BLOCK, BLOCK), f32),
        ],
        1, starts, tokens, gain, wxd, wz, taps, dpar,
    )
    gnorm, stat = call(
        gate_kernel,
        [((T, inner), f32), ((T, LANES), f32)],
        [],
        0, cotangent, wout, gate, ssd, x_low, crow,
    )
    stat = jnp.pad(lax.psum(stat[:, :8], "mp"), ((0, 0), (0, LANES - 8)))
    branch, dwout, dwz, low_gate, gs, sums = call(
        functools.partial(middle_kernel, width=inner * group),
        [
            ((T, D), bf16), ((inner, D), bf16), ((D, inner), bf16), ((T, inner), bf16), ((T, inner), bf16),
            ((16, inner), f32),
        ],
        [((T, inner), bf16)],
        0, cotangent, wout, normed, gate, x_low, ssd, gnorm, crow, stat,
    )
    low_xd, csums, dsums = call(
        backward_kernel,
        [((T, wide), bf16), ((8 * CONV + 8, width), f32), ((16, LANES), f32)],
        [
            ((T, LANES), jnp.int32), ((T, LANES), jnp.int32), ((LANES, inner), bf16), ((T + 8, width), f32),
            ((STATE, inner), f32), ((BLOCK, inner), bf16), ((BLOCK, inner), f32), ((BLOCK, BLOCK), f32),
            ((BLOCK, BLOCK), f32),
        ],
        1, starts, xin, slope, x_low, bc_low, step, sgdt, step_low, decay_low, ssd, states, gs, taps, crow,
        dpar,
    )
    dwxd, gfull, rowdot = call(
        last_kernel,
        [((D, wide), bf16), ((T, D), bf16), ((T, LANES), f32)],
        [],
        0, tokens, inverse, gain, normed, low_gate, low_xd, wz, wxd,
    )

    def scatter(v, axis, dim):
        return lax.psum_scatter(v, axis, scatter_dimension=dim, tiled=True)

    token_own = lax.dynamic_slice_in_dim(tokens, rank * own, own, 1).astype(f32)
    output = (token_own + scatter(branch, "mp", 1).astype(f32)).astype(bf16)
    w_out_grad = scatter(dwout, "dp", 1).astype(f32)
    w_z_grad = scatter(dwz, "dp", 0).astype(f32)
    dwxd_own = scatter(dwxd, "dp", 0)
    w_x_grad = dwxd_own[:, :inner].astype(f32)
    w_dt_grad = dwxd_own[:, width : width + heads].astype(f32)
    w_bc_grad = scatter(dwxd_own[:, inner:width], "mp", 1).astype(f32)

    g_own = scatter(gfull, "mp", 1).astype(f32)
    gain_own = lax.dynamic_slice_in_dim(input_norm_gain, rank * own, own, 0)
    row_mean = (lax.psum(rowdot[:, 0], "mp") / D)[:, None]
    inv = inverse[:, :1]
    hat = token_own * inv
    cot_own = lax.dynamic_slice_in_dim(cotangent, rank * own, own, 1).astype(f32)
    input_grad = (cot_own + inv * (g_own * gain_own - hat * row_mean)).astype(bf16)
    in_gain = jnp.sum(g_own * hat, axis=0)

    csums = jnp.sum(csums.reshape(CONV + 1, 8, width), axis=1)
    sums = jnp.sum(sums.reshape(2, 8, inner), axis=1)
    dsums = jnp.sum(dsums.reshape(2, 8, LANES), axis=1)[:, :heads]
    csums_bc = scatter(csums[:, inner:], "mp", 1)
    conv_grad, conv_bc_grad, sums, dsums, in_gain = lax.psum(
        (csums[:, :inner], csums_bc, sums, dsums, in_gain), "dp"
    )
    d_skip_grad = jnp.sum(sums[1].reshape(heads, HEADDIM), axis=1)
    return (
        output, input_grad, w_z_grad, w_x_grad, w_bc_grad, w_dt_grad, w_out_grad,
        conv_grad[:CONV], conv_grad[CONV], conv_bc_grad[:CONV], conv_bc_grad[CONV],
        dsums[0], dsums[1], d_skip_grad, in_gain, sums[0],
    )


def per_device(
    tokens, cotangent, doc_lengths, w_z, w_x, w_bc, w_dt, w_out, conv_x, conv_x_bias, conv_bc,
    conv_bc_bias, dt_bias, a_rate, d_skip, input_norm_gain, out_gain,
):
    group, size = lax.axis_size("mp"), lax.axis_size("dp")
    T, D = tokens.shape
    shard, inner = w_x.shape
    heads, per = w_dt.shape[1], w_bc.shape[1]
    pair = per * group
    width = inner + pair
    wide = width + LANES
    own = D // group
    columns = w_out.shape[1]
    blocks = T // BLOCK
    messages = blocks * (group - 1)

    def row(v):
        return v[None, :]

    (
        normed, _, _, _, low_gate, low_xd, output, w_out_grad, inverse, part, csums, dsums, sums, rows, colacc,
    ) = call(
        trunk_kernel,
        [
            ((T, D), bf16), ((T + 8, width), f32), ((D, wide), bf16), ((D, inner), bf16), ((T, inner), bf16),
            ((T, wide), bf16), ((T, own), bf16), ((inner, columns), f32), ((T, LANES), f32), ((T, D), bf16),
            ((8 * CONV + 8, width), f32), ((16, LANES), f32), ((16, inner), f32), ((T // LANES, LANES), f32),
            ((8, D), f32),
        ],
        [
            ((8 * CONV + 8, width), f32), ((16, LANES), f32), ((16, inner), f32), ((T // LANES, LANES), f32),
            ((8, D), f32),
            ((T, D), bf16), ((inner, columns), f32), ((T, D), bf16), ((T + 8, width), f32),
            ((T + 8, width), f32), ((T, width), bf16), ((2 * T, inner), bf16),
            ((blocks, STATE, inner), bf16), ((D, wide), bf16), ((D, inner), bf16), ((inner, D), bf16),
            ((T, pair), bf16), ((T, LANES), bf16), ((T, LANES), bf16), ((T, LANES), f32),
            ((8, width), f32), ((8, inner), f32), ((8, LANES), f32),
            ((group, shard, LANES), bf16), ((group, 8, LANES), f32), ((group, T // LANES, LANES), f32),
            ((group, T // LANES, LANES), f32), ((T, LANES), f32), ((LANES, BLOCK), f32),
            ((T, LANES), jnp.int32), ((T, LANES), jnp.int32), ((LANES, inner), bf16), ((T, LANES), f32),
            ((STATE, inner), f32), ((BLOCK, inner), bf16), ((BLOCK, inner), f32), ((BLOCK, BLOCK), f32),
            ((BLOCK, BLOCK), f32), ((2 * blocks, BLOCK, own), bf16),
            ((4, inner, columns), bf16), ((2, inner // 2, columns), bf16), ((2, inner, columns), bf16),
        ],
        0, doc_lengths, tokens, cotangent, w_x, w_z, w_out, w_bc.T, w_dt.T, conv_x, row(conv_x_bias), conv_bc,
        row(conv_bc_bias), row(dt_bias), row(a_rate), row(d_skip), row(input_norm_gain), row(out_gain),
        places="s" + "a" * 5 + "v" * 11,
        sems=[
            (13,), (13,), (group,), (group, 2), (blocks, 2), (4, 6), (4, 6), (4, 4), (4, 4), (4 * group - 4,), (4 * group - 4,),
            (2, messages), (2, messages), (4,), (4,), (4,), (4,),
        ],
        collective=0,
        far=15,
    )
    w_z_grad, w_x_grad, input_grad, w_bc_grad, w_dt_grad, *small_grads = call(
        input_kernel,
        [
            ((shard, inner), f32), ((shard, inner), f32), ((T, own), bf16), ((per, shard), f32),
            ((heads, shard), f32), ((CONV, inner), f32), ((1, inner), f32), ((CONV, per), f32), ((1, per), f32),
            ((1, heads), f32), ((1, heads), f32), ((1, heads), f32), ((1, own), f32), ((1, inner), f32),
        ],
        [
            ((shard, inner), f32), ((shard, wide), f32), ((T, own), bf16), ((8, width + D // 8), f32),
            ((LANES, inner), bf16), ((pair, shard), f32), ((pair, shard), bf16), ((group - 1, per, shard), bf16),
            ((T, LANES), f32), ((T, D), bf16), ((T, inner), bf16), ((T, wide), bf16), ((T, own), bf16),
            ((T, own), bf16), ((8, D), f32), ((8 * CONV + 8, width), f32), ((16, inner), f32), ((16, LANES), f32),
            ((T, D), bf16), ((2, messages, BLOCK, own), bf16), ((BLOCK, own), f32),
            ((D, inner), bf16), ((4, shard, inner), bf16), ((2, shard // 2, inner), bf16), ((2, shard, inner), bf16),
            ((D, wide), bf16), ((4, shard, wide), bf16), ((2, shard // 2, wide), bf16), ((2, shard, wide), bf16),
            ((group, T // LANES, LANES), f32), ((size - 1, 8, width + D // 8), f32),
            ((group - 1, 8, pair + D // 8), f32), ((LANES, BLOCK), f32),
        ],
        0, tokens, inverse, row(input_norm_gain), normed, low_gate, low_xd, part, cotangent, rows, colacc, csums,
        sums, dsums,
        places="aav" + "a" * 10,
        sems=[
            (13,), (group,), (blocks,), (2, messages), (2, messages), (4,), (4,), (4,), (4,), (4,), (4,), (4,), (4,),
            (group - 1,), (group - 1,), (size - 1,), (size - 1,), (group - 1,), (group - 1,),
            (group - 1,), (group - 1,),
        ],
        collective=2,
        far=3,
    )
    (
        output, input_grad, w_z_grad, w_x_grad, w_bc_grad, w_dt_grad, w_out_grad, conv_x_grad, conv_x_bias_grad,
        conv_bc_grad, conv_bc_bias_grad, dt_bias_grad, a_rate_grad, d_skip_grad, in_gain_grad, out_gain_grad,
    ) = hand_on(output, input_grad, w_z_grad, w_x_grad, w_bc_grad, w_dt_grad, w_out_grad, *small_grads)
    return (
        output, input_grad, w_z_grad, w_x_grad, w_bc_grad.T, w_dt_grad.T, w_out_grad,
        conv_x_grad, conv_x_bias_grad[0], conv_bc_grad, conv_bc_bias_grad[0], dt_bias_grad[0], a_rate_grad[0],
        d_skip_grad[0], in_gain_grad[0], out_gain_grad[0],
    )


def solution(mesh):
    row, block, column = P("dp", None), P("dp", "mp"), P("mp")
    return jax.shard_map(
        per_device if (mesh.shape["dp"], mesh.shape["mp"]) == (8, 4) else per_device_any,
        mesh=mesh,
        in_specs=(
            row, row, row, block, block, block, block, P("mp", "dp"), P(None, "mp"), column,
            P(None, "mp"), column, column, column, column, P(), column,
        ),
        out_specs=(
            block, block, block, block, block, block, P("mp", "dp"), P(None, "mp"), column,
            P(None, "mp"), column, column, column, column, column, column,
        ),
        check_vma=False,
    )
```

```python
import functools

import jax
import jax.numpy as jnp
from jax import lax
from jax.experimental import pallas as pl
from jax.experimental.pallas import tpu as pltpu
from jax.sharding import PartitionSpec as P

HEADDIM = 64
STATE = 128
CONV = 4
BLOCK = 256
DOCS = 5
LANES = 128
EPS = 1e-05
f32 = jnp.float32
bf16 = jnp.bfloat16
VMEM_LIMIT = 127 * 2**19


def mm(a, b):
    return jnp.dot(a, b, preferred_element_type=f32)


def mm_nt(a, b):
    return lax.dot_general(a, b, (((1,), (1,)), ((), ())), preferred_element_type=f32)


def mm_tn(a, b):
    return lax.dot_general(a, b, (((0,), (0,)), ((), ())), preferred_element_type=f32)


def halves(v):
    high = v.astype(bf16)
    return high, (v - high.astype(f32)).astype(bf16)


def expand(v, spread):
    high, rest = halves(v)
    return mm(high, spread) + mm(rest, spread)


def gather_heads(v, spread):
    high, rest = halves(v)
    return mm_nt(high, spread) + mm_nt(rest, spread)


def logistic(v):
    return 1.0 / (1.0 + jnp.exp(-v))


def tiles(total, size):
    return [(at, min(size, total - at)) for at in range(0, total, size)]


def fold(v):
    return jnp.sum(v.reshape(v.shape[0] // 8, 8, v.shape[1]), axis=0)


def doc_of(starts, place):
    count = (place >= starts[0]).astype(jnp.int32)
    for k in range(1, DOCS):
        count = count + (place >= starts[k]).astype(jnp.int32)
    return count


def fill_spread(spread):
    rows, columns = spread.shape
    head = lax.broadcasted_iota(jnp.int32, (rows, columns), 0)
    channel = lax.broadcasted_iota(jnp.int32, (rows, columns), 1)
    low = head * HEADDIM
    spread[...] = jnp.where((channel >= low) & (channel < low + HEADDIM), 1.0, 0.0).astype(bf16)


def fill_positions(starts, pos, rpos):
    length = pos.shape[0]

    def body(i, carry):
        at = pl.multiple_of(i * BLOCK, BLOCK)
        place = lax.broadcasted_iota(jnp.int32, (BLOCK, LANES), 0) + at
        begin = jnp.zeros_like(place)
        end = jnp.full_like(place, length)
        for k in range(DOCS):
            begin = jnp.maximum(begin, jnp.where(place >= starts[k], starts[k], 0))
            end = jnp.minimum(end, jnp.where(place < starts[k], starts[k], length))
        pos[pl.ds(at, BLOCK), :] = place - begin
        if rpos is not None:
            rpos[pl.ds(at, BLOCK), :] = end - 1 - place
        return carry

    lax.fori_loop(0, length // BLOCK, body, 0)


def normalize(tok, gain, normed, stat):
    step = 64

    def body(i, carry):
        rows = pl.ds(pl.multiple_of(i * step, step), step)
        v = tok[rows, :].astype(f32)
        inverse = lax.rsqrt(jnp.mean(v * v, axis=1, keepdims=True) + EPS)
        normed[rows, :] = (v * inverse * gain[...]).astype(bf16)
        stat[rows, :] = jnp.broadcast_to(inverse, (step, LANES))
        return carry

    lax.fori_loop(0, tok.shape[0] // step, body, 0)


def project_x(normed, wxd, xin, dtin):
    length, width = normed.shape[0], xin.shape[1]
    xin[pl.ds(0, 8), :] = jnp.zeros((8, width), f32)
    rows = 512

    def body(i, carry):
        at = pl.multiple_of(i * rows, rows)
        left = normed[pl.ds(at, rows), :]
        for c, w in tiles(width, 512):
            xin[pl.ds(at + 8, rows), c : c + w] = mm(left, wxd[:, c : c + w])
        dtin[pl.ds(at, rows), :] = mm(left, wxd[:, width : width + LANES])
        return carry

    lax.fori_loop(0, length // rows, body, 0)


def convolve(xin, taps, pos, slope, x_low, bc_low):
    width, inner = xin.shape[1], x_low.shape[1]

    def tile(b, c, out, at):
        rows = pl.ds(pl.multiple_of(b * BLOCK, BLOCK), BLOCK)
        x = xin[pl.ds(pl.multiple_of(b * BLOCK, BLOCK), BLOCK + 8), pl.ds(c, LANES)]
        place = pos[rows, :]
        tap = taps[:, pl.ds(c, LANES)]
        pre = tap[CONV : CONV + 1] + tap[CONV - 1 : CONV] * x[8:]
        for lag in range(1, CONV):
            earlier = pltpu.roll(x, lag, 0)[8:]
            pre = pre + tap[CONV - 1 - lag : CONV - lag] * jnp.where(place >= lag, earlier, 0.0)
        sg = logistic(pre)
        slope[rows, pl.ds(c, LANES)] = (sg * (1.0 + pre * (1.0 - sg))).astype(bf16)
        out[rows, pl.ds(at, LANES)] = (pre * sg).astype(bf16)

    blocks = x_low.shape[0] // BLOCK
    xcols, bcols = inner // LANES, (width - inner) // LANES

    def x_body(i, carry):
        c = pl.multiple_of((i % xcols) * LANES, LANES)
        tile(i // xcols, c, x_low, c)
        return carry

    def bc_body(i, carry):
        c = pl.multiple_of((i % bcols) * LANES, LANES)
        tile(i // bcols, inner + c, bc_low, c)
        return carry

    lax.fori_loop(0, blocks * xcols, x_body, 0)
    lax.fori_loop(0, blocks * bcols, bc_body, 0)


def softplus(v):
    return jnp.maximum(v, 0.0) + jnp.log1p(jnp.exp(-jnp.abs(v)))


def steps(dtin, dpar, step, sgdt, step_low, decay_low):
    def body(i, carry):
        rows = pl.ds(pl.multiple_of(i * BLOCK, BLOCK), BLOCK)
        v = dtin[rows, :] + dpar[0:1, :]
        soft = softplus(v)
        if step is not None:
            step[rows, :] = soft
            sgdt[rows, :] = logistic(v)
        step_low[rows, :] = soft.astype(bf16)
        decay_low[rows, :] = (-dpar[1:2, :] * soft).astype(bf16)
        return carry

    lax.fori_loop(0, dtin.shape[0] // BLOCK, body, 0)


def block_marks(starts, b):
    at = b * BLOCK
    column = doc_of(starts, lax.broadcasted_iota(jnp.int32, (BLOCK, 1), 0) + at)
    row = doc_of(starts, lax.broadcasted_iota(jnp.int32, (1, BLOCK), 1) + at)
    before = doc_of(starts, at - 1)
    last = doc_of(starts, at + BLOCK - 1)
    return column, row, before, last


def block_decays(b, starts, decay_low, step_low, spread):
    rows = pl.ds(pl.multiple_of(b * BLOCK, BLOCK), BLOCK)
    column, row, before, last = block_marks(starts, b)
    i0 = lax.broadcasted_iota(jnp.int32, (BLOCK, BLOCK), 0)
    i1 = lax.broadcasted_iota(jnp.int32, (BLOCK, BLOCK), 1)
    lower = jnp.where(i0 >= i1, 1.0, 0.0).astype(bf16)
    cum = mm(lower, decay_low[rows, :])
    step_e = mm(step_low[rows, :], spread[...])
    cum_e = expand(jnp.exp(cum), spread[...])
    kept_e = jnp.where(before == last, cum_e[BLOCK - 1 : BLOCK], 0.0)
    in_e = jnp.where(column == before, cum_e, 0.0)
    out_e = expand(jnp.exp(cum[BLOCK - 1 : BLOCK] - cum), spread[...])
    out_e = jnp.where(column == last, out_e, 0.0)
    return cum, step_e, kept_e, in_e, out_e, column, row


def scan_forward(
    starts, x_low, bc_low, step_low, decay_low, ssd, states, spread, state, xs, yin, cbm, tick=None
):
    length, inner = x_low.shape
    state[...] = jnp.zeros_like(state)

    def body(b, carry):
        rows = pl.ds(pl.multiple_of(b * BLOCK, BLOCK), BLOCK)
        cum, step_e, kept_e, in_e, out_e, column, row = block_decays(
            b, starts, decay_low, step_low, spread
        )
        bm, cm = bc_low[rows, :STATE], bc_low[rows, STATE:]
        i0 = lax.broadcasted_iota(jnp.int32, (BLOCK, BLOCK), 0)
        i1 = lax.broadcasted_iota(jnp.int32, (BLOCK, BLOCK), 1)
        cbm[...] = jnp.where((column == row) & (i0 >= i1), mm_nt(cm, bm), 0.0)
        stepped = x_low[rows, :].astype(f32) * step_e
        xs[...] = stepped.astype(bf16)
        entering = state[...].astype(bf16)
        states[b] = entering
        yin[...] = in_e * mm(cm, entering)
        state[...] = kept_e * state[...] + mm_tn(bm, (stepped * out_e).astype(bf16))
        cum_t = cum.T
        first = lax.broadcasted_iota(jnp.int32, (BLOCK, LANES), 1) < HEADDIM
        for j in range(inner // LANES):
            cols = slice(j * LANES, (j + 1) * LANES)
            pair = xs[:, cols]
            part = []
            for h in (2 * j, 2 * j + 1):
                span = jnp.minimum(cum[:, h : h + 1] - cum_t[h : h + 1, :], 0.0)
                part.append(mm((jnp.exp(span) * cbm[...]).astype(bf16), pair))
            y = jnp.where(first, part[0], part[1]) + yin[:, cols]
            ssd[rows, cols] = y.astype(bf16)
        if tick is not None:
            tick(b)
        return carry

    lax.fori_loop(0, length // BLOCK, body, 0)


def project_rows(left, right, out, rows=512, columns=512):
    def body(i, carry):
        at = pl.ds(pl.multiple_of(i * rows, rows), rows)
        part = left[at, :]
        for c, w in tiles(out.shape[1], columns):
            out[at, c : c + w] = mm(part, right[:, c : c + w]).astype(out.dtype)
        return carry

    lax.fori_loop(0, out.shape[0] // rows, body, 0)


def back_rows(left, right, out, rows=512, columns=512):
    def body(i, carry):
        at = pl.ds(pl.multiple_of(i * rows, rows), rows)
        part = left[at, :]
        for c, w in tiles(out.shape[1], columns):
            out[at, c : c + w] = mm_nt(part, right[c : c + w, :]).astype(out.dtype)
        return carry

    lax.fori_loop(0, out.shape[0] // rows, body, 0)


def weight_rows(left, right, out, rows=256, columns=512):
    def body(i, carry):
        at = pl.ds(pl.multiple_of(i * rows, rows), rows)
        part = left[:, at]
        for c, w in tiles(out.shape[1], columns):
            out[at, c : c + w] = mm_tn(part, right[:, c : c + w]).astype(out.dtype)
        return carry

    lax.fori_loop(0, out.shape[0] // rows, body, 0)


def gate_sums(gate, ssd, x_low, gnorm, crow, stat):
    step, inner = 64, gate.shape[1]

    def body(i, carry):
        rows = pl.ds(pl.multiple_of(i * step, step), step)
        squares = jnp.zeros((step, 256), f32)
        crosses = jnp.zeros((step, 256), f32)
        for c in range(0, inner, 256):
            cols = slice(c, c + 256)
            g = gate[rows, cols]
            mixed = ssd[rows, cols].astype(f32) + crow[1:2, cols] * x_low[rows, cols].astype(f32)
            gated = mixed * (g * logistic(g))
            squares = squares + gated * gated
            crosses = crosses + gnorm[rows, cols] * crow[0:1, cols] * gated
        lane = lax.broadcasted_iota(jnp.int32, (step, LANES), 1)
        s1 = jnp.sum(squares, axis=1, keepdims=True)
        s2 = jnp.sum(crosses, axis=1, keepdims=True)
        stat[rows, :] = jnp.where(lane == 0, s1, jnp.where(lane == 1, s2, 0.0))
        return carry

    lax.fori_loop(0, gate.shape[0] // step, body, 0)


def gate_squares(gate, ssd, x_low, crow, stat):
    step, inner = 64, gate.shape[1]

    def body(i, carry):
        rows = pl.ds(pl.multiple_of(i * step, step), step)
        squares = jnp.zeros((step, 256), f32)
        for c in range(0, inner, 256):
            cols = slice(c, c + 256)
            g = gate[rows, cols]
            mixed = ssd[rows, cols].astype(f32) + crow[1:2, cols] * x_low[rows, cols].astype(f32)
            value = mixed * (g * logistic(g))
            squares = squares + value * value
        stat[rows, :] = squares[:, :LANES] + squares[:, LANES:]
        return carry

    lax.fori_loop(0, gate.shape[0] // step, body, 0)


def gate_norm(gate, ssd, x_low, inverse_out, crow, gn):
    step, inner = 64, gate.shape[1]

    def body(i, carry):
        rows = pl.ds(pl.multiple_of(i * step, step), step)
        inverse = inverse_out[rows, :1]
        for c in range(0, inner, 256):
            cols = slice(c, c + 256)
            g = gate[rows, cols]
            mixed = ssd[rows, cols].astype(f32) + crow[1:2, cols] * x_low[rows, cols].astype(f32)
            gn[rows, cols] = (mixed * (g * logistic(g)) * inverse * crow[0:1, cols]).astype(bf16)
        return carry

    lax.fori_loop(0, gate.shape[0] // step, body, 0)


def cross_sums(gnorm, gn, stat):
    step, inner = 64, gn.shape[1]

    def body(i, carry):
        rows = pl.ds(pl.multiple_of(i * step, step), step)
        total = jnp.zeros((step, 256), f32)
        for c in range(0, inner, 256):
            cols = slice(c, c + 256)
            total = total + gnorm[rows, cols] * gn[rows, cols].astype(f32)
        stat[rows, :] = total[:, :LANES] + total[:, LANES:]
        return carry

    lax.fori_loop(0, gn.shape[0] // step, body, 0)


def forward_kernel(
    starts, tok, gain, wxd, wz, taps, dpar,
    normed, inverse, xin, slope, gate, x_low, bc_low, step, sgdt, step_low, decay_low, ssd, states,
    pos, spread, dtin, state, xs, yin, cbm,
):
    fill_spread(spread)
    fill_positions(starts, pos, None)
    normalize(tok, gain, normed, inverse)
    project_x(normed, wxd, xin, dtin)
    convolve(xin, taps, pos, slope, x_low, bc_low)
    steps(dtin, dpar, step, sgdt, step_low, decay_low)
    scan_forward(starts, x_low, bc_low, step_low, decay_low, ssd, states, spread, state, xs, yin, cbm)
    project_rows(normed, wz, gate)


def gate_kernel(cot, wout, gate, ssd, x_low, crow, gnorm, stat):
    back_rows(cot, wout, gnorm)
    gate_sums(gate, ssd, x_low, gnorm, crow, stat)


def gate_backward(gate, ssd, x_low, gnorm, crow, stat, width, gn, low_gate, gs, sums, known=None):
    step, inner = 64, ssd.shape[1]
    sums[...] = jnp.zeros_like(sums)

    def body(i, carry):
        rows = pl.ds(pl.multiple_of(i * step, step), step)
        if known is None:
            inverse = lax.rsqrt(stat[rows, 0:1] / width + EPS)
            mean = inverse * stat[rows, 1:2] / width
        else:
            inverse, mean = known[rows, :1], stat[rows, :1]
        for c in range(0, inner, 256):
            cols = slice(c, c + 256)
            g = gate[rows, cols]
            x = x_low[rows, cols].astype(f32)
            mixed = ssd[rows, cols].astype(f32) + crow[1:2, cols] * x
            sg = logistic(g)
            act = g * sg
            hat = mixed * act * inverse
            if gn is not None:
                gn[rows, cols] = (hat * crow[0:1, cols]).astype(bf16)
            gnorm_here = gnorm[rows, cols]
            grad = inverse * (gnorm_here * crow[0:1, cols] - hat * mean)
            grad_mixed = grad * act
            low_gate[rows, cols] = (grad * mixed * (sg * (1.0 + g * (1.0 - sg)))).astype(bf16)
            gs[rows, cols] = grad_mixed.astype(bf16)
            sums[0:8, cols] += fold(gnorm_here * hat)
            sums[8:16, cols] += fold(grad_mixed * x)
        return carry

    lax.fori_loop(0, ssd.shape[0] // step, body, 0)


def middle_kernel(
    cot, wout, normed, gate, x_low, ssd, gnorm, crow, stat,
    branch, dwout, dwz, low_gate, gs, sums,
    gn, *, width,
):
    gate_backward(gate, ssd, x_low, gnorm, crow, stat, width, gn, low_gate, gs, sums)
    project_rows(gn, wout, branch)
    weight_rows(gn, cot, dwout)
    weight_rows(normed, low_gate, dwz)


def scan_backward(
    starts, x_low, bc_low, step_low, decay_low, ssd, states, gs, slope, crow, step, sgdt, dpar,
    gpre, low_xd, dsums, spread, dstate, xs, gx, cbm, acc, tick=None,
):
    length, inner = x_low.shape
    width = gpre.shape[1]
    blocks = length // BLOCK
    dstate[...] = jnp.zeros_like(dstate)
    dsums[...] = jnp.zeros_like(dsums)
    gpre[pl.ds(length, 8), :] = jnp.zeros((8, width), f32)

    def body(i, carry):
        b = blocks - 1 - i
        rows = pl.ds(pl.multiple_of(b * BLOCK, BLOCK), BLOCK)
        cum, step_e, kept_e, in_e, out_e, column, row = block_decays(
            b, starts, decay_low, step_low, spread
        )
        bm, cm = bc_low[rows, :STATE], bc_low[rows, STATE:]
        i0 = lax.broadcasted_iota(jnp.int32, (BLOCK, BLOCK), 0)
        i1 = lax.broadcasted_iota(jnp.int32, (BLOCK, BLOCK), 1)
        linked = (column == row) & (i0 <= i1)
        cbm[...] = jnp.where(linked, mm_nt(bm, cm), 0.0)
        x = x_low[rows, :].astype(f32)
        stepped = x * step_e
        xs[...] = stepped.astype(bf16)
        cum_t = cum.T
        first = lax.broadcasted_iota(jnp.int32, (BLOCK, LANES), 1) < HEADDIM
        acc[...] = jnp.zeros_like(acc)
        for j in range(inner // LANES):
            cols = slice(j * LANES, (j + 1) * LANES)
            xpair, gpair = xs[:, cols], gs[rows, cols]
            none = jnp.zeros_like(xpair)
            part, total = [], None
            for k in range(2):
                h = 2 * j + k
                kernel = jnp.exp(jnp.minimum(cum_t[h : h + 1, :] - cum[:, h : h + 1], 0.0))
                part.append(mm((kernel * cbm[...]).astype(bf16), gpair))
                own = jnp.where(first, xpair, none) if k == 0 else jnp.where(first, none, xpair)
                here = kernel * mm_nt(own, gpair)
                total = here if total is None else total + here
            acc[...] += total
            gx[:, cols] = jnp.where(first, part[0], part[1])
        dstate_low = dstate[...].astype(bf16)
        entering = states[b]
        leaving = states[jnp.minimum(b + 1, blocks - 1)]
        end = jnp.sum(dstate[...] * leaving.astype(f32), axis=0, keepdims=True)
        g = gs[rows, :].astype(f32)
        g_in = (in_e * g).astype(bf16)
        raw = gx[...] + out_e * mm(bm, dstate_low)
        grad_x = (step_e * raw).astype(bf16).astype(f32)
        gpre[rows, :inner] = (grad_x + crow[1:2, :] * g) * slope[rows, :inner]
        pairs = jnp.where(linked, acc[...], 0.0).astype(bf16)
        db = mm(pairs, cm) + mm_nt((stepped * out_e).astype(bf16), dstate_low)
        dc = mm_tn(pairs, bm) + mm_nt(g_in, entering)
        gpre[rows, inner : inner + STATE] = db * slope[rows, inner : inner + STATE]
        gpre[rows, inner + STATE :] = dc * slope[rows, inner + STATE :]
        raw_x = x * raw
        grad_step = gather_heads(raw_x, spread[...]).astype(bf16).astype(f32)
        dcum = gather_heads(g * ssd[rows, :].astype(f32) - step_e * raw_x, spread[...])
        tail = gather_heads(jnp.broadcast_to(end, (8, inner)), spread[...])[0:1]
        upper = jnp.where(i0 <= i1, 1.0, 0.0).astype(bf16)
        high, rest = halves(dcum)
        later = mm(upper, high) + mm(upper, rest) + tail
        grad_decay = later.astype(bf16).astype(f32)
        total_step = grad_step - dpar[1:2, :] * grad_decay
        if sgdt is None:
            before_step = step[rows, :] + dpar[0:1, :]
            slope_here, step_here = logistic(before_step), softplus(before_step)
        else:
            slope_here, step_here = sgdt[rows, :], step[rows, :]
        grad_dt = total_step * slope_here
        low_xd[rows, width:] = grad_dt.astype(bf16)
        dsums[0:8, :] += fold(grad_dt)
        dsums[8:16, :] -= fold(grad_decay * step_here)
        dstate[...] = kept_e * dstate[...] + mm_tn(cm, g_in)
        if tick is not None:
            tick(i)
        return carry

    lax.fori_loop(0, blocks, body, 0)


def convolve_back(xin, gpre, taps, pos, rpos, low_xd, csums, tick=None):
    width = gpre.shape[1]
    columns = width // LANES
    csums[...] = jnp.zeros_like(csums)

    def body(b, j):
        at = pl.multiple_of(b * BLOCK, BLOCK)
        cols = pl.ds(pl.multiple_of(j * LANES, LANES), LANES)
        rows = pl.ds(at, BLOCK)
        x = xin[pl.ds(at, BLOCK + 8), cols]
        g = gpre[pl.ds(at, BLOCK + 8), cols]
        here = g[:BLOCK]
        place, ahead = pos[rows, :], rpos[rows, :]
        tap = taps[:, cols]
        grad = tap[CONV - 1 : CONV] * here
        csums[pl.ds(8 * CONV, 8), cols] += fold(here)
        csums[pl.ds(8 * (CONV - 1), 8), cols] += fold(here * x[8:])
        for lag in range(1, CONV):
            k = CONV - 1 - lag
            later = pltpu.roll(g, BLOCK + 8 - lag, 0)[:BLOCK]
            earlier = pltpu.roll(x, lag, 0)[8:]
            grad = grad + tap[k : k + 1] * jnp.where(ahead >= lag, later, 0.0)
            csums[pl.ds(8 * k, 8), cols] += fold(here * jnp.where(place >= lag, earlier, 0.0))
        low_xd[rows, cols] = grad.astype(bf16)

    def block(b, carry):
        lax.fori_loop(0, columns, lambda j, c: (body(b, j), c)[1], 0)
        if tick is not None:
            tick(b)
        return carry

    lax.fori_loop(0, (xin.shape[0] - 8) // BLOCK, block, 0)


def backward_kernel(
    starts, xin, slope, x_low, bc_low, step, sgdt, step_low, decay_low, ssd, states, gs, taps, crow, dpar,
    low_xd, csums, dsums,
    pos, rpos, spread, gpre, dstate, xs, gx, cbm, acc,
):
    fill_spread(spread)
    fill_positions(starts, pos, rpos)
    scan_backward(
        starts, x_low, bc_low, step_low, decay_low, ssd, states, gs, slope, crow, step, sgdt, dpar,
        gpre, low_xd, dsums, spread, dstate, xs, gx, cbm, acc,
    )
    convolve_back(xin, gpre, taps, pos, rpos, low_xd, csums)


def last_kernel(tok, inverse, gain, normed, low_gate, low_xd, wz, wxd, dwxd, gfull, rowdot):
    weight_rows(normed, low_xd, dwxd)
    rows = 256

    def body(i, carry):
        at = pl.ds(pl.multiple_of(i * rows, rows), rows)
        total = jnp.zeros((rows, 1), f32)
        for c, w in tiles(gfull.shape[1], 512):
            cols = slice(c, c + w)
            part = mm_nt(low_gate[at, :], wz[cols, :]) + mm_nt(low_xd[at, :], wxd[cols, :])
            gfull[at, cols] = part.astype(bf16)
            total = total + jnp.sum(part * gain[:, cols] * tok[at, cols].astype(f32), axis=1, keepdims=True)
        rowdot[at, :] = total * inverse[at, :]
        return carry

    lax.fori_loop(0, gfull.shape[0] // rows, body, 0)


MESH = pl.DeviceIdType.MESH


def remote(source, target, send, receive, **where):
    return pltpu.make_async_remote_copy(
        src_ref=source, dst_ref=target, send_sem=send, recv_sem=receive, device_id=where, device_id_type=MESH
    )


def add_into(target, source, rows=64):
    def body(i, carry):
        at = pl.ds(pl.multiple_of(i * rows, rows), rows)
        target[at, :] = (target[at, :].astype(f32) + source[at, :].astype(f32)).astype(target.dtype)
        return carry

    lax.fori_loop(0, target.shape[0] // rows, body, 0)


class Ring:
    def __init__(self):
        self.me = lax.axis_index("dp")
        self.core = self.me % 2
        chip = self.me // 2
        y = chip // 2
        self.pos = 2 * y + (chip + y) % 2
        self.partner = self.me + 1 - 2 * self.core
        self.right = self.at(self.pos + 1)
        self.left = self.at(self.pos + 3)
        self.across = self.at(self.pos + 2)

    def at(self, pos):
        pos = pos % 4
        y = pos // 2
        return (2 * y + (pos + y) % 2) * 2 + self.core


def greet(ring, everyone):
    barrier = pltpu.get_barrier_semaphore()
    n, z = lax.axis_size("mp"), lax.axis_index("mp")
    if everyone:
        size = lax.axis_size("dp")
        close = [(ring.me + i) % size for i in range(1, size)]
    else:
        close = [ring.partner, ring.right, ring.left]
    for other in close:
        pl.semaphore_signal(barrier, inc=1, device_id={"dp": other}, device_id_type=MESH)
    for i in range(1, n):
        pl.semaphore_signal(barrier, inc=1, device_id={"mp": (z + i) % n}, device_id_type=MESH)
    return lambda: pl.semaphore_wait(barrier, len(close) + n - 1)


class Scatter:
    def __init__(self, ring, shard, cores, parts, wholes, sems):
        self.ring, self.shard = ring, shard
        self.cores, self.parts, self.wholes = cores, parts, wholes
        self.core_send, self.core_recv, self.ring_send, self.ring_recv = sems
        self.half = cores.shape[1] // 2

    def upper(self, r):
        return self.shard(r).at[pl.ds(0, self.half), :]

    def lower(self, r):
        return self.shard(r).at[pl.ds(self.half, self.half), :]

    def core_copy(self, chip):
        ring = self.ring
        return remote(
            self.shard(2 * chip + 1 - ring.core), self.cores.at[chip],
            self.core_send.at[chip], self.core_recv.at[chip], dp=ring.partner,
        )

    def ring_copy(self, k):
        ring = self.ring
        source = (self.upper(ring.across), self.lower(ring.across), self.shard(ring.right), self.shard(ring.left))[k]
        target = (self.parts.at[0], self.parts.at[1], self.wholes.at[0], self.wholes.at[1])[k]
        return remote(
            source, target, self.ring_send.at[k], self.ring_recv.at[k], dp=(ring.right, ring.left)[k % 2]
        )

    def start(self, chip):
        self.core_copy(chip).start()

    def first(self):
        def body(chip, carry):
            self.core_copy(chip).wait_recv()
            add_into(self.shard(2 * chip + self.ring.core), self.cores.at[chip])
            return carry

        lax.fori_loop(0, 4, body, 0)
        self.ring_copy(0).start()
        self.ring_copy(1).start()

    def second(self):
        self.ring_copy(0).wait_recv()
        add_into(self.upper(self.ring.right), self.parts.at[0])
        self.ring_copy(2).start()
        self.ring_copy(1).wait_recv()
        add_into(self.lower(self.ring.left), self.parts.at[1])
        self.ring_copy(3).start()

    def finish(self, out, rows=64):
        self.ring_copy(2).wait_recv()
        self.ring_copy(3).wait_recv()
        own = self.shard(self.ring.me)

        def body(i, carry):
            at = pl.ds(pl.multiple_of(i * rows, rows), rows)
            out[at, :] = own[at, :].astype(f32) + self.wholes[0, at, :].astype(f32) + self.wholes[1, at, :].astype(f32)
            return carry

        lax.fori_loop(0, out.shape[0] // rows, body, 0)

        def done(chip, carry):
            self.core_copy(chip).wait_send()
            return carry

        lax.fori_loop(0, 4, done, 0)
        for k in range(4):
            self.ring_copy(k).wait_send()


class Line:
    def __init__(self, piece, slot, blocks, sems, total, depth):
        self.piece, self.slot, self.blocks, self.total, self.depth = piece, slot, blocks, total, depth
        self.send, self.recv = sems
        self.n, self.z = lax.axis_size("mp"), lax.axis_index("mp")
        self.place = (self.z, self.n - 1 - self.z)

    def rows(self, t):
        return pl.ds(pl.multiple_of(t * BLOCK, BLOCK), BLOCK)

    def source(self, side, k):
        d = k // self.blocks
        return self.piece(k - d * self.blocks, self.n - 1 - d if side == 0 else d)

    def copy(self, side, place, k):
        return remote(
            self.source(side, k), self.slot(side, place + 1, k), self.send.at[side, k], self.recv.at[side, k],
            mp=self.z + 1 if side == 0 else self.z - 1,
        )

    def arrived(self, side, place, k):
        target = self.slot(side, place, k)
        remote(target, target, self.send.at[side, k], self.recv.at[side, k], mp=self.z).wait_recv()
        return target

    def inject(self, k):
        for side in range(2):
            @pl.when(self.place[side] == 0)
            def _():
                @pl.when(jnp.int32(k) >= self.depth)
                def _():
                    self.copy(side, 0, jnp.maximum(k - self.depth, 0)).wait_send()

                self.copy(side, 0, k).start()

    def forward(self, k, hop):
        for side in range(2):
            @pl.when(self.place[side] == hop)
            def _():
                add_into(self.source(side, k), self.arrived(side, hop, k))
                self.copy(side, hop, k).start()

    def finish(self, t):
        self.total[...] = self.piece(t, self.z)[...].astype(f32)
        for side in range(2):
            for place in range(1, self.n):
                @pl.when(self.place[side] == place)
                def _():
                    self.total[...] += self.arrived(side, place, (self.n - 1 - place) * self.blocks + t)[...].astype(f32)

    def drain(self):
        for side in range(2):
            for place in range(self.n - 1):
                count = (self.n - 1 - place) * self.blocks

                @pl.when(self.place[side] == place)
                def _():
                    def body(k, carry):
                        self.copy(side, place, k).wait_send()
                        return carry

                    lax.fori_loop(count - self.depth if place == 0 else 0, count, body, 0)

    def order(self, i):
        z = self.z
        far = jnp.where(z < 2, 3 - i, i)
        near = z + 1 - 2 * (z % 2)
        return jnp.where(i < 2, far, jnp.where(i == 2, near, z))


class Loads:
    def __init__(self, sems):
        self.sems, self.pairs = sems, []

    def start(self, source, target):
        i = len(self.pairs)
        copy = pltpu.make_async_copy(source, target, self.sems.at[i])
        copy.start()
        self.pairs.append(copy)
        return copy


class Gather:
    def __init__(self, ring, shard, rows, sems):
        self.ring, self.shard, self.half = ring, shard, rows // 2
        self.ring_send, self.ring_recv, self.core_send, self.core_recv = sems
        self.other = 1 - 2 * ring.core

    def ring_copy(self, k, source):
        ring = self.ring
        half = (0, 1, 1, 0, 0, 1)[k]
        piece = self.shard(source).at[pl.ds(half * self.half, self.half), :]
        return remote(
            piece, piece, self.ring_send.at[k], self.ring_recv.at[k], dp=(ring.right, ring.left)[k % 2]
        )

    def core_copy(self, k, source):
        return remote(
            self.shard(source), self.shard(source), self.core_send.at[k], self.core_recv.at[k], dp=self.ring.partner
        )

    def start(self):
        me = self.ring.me
        for k in range(4):
            self.ring_copy(k, me).start()
        self.core_copy(0, me).start()

    def second(self):
        left, right = self.ring.left, self.ring.right
        self.ring_copy(0, left).wait_recv()
        self.ring_copy(4, left).start()
        self.ring_copy(1, right).wait_recv()
        self.ring_copy(5, right).start()

    def beside(self):
        left, right = self.ring.left, self.ring.right
        self.ring_copy(2, left).wait_recv()
        self.core_copy(1, left).start()
        self.ring_copy(3, right).wait_recv()
        self.core_copy(2, right).start()

    def third(self):
        across = self.ring.across
        self.ring_copy(4, across).wait_recv()
        self.ring_copy(5, across).wait_recv()
        self.core_copy(3, across).start()

    def arrived(self, k):
        ring = self.ring
        source = (ring.me, ring.left, ring.right, ring.across)[k] + self.other
        self.core_copy(k, source).wait_recv()

    def drain(self):
        ring = self.ring
        for k, source in enumerate((ring.me, ring.me, ring.me, ring.me, ring.left, ring.right)):
            self.ring_copy(k, source).wait_send()
        for k, source in enumerate((ring.me, ring.left, ring.right, ring.across)):
            self.core_copy(k, source).wait_send()


def cast_into(target, source, rows=64):
    def body(i, carry):
        at = pl.ds(pl.multiple_of(i * rows, rows), rows)
        target[at, :] = source[at, :].astype(target.dtype)
        return carry

    lax.fori_loop(0, target.shape[0] // rows, body, 0)


def trunk_kernel(
    lengths, tok, cot, w_x, w_z, w_out, w_bc, w_dt, conv_x, conv_x_bias, conv_bc, conv_bc_bias, dt_bias, a_rate,
    d_skip, gain, out_gain,
    normed_o, xin_o, wx_o, wz_o, low_gate_o, low_xd_o, out_o, dwout_o, inverse_o, part_o,
    csums_o, dsums_o, sums_o, rows_o, colacc_o,
    csums, dsums, sums, rows, colacc, v_tok, stage_b, normed, xin, first_wide, slope, both, states, wx, wbd, wz, wout,
    bc_low, step_low, decay_low, inverse_out, taps, crow, dpar,
    bc_slots, tap_slots, row_slots, cross_slots, stat, turned,
    pos, rpos, spread, dtin, state, xs, wide, cbm, acc, near, cores, parts, wholes,
    load_sems, store_sems, token_sems, part_sems, out_sems, ring_send, ring_recv, core_send, core_recv, mp_send, mp_recv, line_send, line_recv,
    scatter_core_send, scatter_core_recv, scatter_ring_send, scatter_ring_recv,
):
    ring = Ring()
    loads, stores = Loads(load_sems), Loads(store_sems)
    load_x = loads.start(w_x, wide)
    met = greet(ring, False)
    n, z = lax.axis_size("mp"), lax.axis_index("mp")
    length, features = normed.shape
    x_low, ssd = both.at[pl.ds(0, length), :], both.at[pl.ds(length, length), :]
    stage_a = wide
    inverse = inverse_out
    inner, width = x_low.shape[1], xin.shape[1]
    own = features // n
    pair = width - inner
    bd_rows = pair + 32
    shard, column_shard = stage_a.shape[0], stage_b.shape[1]
    heads, per = w_dt.shape[0], w_bc.shape[0]
    load_tok = loads.start(tok, v_tok)
    load_out = loads.start(w_out, stage_b)
    starts = [jnp.int32(0)]
    for k in range(DOCS - 1):
        starts.append(starts[-1] + lengths[0, k])

    def exchange(k, i):
        slots = (bc_slots, tap_slots, row_slots, cross_slots)[k]
        at = k * (n - 1) + i - 1
        return remote(slots.at[0], slots.at[i], mp_send.at[at], mp_recv.at[at], mp=(z + i) % n)

    def rows_of(ref, low, high):
        def shard_of(r):
            return ref.at[pl.ds(pl.multiple_of(r * shard, shard), shard), pl.ds(low, high - low)]

        return shard_of

    def columns_of(r):
        return wout.at[:, pl.ds(pl.multiple_of(r * column_shard, column_shard), column_shard)]

    sems = [tuple(group.at[k] for group in (ring_send, ring_recv, core_send, core_recv)) for k in range(4)]
    get_x = Gather(ring, rows_of(wx, 0, inner), shard, sems[0])
    get_bd = Gather(
        ring, lambda r: wbd.at[pl.ds(0, bd_rows), pl.ds(pl.multiple_of(r * shard, shard), shard)], bd_rows, sems[1]
    )
    get_z = Gather(ring, rows_of(wz, 0, inner), shard, sems[2])
    get_out = Gather(ring, columns_of, inner, sems[3])

    load_x.wait()
    cast_into(get_x.shard(ring.me), stage_a)
    met()
    get_x.start()
    bc_slots[0] = w_bc[...].astype(bf16)
    tap_slots[0] = jnp.zeros_like(tap_slots[0])
    tap_slots[0, :CONV, :per] = conv_bc[...]
    tap_slots[0, CONV : CONV + 1, :per] = conv_bc_bias[...]
    my_columns = pl.ds(pl.multiple_of(ring.me * shard, shard), shard)
    wbd[pair : pair + heads, my_columns] = w_dt[...].astype(bf16)
    wbd[pair + heads : bd_rows, my_columns] = jnp.zeros((bd_rows - pair - heads, shard), bf16)
    wbd[bd_rows:, :] = jnp.zeros((wbd.shape[0] - bd_rows, features), bf16)
    dpar[...] = jnp.zeros_like(dpar)
    dpar[0:1, :heads] = dt_bias[...]
    dpar[1:2, :heads] = a_rate[...]
    dpar[2:3, :heads] = d_skip[...]
    for k in range(2):
        for i in range(1, n):
            exchange(k, i).start()
    load_z = loads.start(w_z, stage_a)
    fill_spread(spread)
    fill_positions(starts, pos, rpos)
    crow[0:1, :] = out_gain[...]
    crow[1:2, :] = expand(dpar[...], spread[...])[2:3]
    load_tok.wait()
    normalize(v_tok, gain, normed, inverse)
    load_cot = loads.start(cot, v_tok)
    store_normed = stores.start(normed, normed_o)
    store_inverse = stores.start(inverse, inverse_o)
    for k in range(2):
        for i in range(1, n):
            exchange(k, i).wait()
    for m in range(n):
        wbd[m * per : (m + 1) * per, my_columns] = bc_slots[(z - m + n) % n]
    get_bd.start()
    first = lax.broadcasted_iota(jnp.int32, (8, LANES), 1) < per
    for j in range(pair // LANES):
        low, high = (z - 2 * j + n) % n, (z - 2 * j - 1 + n) % n
        columns = slice(inner + j * LANES, inner + (j + 1) * LANES)
        taps[:, columns] = jnp.where(first, tap_slots[low], pltpu.roll(tap_slots[high], per, 1))
    taps[:, :inner] = jnp.zeros((8, inner), f32)
    taps[:CONV, :inner] = conv_x[...]
    taps[CONV : CONV + 1, :inner] = conv_x_bias[...]
    load_z.wait()
    cast_into(get_z.shard(ring.me), stage_a)
    load_out.wait()
    cast_into(get_out.shard(ring.me), stage_b)
    xin[pl.ds(0, 8), :] = jnp.zeros((8, width), f32)

    def project_chip(k, source):
        get_x.arrived(k)
        part = pl.ds(pl.multiple_of((source // 2) * 2 * shard, 2 * shard), 2 * shard)

        def body(i, carry):
            at = pl.multiple_of(i * 512, 512)
            left = normed[pl.ds(at, 512), part]
            for c, w in tiles(inner, 512):
                here = mm(left, wx[part, c : c + w])
                if k == 0:
                    xin[pl.ds(at + 8, 512), c : c + w] = here
                else:
                    xin[pl.ds(at + 8, 512), c : c + w] += here
            return carry

        lax.fori_loop(0, length // 512, body, 0)

    def project_bd(i, carry):
        at = pl.multiple_of(i * 512, 512)
        here = mm_nt(normed[pl.ds(at, 512), :], wbd[...])
        xin[pl.ds(at + 8, 512), inner:] = here[:, :pair]
        dtin[pl.ds(at, 512), :] = here[:, pair:]
        return carry

    get_x.second()
    project_chip(0, ring.me)
    get_x.beside()
    get_bd.second()
    get_z.start()
    get_bd.beside()
    project_chip(1, ring.left)
    project_chip(2, ring.right)
    get_x.third()
    get_bd.third()
    project_chip(3, ring.across)
    store_wx = stores.start(wx, wx_o)
    for i in range(4):
        get_bd.arrived(i)
    lax.fori_loop(0, length // 512, project_bd, 0)
    store_xin = stores.start(xin, xin_o)
    steps(dtin, dpar, None, None, step_low, decay_low)
    convolve(xin, taps, pos, slope, x_low, bc_low)
    get_z.second()
    get_out.start()

    def forward_tick(b):
        @pl.when(b == 0)
        def _():
            get_z.beside()

        @pl.when(b == 3)
        def _():
            get_z.third()

    scan_forward(
        starts, x_low, bc_low, step_low, decay_low, ssd, states, spread, state, xs, wide, cbm, forward_tick
    )
    for k in range(4):
        get_z.arrived(k)
    gate = first_wide.at[pl.ds(0, length), pl.ds(0, inner)]
    gnorm = xin.at[pl.ds(0, length), pl.ds(0, inner)]
    project_rows(normed, wz, gate)
    store_wz = stores.start(wz, wz_o)
    get_out.second()
    gate_squares(gate, ssd, x_low, crow, stat)

    def put_rows(target):
        for b in range(length // BLOCK):
            line_sum = jnp.sum(stat[b * BLOCK : (b + 1) * BLOCK, :].T, axis=0, keepdims=True)
            for j in range(BLOCK // LANES):
                at = b * (BLOCK // LANES) + j
                target[at : at + 1, :] = line_sum[:, j * LANES : (j + 1) * LANES]

    def sum_rows(slots, out, finish):
        sums_here = finish(functools.reduce(lambda p, q: p + q, [slots[i] for i in range(n)]))
        for b in range(length // BLOCK):
            at = b * (BLOCK // LANES)
            row = jnp.concatenate([sums_here[at + j : at + j + 1] for j in range(BLOCK // LANES)], axis=1)
            turned[...] = jnp.broadcast_to(row, turned.shape)
            out[b * BLOCK : (b + 1) * BLOCK, :] = turned[...].T

    put_rows(row_slots.at[0])
    get_x.drain()
    get_bd.drain()
    store_wx.wait()
    for i in range(1, n):
        exchange(2, i).start()
    load_cot.wait()
    store_xin.wait()

    def back_chip(k, source):
        if k < 3:
            get_out.arrived(k)
        part = pl.ds(pl.multiple_of((source // 2) * 2 * column_shard, 2 * column_shard), 2 * column_shard)

        def body(i, carry):
            at = pl.ds(pl.multiple_of(i * 512, 512), 512)
            left = v_tok[at, part]
            for c, w in tiles(inner, 512):
                here = mm_nt(left, wout[c : c + w, part])
                if k == 0:
                    gnorm[at, c : c + w] = here
                else:
                    gnorm[at, c : c + w] += here
            return carry

        lax.fori_loop(0, length // 512, body, 0)

    back_chip(0, ring.me)
    get_out.beside()
    back_chip(1, ring.left)
    back_chip(2, ring.right)
    for i in range(1, n):
        exchange(2, i).wait()
    store_inverse.wait()
    sum_rows(row_slots, inverse_out, lambda total: lax.rsqrt(total / (inner * n) + EPS))
    get_out.third()
    store_normed.wait()
    gn = normed.at[:, pl.ds(0, inner)]
    gs = normed.at[:, pl.ds(inner, inner)]
    get_z.drain()
    store_wz.wait()
    gate_norm(gate, ssd, x_low, inverse_out, crow, gn)
    get_out.arrived(3)

    fold_columns = inner // own

    def piece(t, q):
        row = pl.multiple_of((q // fold_columns) * length + t * BLOCK, BLOCK)
        return wz.at[pl.ds(row, BLOCK), pl.ds(pl.multiple_of((q % fold_columns) * own, own), own)]

    def slot(side, place, k):
        if place == 2:
            return near.at[k]
        row = pl.multiple_of((k // fold_columns) * BLOCK, BLOCK)
        return wx.at[pl.ds(row, BLOCK), pl.ds(pl.multiple_of((k % fold_columns) * own, own), own)]

    total = wide.at[:, pl.ds(0, own)]
    line = Line(piece, slot, length // BLOCK, (line_send, line_recv), total, 4)

    def quarter(i, carry):
        q = line.order(i)
        columns = pl.ds(pl.multiple_of(q * own, own), own)
        for r in range(0, length, 512):
            at = pl.ds(pl.multiple_of((q // fold_columns) * length + r, 512), 512)
            cols = pl.ds(pl.multiple_of((q % fold_columns) * own, own), own)
            wz[at, cols] = mm(gn[r : r + 512, :], wout[:, columns]).astype(bf16)
            if r == 0:
                @pl.when(i == 0)
                def _():
                    line.inject(0)
                    line.inject(1)

        return carry

    quarter(0, 0)
    back_chip(3, ring.across)
    cross_sums(gnorm, gn, stat)
    put_rows(cross_slots.at[0])
    for i in range(1, n):
        exchange(3, i).start()
    line.inject(2)
    lax.fori_loop(1, n, quarter, 0)
    line.inject(3)
    get_out.drain()
    grads = wout
    scatter = Scatter(
        ring, lambda r: grads.at[:, pl.ds(pl.multiple_of(r * column_shard, column_shard), column_shard)],
        cores, parts, wholes, (scatter_core_send, scatter_core_recv, scatter_ring_send, scatter_ring_recv),
    )
    chunk = 2 * column_shard

    def weight(j, carry):
        columns = pl.ds(pl.multiple_of(j * chunk, chunk), chunk)
        for r in range(0, inner, 256):
            grads[r : r + 256, columns] = mm_tn(gn[:, r : r + 256], v_tok[:, columns]).astype(bf16)
        scatter.start(j)
        return carry

    lax.fori_loop(0, 4, weight, 0)
    line.inject(4)
    line.forward(0, 1)
    xd = v_tok.at[:, pl.ds(0, width + LANES)]
    token_own = v_tok.at[:, pl.ds(width + LANES, own)]
    load_own = loads.start(tok.at[:, pl.ds(pl.multiple_of(z * own, own), own)], token_own)
    for i in range(1, n):
        exchange(3, i).wait()
    sum_rows(cross_slots, stat, lambda total: total / (inner * n))
    low_gate = gn
    gate_backward(gate, ssd, x_low, gnorm, crow, stat, inner * n, None, low_gate, gs, sums, known=inverse_out)
    load_xin = loads.start(xin_o, xin)
    stores.start(low_gate, low_gate_o)
    stores.start(sums, sums_o)
    line.inject(5)
    line.forward(1, 1)
    line.forward(0, 2)
    scatter.first()

    def scan_tick(i):
        line.inject(i + 6)
        line.forward(i + 2, 1)

        @pl.when(i < 3)
        def _():
            line.forward(i + 1, 2)

        @pl.when(i == 1)
        def _():
            scatter.second()

    gpre = first_wide
    scan_backward(
        starts, x_low, bc_low, step_low, decay_low, ssd, states, gs, slope, crow, dtin, None, dpar,
        gpre, xd, dsums, spread, state, xs, wide, cbm, acc, scan_tick,
    )
    weight_loads = [loads.start(wz_o, both)]
    inverse_in = dtin
    weight_loads.append(loads.start(inverse_o, inverse_in))

    def token_copy(i):
        return pltpu.make_async_copy(
            tok.at[:, pl.ds(pl.multiple_of(line.order(i) * own, own), own)],
            normed.at[:, pl.ds(pl.multiple_of(inner + (i % 2) * own, own), own)], token_sems.at[i],
        )

    token_copy(0).start()
    token_copy(1).start()
    scatter.finish(stage_b)
    stores.start(stage_b, dwout_o)
    for h in range(2):
        weight_loads.append(
            loads.start(wx_o.at[pl.ds(h * length, length), :], wout.at[:, pl.ds(h * inner, inner)])
        )
    load_xin.wait()

    def conv_tick(b):
        @pl.when(b % 2 == 1)
        def _():
            line.inject(10 + b // 2)
            line.forward(6 + b // 2, 1)

    convolve_back(xin, gpre, taps, pos, rpos, xd, csums, conv_tick)
    for source, target in ((xd, low_xd_o), (csums, csums_o), (dsums, dsums_o)):
        stores.start(source, target)
    for copy in weight_loads:
        copy.wait()
    stat[...] = jnp.zeros_like(stat)
    half = own // 2

    def part_copy(i, h):
        column = pl.multiple_of(line.order(i) * own + h * half, half)
        return pltpu.make_async_copy(
            cores.at[(i % 2) * 2 + h], part_o.at[:, pl.ds(column, half)], part_sems.at[i, h]
        )

    def grad_quarter(i, carry):
        q = line.order(i)
        columns = pl.ds(pl.multiple_of(q * own, own), own)
        low = pl.ds(pl.multiple_of((q % 2) * own, own), own)
        high = q // 2
        x_columns = pl.ds(pl.multiple_of(high * inner, inner), inner)
        token_columns = pl.ds(pl.multiple_of(inner + (i % 2) * own, own), own)
        token_copy(i).wait()

        @pl.when(i >= 2)
        def _():
            for h in range(2):
                part_copy(jnp.maximum(i - 2, 0), h).wait()

        for r in range(0, length, 256):
            at = slice(r, r + 256)
            here = mm_nt(low_gate[at, :], both[columns, :])
            here = here + mm_nt(xd[at, :inner], wout[low, x_columns])
            here = here + mm(xd[at, inner:], wbd[:, columns])
            for h in range(2):
                cores[(i % 2) * 2 + h, at, :] = here[:, h * half : (h + 1) * half].astype(bf16)
            along = here * (normed[at, token_columns].astype(f32) * inverse_in[at, :1])
            folded = fold(along)
            if r == 0:
                colacc[:, columns] = folded
            else:
                colacc[:, columns] += folded
            along = along * gain[:, columns]
            sum_lanes = along[:, :LANES]
            for c in range(LANES, own, LANES):
                sum_lanes = sum_lanes + along[:, c : c + LANES]
            stat[at, :] += sum_lanes
        for h in range(2):
            part_copy(i, h).start()

        @pl.when(i < 2)
        def _():
            token_copy(jnp.minimum(i + 2, n - 1)).start()

        return carry

    lax.fori_loop(0, n, grad_quarter, 0)
    put_rows(rows)
    stores.start(rows, rows_o)
    stores.start(colacc, colacc_o)
    load_own.wait()

    def last(t, carry):
        line.finish(t)
        value = (token_own[line.rows(t), :].astype(f32) + total[...]).astype(bf16)
        for h in range(2):
            wholes[h, line.rows(t), :] = value[:, h * half : (h + 1) * half]
            out_copy(t, h).start()
        return carry

    def out_copy(t, h):
        return pltpu.make_async_copy(
            wholes.at[h, line.rows(t), :], out_o.at[line.rows(t), pl.ds(h * half, half)], out_sems.at[t, h]
        )

    lax.fori_loop(0, line.blocks, last, 0)
    line.drain()
    for t in range(line.blocks):
        for h in range(2):
            out_copy(t, h).wait()
    for i in range(2, n):
        for h in range(2):
            part_copy(i, h).wait()
    for copy in stores.pairs:
        if not any(copy is done for done in (store_normed, store_inverse, store_xin, store_wx, store_wz)):
            copy.wait()


def input_kernel(
    tok, inverse, gain, normed, low_gate, low_xd, part_o, cot, rows_o, colacc, csums, sums, dsums,
    dwz_o, dwx_o, grad_o, dwbc_o, dwdt_o, conv_x_o, conv_x_bias_o, conv_bc_o, conv_bc_bias_o, dt_bias_o, a_rate_o,
    d_skip_o, in_gain_o, out_gain_o,
    dwbc, dwdt, conv_x, conv_x_bias, conv_bc, conv_bc_bias, dt_bias, a_rate, d_skip, in_gain, out_gain,
    dwz, dwxd, grad, smalls, spread, bc_turned, bc_own, bc_slots,
    v_inverse, v_normed, v_gate, v_xd, v_cot, v_tok, v_colacc, v_csums, v_sums, v_dsums,
    part, slots, total, z_grads, z_cores, z_parts, z_wholes, x_grads, x_cores, x_parts, x_wholes,
    rows_slots, dp_in, mp_in, turned,
    load_sems, part_sems, grad_sems, line_send, line_recv, z_core_send, z_core_recv, z_ring_send, z_ring_recv,
    x_core_send, x_core_recv, x_ring_send, x_ring_recv,
    rows_send, rows_recv, dp_send, dp_recv, mp_send, mp_recv, bc_send, bc_recv,
):
    ring = Ring()
    met = greet(ring, True)
    loads = Loads(load_sems)
    n = lax.axis_size("mp")
    z = lax.axis_index("mp")
    size = lax.axis_size("dp")
    length, features = part.shape
    inner = v_gate.shape[1]
    width = v_csums.shape[1]
    heads, per = dwdt.shape[0], dwbc.shape[0]
    own = features // n

    def quarter_columns(q):
        return pl.ds(pl.multiple_of(q * own, own), own)

    line = Line(
        lambda t, q: part.at[pl.ds(pl.multiple_of(t * BLOCK, BLOCK), BLOCK), quarter_columns(q)],
        lambda side, place, k: slots.at[side, k], length // BLOCK, (line_send, line_recv), total, 3,
    )

    def part_copy(i):
        columns = quarter_columns(line.order(i))
        return pltpu.make_async_copy(part_o.at[:, columns], part.at[:, columns], part_sems.at[i])

    load_rows = loads.start(rows_o, rows_slots.at[0])
    part_copy(0).start()

    def rows_copy(i):
        return remote(
            rows_slots.at[0], rows_slots.at[i], rows_send.at[i - 1], rows_recv.at[i - 1], mp=(z + i) % n
        )

    load_rows.wait()
    met()
    for i in range(1, n):
        rows_copy(i).start()
    part_copy(0).wait()
    line.inject(0)
    line.inject(1)
    for i in range(1, n):
        part_copy(i).start()
    load_gate, load_normed, load_xd = [
        loads.start(source, target) for source, target in ((low_gate, v_gate), (normed, v_normed), (low_xd, v_xd))
    ]
    load_sums = [
        loads.start(source, target)
        for source, target in ((colacc, v_colacc), (csums, v_csums), (sums, v_sums), (dsums, v_dsums))
    ]
    own_columns = quarter_columns(z)
    later = [
        loads.start(source, target)
        for source, target in (
            (cot.at[:, own_columns], v_cot), (tok.at[:, own_columns], v_tok), (inverse, v_inverse),
        )
    ]

    gain_width = features // 8

    def dp_copy(i):
        return remote(
            smalls, dp_in.at[i - 1], dp_send.at[i - 1], dp_recv.at[i - 1], dp=(ring.me + i) % size
        )

    def mp_copy(i):
        return remote(
            smalls.at[:, pl.ds(inner, width - inner + gain_width)], mp_in.at[i - 1],
            mp_send.at[i - 1], mp_recv.at[i - 1], mp=(z + i) % n,
        )

    for copy in load_sums:
        copy.wait()
    smalls[...] = jnp.zeros_like(smalls)
    for k in range(CONV + 1):
        smalls[k : k + 1, :width] = jnp.sum(v_csums[8 * k : 8 * k + 8, :], axis=0, keepdims=True)
    for k in range(2):
        smalls[CONV + 1 + k : CONV + 2 + k, :inner] = jnp.sum(v_sums[8 * k : 8 * k + 8, :], axis=0, keepdims=True)
        smalls[7:8, k * LANES : (k + 1) * LANES] = jnp.sum(v_dsums[8 * k : 8 * k + 8, :], axis=0, keepdims=True)
    for k in range(8):
        columns = slice(k * gain_width, (k + 1) * gain_width)
        smalls[k : k + 1, width:] = jnp.sum(v_colacc[:, columns], axis=0, keepdims=True)
    for i in range(1, size):
        dp_copy(i).start()
    shard = dwz.shape[0]
    z_scatter = Scatter(
        ring, lambda r: z_grads.at[pl.ds(pl.multiple_of(r * shard, shard), shard), :], z_cores, z_parts, z_wholes,
        (z_core_send, z_core_recv, z_ring_send, z_ring_recv),
    )
    x_scatter = Scatter(
        ring, lambda r: x_grads.at[pl.ds(pl.multiple_of(r * shard, shard), shard), :], x_cores, x_parts, x_wholes,
        (x_core_send, x_core_recv, x_ring_send, x_ring_recv),
    )

    def weight(j, right, grads):
        for c in range(0, 2 * shard, shard):
            rows = pl.ds(pl.multiple_of(j * 2 * shard + c, shard), shard)
            left = v_normed[:, rows]
            for at, w in tiles(grads.shape[1], 512):
                grads[rows, at : at + w] = mm_tn(left, right[:, at : at + w]).astype(bf16)

    load_gate.wait()
    load_normed.wait()

    def z_weight(j, carry):
        weight(j, v_gate, z_grads)
        z_scatter.start(j)
        return carry

    lax.fori_loop(0, 4, z_weight, 0)
    for i in range(1, n):
        part_copy(i).wait()
    line.inject(2)
    line.forward(0, 1)
    load_xd.wait()

    def x_weight(j, carry):
        weight(j, v_xd, x_grads)
        x_scatter.start(j)

        @pl.when(j == 1)
        def _():
            z_scatter.first()

        @pl.when(j % 2 == 1)
        def _():
            line.inject(3 + j // 2)
            line.forward(1 + j // 2, 1)

        return carry

    lax.fori_loop(0, 4, x_weight, 0)
    line.forward(0, 2)
    z_scatter.second()
    line.inject(5)
    line.forward(3, 1)
    line.forward(1, 2)
    x_scatter.first()
    line.inject(6)
    line.forward(4, 1)
    line.forward(2, 2)
    for i in range(1, size):
        dp_copy(i).wait()
    smalls[...] += functools.reduce(lambda a, b: a + b, [dp_in[i] for i in range(size - 1)])
    for i in range(1, n):
        mp_copy(i).start()
    line.inject(7)
    line.forward(5, 1)
    line.forward(3, 2)
    z_scatter.finish(dwz)
    store_z = loads.start(dwz, dwz_o)
    x_scatter.second()
    line.inject(8)
    line.forward(6, 1)
    line.inject(9)
    line.forward(7, 1)
    line.inject(10)
    x_scatter.finish(dwxd)

    bc_turned[...] = dwxd[:, inner:width].T
    bc_own[...] = bc_turned[...].astype(bf16)

    def weight_copy(i):
        other = (z + i) % n
        return remote(
            bc_own.at[pl.ds(pl.multiple_of(other * per, per), per), :], bc_slots.at[i - 1],
            bc_send.at[i - 1], bc_recv.at[i - 1], mp=other,
        )

    for i in range(1, n):
        weight_copy(i).start()
    line.inject(11)
    store_x = loads.start(dwxd.at[:, pl.ds(0, inner)], dwx_o)
    dwdt[...] = dwxd[:, width:].T[:heads]
    for i in range(1, n):
        rows_copy(i).wait()
        mp_copy(i).wait()
    smalls[:, inner:] += functools.reduce(lambda a, b: a + b, [mp_in[i] for i in range(n - 1)])
    share = LANES // per

    def mine(v):
        turns = [v] + [pltpu.roll(v, LANES - k * per, 1) for k in range(1, share)]
        which = jnp.full(v.shape, z % share, jnp.int32)
        return functools.reduce(lambda a, k: jnp.where(which == k, turns[k], a), range(1, share), turns[0])

    lanes = pl.ds(pl.multiple_of(inner + (z // share) * LANES, LANES), LANES)
    conv_x[...] = smalls[:CONV, :inner]
    conv_x_bias[...] = smalls[CONV : CONV + 1, :inner]
    taps = mine(smalls[:8, lanes])
    conv_bc[...] = taps[:CONV, :per]
    conv_bc_bias[...] = taps[CONV : CONV + 1, :per]
    out_gain[...] = smalls[5:6, :inner]
    fill_spread(spread)
    d_skip[...] = gather_heads(smalls[0:8, :inner], spread[...])[6:7, :heads]
    dt_bias[...] = smalls[7:8, :heads]
    a_rate[...] = smalls[7:8, LANES : LANES + heads]
    rows_own = own // gain_width
    for k in range(rows_own):
        in_gain[:, k * gain_width : (k + 1) * gain_width] = smalls[
            pl.ds(z * rows_own + k, 1), width : width + gain_width
        ]
    for i in range(1, n):
        weight_copy(i).wait()
    dwbc[...] = functools.reduce(
        lambda a, b: a + b, [bc_slots[i].astype(f32) for i in range(n - 1)],
        bc_turned[pl.ds(pl.multiple_of(z * per, per), per), :],
    )
    small = [
        loads.start(source, target)
        for source, target in (
            (dwbc, dwbc_o), (dwdt, dwdt_o), (conv_x, conv_x_o), (conv_x_bias, conv_x_bias_o), (conv_bc, conv_bc_o),
            (conv_bc_bias, conv_bc_bias_o), (dt_bias, dt_bias_o), (a_rate, a_rate_o), (d_skip, d_skip_o),
            (in_gain, in_gain_o), (out_gain, out_gain_o),
        )
    ]
    for copy in later:
        copy.wait()
    means = functools.reduce(lambda a, b: a + b, [rows_slots[i] for i in range(n)]) / features
    rows_slots[0] = means

    def last(t, carry):
        line.finish(t)
        rows = line.rows(t)
        lines = BLOCK // LANES
        row = jnp.concatenate([rows_slots[0, pl.ds(t * lines + j, 1), :] for j in range(lines)], axis=1)
        turned[...] = jnp.broadcast_to(row, turned.shape)
        mean = turned[...].T
        for c in range(0, own, LANES):
            columns = slice(c, c + LANES)
            hat = v_tok[rows, columns].astype(f32) * v_inverse[rows, :]
            gain_here = gain[:, pl.ds(pl.multiple_of(z * own + c, LANES), LANES)]
            change = v_inverse[rows, :] * (total[:, columns] * gain_here - hat * mean)
            grad[rows, columns] = (v_cot[rows, columns].astype(f32) + change).astype(bf16)
        grad_copy(t).start()
        return carry

    def grad_copy(t):
        return pltpu.make_async_copy(grad.at[line.rows(t), :], grad_o.at[line.rows(t), :], grad_sems.at[t])

    lax.fori_loop(0, line.blocks, last, 0)
    line.drain()
    for copy in (store_z, store_x, *small):
        copy.wait()
    for t in range(line.blocks):
        grad_copy(t).wait()


def hand_on_kernel(*refs):
    count = (len(refs) - 2) // 3
    sources, targets, buffers = refs[:count], refs[count : 2 * count], refs[2 * count : 3 * count]
    into, out = refs[-2:]
    there = [pltpu.make_async_copy(sources[k], buffers[k], into.at[k]) for k in range(count)]
    back = [pltpu.make_async_copy(buffers[k], targets[k], out.at[k]) for k in range(count)]
    for copy in there:
        copy.start()
    for k in range(count):
        there[k].wait()
        back[k].start()
    for copy in back:
        copy.wait()


def hand_on(*arrays):
    kinds = [(v.shape, v.dtype) for v in arrays]
    count = len(arrays)
    return call(
        hand_on_kernel, kinds, kinds, 0, *arrays,
        places="a" * len(arrays), sems=[(count,)] * 2, far=len(arrays),
    )


def call(kernel, outs, scratch, smem, *operands, places=None, sems=(), collective=None, far=0):
    spaces = {"s": pltpu.SMEM, "v": pltpu.VMEM, "a": pl.ANY}
    if places is None:
        places = "s" * smem + "v" * (len(operands) - smem)
    extra = {} if collective is None else dict(collective_id=collective, has_side_effects=True)
    return pl.pallas_call(
        kernel,
        out_shape=[jax.ShapeDtypeStruct(shape, kind) for shape, kind in outs],
        in_specs=[pl.BlockSpec(memory_space=spaces[c]) for c in places],
        out_specs=[pl.BlockSpec(memory_space=pl.ANY if i < far else pltpu.VMEM) for i in range(len(outs))],
        scratch_shapes=[pltpu.VMEM(shape, kind) for shape, kind in scratch]
        + [pltpu.SemaphoreType.DMA(shape) for shape in sems],
        compiler_params=pltpu.CompilerParams(vmem_limit_bytes=VMEM_LIMIT, **extra),
    )(*operands)


def per_device_any(
    tokens, cotangent, doc_lengths, w_z, w_x, w_bc, w_dt, w_out, conv_x, conv_x_bias, conv_bc,
    conv_bc_bias, dt_bias, a_rate, d_skip, input_norm_gain, out_gain,
):
    group = lax.axis_size("mp")
    rank = lax.axis_index("mp")
    T, D = tokens.shape
    inner, heads = w_x.shape[1], w_dt.shape[1]
    pair = 2 * STATE
    width = inner + pair
    wide = width + LANES
    own = D // group

    lengths = doc_lengths[0]
    starts = jnp.cumsum(lengths) - lengths
    packed = jnp.concatenate([w_bc, conv_bc, conv_bc_bias[None, :]], axis=0)
    packed = lax.all_gather(packed, "mp", axis=1, tiled=True)
    shard = w_bc.shape[0]
    w_bc_all, taps_bc = packed[:shard], packed[shard:]
    wxd = jnp.concatenate(
        [w_x.astype(bf16), w_bc_all.astype(bf16), w_dt.astype(bf16), jnp.zeros((shard, LANES - heads), bf16)],
        axis=1,
    )
    wxd = lax.all_gather(wxd, "dp", axis=0, tiled=True)
    wz = lax.all_gather(w_z.astype(bf16), "dp", axis=0, tiled=True)
    wout = lax.all_gather(w_out.astype(bf16), "dp", axis=1, tiled=True)
    taps = jnp.concatenate([jnp.concatenate([conv_x, conv_x_bias[None, :]], axis=0), taps_bc], axis=1)
    taps = jnp.pad(taps, ((0, 8 - CONV - 1), (0, 0)))
    crow = jnp.pad(jnp.stack([out_gain, jnp.repeat(d_skip, HEADDIM)]), ((0, 6), (0, 0)))
    dpar = jnp.pad(jnp.stack([dt_bias, a_rate]), ((0, 6), (0, LANES - heads)))
    gain = input_norm_gain[None, :]

    blocks = T // BLOCK
    (
        normed, inverse, xin, slope, gate, x_low, bc_low, step, sgdt, step_low, decay_low, ssd, states,
    ) = call(
        forward_kernel,
        [
            ((T, D), bf16), ((T, LANES), f32), ((T + 8, width), f32), ((T, width), bf16), ((T, inner), f32),
            ((T, inner), bf16), ((T, pair), bf16), ((T, LANES), f32), ((T, LANES), f32),
            ((T, LANES), bf16), ((T, LANES), bf16), ((T, inner), bf16), ((blocks, STATE, inner), bf16),
        ],
        [
            ((T, LANES), jnp.int32), ((LANES, inner), bf16), ((T, LANES), f32), ((STATE, inner), f32),
            ((BLOCK, inner), bf16), ((BLOCK, inner), f32), ((BLOCK, BLOCK), f32),
        ],
        1, starts, tokens, gain, wxd, wz, taps, dpar,
    )
    gnorm, stat = call(
        gate_kernel,
        [((T, inner), f32), ((T, LANES), f32)],
        [],
        0, cotangent, wout, gate, ssd, x_low, crow,
    )
    stat = jnp.pad(lax.psum(stat[:, :8], "mp"), ((0, 0), (0, LANES - 8)))
    branch, dwout, dwz, low_gate, gs, sums = call(
        functools.partial(middle_kernel, width=inner * group),
        [
            ((T, D), bf16), ((inner, D), bf16), ((D, inner), bf16), ((T, inner), bf16), ((T, inner), bf16),
            ((16, inner), f32),
        ],
        [((T, inner), bf16)],
        0, cotangent, wout, normed, gate, x_low, ssd, gnorm, crow, stat,
    )
    low_xd, csums, dsums = call(
        backward_kernel,
        [((T, wide), bf16), ((8 * CONV + 8, width), f32), ((16, LANES), f32)],
        [
            ((T, LANES), jnp.int32), ((T, LANES), jnp.int32), ((LANES, inner), bf16), ((T + 8, width), f32),
            ((STATE, inner), f32), ((BLOCK, inner), bf16), ((BLOCK, inner), f32), ((BLOCK, BLOCK), f32),
            ((BLOCK, BLOCK), f32),
        ],
        1, starts, xin, slope, x_low, bc_low, step, sgdt, step_low, decay_low, ssd, states, gs, taps, crow,
        dpar,
    )
    dwxd, gfull, rowdot = call(
        last_kernel,
        [((D, wide), bf16), ((T, D), bf16), ((T, LANES), f32)],
        [],
        0, tokens, inverse, gain, normed, low_gate, low_xd, wz, wxd,
    )

    def scatter(v, axis, dim):
        return lax.psum_scatter(v, axis, scatter_dimension=dim, tiled=True)

    token_own = lax.dynamic_slice_in_dim(tokens, rank * own, own, 1).astype(f32)
    output = (token_own + scatter(branch, "mp", 1).astype(f32)).astype(bf16)
    w_out_grad = scatter(dwout, "dp", 1).astype(f32)
    w_z_grad = scatter(dwz, "dp", 0).astype(f32)
    dwxd_own = scatter(dwxd, "dp", 0)
    w_x_grad = dwxd_own[:, :inner].astype(f32)
    w_dt_grad = dwxd_own[:, width : width + heads].astype(f32)
    w_bc_grad = scatter(dwxd_own[:, inner:width], "mp", 1).astype(f32)

    g_own = scatter(gfull, "mp", 1).astype(f32)
    gain_own = lax.dynamic_slice_in_dim(input_norm_gain, rank * own, own, 0)
    row_mean = (lax.psum(rowdot[:, 0], "mp") / D)[:, None]
    inv = inverse[:, :1]
    hat = token_own * inv
    cot_own = lax.dynamic_slice_in_dim(cotangent, rank * own, own, 1).astype(f32)
    input_grad = (cot_own + inv * (g_own * gain_own - hat * row_mean)).astype(bf16)
    in_gain = jnp.sum(g_own * hat, axis=0)

    csums = jnp.sum(csums.reshape(CONV + 1, 8, width), axis=1)
    sums = jnp.sum(sums.reshape(2, 8, inner), axis=1)
    dsums = jnp.sum(dsums.reshape(2, 8, LANES), axis=1)[:, :heads]
    csums_bc = scatter(csums[:, inner:], "mp", 1)
    conv_grad, conv_bc_grad, sums, dsums, in_gain = lax.psum(
        (csums[:, :inner], csums_bc, sums, dsums, in_gain), "dp"
    )
    d_skip_grad = jnp.sum(sums[1].reshape(heads, HEADDIM), axis=1)
    return (
        output, input_grad, w_z_grad, w_x_grad, w_bc_grad, w_dt_grad, w_out_grad,
        conv_grad[:CONV], conv_grad[CONV], conv_bc_grad[:CONV], conv_bc_grad[CONV],
        dsums[0], dsums[1], d_skip_grad, in_gain, sums[0],
    )


def per_device(
    tokens, cotangent, doc_lengths, w_z, w_x, w_bc, w_dt, w_out, conv_x, conv_x_bias, conv_bc,
    conv_bc_bias, dt_bias, a_rate, d_skip, input_norm_gain, out_gain,
):
    group, size = lax.axis_size("mp"), lax.axis_size("dp")
    T, D = tokens.shape
    shard, inner = w_x.shape
    heads, per = w_dt.shape[1], w_bc.shape[1]
    pair = per * group
    width = inner + pair
    wide = width + LANES
    own = D // group
    columns = w_out.shape[1]
    blocks = T // BLOCK
    messages = blocks * (group - 1)

    def row(v):
        return v[None, :]

    (
        normed, _, _, _, low_gate, low_xd, output, w_out_grad, inverse, part, csums, dsums, sums, rows, colacc,
    ) = call(
        trunk_kernel,
        [
            ((T, D), bf16), ((T + 8, width), f32), ((D, inner), bf16), ((D, inner), bf16), ((T, inner), bf16),
            ((T, wide), bf16), ((T, own), bf16), ((inner, columns), f32), ((T, LANES), f32), ((T, D), bf16),
            ((8 * CONV + 8, width), f32), ((16, LANES), f32), ((16, inner), f32), ((T // LANES, LANES), f32),
            ((8, D), f32),
        ],
        [
            ((8 * CONV + 8, width), f32), ((16, LANES), f32), ((16, inner), f32), ((T // LANES, LANES), f32),
            ((8, D), f32),
            ((T, D), bf16), ((inner, columns), f32), ((T, D), bf16), ((T + 8, width), f32),
            ((T + 8, width), f32), ((T, width), bf16), ((2 * T, inner), bf16),
            ((blocks, STATE, inner), bf16), ((D, inner), bf16), ((pair + LANES, D), bf16),
            ((D, inner), bf16), ((inner, D), bf16),
            ((T, pair), bf16), ((T, LANES), bf16), ((T, LANES), bf16), ((T, LANES), f32),
            ((8, width), f32), ((8, inner), f32), ((8, LANES), f32),
            ((group, per, shard), bf16), ((group, 8, LANES), f32), ((group, T // LANES, LANES), f32),
            ((group, T // LANES, LANES), f32), ((T, LANES), f32), ((LANES, BLOCK), f32),
            ((T, LANES), jnp.int32), ((T, LANES), jnp.int32), ((LANES, inner), bf16), ((T, LANES), f32),
            ((STATE, inner), f32), ((BLOCK, inner), bf16), ((BLOCK, inner), f32), ((BLOCK, BLOCK), f32),
            ((BLOCK, BLOCK), f32), ((2 * blocks, BLOCK, own), bf16),
            ((4, inner, columns), bf16), ((2, inner // 2, columns), bf16), ((2, inner, columns), bf16),
        ],
        0, doc_lengths, tokens, cotangent, w_x, w_z, w_out, w_bc.T, w_dt.T, conv_x, row(conv_x_bias), conv_bc,
        row(conv_bc_bias), row(dt_bias), row(a_rate), row(d_skip), row(input_norm_gain), row(out_gain),
        places="s" + "a" * 5 + "v" * 11,
        sems=[
            (13,), (13,), (group,), (group, 2), (blocks, 2), (4, 6), (4, 6), (4, 4), (4, 4), (4 * group - 4,), (4 * group - 4,),
            (2, messages), (2, messages), (4,), (4,), (4,), (4,),
        ],
        collective=0,
        far=15,
    )
    w_z_grad, w_x_grad, input_grad, w_bc_grad, w_dt_grad, *small_grads = call(
        input_kernel,
        [
            ((shard, inner), f32), ((shard, inner), f32), ((T, own), bf16), ((per, shard), f32),
            ((heads, shard), f32), ((CONV, inner), f32), ((1, inner), f32), ((CONV, per), f32), ((1, per), f32),
            ((1, heads), f32), ((1, heads), f32), ((1, heads), f32), ((1, own), f32), ((1, inner), f32),
        ],
        [
            ((per, shard), f32), ((heads, shard), f32), ((CONV, inner), f32), ((1, inner), f32), ((CONV, per), f32),
            ((1, per), f32), ((1, heads), f32), ((1, heads), f32), ((1, heads), f32), ((1, own), f32),
            ((1, inner), f32),
            ((shard, inner), f32), ((shard, wide), f32), ((T, own), bf16), ((8, width + D // 8), f32),
            ((LANES, inner), bf16), ((pair, shard), f32), ((pair, shard), bf16), ((group - 1, per, shard), bf16),
            ((T, LANES), f32), ((T, D), bf16), ((T, inner), bf16), ((T, wide), bf16), ((T, own), bf16),
            ((T, own), bf16), ((8, D), f32), ((8 * CONV + 8, width), f32), ((16, inner), f32), ((16, LANES), f32),
            ((T, D), bf16), ((2, messages, BLOCK, own), bf16), ((BLOCK, own), f32),
            ((D, inner), bf16), ((4, shard, inner), bf16), ((2, shard // 2, inner), bf16), ((2, shard, inner), bf16),
            ((D, wide), bf16), ((4, shard, wide), bf16), ((2, shard // 2, wide), bf16), ((2, shard, wide), bf16),
            ((group, T // LANES, LANES), f32), ((size - 1, 8, width + D // 8), f32),
            ((group - 1, 8, pair + D // 8), f32), ((LANES, BLOCK), f32),
        ],
        0, tokens, inverse, row(input_norm_gain), normed, low_gate, low_xd, part, cotangent, rows, colacc, csums,
        sums, dsums,
        places="aav" + "a" * 10,
        sems=[
            (24,), (group,), (blocks,), (2, messages), (2, messages), (4,), (4,), (4,), (4,), (4,), (4,), (4,), (4,),
            (group - 1,), (group - 1,), (size - 1,), (size - 1,), (group - 1,), (group - 1,),
            (group - 1,), (group - 1,),
        ],
        collective=2,
        far=14,
    )
    (
        output, input_grad, w_z_grad, w_x_grad, w_bc_grad, w_dt_grad, w_out_grad, conv_x_grad, conv_x_bias_grad,
        conv_bc_grad, conv_bc_bias_grad, dt_bias_grad, a_rate_grad, d_skip_grad, in_gain_grad, out_gain_grad,
    ) = hand_on(output, input_grad, w_z_grad, w_x_grad, w_bc_grad, w_dt_grad, w_out_grad, *small_grads)
    return (
        output, input_grad, w_z_grad, w_x_grad, w_bc_grad.T, w_dt_grad.T, w_out_grad,
        conv_x_grad, conv_x_bias_grad[0], conv_bc_grad, conv_bc_bias_grad[0], dt_bias_grad[0], a_rate_grad[0],
        d_skip_grad[0], in_gain_grad[0], out_gain_grad[0],
    )


def solution(mesh):
    row, block, column = P("dp", None), P("dp", "mp"), P("mp")
    return jax.shard_map(
        per_device if (mesh.shape["dp"], mesh.shape["mp"]) == (8, 4) else per_device_any,
        mesh=mesh,
        in_specs=(
            row, row, row, block, block, block, block, P("mp", "dp"), P(None, "mp"), column,
            P(None, "mp"), column, column, column, column, P(), column,
        ),
        out_specs=(
            block, block, block, block, block, block, P("mp", "dp"), P(None, "mp"), column,
            P(None, "mp"), column, column, column, column, column, column,
        ),
        check_vma=False,
    )
```

```python
import functools

import jax
import jax.numpy as jnp
from jax import lax
from jax.experimental import pallas as pl
from jax.experimental.pallas import tpu as pltpu
from jax.sharding import PartitionSpec as P

HEADDIM = 64
STATE = 128
CONV = 4
BLOCK = 256
DOCS = 5
LANES = 128
EPS = 1e-05
f32 = jnp.float32
bf16 = jnp.bfloat16
VMEM_LIMIT = 127 * 2**19


def mm(a, b):
    return jnp.dot(a, b, preferred_element_type=f32)


def mm_nt(a, b):
    return lax.dot_general(a, b, (((1,), (1,)), ((), ())), preferred_element_type=f32)


def mm_tn(a, b):
    return lax.dot_general(a, b, (((0,), (0,)), ((), ())), preferred_element_type=f32)


def halves(v):
    high = v.astype(bf16)
    return high, (v - high.astype(f32)).astype(bf16)


def expand(v, spread):
    high, rest = halves(v)
    return mm(high, spread) + mm(rest, spread)


def gather_heads(v, spread):
    high, rest = halves(v)
    return mm_nt(high, spread) + mm_nt(rest, spread)


def logistic(v):
    return 1.0 / (1.0 + jnp.exp(-v))


def tiles(total, size):
    return [(at, min(size, total - at)) for at in range(0, total, size)]


def fold(v):
    return jnp.sum(v.reshape(v.shape[0] // 8, 8, v.shape[1]), axis=0)


def doc_of(starts, place):
    count = (place >= starts[0]).astype(jnp.int32)
    for k in range(1, DOCS):
        count = count + (place >= starts[k]).astype(jnp.int32)
    return count


def fill_spread(spread):
    rows, columns = spread.shape
    head = lax.broadcasted_iota(jnp.int32, (rows, columns), 0)
    channel = lax.broadcasted_iota(jnp.int32, (rows, columns), 1)
    low = head * HEADDIM
    spread[...] = jnp.where((channel >= low) & (channel < low + HEADDIM), 1.0, 0.0).astype(bf16)


def fill_positions(starts, pos, rpos):
    length = pos.shape[0]

    def body(i, carry):
        at = pl.multiple_of(i * BLOCK, BLOCK)
        place = lax.broadcasted_iota(jnp.int32, (BLOCK, LANES), 0) + at
        begin = jnp.zeros_like(place)
        end = jnp.full_like(place, length)
        for k in range(DOCS):
            begin = jnp.maximum(begin, jnp.where(place >= starts[k], starts[k], 0))
            end = jnp.minimum(end, jnp.where(place < starts[k], starts[k], length))
        pos[pl.ds(at, BLOCK), :] = place - begin
        if rpos is not None:
            rpos[pl.ds(at, BLOCK), :] = end - 1 - place
        return carry

    lax.fori_loop(0, length // BLOCK, body, 0)


def normalize(tok, gain, normed, stat):
    step = 64

    def body(i, carry):
        rows = pl.ds(pl.multiple_of(i * step, step), step)
        v = tok[rows, :].astype(f32)
        inverse = lax.rsqrt(jnp.mean(v * v, axis=1, keepdims=True) + EPS)
        normed[rows, :] = (v * inverse * gain[...]).astype(bf16)
        stat[rows, :] = jnp.broadcast_to(inverse, (step, LANES))
        return carry

    lax.fori_loop(0, tok.shape[0] // step, body, 0)


def project_x(normed, wxd, xin, dtin):
    length, width = normed.shape[0], xin.shape[1]
    xin[pl.ds(0, 8), :] = jnp.zeros((8, width), f32)
    rows = 512

    def body(i, carry):
        at = pl.multiple_of(i * rows, rows)
        left = normed[pl.ds(at, rows), :]
        for c, w in tiles(width, 512):
            xin[pl.ds(at + 8, rows), c : c + w] = mm(left, wxd[:, c : c + w])
        dtin[pl.ds(at, rows), :] = mm(left, wxd[:, width : width + LANES])
        return carry

    lax.fori_loop(0, length // rows, body, 0)


def convolve(xin, taps, pos, slope, x_low, bc_low):
    width, inner = xin.shape[1], x_low.shape[1]

    def tile(b, c, out, at):
        rows = pl.ds(pl.multiple_of(b * BLOCK, BLOCK), BLOCK)
        x = xin[pl.ds(pl.multiple_of(b * BLOCK, BLOCK), BLOCK + 8), pl.ds(c, LANES)]
        place = pos[rows, :]
        tap = taps[:, pl.ds(c, LANES)]
        pre = tap[CONV : CONV + 1] + tap[CONV - 1 : CONV] * x[8:]
        for lag in range(1, CONV):
            earlier = pltpu.roll(x, lag, 0)[8:]
            pre = pre + tap[CONV - 1 - lag : CONV - lag] * jnp.where(place >= lag, earlier, 0.0)
        sg = logistic(pre)
        slope[rows, pl.ds(c, LANES)] = (sg * (1.0 + pre * (1.0 - sg))).astype(bf16)
        out[rows, pl.ds(at, LANES)] = (pre * sg).astype(bf16)

    blocks = x_low.shape[0] // BLOCK
    xcols, bcols = inner // LANES, (width - inner) // LANES

    def x_body(i, carry):
        c = pl.multiple_of((i % xcols) * LANES, LANES)
        tile(i // xcols, c, x_low, c)
        return carry

    def bc_body(i, carry):
        c = pl.multiple_of((i % bcols) * LANES, LANES)
        tile(i // bcols, inner + c, bc_low, c)
        return carry

    lax.fori_loop(0, blocks * xcols, x_body, 0)
    lax.fori_loop(0, blocks * bcols, bc_body, 0)


def softplus(v):
    return jnp.maximum(v, 0.0) + jnp.log1p(jnp.exp(-jnp.abs(v)))


def steps(dtin, dpar, step, sgdt, step_low, decay_low):
    def body(i, carry):
        rows = pl.ds(pl.multiple_of(i * BLOCK, BLOCK), BLOCK)
        v = dtin[rows, :] + dpar[0:1, :]
        soft = softplus(v)
        if step is not None:
            step[rows, :] = soft
            sgdt[rows, :] = logistic(v)
        step_low[rows, :] = soft.astype(bf16)
        decay_low[rows, :] = (-dpar[1:2, :] * soft).astype(bf16)
        return carry

    lax.fori_loop(0, dtin.shape[0] // BLOCK, body, 0)


def block_marks(starts, b):
    at = b * BLOCK
    column = doc_of(starts, lax.broadcasted_iota(jnp.int32, (BLOCK, 1), 0) + at)
    row = doc_of(starts, lax.broadcasted_iota(jnp.int32, (1, BLOCK), 1) + at)
    before = doc_of(starts, at - 1)
    last = doc_of(starts, at + BLOCK - 1)
    return column, row, before, last


def block_decays(b, starts, decay_low, step_low, spread):
    rows = pl.ds(pl.multiple_of(b * BLOCK, BLOCK), BLOCK)
    column, row, before, last = block_marks(starts, b)
    i0 = lax.broadcasted_iota(jnp.int32, (BLOCK, BLOCK), 0)
    i1 = lax.broadcasted_iota(jnp.int32, (BLOCK, BLOCK), 1)
    lower = jnp.where(i0 >= i1, 1.0, 0.0).astype(bf16)
    cum = mm(lower, decay_low[rows, :])
    step_e = mm(step_low[rows, :], spread[...])
    cum_e = expand(jnp.exp(cum), spread[...])
    kept_e = jnp.where(before == last, cum_e[BLOCK - 1 : BLOCK], 0.0)
    in_e = jnp.where(column == before, cum_e, 0.0)
    out_e = expand(jnp.exp(cum[BLOCK - 1 : BLOCK] - cum), spread[...])
    out_e = jnp.where(column == last, out_e, 0.0)
    return cum, step_e, kept_e, in_e, out_e, column, row


def scan_forward(
    starts, x_low, bc_low, step_low, decay_low, ssd, states, spread, state, xs, yin, cbm, tick=None
):
    length, inner = x_low.shape
    state[...] = jnp.zeros_like(state)

    def body(b, carry):
        rows = pl.ds(pl.multiple_of(b * BLOCK, BLOCK), BLOCK)
        cum, step_e, kept_e, in_e, out_e, column, row = block_decays(
            b, starts, decay_low, step_low, spread
        )
        bm, cm = bc_low[rows, :STATE], bc_low[rows, STATE:]
        i0 = lax.broadcasted_iota(jnp.int32, (BLOCK, BLOCK), 0)
        i1 = lax.broadcasted_iota(jnp.int32, (BLOCK, BLOCK), 1)
        cbm[...] = jnp.where((column == row) & (i0 >= i1), mm_nt(cm, bm), 0.0)
        stepped = x_low[rows, :].astype(f32) * step_e
        xs[...] = stepped.astype(bf16)
        entering = state[...].astype(bf16)
        states[b] = entering
        yin[...] = in_e * mm(cm, entering)
        state[...] = kept_e * state[...] + mm_tn(bm, (stepped * out_e).astype(bf16))
        cum_t = cum.T
        first = lax.broadcasted_iota(jnp.int32, (BLOCK, LANES), 1) < HEADDIM
        for j in range(inner // LANES):
            cols = slice(j * LANES, (j + 1) * LANES)
            pair = xs[:, cols]
            part = []
            for h in (2 * j, 2 * j + 1):
                span = jnp.minimum(cum[:, h : h + 1] - cum_t[h : h + 1, :], 0.0)
                part.append(mm((jnp.exp(span) * cbm[...]).astype(bf16), pair))
            y = jnp.where(first, part[0], part[1]) + yin[:, cols]
            ssd[rows, cols] = y.astype(bf16)
        if tick is not None:
            tick(b)
        return carry

    lax.fori_loop(0, length // BLOCK, body, 0)


def project_rows(left, right, out, rows=512, columns=512):
    def body(i, carry):
        at = pl.ds(pl.multiple_of(i * rows, rows), rows)
        part = left[at, :]
        for c, w in tiles(out.shape[1], columns):
            out[at, c : c + w] = mm(part, right[:, c : c + w]).astype(out.dtype)
        return carry

    lax.fori_loop(0, out.shape[0] // rows, body, 0)


def back_rows(left, right, out, rows=512, columns=512):
    def body(i, carry):
        at = pl.ds(pl.multiple_of(i * rows, rows), rows)
        part = left[at, :]
        for c, w in tiles(out.shape[1], columns):
            out[at, c : c + w] = mm_nt(part, right[c : c + w, :]).astype(out.dtype)
        return carry

    lax.fori_loop(0, out.shape[0] // rows, body, 0)


def weight_rows(left, right, out, rows=256, columns=512):
    def body(i, carry):
        at = pl.ds(pl.multiple_of(i * rows, rows), rows)
        part = left[:, at]
        for c, w in tiles(out.shape[1], columns):
            out[at, c : c + w] = mm_tn(part, right[:, c : c + w]).astype(out.dtype)
        return carry

    lax.fori_loop(0, out.shape[0] // rows, body, 0)


def gate_sums(gate, ssd, x_low, gnorm, crow, stat):
    step, inner = 64, gate.shape[1]

    def body(i, carry):
        rows = pl.ds(pl.multiple_of(i * step, step), step)
        squares = jnp.zeros((step, 256), f32)
        crosses = jnp.zeros((step, 256), f32)
        for c in range(0, inner, 256):
            cols = slice(c, c + 256)
            g = gate[rows, cols]
            mixed = ssd[rows, cols].astype(f32) + crow[1:2, cols] * x_low[rows, cols].astype(f32)
            gated = mixed * (g * logistic(g))
            squares = squares + gated * gated
            crosses = crosses + gnorm[rows, cols] * crow[0:1, cols] * gated
        lane = lax.broadcasted_iota(jnp.int32, (step, LANES), 1)
        s1 = jnp.sum(squares, axis=1, keepdims=True)
        s2 = jnp.sum(crosses, axis=1, keepdims=True)
        stat[rows, :] = jnp.where(lane == 0, s1, jnp.where(lane == 1, s2, 0.0))
        return carry

    lax.fori_loop(0, gate.shape[0] // step, body, 0)


def gate_squares(gate, ssd, x_low, crow, stat):
    step, inner = 64, gate.shape[1]

    def body(i, carry):
        rows = pl.ds(pl.multiple_of(i * step, step), step)
        squares = jnp.zeros((step, 256), f32)
        for c in range(0, inner, 256):
            cols = slice(c, c + 256)
            g = gate[rows, cols]
            mixed = ssd[rows, cols].astype(f32) + crow[1:2, cols] * x_low[rows, cols].astype(f32)
            value = mixed * (g * logistic(g))
            squares = squares + value * value
        stat[rows, :] = squares[:, :LANES] + squares[:, LANES:]
        return carry

    lax.fori_loop(0, gate.shape[0] // step, body, 0)


def gate_norm(gate, ssd, x_low, inverse_out, crow, gn):
    step, inner = 64, gate.shape[1]

    def body(i, carry):
        rows = pl.ds(pl.multiple_of(i * step, step), step)
        inverse = inverse_out[rows, :1]
        for c in range(0, inner, 256):
            cols = slice(c, c + 256)
            g = gate[rows, cols]
            mixed = ssd[rows, cols].astype(f32) + crow[1:2, cols] * x_low[rows, cols].astype(f32)
            gn[rows, cols] = (mixed * (g * logistic(g)) * inverse * crow[0:1, cols]).astype(bf16)
        return carry

    lax.fori_loop(0, gate.shape[0] // step, body, 0)


def cross_sums(gnorm, gn, stat):
    step, inner = 64, gn.shape[1]

    def body(i, carry):
        rows = pl.ds(pl.multiple_of(i * step, step), step)
        total = jnp.zeros((step, 256), f32)
        for c in range(0, inner, 256):
            cols = slice(c, c + 256)
            total = total + gnorm[rows, cols] * gn[rows, cols].astype(f32)
        stat[rows, :] = total[:, :LANES] + total[:, LANES:]
        return carry

    lax.fori_loop(0, gn.shape[0] // step, body, 0)


def forward_kernel(
    starts, tok, gain, wxd, wz, taps, dpar,
    normed, inverse, xin, slope, gate, x_low, bc_low, step, sgdt, step_low, decay_low, ssd, states,
    pos, spread, dtin, state, xs, yin, cbm,
):
    fill_spread(spread)
    fill_positions(starts, pos, None)
    normalize(tok, gain, normed, inverse)
    project_x(normed, wxd, xin, dtin)
    convolve(xin, taps, pos, slope, x_low, bc_low)
    steps(dtin, dpar, step, sgdt, step_low, decay_low)
    scan_forward(starts, x_low, bc_low, step_low, decay_low, ssd, states, spread, state, xs, yin, cbm)
    project_rows(normed, wz, gate)


def gate_kernel(cot, wout, gate, ssd, x_low, crow, gnorm, stat):
    back_rows(cot, wout, gnorm)
    gate_sums(gate, ssd, x_low, gnorm, crow, stat)


def gate_backward(gate, ssd, x_low, gnorm, crow, stat, width, gn, low_gate, gs, sums, known=None):
    step, inner = 64, ssd.shape[1]
    sums[...] = jnp.zeros_like(sums)

    def body(i, carry):
        rows = pl.ds(pl.multiple_of(i * step, step), step)
        if known is None:
            inverse = lax.rsqrt(stat[rows, 0:1] / width + EPS)
            mean = inverse * stat[rows, 1:2] / width
        else:
            inverse, mean = known[rows, :1], stat[rows, :1]
        for c in range(0, inner, 256):
            cols = slice(c, c + 256)
            g = gate[rows, cols]
            x = x_low[rows, cols].astype(f32)
            mixed = ssd[rows, cols].astype(f32) + crow[1:2, cols] * x
            sg = logistic(g)
            act = g * sg
            hat = mixed * act * inverse
            if gn is not None:
                gn[rows, cols] = (hat * crow[0:1, cols]).astype(bf16)
            gnorm_here = gnorm[rows, cols]
            grad = inverse * (gnorm_here * crow[0:1, cols] - hat * mean)
            grad_mixed = grad * act
            low_gate[rows, cols] = (grad * mixed * (sg * (1.0 + g * (1.0 - sg)))).astype(bf16)
            gs[rows, cols] = grad_mixed.astype(bf16)
            sums[0:8, cols] += fold(gnorm_here * hat)
            sums[8:16, cols] += fold(grad_mixed * x)
        return carry

    lax.fori_loop(0, ssd.shape[0] // step, body, 0)


def middle_kernel(
    cot, wout, normed, gate, x_low, ssd, gnorm, crow, stat,
    branch, dwout, dwz, low_gate, gs, sums,
    gn, *, width,
):
    gate_backward(gate, ssd, x_low, gnorm, crow, stat, width, gn, low_gate, gs, sums)
    project_rows(gn, wout, branch)
    weight_rows(gn, cot, dwout)
    weight_rows(normed, low_gate, dwz)


def scan_backward(
    starts, x_low, bc_low, step_low, decay_low, ssd, states, gs, slope, crow, step, sgdt, dpar,
    gpre, low_xd, dsums, spread, dstate, xs, gx, cbm, acc, tick=None,
):
    length, inner = x_low.shape
    width = gpre.shape[1]
    blocks = length // BLOCK
    dstate[...] = jnp.zeros_like(dstate)
    dsums[...] = jnp.zeros_like(dsums)
    gpre[pl.ds(length, 8), :] = jnp.zeros((8, width), f32)

    def body(i, carry):
        b = blocks - 1 - i
        rows = pl.ds(pl.multiple_of(b * BLOCK, BLOCK), BLOCK)
        cum, step_e, kept_e, in_e, out_e, column, row = block_decays(
            b, starts, decay_low, step_low, spread
        )
        bm, cm = bc_low[rows, :STATE], bc_low[rows, STATE:]
        i0 = lax.broadcasted_iota(jnp.int32, (BLOCK, BLOCK), 0)
        i1 = lax.broadcasted_iota(jnp.int32, (BLOCK, BLOCK), 1)
        linked = (column == row) & (i0 <= i1)
        cbm[...] = jnp.where(linked, mm_nt(bm, cm), 0.0)
        x = x_low[rows, :].astype(f32)
        stepped = x * step_e
        xs[...] = stepped.astype(bf16)
        cum_t = cum.T
        first = lax.broadcasted_iota(jnp.int32, (BLOCK, LANES), 1) < HEADDIM
        acc[...] = jnp.zeros_like(acc)
        for j in range(inner // LANES):
            cols = slice(j * LANES, (j + 1) * LANES)
            xpair, gpair = xs[:, cols], gs[rows, cols]
            none = jnp.zeros_like(xpair)
            part, total = [], None
            for k in range(2):
                h = 2 * j + k
                kernel = jnp.exp(jnp.minimum(cum_t[h : h + 1, :] - cum[:, h : h + 1], 0.0))
                part.append(mm((kernel * cbm[...]).astype(bf16), gpair))
                own = jnp.where(first, xpair, none) if k == 0 else jnp.where(first, none, xpair)
                here = kernel * mm_nt(own, gpair)
                total = here if total is None else total + here
            acc[...] += total
            gx[:, cols] = jnp.where(first, part[0], part[1])
        dstate_low = dstate[...].astype(bf16)
        entering = states[b]
        leaving = states[jnp.minimum(b + 1, blocks - 1)]
        end = jnp.sum(dstate[...] * leaving.astype(f32), axis=0, keepdims=True)
        g = gs[rows, :].astype(f32)
        g_in = (in_e * g).astype(bf16)
        raw = gx[...] + out_e * mm(bm, dstate_low)
        grad_x = (step_e * raw).astype(bf16).astype(f32)
        gpre[rows, :inner] = (grad_x + crow[1:2, :] * g) * slope[rows, :inner]
        pairs = jnp.where(linked, acc[...], 0.0).astype(bf16)
        db = mm(pairs, cm) + mm_nt((stepped * out_e).astype(bf16), dstate_low)
        dc = mm_tn(pairs, bm) + mm_nt(g_in, entering)
        gpre[rows, inner : inner + STATE] = db * slope[rows, inner : inner + STATE]
        gpre[rows, inner + STATE :] = dc * slope[rows, inner + STATE :]
        raw_x = x * raw
        grad_step = gather_heads(raw_x, spread[...]).astype(bf16).astype(f32)
        dcum = gather_heads(g * ssd[rows, :].astype(f32) - step_e * raw_x, spread[...])
        tail = gather_heads(jnp.broadcast_to(end, (8, inner)), spread[...])[0:1]
        upper = jnp.where(i0 <= i1, 1.0, 0.0).astype(bf16)
        high, rest = halves(dcum)
        later = mm(upper, high) + mm(upper, rest) + tail
        grad_decay = later.astype(bf16).astype(f32)
        total_step = grad_step - dpar[1:2, :] * grad_decay
        if sgdt is None:
            before_step = step[rows, :] + dpar[0:1, :]
            slope_here, step_here = logistic(before_step), softplus(before_step)
        else:
            slope_here, step_here = sgdt[rows, :], step[rows, :]
        grad_dt = total_step * slope_here
        low_xd[rows, width:] = grad_dt.astype(bf16)
        dsums[0:8, :] += fold(grad_dt)
        dsums[8:16, :] -= fold(grad_decay * step_here)
        dstate[...] = kept_e * dstate[...] + mm_tn(cm, g_in)
        if tick is not None:
            tick(i)
        return carry

    lax.fori_loop(0, blocks, body, 0)


def convolve_back(xin, gpre, taps, pos, rpos, low_xd, csums, tick=None):
    width = gpre.shape[1]
    columns = width // LANES
    csums[...] = jnp.zeros_like(csums)

    def body(b, j):
        at = pl.multiple_of(b * BLOCK, BLOCK)
        cols = pl.ds(pl.multiple_of(j * LANES, LANES), LANES)
        rows = pl.ds(at, BLOCK)
        x = xin[pl.ds(at, BLOCK + 8), cols]
        g = gpre[pl.ds(at, BLOCK + 8), cols]
        here = g[:BLOCK]
        place, ahead = pos[rows, :], rpos[rows, :]
        tap = taps[:, cols]
        grad = tap[CONV - 1 : CONV] * here
        csums[pl.ds(8 * CONV, 8), cols] += fold(here)
        csums[pl.ds(8 * (CONV - 1), 8), cols] += fold(here * x[8:])
        for lag in range(1, CONV):
            k = CONV - 1 - lag
            later = pltpu.roll(g, BLOCK + 8 - lag, 0)[:BLOCK]
            earlier = pltpu.roll(x, lag, 0)[8:]
            grad = grad + tap[k : k + 1] * jnp.where(ahead >= lag, later, 0.0)
            csums[pl.ds(8 * k, 8), cols] += fold(here * jnp.where(place >= lag, earlier, 0.0))
        low_xd[rows, cols] = grad.astype(bf16)

    def block(b, carry):
        lax.fori_loop(0, columns, lambda j, c: (body(b, j), c)[1], 0)
        if tick is not None:
            tick(b)
        return carry

    lax.fori_loop(0, (xin.shape[0] - 8) // BLOCK, block, 0)


def backward_kernel(
    starts, xin, slope, x_low, bc_low, step, sgdt, step_low, decay_low, ssd, states, gs, taps, crow, dpar,
    low_xd, csums, dsums,
    pos, rpos, spread, gpre, dstate, xs, gx, cbm, acc,
):
    fill_spread(spread)
    fill_positions(starts, pos, rpos)
    scan_backward(
        starts, x_low, bc_low, step_low, decay_low, ssd, states, gs, slope, crow, step, sgdt, dpar,
        gpre, low_xd, dsums, spread, dstate, xs, gx, cbm, acc,
    )
    convolve_back(xin, gpre, taps, pos, rpos, low_xd, csums)


def last_kernel(tok, inverse, gain, normed, low_gate, low_xd, wz, wxd, dwxd, gfull, rowdot):
    weight_rows(normed, low_xd, dwxd)
    rows = 256

    def body(i, carry):
        at = pl.ds(pl.multiple_of(i * rows, rows), rows)
        total = jnp.zeros((rows, 1), f32)
        for c, w in tiles(gfull.shape[1], 512):
            cols = slice(c, c + w)
            part = mm_nt(low_gate[at, :], wz[cols, :]) + mm_nt(low_xd[at, :], wxd[cols, :])
            gfull[at, cols] = part.astype(bf16)
            total = total + jnp.sum(part * gain[:, cols] * tok[at, cols].astype(f32), axis=1, keepdims=True)
        rowdot[at, :] = total * inverse[at, :]
        return carry

    lax.fori_loop(0, gfull.shape[0] // rows, body, 0)


MESH = pl.DeviceIdType.MESH


def remote(source, target, send, receive, **where):
    return pltpu.make_async_remote_copy(
        src_ref=source, dst_ref=target, send_sem=send, recv_sem=receive, device_id=where, device_id_type=MESH
    )


def add_into(target, source, rows=64):
    def body(i, carry):
        at = pl.ds(pl.multiple_of(i * rows, rows), rows)
        target[at, :] = (target[at, :].astype(f32) + source[at, :].astype(f32)).astype(target.dtype)
        return carry

    lax.fori_loop(0, target.shape[0] // rows, body, 0)


class Ring:
    def __init__(self):
        self.me = lax.axis_index("dp")
        self.core = self.me % 2
        chip = self.me // 2
        y = chip // 2
        self.pos = 2 * y + (chip + y) % 2
        self.partner = self.me + 1 - 2 * self.core
        self.right = self.at(self.pos + 1)
        self.left = self.at(self.pos + 3)
        self.across = self.at(self.pos + 2)

    def at(self, pos):
        pos = pos % 4
        y = pos // 2
        return (2 * y + (pos + y) % 2) * 2 + self.core


def greet(ring, everyone):
    barrier = pltpu.get_barrier_semaphore()
    n, z = lax.axis_size("mp"), lax.axis_index("mp")
    if everyone:
        size = lax.axis_size("dp")
        close = [(ring.me + i) % size for i in range(1, size)]
    else:
        close = [ring.partner, ring.right, ring.left]
    for other in close:
        pl.semaphore_signal(barrier, inc=1, device_id={"dp": other}, device_id_type=MESH)
    for i in range(1, n):
        pl.semaphore_signal(barrier, inc=1, device_id={"mp": (z + i) % n}, device_id_type=MESH)
    return lambda: pl.semaphore_wait(barrier, len(close) + n - 1)


class Scatter:
    def __init__(self, ring, shard, cores, parts, wholes, sems):
        self.ring, self.shard = ring, shard
        self.cores, self.parts, self.wholes = cores, parts, wholes
        self.core_send, self.core_recv, self.ring_send, self.ring_recv = sems
        self.half = cores.shape[1] // 2

    def upper(self, r):
        return self.shard(r).at[pl.ds(0, self.half), :]

    def lower(self, r):
        return self.shard(r).at[pl.ds(self.half, self.half), :]

    def core_copy(self, chip):
        ring = self.ring
        return remote(
            self.shard(2 * chip + 1 - ring.core), self.cores.at[chip],
            self.core_send.at[chip], self.core_recv.at[chip], dp=ring.partner,
        )

    def ring_copy(self, k):
        ring = self.ring
        source = (self.upper(ring.across), self.lower(ring.across), self.shard(ring.right), self.shard(ring.left))[k]
        target = (self.parts.at[0], self.parts.at[1], self.wholes.at[0], self.wholes.at[1])[k]
        return remote(
            source, target, self.ring_send.at[k], self.ring_recv.at[k], dp=(ring.right, ring.left)[k % 2]
        )

    def start(self, chip):
        self.core_copy(chip).start()

    def first(self):
        def body(chip, carry):
            self.core_copy(chip).wait_recv()
            add_into(self.shard(2 * chip + self.ring.core), self.cores.at[chip])
            return carry

        lax.fori_loop(0, 4, body, 0)
        self.ring_copy(0).start()
        self.ring_copy(1).start()

    def second(self):
        self.ring_copy(0).wait_recv()
        add_into(self.upper(self.ring.right), self.parts.at[0])
        self.ring_copy(2).start()
        self.ring_copy(1).wait_recv()
        add_into(self.lower(self.ring.left), self.parts.at[1])
        self.ring_copy(3).start()

    def finish(self, out, rows=64):
        self.ring_copy(2).wait_recv()
        self.ring_copy(3).wait_recv()
        own = self.shard(self.ring.me)

        def body(i, carry):
            at = pl.ds(pl.multiple_of(i * rows, rows), rows)
            out[at, :] = own[at, :].astype(f32) + self.wholes[0, at, :].astype(f32) + self.wholes[1, at, :].astype(f32)
            return carry

        lax.fori_loop(0, out.shape[0] // rows, body, 0)

        def done(chip, carry):
            self.core_copy(chip).wait_send()
            return carry

        lax.fori_loop(0, 4, done, 0)
        for k in range(4):
            self.ring_copy(k).wait_send()


class Line:
    def __init__(self, piece, slot, blocks, sems, total, depth):
        self.piece, self.slot, self.blocks, self.total, self.depth = piece, slot, blocks, total, depth
        self.send, self.recv = sems
        self.n, self.z = lax.axis_size("mp"), lax.axis_index("mp")
        self.place = (self.z, self.n - 1 - self.z)

    def rows(self, t):
        return pl.ds(pl.multiple_of(t * BLOCK, BLOCK), BLOCK)

    def source(self, side, k):
        d = k // self.blocks
        return self.piece(k - d * self.blocks, self.n - 1 - d if side == 0 else d)

    def copy(self, side, place, k):
        return remote(
            self.source(side, k), self.slot(side, place + 1, k), self.send.at[side, k], self.recv.at[side, k],
            mp=self.z + 1 if side == 0 else self.z - 1,
        )

    def arrived(self, side, place, k):
        target = self.slot(side, place, k)
        remote(target, target, self.send.at[side, k], self.recv.at[side, k], mp=self.z).wait_recv()
        return target

    def inject(self, k):
        for side in range(2):
            @pl.when(self.place[side] == 0)
            def _():
                @pl.when(jnp.int32(k) >= self.depth)
                def _():
                    self.copy(side, 0, jnp.maximum(k - self.depth, 0)).wait_send()

                self.copy(side, 0, k).start()

    def forward(self, k, hop):
        for side in range(2):
            @pl.when(self.place[side] == hop)
            def _():
                add_into(self.source(side, k), self.arrived(side, hop, k))
                self.copy(side, hop, k).start()

    def finish(self, t):
        self.total[...] = self.piece(t, self.z)[...].astype(f32)
        for side in range(2):
            for place in range(1, self.n):
                @pl.when(self.place[side] == place)
                def _():
                    self.total[...] += self.arrived(side, place, (self.n - 1 - place) * self.blocks + t)[...].astype(f32)

    def drain(self):
        for side in range(2):
            for place in range(self.n - 1):
                count = (self.n - 1 - place) * self.blocks

                @pl.when(self.place[side] == place)
                def _():
                    def body(k, carry):
                        self.copy(side, place, k).wait_send()
                        return carry

                    lax.fori_loop(count - self.depth if place == 0 else 0, count, body, 0)

    def order(self, i):
        z = self.z
        far = jnp.where(z < 2, 3 - i, i)
        near = z + 1 - 2 * (z % 2)
        return jnp.where(i < 2, far, jnp.where(i == 2, near, z))


class Loads:
    def __init__(self, sems):
        self.sems, self.pairs = sems, []

    def start(self, source, target):
        i = len(self.pairs)
        copy = pltpu.make_async_copy(source, target, self.sems.at[i])
        copy.start()
        self.pairs.append(copy)
        return copy


class Gather:
    def __init__(self, ring, shard, rows, sems):
        self.ring, self.shard, self.half = ring, shard, rows // 2
        self.ring_send, self.ring_recv, self.core_send, self.core_recv = sems
        self.other = 1 - 2 * ring.core

    def ring_copy(self, k, source):
        ring = self.ring
        half = (0, 1, 1, 0, 0, 1)[k]
        piece = self.shard(source).at[pl.ds(half * self.half, self.half), :]
        return remote(
            piece, piece, self.ring_send.at[k], self.ring_recv.at[k], dp=(ring.right, ring.left)[k % 2]
        )

    def core_copy(self, k, source):
        return remote(
            self.shard(source), self.shard(source), self.core_send.at[k], self.core_recv.at[k], dp=self.ring.partner
        )

    def start(self):
        me = self.ring.me
        for k in range(4):
            self.ring_copy(k, me).start()
        self.core_copy(0, me).start()

    def second(self):
        left, right = self.ring.left, self.ring.right
        self.ring_copy(0, left).wait_recv()
        self.ring_copy(4, left).start()
        self.ring_copy(1, right).wait_recv()
        self.ring_copy(5, right).start()

    def beside(self):
        left, right = self.ring.left, self.ring.right
        self.ring_copy(2, left).wait_recv()
        self.core_copy(1, left).start()
        self.ring_copy(3, right).wait_recv()
        self.core_copy(2, right).start()

    def third(self):
        across = self.ring.across
        self.ring_copy(4, across).wait_recv()
        self.ring_copy(5, across).wait_recv()
        self.core_copy(3, across).start()

    def arrived(self, k):
        ring = self.ring
        source = (ring.me, ring.left, ring.right, ring.across)[k] + self.other
        self.core_copy(k, source).wait_recv()

    def drain(self):
        ring = self.ring
        for k, source in enumerate((ring.me, ring.me, ring.me, ring.me, ring.left, ring.right)):
            self.ring_copy(k, source).wait_send()
        for k, source in enumerate((ring.me, ring.left, ring.right, ring.across)):
            self.core_copy(k, source).wait_send()


def cast_into(target, source, rows=64):
    def body(i, carry):
        at = pl.ds(pl.multiple_of(i * rows, rows), rows)
        target[at, :] = source[at, :].astype(target.dtype)
        return carry

    lax.fori_loop(0, target.shape[0] // rows, body, 0)


def trunk_kernel(
    lengths, tok, cot, w_x, w_z, w_out, w_bc, w_dt, conv_x, conv_x_bias, conv_bc, conv_bc_bias, dt_bias, a_rate,
    d_skip, gain, out_gain,
    normed_o, xin_o, wx_o, wz_o, low_gate_o, low_xd_o, out_o, dwout_o, inverse_o, part_o,
    csums_o, dsums_o, sums_o, rows_o, colacc_o,
    csums, dsums, sums, rows, colacc, v_tok, stage_b, normed, xin, first_wide, slope, both, states, wx, wbd, wz, wout,
    bc_low, step_low, decay_low, inverse_out, taps, crow, dpar,
    bc_slots, tap_slots, row_slots, cross_slots, stat, turned,
    pos, rpos, spread, dtin, state, xs, wide, cbm, acc, near, cores, parts, wholes,
    load_sems, store_sems, token_sems, part_sems, out_sems, ring_send, ring_recv, core_send, core_recv, mp_send, mp_recv, line_send, line_recv,
    scatter_core_send, scatter_core_recv, scatter_ring_send, scatter_ring_recv,
):
    ring = Ring()
    loads, stores = Loads(load_sems), Loads(store_sems)
    load_x = loads.start(w_x, wide)
    met = greet(ring, False)
    n, z = lax.axis_size("mp"), lax.axis_index("mp")
    length, features = normed.shape
    x_low, ssd = both.at[pl.ds(0, length), :], both.at[pl.ds(length, length), :]
    stage_a = wide
    inverse = inverse_out
    inner, width = x_low.shape[1], xin.shape[1]
    own = features // n
    pair = width - inner
    bd_rows = pair + 32
    shard, column_shard = stage_a.shape[0], stage_b.shape[1]
    heads, per = w_dt.shape[0], w_bc.shape[0]
    load_tok = loads.start(tok, v_tok)
    load_out = loads.start(w_out, stage_b)
    starts = [jnp.int32(0)]
    for k in range(DOCS - 1):
        starts.append(starts[-1] + lengths[0, k])

    def exchange(k, i):
        slots = (bc_slots, tap_slots, row_slots, cross_slots)[k]
        at = k * (n - 1) + i - 1
        return remote(slots.at[0], slots.at[i], mp_send.at[at], mp_recv.at[at], mp=(z + i) % n)

    def rows_of(ref, low, high):
        def shard_of(r):
            return ref.at[pl.ds(pl.multiple_of(r * shard, shard), shard), pl.ds(low, high - low)]

        return shard_of

    def columns_of(r):
        return wout.at[:, pl.ds(pl.multiple_of(r * column_shard, column_shard), column_shard)]

    sems = [tuple(group.at[k] for group in (ring_send, ring_recv, core_send, core_recv)) for k in range(4)]
    get_x = Gather(ring, rows_of(wx, 0, inner), shard, sems[0])
    get_bd = Gather(
        ring, lambda r: wbd.at[pl.ds(0, bd_rows), pl.ds(pl.multiple_of(r * shard, shard), shard)], bd_rows, sems[1]
    )
    get_z = Gather(ring, rows_of(wz, 0, inner), shard, sems[2])
    get_out = Gather(ring, columns_of, inner, sems[3])

    load_x.wait()
    cast_into(get_x.shard(ring.me), stage_a)
    met()
    get_x.start()
    bc_slots[0] = w_bc[...].astype(bf16)
    tap_slots[0] = jnp.zeros_like(tap_slots[0])
    tap_slots[0, :CONV, :per] = conv_bc[...]
    tap_slots[0, CONV : CONV + 1, :per] = conv_bc_bias[...]
    my_columns = pl.ds(pl.multiple_of(ring.me * shard, shard), shard)
    wbd[pair : pair + heads, my_columns] = w_dt[...].astype(bf16)
    wbd[pair + heads : bd_rows, my_columns] = jnp.zeros((bd_rows - pair - heads, shard), bf16)
    wbd[bd_rows:, :] = jnp.zeros((wbd.shape[0] - bd_rows, features), bf16)
    dpar[...] = jnp.zeros_like(dpar)
    dpar[0:1, :heads] = dt_bias[...]
    dpar[1:2, :heads] = a_rate[...]
    dpar[2:3, :heads] = d_skip[...]
    for k in range(2):
        for i in range(1, n):
            exchange(k, i).start()
    load_z = loads.start(w_z, stage_a)
    fill_spread(spread)
    fill_positions(starts, pos, rpos)
    crow[0:1, :] = out_gain[...]
    crow[1:2, :] = expand(dpar[...], spread[...])[2:3]
    load_tok.wait()
    normalize(v_tok, gain, normed, inverse)
    load_cot = loads.start(cot, v_tok)
    store_normed = stores.start(normed, normed_o)
    store_inverse = stores.start(inverse, inverse_o)
    for k in range(2):
        for i in range(1, n):
            exchange(k, i).wait()
    for m in range(n):
        wbd[m * per : (m + 1) * per, my_columns] = bc_slots[(z - m + n) % n]
    get_bd.start()
    first = lax.broadcasted_iota(jnp.int32, (8, LANES), 1) < per
    for j in range(pair // LANES):
        low, high = (z - 2 * j + n) % n, (z - 2 * j - 1 + n) % n
        columns = slice(inner + j * LANES, inner + (j + 1) * LANES)
        taps[:, columns] = jnp.where(first, tap_slots[low], pltpu.roll(tap_slots[high], per, 1))
    taps[:, :inner] = jnp.zeros((8, inner), f32)
    taps[:CONV, :inner] = conv_x[...]
    taps[CONV : CONV + 1, :inner] = conv_x_bias[...]
    load_z.wait()
    cast_into(get_z.shard(ring.me), stage_a)
    load_out.wait()
    cast_into(get_out.shard(ring.me), stage_b)
    xin[pl.ds(0, 8), :] = jnp.zeros((8, width), f32)

    def project_chip(k, source):
        get_x.arrived(k)
        part = pl.ds(pl.multiple_of((source // 2) * 2 * shard, 2 * shard), 2 * shard)

        def body(i, carry):
            at = pl.multiple_of(i * 512, 512)
            left = normed[pl.ds(at, 512), part]
            for c, w in tiles(inner, 512):
                here = mm(left, wx[part, c : c + w])
                if k == 0:
                    xin[pl.ds(at + 8, 512), c : c + w] = here
                else:
                    xin[pl.ds(at + 8, 512), c : c + w] += here
            return carry

        lax.fori_loop(0, length // 512, body, 0)

    def project_bd(i, carry):
        at = pl.multiple_of(i * 512, 512)
        here = mm_nt(normed[pl.ds(at, 512), :], wbd[...])
        xin[pl.ds(at + 8, 512), inner:] = here[:, :pair]
        dtin[pl.ds(at, 512), :] = here[:, pair:]
        return carry

    get_x.second()
    project_chip(0, ring.me)
    get_x.beside()
    get_bd.second()
    get_z.start()
    get_bd.beside()
    project_chip(1, ring.left)
    project_chip(2, ring.right)
    get_x.third()
    get_bd.third()
    project_chip(3, ring.across)
    store_wx = stores.start(wx, wx_o)
    for i in range(4):
        get_bd.arrived(i)
    lax.fori_loop(0, length // 512, project_bd, 0)
    store_xin = stores.start(xin, xin_o)
    steps(dtin, dpar, None, None, step_low, decay_low)
    convolve(xin, taps, pos, slope, x_low, bc_low)
    get_z.second()
    get_out.start()

    def forward_tick(b):
        @pl.when(b == 0)
        def _():
            get_z.beside()

        @pl.when(b == 3)
        def _():
            get_z.third()

    scan_forward(
        starts, x_low, bc_low, step_low, decay_low, ssd, states, spread, state, xs, wide, cbm, forward_tick
    )
    for k in range(4):
        get_z.arrived(k)
    gate = first_wide.at[pl.ds(0, length), pl.ds(0, inner)]
    gnorm = xin.at[pl.ds(0, length), pl.ds(0, inner)]
    project_rows(normed, wz, gate)
    store_wz = stores.start(wz, wz_o)
    get_out.second()
    gate_squares(gate, ssd, x_low, crow, stat)

    def put_rows(target):
        for b in range(length // BLOCK):
            line_sum = jnp.sum(stat[b * BLOCK : (b + 1) * BLOCK, :].T, axis=0, keepdims=True)
            for j in range(BLOCK // LANES):
                at = b * (BLOCK // LANES) + j
                target[at : at + 1, :] = line_sum[:, j * LANES : (j + 1) * LANES]

    def sum_rows(slots, out, finish):
        sums_here = finish(functools.reduce(lambda p, q: p + q, [slots[i] for i in range(n)]))
        for b in range(length // BLOCK):
            at = b * (BLOCK // LANES)
            row = jnp.concatenate([sums_here[at + j : at + j + 1] for j in range(BLOCK // LANES)], axis=1)
            turned[...] = jnp.broadcast_to(row, turned.shape)
            out[b * BLOCK : (b + 1) * BLOCK, :] = turned[...].T

    put_rows(row_slots.at[0])
    get_x.drain()
    get_bd.drain()
    store_wx.wait()
    for i in range(1, n):
        exchange(2, i).start()
    load_cot.wait()
    store_xin.wait()

    def back_chip(k, source):
        if k < 3:
            get_out.arrived(k)
        part = pl.ds(pl.multiple_of((source // 2) * 2 * column_shard, 2 * column_shard), 2 * column_shard)

        def body(i, carry):
            at = pl.ds(pl.multiple_of(i * 512, 512), 512)
            left = v_tok[at, part]
            for c, w in tiles(inner, 512):
                here = mm_nt(left, wout[c : c + w, part])
                if k == 0:
                    gnorm[at, c : c + w] = here
                else:
                    gnorm[at, c : c + w] += here
            return carry

        lax.fori_loop(0, length // 512, body, 0)

    back_chip(0, ring.me)
    get_out.beside()
    back_chip(1, ring.left)
    back_chip(2, ring.right)
    for i in range(1, n):
        exchange(2, i).wait()
    store_inverse.wait()
    sum_rows(row_slots, inverse_out, lambda total: lax.rsqrt(total / (inner * n) + EPS))
    get_out.third()
    store_normed.wait()
    gn = normed.at[:, pl.ds(0, inner)]
    gs = normed.at[:, pl.ds(inner, inner)]
    get_z.drain()
    store_wz.wait()
    gate_norm(gate, ssd, x_low, inverse_out, crow, gn)
    get_out.arrived(3)

    fold_columns = inner // own

    def piece(t, q):
        row = pl.multiple_of((q // fold_columns) * length + t * BLOCK, BLOCK)
        return wz.at[pl.ds(row, BLOCK), pl.ds(pl.multiple_of((q % fold_columns) * own, own), own)]

    def slot(side, place, k):
        if place == 2:
            return near.at[k]
        row = pl.multiple_of((k // fold_columns) * BLOCK, BLOCK)
        return wx.at[pl.ds(row, BLOCK), pl.ds(pl.multiple_of((k % fold_columns) * own, own), own)]

    total = wide.at[:, pl.ds(0, own)]
    line = Line(piece, slot, length // BLOCK, (line_send, line_recv), total, 4)

    def quarter(i, carry, first_quarter=False):
        q = line.order(i)
        columns = pl.ds(pl.multiple_of(q * own, own), own)
        tall = 256 if first_quarter else 512
        for r in range(0, length, tall):
            at = pl.ds(pl.multiple_of((q // fold_columns) * length + r, tall), tall)
            cols = pl.ds(pl.multiple_of((q % fold_columns) * own, own), own)
            wz[at, cols] = mm(gn[r : r + tall, :], wout[:, columns]).astype(bf16)
            if first_quarter and r < 512:
                line.inject(r // 256)

        return carry

    quarter(0, 0, True)
    back_chip(3, ring.across)
    cross_sums(gnorm, gn, stat)
    put_rows(cross_slots.at[0])
    for i in range(1, n):
        exchange(3, i).start()
    line.inject(2)
    lax.fori_loop(1, n, quarter, 0)
    line.inject(3)
    get_out.drain()
    grads = wout
    scatter = Scatter(
        ring, lambda r: grads.at[:, pl.ds(pl.multiple_of(r * column_shard, column_shard), column_shard)],
        cores, parts, wholes, (scatter_core_send, scatter_core_recv, scatter_ring_send, scatter_ring_recv),
    )
    chunk = 2 * column_shard

    def weight(j, carry):
        columns = pl.ds(pl.multiple_of(j * chunk, chunk), chunk)
        for r in range(0, inner, 256):
            grads[r : r + 256, columns] = mm_tn(gn[:, r : r + 256], v_tok[:, columns]).astype(bf16)
        scatter.start(j)
        return carry

    lax.fori_loop(0, 4, weight, 0)
    line.inject(4)
    line.forward(0, 1)
    xd = v_tok.at[:, pl.ds(0, width + LANES)]
    token_own = v_tok.at[:, pl.ds(width + LANES, own)]
    load_own = loads.start(tok.at[:, pl.ds(pl.multiple_of(z * own, own), own)], token_own)
    for i in range(1, n):
        exchange(3, i).wait()
    sum_rows(cross_slots, stat, lambda total: total / (inner * n))
    low_gate = gn
    gate_backward(gate, ssd, x_low, gnorm, crow, stat, inner * n, None, low_gate, gs, sums, known=inverse_out)
    load_xin = loads.start(xin_o, xin)
    stores.start(low_gate, low_gate_o)
    stores.start(sums, sums_o)
    line.inject(5)
    line.forward(1, 1)
    line.forward(0, 2)
    scatter.first()

    def scan_tick(i):
        line.inject(i + 6)
        line.forward(i + 2, 1)

        @pl.when(i < 3)
        def _():
            line.forward(i + 1, 2)

        @pl.when(i == 1)
        def _():
            scatter.second()

    gpre = first_wide
    scan_backward(
        starts, x_low, bc_low, step_low, decay_low, ssd, states, gs, slope, crow, dtin, None, dpar,
        gpre, xd, dsums, spread, state, xs, wide, cbm, acc, scan_tick,
    )
    weight_loads = [loads.start(wz_o, both)]
    inverse_in = dtin
    weight_loads.append(loads.start(inverse_o, inverse_in))

    def token_copy(i):
        return pltpu.make_async_copy(
            tok.at[:, pl.ds(pl.multiple_of(line.order(i) * own, own), own)],
            normed.at[:, pl.ds(pl.multiple_of(inner + (i % 2) * own, own), own)], token_sems.at[i],
        )

    token_copy(0).start()
    token_copy(1).start()
    scatter.finish(stage_b)
    stores.start(stage_b, dwout_o)
    for h in range(2):
        weight_loads.append(
            loads.start(wx_o.at[pl.ds(h * length, length), :], wout.at[:, pl.ds(h * inner, inner)])
        )
    load_xin.wait()

    def conv_tick(b):
        @pl.when(b % 2 == 1)
        def _():
            line.inject(10 + b // 2)
            line.forward(6 + b // 2, 1)

    convolve_back(xin, gpre, taps, pos, rpos, xd, csums, conv_tick)
    for source, target in ((xd, low_xd_o), (csums, csums_o), (dsums, dsums_o)):
        stores.start(source, target)
    for copy in weight_loads:
        copy.wait()
    stat[...] = jnp.zeros_like(stat)
    half = own // 2

    def part_copy(i, h):
        column = pl.multiple_of(line.order(i) * own + h * half, half)
        return pltpu.make_async_copy(
            cores.at[(i % 2) * 2 + h], part_o.at[:, pl.ds(column, half)], part_sems.at[i, h]
        )

    def grad_quarter(i, carry):
        q = line.order(i)
        columns = pl.ds(pl.multiple_of(q * own, own), own)
        low = pl.ds(pl.multiple_of((q % 2) * own, own), own)
        high = q // 2
        x_columns = pl.ds(pl.multiple_of(high * inner, inner), inner)
        token_columns = pl.ds(pl.multiple_of(inner + (i % 2) * own, own), own)
        token_copy(i).wait()

        @pl.when(i >= 2)
        def _():
            for h in range(2):
                part_copy(jnp.maximum(i - 2, 0), h).wait()

        for r in range(0, length, 256):
            at = slice(r, r + 256)
            here = mm_nt(low_gate[at, :], both[columns, :])
            here = here + mm_nt(xd[at, :inner], wout[low, x_columns])
            here = here + mm(xd[at, inner:], wbd[:, columns])
            for h in range(2):
                cores[(i % 2) * 2 + h, at, :] = here[:, h * half : (h + 1) * half].astype(bf16)
            along = here * (normed[at, token_columns].astype(f32) * inverse_in[at, :1])
            folded = fold(along)
            if r == 0:
                colacc[:, columns] = folded
            else:
                colacc[:, columns] += folded
            along = along * gain[:, columns]
            sum_lanes = along[:, :LANES]
            for c in range(LANES, own, LANES):
                sum_lanes = sum_lanes + along[:, c : c + LANES]
            stat[at, :] += sum_lanes
        for h in range(2):
            part_copy(i, h).start()

        @pl.when(i < 2)
        def _():
            token_copy(jnp.minimum(i + 2, n - 1)).start()

        return carry

    lax.fori_loop(0, n, grad_quarter, 0)
    put_rows(rows)
    stores.start(rows, rows_o)
    stores.start(colacc, colacc_o)
    load_own.wait()

    def last(t, carry):
        line.finish(t)
        value = (token_own[line.rows(t), :].astype(f32) + total[...]).astype(bf16)
        for h in range(2):
            wholes[h, line.rows(t), :] = value[:, h * half : (h + 1) * half]
            out_copy(t, h).start()
        return carry

    def out_copy(t, h):
        return pltpu.make_async_copy(
            wholes.at[h, line.rows(t), :], out_o.at[line.rows(t), pl.ds(h * half, half)], out_sems.at[t, h]
        )

    lax.fori_loop(0, line.blocks, last, 0)
    line.drain()
    for t in range(line.blocks):
        for h in range(2):
            out_copy(t, h).wait()
    for i in range(2, n):
        for h in range(2):
            part_copy(i, h).wait()
    for copy in stores.pairs:
        if not any(copy is done for done in (store_normed, store_inverse, store_xin, store_wx, store_wz)):
            copy.wait()


def input_kernel(
    tok, inverse, gain, normed, low_gate, low_xd, part_o, cot, rows_o, colacc, csums, sums, dsums,
    dwz_o, dwx_o, grad_o, dwbc_o, dwdt_o, conv_x_o, conv_x_bias_o, conv_bc_o, conv_bc_bias_o, dt_bias_o, a_rate_o,
    d_skip_o, in_gain_o, out_gain_o,
    dwbc, dwdt, conv_x, conv_x_bias, conv_bc, conv_bc_bias, dt_bias, a_rate, d_skip, in_gain, out_gain,
    dwz, dwxd, grad, smalls, spread, bc_turned, bc_own, bc_slots,
    v_inverse, v_normed, v_gate, v_xd, v_cot, v_tok, v_colacc, v_csums, v_sums, v_dsums,
    part, slots, total, z_grads, z_cores, z_parts, z_wholes, x_grads, x_cores, x_parts, x_wholes,
    rows_slots, dp_in, mp_in, turned,
    load_sems, part_sems, grad_sems, line_send, line_recv, z_core_send, z_core_recv, z_ring_send, z_ring_recv,
    x_core_send, x_core_recv, x_ring_send, x_ring_recv,
    rows_send, rows_recv, dp_send, dp_recv, mp_send, mp_recv, bc_send, bc_recv,
):
    ring = Ring()
    met = greet(ring, True)
    loads = Loads(load_sems)
    n = lax.axis_size("mp")
    z = lax.axis_index("mp")
    size = lax.axis_size("dp")
    length, features = part.shape
    inner = v_gate.shape[1]
    width = v_csums.shape[1]
    heads, per = dwdt.shape[0], dwbc.shape[0]
    own = features // n

    def quarter_columns(q):
        return pl.ds(pl.multiple_of(q * own, own), own)

    line = Line(
        lambda t, q: part.at[pl.ds(pl.multiple_of(t * BLOCK, BLOCK), BLOCK), quarter_columns(q)],
        lambda side, place, k: slots.at[side, k], length // BLOCK, (line_send, line_recv), total, 3,
    )

    def part_copy(i):
        columns = quarter_columns(line.order(i))
        return pltpu.make_async_copy(part_o.at[:, columns], part.at[:, columns], part_sems.at[i])

    load_rows = loads.start(rows_o, rows_slots.at[0])
    part_copy(0).start()

    def rows_copy(i):
        return remote(
            rows_slots.at[0], rows_slots.at[i], rows_send.at[i - 1], rows_recv.at[i - 1], mp=(z + i) % n
        )

    load_rows.wait()
    met()
    for i in range(1, n):
        rows_copy(i).start()
    part_copy(0).wait()
    line.inject(0)
    line.inject(1)
    for i in range(1, n):
        part_copy(i).start()
    load_gate, load_normed, load_xd = [
        loads.start(source, target) for source, target in ((low_gate, v_gate), (normed, v_normed), (low_xd, v_xd))
    ]
    load_sums = [
        loads.start(source, target)
        for source, target in ((colacc, v_colacc), (csums, v_csums), (sums, v_sums), (dsums, v_dsums))
    ]
    own_columns = quarter_columns(z)
    later = [
        loads.start(source, target)
        for source, target in (
            (cot.at[:, own_columns], v_cot), (tok.at[:, own_columns], v_tok), (inverse, v_inverse),
        )
    ]

    gain_width = features // 8

    def dp_copy(i):
        return remote(
            smalls, dp_in.at[i - 1], dp_send.at[i - 1], dp_recv.at[i - 1], dp=(ring.me + i) % size
        )

    def mp_copy(i):
        return remote(
            smalls.at[:, pl.ds(inner, width - inner + gain_width)], mp_in.at[i - 1],
            mp_send.at[i - 1], mp_recv.at[i - 1], mp=(z + i) % n,
        )

    for copy in load_sums:
        copy.wait()
    smalls[...] = jnp.zeros_like(smalls)
    for k in range(CONV + 1):
        smalls[k : k + 1, :width] = jnp.sum(v_csums[8 * k : 8 * k + 8, :], axis=0, keepdims=True)
    for k in range(2):
        smalls[CONV + 1 + k : CONV + 2 + k, :inner] = jnp.sum(v_sums[8 * k : 8 * k + 8, :], axis=0, keepdims=True)
        smalls[7:8, k * LANES : (k + 1) * LANES] = jnp.sum(v_dsums[8 * k : 8 * k + 8, :], axis=0, keepdims=True)
    for k in range(8):
        columns = slice(k * gain_width, (k + 1) * gain_width)
        smalls[k : k + 1, width:] = jnp.sum(v_colacc[:, columns], axis=0, keepdims=True)
    for i in range(1, size):
        dp_copy(i).start()
    shard = dwz.shape[0]
    z_scatter = Scatter(
        ring, lambda r: z_grads.at[pl.ds(pl.multiple_of(r * shard, shard), shard), :], z_cores, z_parts, z_wholes,
        (z_core_send, z_core_recv, z_ring_send, z_ring_recv),
    )
    x_scatter = Scatter(
        ring, lambda r: x_grads.at[pl.ds(pl.multiple_of(r * shard, shard), shard), :], x_cores, x_parts, x_wholes,
        (x_core_send, x_core_recv, x_ring_send, x_ring_recv),
    )

    def weight(j, right, grads):
        for c in range(0, 2 * shard, shard):
            rows = pl.ds(pl.multiple_of(j * 2 * shard + c, shard), shard)
            left = v_normed[:, rows]
            for at, w in tiles(grads.shape[1], 512):
                grads[rows, at : at + w] = mm_tn(left, right[:, at : at + w]).astype(bf16)

    load_gate.wait()
    load_normed.wait()

    def z_weight(j, carry):
        weight(j, v_gate, z_grads)
        z_scatter.start(j)
        return carry

    lax.fori_loop(0, 4, z_weight, 0)
    for i in range(1, n):
        part_copy(i).wait()
    line.inject(2)
    line.forward(0, 1)
    load_xd.wait()

    def x_weight(j, carry):
        weight(j, v_xd, x_grads)
        x_scatter.start(j)

        @pl.when(j == 1)
        def _():
            z_scatter.first()

        @pl.when(j % 2 == 1)
        def _():
            line.inject(3 + j // 2)
            line.forward(1 + j // 2, 1)

        return carry

    lax.fori_loop(0, 4, x_weight, 0)
    line.forward(0, 2)
    z_scatter.second()
    line.inject(5)
    line.forward(3, 1)
    line.forward(1, 2)
    x_scatter.first()
    line.inject(6)
    line.forward(4, 1)
    line.forward(2, 2)
    for i in range(1, size):
        dp_copy(i).wait()
    smalls[...] += functools.reduce(lambda a, b: a + b, [dp_in[i] for i in range(size - 1)])
    for i in range(1, n):
        mp_copy(i).start()
    line.inject(7)
    line.forward(5, 1)
    line.forward(3, 2)
    z_scatter.finish(dwz)
    store_z = loads.start(dwz, dwz_o)
    x_scatter.second()
    line.inject(8)
    line.forward(6, 1)
    line.inject(9)
    line.forward(7, 1)
    line.inject(10)
    x_scatter.finish(dwxd)

    bc_turned[...] = dwxd[:, inner:width].T
    bc_own[...] = bc_turned[...].astype(bf16)

    def weight_copy(i):
        other = (z + i) % n
        return remote(
            bc_own.at[pl.ds(pl.multiple_of(other * per, per), per), :], bc_slots.at[i - 1],
            bc_send.at[i - 1], bc_recv.at[i - 1], mp=other,
        )

    for i in range(1, n):
        weight_copy(i).start()
    line.inject(11)
    store_x = loads.start(dwxd.at[:, pl.ds(0, inner)], dwx_o)
    dwdt[...] = dwxd[:, width:].T[:heads]
    for i in range(1, n):
        rows_copy(i).wait()
        mp_copy(i).wait()
    smalls[:, inner:] += functools.reduce(lambda a, b: a + b, [mp_in[i] for i in range(n - 1)])
    share = LANES // per

    def mine(v):
        turns = [v] + [pltpu.roll(v, LANES - k * per, 1) for k in range(1, share)]
        which = jnp.full(v.shape, z % share, jnp.int32)
        return functools.reduce(lambda a, k: jnp.where(which == k, turns[k], a), range(1, share), turns[0])

    lanes = pl.ds(pl.multiple_of(inner + (z // share) * LANES, LANES), LANES)
    conv_x[...] = smalls[:CONV, :inner]
    conv_x_bias[...] = smalls[CONV : CONV + 1, :inner]
    taps = mine(smalls[:8, lanes])
    conv_bc[...] = taps[:CONV, :per]
    conv_bc_bias[...] = taps[CONV : CONV + 1, :per]
    out_gain[...] = smalls[5:6, :inner]
    fill_spread(spread)
    d_skip[...] = gather_heads(smalls[0:8, :inner], spread[...])[6:7, :heads]
    dt_bias[...] = smalls[7:8, :heads]
    a_rate[...] = smalls[7:8, LANES : LANES + heads]
    rows_own = own // gain_width
    for k in range(rows_own):
        in_gain[:, k * gain_width : (k + 1) * gain_width] = smalls[
            pl.ds(z * rows_own + k, 1), width : width + gain_width
        ]
    for i in range(1, n):
        weight_copy(i).wait()
    dwbc[...] = functools.reduce(
        lambda a, b: a + b, [bc_slots[i].astype(f32) for i in range(n - 1)],
        bc_turned[pl.ds(pl.multiple_of(z * per, per), per), :],
    )
    small = [
        loads.start(source, target)
        for source, target in (
            (dwbc, dwbc_o), (dwdt, dwdt_o), (conv_x, conv_x_o), (conv_x_bias, conv_x_bias_o), (conv_bc, conv_bc_o),
            (conv_bc_bias, conv_bc_bias_o), (dt_bias, dt_bias_o), (a_rate, a_rate_o), (d_skip, d_skip_o),
            (in_gain, in_gain_o), (out_gain, out_gain_o),
        )
    ]
    for copy in later:
        copy.wait()
    means = functools.reduce(lambda a, b: a + b, [rows_slots[i] for i in range(n)]) / features
    rows_slots[0] = means

    def last(t, carry):
        line.finish(t)
        rows = line.rows(t)
        lines = BLOCK // LANES
        row = jnp.concatenate([rows_slots[0, pl.ds(t * lines + j, 1), :] for j in range(lines)], axis=1)
        turned[...] = jnp.broadcast_to(row, turned.shape)
        mean = turned[...].T
        for c in range(0, own, LANES):
            columns = slice(c, c + LANES)
            hat = v_tok[rows, columns].astype(f32) * v_inverse[rows, :]
            gain_here = gain[:, pl.ds(pl.multiple_of(z * own + c, LANES), LANES)]
            change = v_inverse[rows, :] * (total[:, columns] * gain_here - hat * mean)
            grad[rows, columns] = (v_cot[rows, columns].astype(f32) + change).astype(bf16)
        grad_copy(t).start()
        return carry

    def grad_copy(t):
        return pltpu.make_async_copy(grad.at[line.rows(t), :], grad_o.at[line.rows(t), :], grad_sems.at[t])

    lax.fori_loop(0, line.blocks, last, 0)
    line.drain()
    for copy in (store_z, store_x, *small):
        copy.wait()
    for t in range(line.blocks):
        grad_copy(t).wait()


def hand_on_kernel(*refs):
    count = (len(refs) - 2) // 3
    sources, targets, buffers = refs[:count], refs[count : 2 * count], refs[2 * count : 3 * count]
    into, out = refs[-2:]
    there = [pltpu.make_async_copy(sources[k], buffers[k], into.at[k]) for k in range(count)]
    back = [pltpu.make_async_copy(buffers[k], targets[k], out.at[k]) for k in range(count)]
    for copy in there:
        copy.start()
    for k in range(count):
        there[k].wait()
        back[k].start()
    for copy in back:
        copy.wait()


def hand_on(*arrays):
    kinds = [(v.shape, v.dtype) for v in arrays]
    count = len(arrays)
    return call(
        hand_on_kernel, kinds, kinds, 0, *arrays,
        places="a" * len(arrays), sems=[(count,)] * 2, far=len(arrays),
    )


def call(kernel, outs, scratch, smem, *operands, places=None, sems=(), collective=None, far=0):
    spaces = {"s": pltpu.SMEM, "v": pltpu.VMEM, "a": pl.ANY}
    if places is None:
        places = "s" * smem + "v" * (len(operands) - smem)
    extra = {} if collective is None else dict(collective_id=collective, has_side_effects=True)
    return pl.pallas_call(
        kernel,
        out_shape=[jax.ShapeDtypeStruct(shape, kind) for shape, kind in outs],
        in_specs=[pl.BlockSpec(memory_space=spaces[c]) for c in places],
        out_specs=[pl.BlockSpec(memory_space=pl.ANY if i < far else pltpu.VMEM) for i in range(len(outs))],
        scratch_shapes=[pltpu.VMEM(shape, kind) for shape, kind in scratch]
        + [pltpu.SemaphoreType.DMA(shape) for shape in sems],
        compiler_params=pltpu.CompilerParams(vmem_limit_bytes=VMEM_LIMIT, **extra),
    )(*operands)


def per_device_any(
    tokens, cotangent, doc_lengths, w_z, w_x, w_bc, w_dt, w_out, conv_x, conv_x_bias, conv_bc,
    conv_bc_bias, dt_bias, a_rate, d_skip, input_norm_gain, out_gain,
):
    group = lax.axis_size("mp")
    rank = lax.axis_index("mp")
    T, D = tokens.shape
    inner, heads = w_x.shape[1], w_dt.shape[1]
    pair = 2 * STATE
    width = inner + pair
    wide = width + LANES
    own = D // group

    lengths = doc_lengths[0]
    starts = jnp.cumsum(lengths) - lengths
    packed = jnp.concatenate([w_bc, conv_bc, conv_bc_bias[None, :]], axis=0)
    packed = lax.all_gather(packed, "mp", axis=1, tiled=True)
    shard = w_bc.shape[0]
    w_bc_all, taps_bc = packed[:shard], packed[shard:]
    wxd = jnp.concatenate(
        [w_x.astype(bf16), w_bc_all.astype(bf16), w_dt.astype(bf16), jnp.zeros((shard, LANES - heads), bf16)],
        axis=1,
    )
    wxd = lax.all_gather(wxd, "dp", axis=0, tiled=True)
    wz = lax.all_gather(w_z.astype(bf16), "dp", axis=0, tiled=True)
    wout = lax.all_gather(w_out.astype(bf16), "dp", axis=1, tiled=True)
    taps = jnp.concatenate([jnp.concatenate([conv_x, conv_x_bias[None, :]], axis=0), taps_bc], axis=1)
    taps = jnp.pad(taps, ((0, 8 - CONV - 1), (0, 0)))
    crow = jnp.pad(jnp.stack([out_gain, jnp.repeat(d_skip, HEADDIM)]), ((0, 6), (0, 0)))
    dpar = jnp.pad(jnp.stack([dt_bias, a_rate]), ((0, 6), (0, LANES - heads)))
    gain = input_norm_gain[None, :]

    blocks = T // BLOCK
    (
        normed, inverse, xin, slope, gate, x_low, bc_low, step, sgdt, step_low, decay_low, ssd, states,
    ) = call(
        forward_kernel,
        [
            ((T, D), bf16), ((T, LANES), f32), ((T + 8, width), f32), ((T, width), bf16), ((T, inner), f32),
            ((T, inner), bf16), ((T, pair), bf16), ((T, LANES), f32), ((T, LANES), f32),
            ((T, LANES), bf16), ((T, LANES), bf16), ((T, inner), bf16), ((blocks, STATE, inner), bf16),
        ],
        [
            ((T, LANES), jnp.int32), ((LANES, inner), bf16), ((T, LANES), f32), ((STATE, inner), f32),
            ((BLOCK, inner), bf16), ((BLOCK, inner), f32), ((BLOCK, BLOCK), f32),
        ],
        1, starts, tokens, gain, wxd, wz, taps, dpar,
    )
    gnorm, stat = call(
        gate_kernel,
        [((T, inner), f32), ((T, LANES), f32)],
        [],
        0, cotangent, wout, gate, ssd, x_low, crow,
    )
    stat = jnp.pad(lax.psum(stat[:, :8], "mp"), ((0, 0), (0, LANES - 8)))
    branch, dwout, dwz, low_gate, gs, sums = call(
        functools.partial(middle_kernel, width=inner * group),
        [
            ((T, D), bf16), ((inner, D), bf16), ((D, inner), bf16), ((T, inner), bf16), ((T, inner), bf16),
            ((16, inner), f32),
        ],
        [((T, inner), bf16)],
        0, cotangent, wout, normed, gate, x_low, ssd, gnorm, crow, stat,
    )
    low_xd, csums, dsums = call(
        backward_kernel,
        [((T, wide), bf16), ((8 * CONV + 8, width), f32), ((16, LANES), f32)],
        [
            ((T, LANES), jnp.int32), ((T, LANES), jnp.int32), ((LANES, inner), bf16), ((T + 8, width), f32),
            ((STATE, inner), f32), ((BLOCK, inner), bf16), ((BLOCK, inner), f32), ((BLOCK, BLOCK), f32),
            ((BLOCK, BLOCK), f32),
        ],
        1, starts, xin, slope, x_low, bc_low, step, sgdt, step_low, decay_low, ssd, states, gs, taps, crow,
        dpar,
    )
    dwxd, gfull, rowdot = call(
        last_kernel,
        [((D, wide), bf16), ((T, D), bf16), ((T, LANES), f32)],
        [],
        0, tokens, inverse, gain, normed, low_gate, low_xd, wz, wxd,
    )

    def scatter(v, axis, dim):
        return lax.psum_scatter(v, axis, scatter_dimension=dim, tiled=True)

    token_own = lax.dynamic_slice_in_dim(tokens, rank * own, own, 1).astype(f32)
    output = (token_own + scatter(branch, "mp", 1).astype(f32)).astype(bf16)
    w_out_grad = scatter(dwout, "dp", 1).astype(f32)
    w_z_grad = scatter(dwz, "dp", 0).astype(f32)
    dwxd_own = scatter(dwxd, "dp", 0)
    w_x_grad = dwxd_own[:, :inner].astype(f32)
    w_dt_grad = dwxd_own[:, width : width + heads].astype(f32)
    w_bc_grad = scatter(dwxd_own[:, inner:width], "mp", 1).astype(f32)

    g_own = scatter(gfull, "mp", 1).astype(f32)
    gain_own = lax.dynamic_slice_in_dim(input_norm_gain, rank * own, own, 0)
    row_mean = (lax.psum(rowdot[:, 0], "mp") / D)[:, None]
    inv = inverse[:, :1]
    hat = token_own * inv
    cot_own = lax.dynamic_slice_in_dim(cotangent, rank * own, own, 1).astype(f32)
    input_grad = (cot_own + inv * (g_own * gain_own - hat * row_mean)).astype(bf16)
    in_gain = jnp.sum(g_own * hat, axis=0)

    csums = jnp.sum(csums.reshape(CONV + 1, 8, width), axis=1)
    sums = jnp.sum(sums.reshape(2, 8, inner), axis=1)
    dsums = jnp.sum(dsums.reshape(2, 8, LANES), axis=1)[:, :heads]
    csums_bc = scatter(csums[:, inner:], "mp", 1)
    conv_grad, conv_bc_grad, sums, dsums, in_gain = lax.psum(
        (csums[:, :inner], csums_bc, sums, dsums, in_gain), "dp"
    )
    d_skip_grad = jnp.sum(sums[1].reshape(heads, HEADDIM), axis=1)
    return (
        output, input_grad, w_z_grad, w_x_grad, w_bc_grad, w_dt_grad, w_out_grad,
        conv_grad[:CONV], conv_grad[CONV], conv_bc_grad[:CONV], conv_bc_grad[CONV],
        dsums[0], dsums[1], d_skip_grad, in_gain, sums[0],
    )


def per_device(
    tokens, cotangent, doc_lengths, w_z, w_x, w_bc, w_dt, w_out, conv_x, conv_x_bias, conv_bc,
    conv_bc_bias, dt_bias, a_rate, d_skip, input_norm_gain, out_gain,
):
    group, size = lax.axis_size("mp"), lax.axis_size("dp")
    T, D = tokens.shape
    shard, inner = w_x.shape
    heads, per = w_dt.shape[1], w_bc.shape[1]
    pair = per * group
    width = inner + pair
    wide = width + LANES
    own = D // group
    columns = w_out.shape[1]
    blocks = T // BLOCK
    messages = blocks * (group - 1)

    def row(v):
        return v[None, :]

    (
        normed, _, _, _, low_gate, low_xd, output, w_out_grad, inverse, part, csums, dsums, sums, rows, colacc,
    ) = call(
        trunk_kernel,
        [
            ((T, D), bf16), ((T + 8, width), f32), ((D, inner), bf16), ((D, inner), bf16), ((T, inner), bf16),
            ((T, wide), bf16), ((T, own), bf16), ((inner, columns), f32), ((T, LANES), f32), ((T, D), bf16),
            ((8 * CONV + 8, width), f32), ((16, LANES), f32), ((16, inner), f32), ((T // LANES, LANES), f32),
            ((8, D), f32),
        ],
        [
            ((8 * CONV + 8, width), f32), ((16, LANES), f32), ((16, inner), f32), ((T // LANES, LANES), f32),
            ((8, D), f32),
            ((T, D), bf16), ((inner, columns), f32), ((T, D), bf16), ((T + 8, width), f32),
            ((T + 8, width), f32), ((T, width), bf16), ((2 * T, inner), bf16),
            ((blocks, STATE, inner), bf16), ((D, inner), bf16), ((pair + LANES, D), bf16),
            ((D, inner), bf16), ((inner, D), bf16),
            ((T, pair), bf16), ((T, LANES), bf16), ((T, LANES), bf16), ((T, LANES), f32),
            ((8, width), f32), ((8, inner), f32), ((8, LANES), f32),
            ((group, per, shard), bf16), ((group, 8, LANES), f32), ((group, T // LANES, LANES), f32),
            ((group, T // LANES, LANES), f32), ((T, LANES), f32), ((LANES, BLOCK), f32),
            ((T, LANES), jnp.int32), ((T, LANES), jnp.int32), ((LANES, inner), bf16), ((T, LANES), f32),
            ((STATE, inner), f32), ((BLOCK, inner), bf16), ((BLOCK, inner), f32), ((BLOCK, BLOCK), f32),
            ((BLOCK, BLOCK), f32), ((2 * blocks, BLOCK, own), bf16),
            ((4, inner, columns), bf16), ((2, inner // 2, columns), bf16), ((2, inner, columns), bf16),
        ],
        0, doc_lengths, tokens, cotangent, w_x, w_z, w_out, w_bc.T, w_dt.T, conv_x, row(conv_x_bias), conv_bc,
        row(conv_bc_bias), row(dt_bias), row(a_rate), row(d_skip), row(input_norm_gain), row(out_gain),
        places="s" + "a" * 5 + "v" * 11,
        sems=[
            (13,), (13,), (group,), (group, 2), (blocks, 2), (4, 6), (4, 6), (4, 4), (4, 4), (4 * group - 4,), (4 * group - 4,),
            (2, messages), (2, messages), (4,), (4,), (4,), (4,),
        ],
        collective=0,
        far=15,
    )
    w_z_grad, w_x_grad, input_grad, w_bc_grad, w_dt_grad, *small_grads = call(
        input_kernel,
        [
            ((shard, inner), f32), ((shard, inner), f32), ((T, own), bf16), ((per, shard), f32),
            ((heads, shard), f32), ((CONV, inner), f32), ((1, inner), f32), ((CONV, per), f32), ((1, per), f32),
            ((1, heads), f32), ((1, heads), f32), ((1, heads), f32), ((1, own), f32), ((1, inner), f32),
        ],
        [
            ((per, shard), f32), ((heads, shard), f32), ((CONV, inner), f32), ((1, inner), f32), ((CONV, per), f32),
            ((1, per), f32), ((1, heads), f32), ((1, heads), f32), ((1, heads), f32), ((1, own), f32),
            ((1, inner), f32),
            ((shard, inner), f32), ((shard, wide), f32), ((T, own), bf16), ((8, width + D // 8), f32),
            ((LANES, inner), bf16), ((pair, shard), f32), ((pair, shard), bf16), ((group - 1, per, shard), bf16),
            ((T, LANES), f32), ((T, D), bf16), ((T, inner), bf16), ((T, wide), bf16), ((T, own), bf16),
            ((T, own), bf16), ((8, D), f32), ((8 * CONV + 8, width), f32), ((16, inner), f32), ((16, LANES), f32),
            ((T, D), bf16), ((2, messages, BLOCK, own), bf16), ((BLOCK, own), f32),
            ((D, inner), bf16), ((4, shard, inner), bf16), ((2, shard // 2, inner), bf16), ((2, shard, inner), bf16),
            ((D, wide), bf16), ((4, shard, wide), bf16), ((2, shard // 2, wide), bf16), ((2, shard, wide), bf16),
            ((group, T // LANES, LANES), f32), ((size - 1, 8, width + D // 8), f32),
            ((group - 1, 8, pair + D // 8), f32), ((LANES, BLOCK), f32),
        ],
        0, tokens, inverse, row(input_norm_gain), normed, low_gate, low_xd, part, cotangent, rows, colacc, csums,
        sums, dsums,
        places="aav" + "a" * 10,
        sems=[
            (24,), (group,), (blocks,), (2, messages), (2, messages), (4,), (4,), (4,), (4,), (4,), (4,), (4,), (4,),
            (group - 1,), (group - 1,), (size - 1,), (size - 1,), (group - 1,), (group - 1,),
            (group - 1,), (group - 1,),
        ],
        collective=2,
        far=14,
    )
    (
        output, input_grad, w_z_grad, w_x_grad, w_bc_grad, w_dt_grad, w_out_grad, conv_x_grad, conv_x_bias_grad,
        conv_bc_grad, conv_bc_bias_grad, dt_bias_grad, a_rate_grad, d_skip_grad, in_gain_grad, out_gain_grad,
    ) = hand_on(output, input_grad, w_z_grad, w_x_grad, w_bc_grad, w_dt_grad, w_out_grad, *small_grads)
    return (
        output, input_grad, w_z_grad, w_x_grad, w_bc_grad.T, w_dt_grad.T, w_out_grad,
        conv_x_grad, conv_x_bias_grad[0], conv_bc_grad, conv_bc_bias_grad[0], dt_bias_grad[0], a_rate_grad[0],
        d_skip_grad[0], in_gain_grad[0], out_gain_grad[0],
    )


def solution(mesh):
    row, block, column = P("dp", None), P("dp", "mp"), P("mp")
    return jax.shard_map(
        per_device if (mesh.shape["dp"], mesh.shape["mp"]) == (8, 4) else per_device_any,
        mesh=mesh,
        in_specs=(
            row, row, row, block, block, block, block, P("mp", "dp"), P(None, "mp"), column,
            P(None, "mp"), column, column, column, column, P(), column,
        ),
        out_specs=(
            block, block, block, block, block, block, P("mp", "dp"), P(None, "mp"), column,
            P(None, "mp"), column, column, column, column, column, column,
        ),
        check_vma=False,
    )
```
